32 devices in a mesh: dp: 8 (over z, x), tensor: 4 (over y, core).
Axes of the slice: x: 2, y: 2, z: 4, core: 2. Of those that a mesh axis runs over, the one named last changes fastest.
Arguments:
- tokens: bfloat16 [16384, 1024], P(('dp', 'tensor')), may hold values from -6 to 6
- out_grad: bfloat16 [16384, 1024], P(('dp', 'tensor')), may hold values from -6 to 6
- seq_lengths: int32 [16], P('dp'), may hold values from 256 to 1024, as said below
- norm_gains: float32 [2, 1024], replicated, may hold values from 0.25 to 1.75
- row_biases: float32 [4, 1024], replicated, may hold values from -1.5 to 1.5
- qkv_weight: bfloat16 [1024, 3072], P('dp', 'tensor'), may hold values from -0.1875 to 0.1875
- qkv_bias: float32 [3072], P('tensor'), may hold values from -2.5 to 2.5
- dense_weight: bfloat16 [1024, 1024], P('tensor', 'dp'), may hold values from -0.75 to 0.75
- fc1_weight: bfloat16 [1024, 4096], P('dp', 'tensor'), may hold values from -0.1875 to 0.1875
- fc1_bias: float32 [4096], P('tensor'), may hold values from -2.5 to 2.5
- fc2_weight: bfloat16 [4096, 1024], P('tensor', 'dp'), may hold values from -0.09375 to 0.09375
- block_slot: int32 [768], replicated, may hold values from 0 to 767, as said below
- left_stat: float32 [768, 128, 128], P(('dp', 'tensor'))
- right_stat: float32 [768, 128, 128], P(('dp', 'tensor'))
- left_root: float32 [768, 128, 128], P(('dp', 'tensor'))
- right_root: float32 [768, 128, 128], P(('dp', 'tensor'))
- row_accum: float32 [6, 1024], replicated, may hold values from 0.5 to 2
- qkv_bias_accum: float32 [3072], P('tensor'), may hold values from 0.5 to 2
- fc1_bias_accum: float32 [4096], P('tensor'), may hold values from 0.5 to 2
Outputs:
- layer_out: bfloat16 [16384, 1024], P(('dp', 'tensor'))
- input_grad: float32 [16384, 1024], P(('dp', 'tensor'))
- block_grad: float32 [768, 128, 128], P(('dp', 'tensor'))
- left_new: float32 [768, 128, 128], P(('dp', 'tensor'))
- right_new: float32 [768, 128, 128], P(('dp', 'tensor'))
- block_update: float32 [768, 128, 128], P(('dp', 'tensor'))
- row_accum_new: float32 [6, 1024], replicated
- row_update: float32 [6, 1024], replicated
- qkv_bias_accum_new: float32 [3072], P('tensor')
- qkv_bias_update: float32 [3072], P('tensor')
- fc1_bias_accum_new: float32 [4096], P('tensor')
- fc1_bias_update: float32 [4096], P('tensor')
The draws below stay inside these ranges and needn't reach their ends.
Inputs may be any that keep to these rules, and one draw needn't show every extreme that they name: `seq_lengths`: some sequence has exactly 1024 real tokens. `block_slot`: a permutation of the 768 slots; block t * 192 + j gets a slot s for which (s // 24) modulo the tensor axis's size is t.
All inputs are finite; a program needn't handle non-finite values.
Results may differ from the reference program's by a relative error of at most 0.0088.
Values may be sent and summed in bfloat16 or wider, within the bound.
A program may use at most 192 MiB of HBM per device.

```python
import math
import jax
import jax.numpy as jnp
from jax import lax

D = 1024
HEADS = 16
HEAD = 64
ROT = 16
FF = 4096
LEN = 1024
BLOCK = 128
SEQS = 16
TOKENS = 16384
BLK_T = 192
BLOCKS = 768
N_TENSOR = 4
DEVICES = 32


def draw_seq_lengths(key, part):
    drawn = jax.random.randint(jax.random.fold_in(key, 1), (SEQS,), LEN // 4, LEN + 1)
    chosen = jax.random.randint(jax.random.fold_in(key, 2), (), 0, SEQS)
    return jnp.where(jnp.arange(SEQS) == chosen, LEN, drawn).astype(jnp.int32)


def draw_block_slot(key, part):
    per_dev = BLOCKS // DEVICES
    pieces = []
    for tensor_pos in range(N_TENSOR):
        ranking = jax.random.permutation(jax.random.fold_in(jax.random.fold_in(key, 3), tensor_pos), BLK_T)
        slot_ids = (ranking // per_dev * N_TENSOR + tensor_pos) * per_dev + ranking % per_dev
        pieces.append(slot_ids)
    return jnp.concatenate(pieces).astype(jnp.int32)


def symmetric_draw(key, diag_lo, diag_hi, spread):
    diagonal_part = jnp.exp(jax.random.uniform(jax.random.fold_in(key, 1), (BLOCKS, BLOCK), minval=math.log(diag_lo), maxval=math.log(diag_hi)))
    noise_part = jnp.clip(jax.random.normal(jax.random.fold_in(key, 2), (BLOCKS, BLOCK, BLOCK)), -4.0, 4.0)
    symmetric = (noise_part + jnp.swapaxes(noise_part, 1, 2)) * (spread / math.sqrt(2.0))
    identity = jnp.eye(BLOCK, dtype=jnp.float32)
    return (symmetric * (1.0 - identity) + diagonal_part[:, :, None] * identity).astype(jnp.float32)


def draw_left_stat(key, part):
    return symmetric_draw(jax.random.fold_in(key, 11), 0.5 * BLOCK, 1.5 * BLOCK, 0.22 * math.sqrt(BLOCK))


def draw_right_stat(key, part):
    return symmetric_draw(jax.random.fold_in(key, 12), 0.5 * BLOCK, 1.5 * BLOCK, 0.22 * math.sqrt(BLOCK))


def draw_left_root(key, part):
    return symmetric_draw(jax.random.fold_in(key, 13), 0.5, 2.0, 0.3 / math.sqrt(BLOCK))


def draw_right_root(key, part):
    return symmetric_draw(jax.random.fold_in(key, 14), 0.5, 2.0, 0.3 / math.sqrt(BLOCK))


def shard_levels(own_key, extent, cuts, least, top_value):
    level = 1.0
    for dim, shards_of in cuts:
        steps = jax.random.uniform(jax.random.fold_in(jax.random.fold_in(own_key, 6), dim), (shards_of,), jnp.float32, least / len(cuts), top_value / len(cuts))
        level = level * jnp.repeat(jnp.exp(steps), extent[dim] // shards_of).reshape((-1,) + (1,) * (len(extent) - 1 - dim))
    return level


def scatter_about(stream_key, extent, scale, most, cuts=(), held_as=jnp.bfloat16):
    entries = scale * jax.random.normal(stream_key, extent, jnp.float32)
    if cuts:
        entries = entries * shard_levels(stream_key, extent, cuts, -0.22, 0.18)
    return jnp.clip(entries, -most, most).astype(held_as)


def setup_inputs(seed: int = 0) -> dict:
    key_list = jax.random.split(jax.random.key(seed), 20)
    tokens = scatter_about(key_list[0], (TOKENS, D), 1.0, 6.0, ((0, 32),))
    out_grad = scatter_about(key_list[1], (TOKENS, D), 1.0, 6.0, ((0, 32),))
    seq_lengths = draw_seq_lengths(jax.random.fold_in(key_list[19], 71), 0)
    norm_gains = jnp.clip(1.0 + 0.15 * jax.random.normal(key_list[3], (2, D), jnp.float32), 0.25, 1.75)
    row_biases = scatter_about(key_list[4], (4, D), 0.3, 1.5, (), jnp.float32)
    qkv_weight = scatter_about(key_list[5], (D, 3 * D), D ** -0.5, 0.1875, ((0, 8), (1, 4)))
    qkv_bias = scatter_about(key_list[6], (3 * D,), 0.5, 2.5, ((0, 4),), jnp.float32)
    dense_weight = scatter_about(key_list[7], (D, D), HEAD ** -0.5, 0.75, ((0, 4), (1, 8)))
    fc1_weight = scatter_about(key_list[8], (D, FF), D ** -0.5, 0.1875, ((0, 8), (1, 4)))
    fc1_bias = scatter_about(key_list[9], (FF,), 0.5, 2.5, ((0, 4),), jnp.float32)
    fc2_weight = scatter_about(key_list[10], (FF, D), FF ** -0.5, 0.09375, ((0, 4), (1, 8)))
    block_slot = draw_block_slot(jax.random.fold_in(key_list[19], 71), 0)
    left_stat = draw_left_stat(jax.random.fold_in(key_list[19], 71), 0)
    right_stat = draw_right_stat(jax.random.fold_in(key_list[19], 71), 0)
    left_root = draw_left_root(jax.random.fold_in(key_list[19], 71), 0)
    right_root = draw_right_root(jax.random.fold_in(key_list[19], 71), 0)
    row_accum = jnp.clip(jnp.exp(jax.random.uniform(key_list[16], (6, D), jnp.float32, math.log(0.5), math.log(2.0))), 0.5, 2.0)
    qkv_bias_accum = jnp.clip(jnp.exp(math.log(2.0) - 1.3862944 * jax.random.uniform(key_list[17], (3 * D,), jnp.float32) ** shard_levels(key_list[17], (3 * D,), ((0, 4),), -0.2, 0.2)), 0.5, 2.0)
    fc1_bias_accum = jnp.clip(jnp.exp(math.log(2.0) - 1.3862944 * jax.random.uniform(key_list[18], (FF,), jnp.float32) ** shard_levels(key_list[18], (FF,), ((0, 4),), -0.2, 0.2)), 0.5, 2.0)
    return dict(tokens=tokens, out_grad=out_grad, seq_lengths=seq_lengths, norm_gains=norm_gains, row_biases=row_biases, qkv_weight=qkv_weight, qkv_bias=qkv_bias, dense_weight=dense_weight, fc1_weight=fc1_weight, fc1_bias=fc1_bias, fc2_weight=fc2_weight, block_slot=block_slot, left_stat=left_stat, right_stat=right_stat, left_root=left_root, right_root=right_root, row_accum=row_accum, qkv_bias_accum=qkv_bias_accum, fc1_bias_accum=fc1_bias_accum)


@jax.custom_vjp
def low(v):
    return lax.optimization_barrier(v.astype(jnp.bfloat16)).astype(jnp.float32)

@jax.custom_vjp
def low_back(v):
    return v

def low_keep(v):
    return (low(v), None)

def low_pass(kept, grad):
    return (grad,)

def back_keep(v):
    return (v, None)

def back_low(kept, grad):
    return (low(grad),)
low.defvjp(low_keep, low_pass)
low_back.defvjp(back_keep, back_low)
highest = lax.Precision.HIGHEST
masked_score = -1e+30
shampoo_rate = 0.03
adagrad_rate = 0.1
stat_decay = 0.5

def layer_norm(values, gain_vec, shift_vec):
    average = lax.optimization_barrier(jnp.mean(values, axis=-1, keepdims=True))
    centered = values - average
    variance = lax.optimization_barrier(jnp.mean(centered * centered, axis=-1, keepdims=True))
    return centered * lax.rsqrt(variance + 1e-05) * gain_vec + shift_vec

def rotary_tables():
    half_rot = ROT // 2
    exponent = jnp.arange(half_rot, dtype=jnp.float32) * (2.0 / ROT)
    inverse = jnp.power(10000.0, -exponent)
    angles = jnp.arange(LEN, dtype=jnp.float32)[:, None] * inverse[None, :]
    return (jnp.cos(angles), jnp.sin(angles))

def apply_rotary(vectors, cosine, sine):
    half_rot = ROT // 2
    first_half = vectors[..., :half_rot]
    second = vectors[..., half_rot:ROT]
    cos_wide = cosine[:, None, :]
    sin_wide = sine[:, None, :]
    rot_first = first_half * cos_wide - second * sin_wide
    rot_second = second * cos_wide + first_half * sin_wide
    return jnp.concatenate([rot_first, rot_second, vectors[..., ROT:]], axis=-1)

def attention(queries, keys_all, values, limits):
    block_rows = min(512, LEN)
    score_scale = 1.0 / math.sqrt(HEAD)

    def one_block(block_index):
        block_start = block_index * block_rows
        query_block = lax.dynamic_slice_in_dim(queries, block_start, block_rows, 1)
        scores = jnp.einsum('bqhd,bkhd->bhqk', query_block, keys_all, precision=highest) * score_scale
        query_pos = block_start + jnp.arange(block_rows)
        key_pos = jnp.arange(LEN)
        allowed = (key_pos[None, None, :] <= query_pos[None, :, None]) & (key_pos[None, None, :] < limits[:, None, None])
        scores = low_back(jnp.where(allowed[:, None], scores, masked_score))
        row_max = lax.optimization_barrier(jnp.max(scores, axis=-1, keepdims=True))
        unnormed = jnp.exp(scores - row_max)
        probabilities = low(unnormed / lax.optimization_barrier(jnp.sum(unnormed, axis=-1, keepdims=True)))
        return jnp.einsum('bhqk,bkhd->bqhd', probabilities, values, precision=highest)
    blocks = lax.map(jax.checkpoint(one_block), jnp.arange(LEN // block_rows))
    return jnp.moveaxis(blocks, 0, 1).reshape(queries.shape)

def forward_batch(param_set, inputs, limits):
    gains, biases, qkv_weight, qkv_bias, dense_weight, fc1_weight, fc1_bias, fc2_weight = param_set
    batch_seqs = inputs.shape[0]
    normed_attn = low(layer_norm(inputs, gains[0], biases[0]))
    normed_mlp = low(layer_norm(inputs, gains[1], biases[1]))
    projected = low_back(jnp.einsum('bld,de->ble', normed_attn, qkv_weight, precision=highest) + qkv_bias)
    shaped = projected.reshape(batch_seqs, LEN, HEADS, 3 * HEAD)
    cosine, sine = rotary_tables()
    queries = low(apply_rotary(shaped[..., :HEAD], cosine, sine))
    keys_all = low(apply_rotary(shaped[..., HEAD:2 * HEAD], cosine, sine))
    values = low(shaped[..., 2 * HEAD:])
    context = attention(queries, keys_all, values, limits).reshape(batch_seqs, LEN, D)
    context = low(low_back(context))
    attn_part = jnp.einsum('blc,cd->bld', context, dense_weight, precision=highest)
    hidden_pre = low_back(jnp.einsum('bld,df->blf', normed_mlp, fc1_weight, precision=highest) + fc1_bias)
    activated = low(jax.nn.gelu(hidden_pre, approximate=False))
    mlp_part = jnp.einsum('blf,fd->bld', activated, fc2_weight, precision=highest)
    branches = low_back(attn_part + mlp_part)
    return inputs + branches + biases[2] + biases[3]

def cut_blocks(matrix):
    rows_all, cols_all = matrix.shape
    shaped = matrix.reshape(rows_all // BLOCK, BLOCK, cols_all // BLOCK, BLOCK)
    return shaped.transpose(0, 2, 1, 3).reshape(-1, BLOCK, BLOCK)

def shampoo_step(grad_blocks, left_old, right_old, left_inv, right_inv):
    left_next = stat_decay * left_old + (1.0 - stat_decay) * jnp.einsum('sij,skj->sik', grad_blocks, grad_blocks, precision=highest)
    right_next = stat_decay * right_old + (1.0 - stat_decay) * jnp.einsum('sji,sjk->sik', grad_blocks, grad_blocks, precision=highest)
    pushed = jnp.einsum('sij,sjk->sik', left_inv, grad_blocks, precision=highest)
    change = -shampoo_rate * jnp.einsum('sij,sjk->sik', pushed, right_inv, precision=highest)
    return (left_next, right_next, change)

def adagrad_step(grad_vec, accum):
    accum_next = accum + grad_vec * grad_vec
    return (accum_next, -adagrad_rate * grad_vec * lax.rsqrt(accum_next))

def reference(tokens, out_grad, seq_lengths, norm_gains, row_biases, qkv_weight, qkv_bias, dense_weight, fc1_weight, fc1_bias, fc2_weight, block_slot, left_stat, right_stat, left_root, right_root, row_accum, qkv_bias_accum, fc1_bias_accum):
    param_set = (norm_gains.astype(jnp.float32), row_biases.astype(jnp.float32), qkv_weight.astype(jnp.float32), qkv_bias.astype(jnp.float32), dense_weight.astype(jnp.float32), fc1_weight.astype(jnp.float32), fc1_bias.astype(jnp.float32), fc2_weight.astype(jnp.float32))
    per_step = max(1, min(SEQS, 4096 // LEN))
    while SEQS % per_step != 0:
        per_step -= 1
    step_count = SEQS // per_step
    inputs_all = tokens.astype(jnp.float32).reshape(step_count, per_step, LEN, D)
    cot_all = out_grad.astype(jnp.float32).reshape(step_count, per_step, LEN, D)
    limit_all = seq_lengths.reshape(step_count, per_step)

    def batch_step(carry, batch_items):
        inputs, cotangent, limits = batch_items
        outputs, pullback = jax.vjp(lambda params_now, inputs_now: forward_batch(params_now, inputs_now, limits), param_set, inputs)
        valid = (jnp.arange(LEN)[None, :] < limits[:, None]).astype(jnp.float32)
        param_grads, input_grads = pullback(cotangent * valid[:, :, None])
        carry = jax.tree.map(lambda total, extra: total + extra, carry, param_grads)
        return (carry, (outputs, input_grads))
    zero_grads = jax.tree.map(jnp.zeros_like, param_set)
    grads, (outputs, input_grads) = lax.scan(batch_step, zero_grads, (inputs_all, cot_all, limit_all))
    gain_grads, bias_grads, qkv_grad, qkv_bias_grad, dense_grad, fc1_grad, fc1_bias_grad, fc2_grad = grads
    grad_scale = 1.0 / math.sqrt(TOKENS)
    qkv_cols = 3 * D // N_TENSOR
    attn_rows = D // N_TENSOR
    hidden_cols = FF // N_TENSOR
    pieces = []
    for tensor_pos in range(N_TENSOR):
        pieces.append(cut_blocks(qkv_grad[:, tensor_pos * qkv_cols:(tensor_pos + 1) * qkv_cols]))
        pieces.append(cut_blocks(dense_grad[tensor_pos * attn_rows:(tensor_pos + 1) * attn_rows, :]))
        pieces.append(cut_blocks(fc1_grad[:, tensor_pos * hidden_cols:(tensor_pos + 1) * hidden_cols]))
        pieces.append(cut_blocks(fc2_grad[tensor_pos * hidden_cols:(tensor_pos + 1) * hidden_cols, :]))
    block_grads = jnp.concatenate(pieces, axis=0) * grad_scale
    slot_grads = block_grads[jnp.argsort(block_slot)]
    left_next, right_next, change = shampoo_step(slot_grads, left_stat, right_stat, left_root, right_root)
    row_grads = jnp.concatenate([gain_grads, bias_grads], axis=0) * grad_scale
    row_next, row_change = adagrad_step(row_grads, row_accum)
    qkv_next, qkv_change = adagrad_step(qkv_bias_grad * grad_scale, qkv_bias_accum)
    fc1_next, fc1_change = adagrad_step(fc1_bias_grad * grad_scale, fc1_bias_accum)
    layer_out = outputs.reshape(TOKENS, D).astype(jnp.bfloat16)
    input_grad = input_grads.reshape(TOKENS, D)
    return (layer_out, input_grad, slot_grads, left_next, right_next, change, row_next, row_change, qkv_next, qkv_change, fc1_next, fc1_change)
```

```python
import functools
import math

import jax
import jax.numpy as jnp
import numpy as np
from jax import lax
from jax.experimental import pallas as pl
from jax.experimental.pallas import tpu as pltpu
from jax.sharding import PartitionSpec as P

HEAD = 64
ROT = 16
LEN = 1024
BLOCK = 128
TILE = 256
MESH = pl.DeviceIdType.MESH
VMEM_LIMIT = 60 * 1024 * 1024

highest = lax.Precision.HIGHEST
masked_score = -1e30
shampoo_rate = 0.03
adagrad_rate = 0.1
stat_decay = 0.5
f32 = jnp.float32
bf16 = jnp.bfloat16


def adagrad_step(grad_vec, accum):
    accum_next = accum + grad_vec * grad_vec
    return (accum_next, -adagrad_rate * grad_vec * lax.rsqrt(accum_next))


def rotary_wide():
    half = ROT // 2
    inverse = np.power(np.float32(10000.0), -(np.arange(half, dtype=np.float32) * np.float32(2.0 / ROT)))
    angles = np.arange(LEN, dtype=np.float32)[:, None] * inverse.astype(np.float32)[None, :]
    cosine, sine = np.cos(angles), np.sin(angles)
    rest = HEAD - ROT
    cos_one = np.concatenate([cosine, cosine, np.ones((LEN, rest), np.float32)], axis=1)
    sin_one = np.concatenate([-sine, sine, np.zeros((LEN, rest), np.float32)], axis=1)
    wide = np.concatenate([cos_one, cos_one, sin_one, sin_one], axis=1)
    return wide.astype(np.float32)


def ring_place(me, count):
    low, high = me % 2, me // 2
    return low * (count - 1 - high) + (1 - low) * high


def ring_device(place, count):
    upper = place // (count // 2)
    return (1 - upper) * (2 * place) + upper * (2 * (count - 1 - place) + 1)


def hop_count(half, way, count):
    far = count // 2
    return far if half == way else far - 1


def for_hops(first, last, body, count):
    if count <= 8:
        for hop in range(first, last):
            body(hop)
    elif last > first:

        @pl.loop(first, last)
        def _(hop):
            body(hop)


class Ring:
    def __init__(self, count):
        self.count = count
        self.me = lax.axis_index("dp")
        self.tensor = lax.axis_index("tensor")
        self.place = ring_place(self.me, count)
        self.peer = [
            (ring_device((self.place + step) % count, count), self.tensor) for step in (1, count - 1)
        ]

    def at(self, offset):
        return ring_device((self.place + offset + 2 * self.count) % self.count, self.count)


class Gather:
    def __init__(self, ring, locals_, fulls, send, recv):
        self.ring, self.locals, self.fulls, self.send, self.recv = ring, locals_, fulls, send, recv
        self.far = ring.count // 2

    def part(self, ref, w, half, owner=None):
        rows, cols = self.locals[w].shape
        base = 0 if owner is None else owner * rows
        if rows % 32 == 0:
            return ref.at[pl.ds(pl.multiple_of(base + half * (rows // 2), 16), rows // 2)]
        return ref.at[pl.ds(base, rows), pl.ds(half * (cols // 2), cols // 2)]

    def sem(self, w, half, way, hop):
        return ((w * 2 + half) * 2 + way) * self.far + hop - 1

    def copy(self, w, half, way, hop, source):
        owner = self.ring.at((1 - hop) if way == 0 else (hop - 1))
        src = self.part(self.locals[w], w, half) if source else self.part(self.fulls[w], w, half, owner)
        return pltpu.make_async_remote_copy(
            src_ref=src,
            dst_ref=self.part(self.fulls[w], w, half, owner),
            send_sem=self.send.at[self.sem(w, half, way, hop)],
            recv_sem=self.recv.at[self.sem(w, half, way, hop)],
            device_id=self.ring.peer[way],
            device_id_type=MESH,
        )

    def arrival(self, w, half, way, hop):
        owner = self.ring.at(-hop if way == 0 else hop)
        dst = self.part(self.fulls[w], w, half, owner)
        return pltpu.make_async_remote_copy(
            src_ref=dst,
            dst_ref=dst,
            send_sem=self.send.at[self.sem(w, half, way, hop)],
            recv_sem=self.recv.at[self.sem(w, half, way, hop)],
            device_id=self.ring.peer[way],
            device_id_type=MESH,
        )

    def begin(self, w):
        for half in range(2):
            for way in range(2):
                if hop_count(half, way, self.ring.count) >= 1:
                    self.copy(w, half, way, 1, True).start()

    def forward(self, w, hop, last):
        for half in range(2):
            for way in range(2):
                hops = self.far if half == way else self.far - 1
                if last and hops != self.far:
                    continue
                self.arrival(w, half, way, hop).wait_recv()
                if not last:
                    more = self.far if half == way else self.far - 1
                    if more == self.far:
                        self.copy(w, half, way, hop + 1, False).start()
                    else:

                        @pl.when(hop + 1 <= more)
                        def _():
                            self.copy(w, half, way, hop + 1, False).start()

    def finish(self, w):
        for half in range(2):
            for way in range(2):
                hops = hop_count(half, way, self.ring.count)
                if hops >= 1:
                    self.copy(w, half, way, 1, True).wait_send()
                for_hops(
                    2, hops + 1, lambda hop: self.copy(w, half, way, hop, False).wait_send(), self.ring.count
                )


class Rows:
    def __init__(self, local, full, send, recv, own):
        self.tensor = lax.axis_index("tensor")
        self.dp = lax.axis_index("dp")
        self.near = self.tensor + 1 - 2 * (self.tensor % 2)
        self.across = (self.tensor + 2) % 4
        self.local, self.full, self.send, self.recv, self.own = local, full, send, recv, own
        self.rows = local.shape[0]

    def slot(self, owner, piece=None):
        if piece is None:
            return self.full.at[pl.ds(pl.multiple_of(owner * self.rows, 16), self.rows)]
        half = self.rows // 2
        return self.full.at[pl.ds(pl.multiple_of(owner * self.rows + piece * half, 16), half)]

    def remote(self, src, dst, sem, device):
        return pltpu.make_async_remote_copy(
            src_ref=src,
            dst_ref=dst,
            send_sem=self.send.at[sem],
            recv_sem=self.recv.at[sem],
            device_id=(self.dp, device),
            device_id_type=MESH,
        )

    def keep(self):
        return pltpu.make_async_copy(self.local, self.slot(self.tensor), self.own)

    def pair(self):
        return self.remote(self.local, self.slot(self.tensor), 0, self.near)

    def cross(self, piece):
        half = self.rows // 2
        return self.remote(
            self.local.at[pl.ds(piece * half, half)], self.slot(self.tensor, piece), 1 + piece, self.across
        )

    def onward(self, piece):
        here = self.slot(self.across, piece)
        return self.remote(here, here, 3 + piece, self.near)

    def begin_near(self):
        self.keep().start()
        self.pair().start()

    def begin_cross(self):
        for piece in range(2):
            self.cross(piece).start()

    def pass_on(self):
        for piece in range(2):
            self.cross(piece).wait_recv()
            self.onward(piece).start()

    def finish(self):
        self.keep().wait()
        self.pair().wait()
        for piece in range(2):
            self.cross(piece).wait_send()
            self.onward(piece).wait()


def greet(devices):
    barrier = pltpu.get_barrier_semaphore()
    for device in devices:
        pl.semaphore_signal(barrier, inc=1, device_id=device, device_id_type=MESH)
    pl.semaphore_wait(barrier, len(devices))


def gather_kernel(count, x, dy, wq, wd, w1, w2, xf, dyf, wqf, wdf, w1f, w2f, rs, rr, ro, gs, gr, go):
    ring = Ring(count)
    locals_, fulls = (wq, wd, w1, w2), (wqf, wdf, w1f, w2f)
    gather = Gather(ring, locals_, fulls, gs, gr)
    rx = Rows(x, xf, rs.at[0], rr.at[0], ro.at[0])
    ry = Rows(dy, dyf, rs.at[1], rr.at[1], ro.at[1])
    greet([ring.peer[0], ring.peer[1], (ring.me, rx.near), (ring.me, rx.across)])
    gather.begin(0)
    rx.begin_cross()
    rx.begin_near()
    ry.begin_near()
    own = []
    for w in range(4):
        rows = locals_[w].shape[0]
        own.append(
            pltpu.make_async_copy(
                locals_[w], fulls[w].at[pl.ds(pl.multiple_of(ring.me * rows, 16), rows)], go.at[w]
            )
        )
        own[-1].start()
    far = count // 2
    for w in range(4):
        for_hops(1, far, lambda hop: gather.forward(w, hop, False), count)
        if w < 3:
            gather.begin(w + 1)
        gather.forward(w, far, True)
        if w == 1:
            rx.pass_on()
            ry.begin_cross()
    ry.pass_on()
    for w in range(4):
        gather.finish(w)
        own[w].wait()
    rx.finish()
    ry.finish()


def gather_all(count, x, dy, wq, wd, w1, w2):
    far = count // 2
    outs = [jax.ShapeDtypeStruct((4 * v.shape[0], v.shape[1]), v.dtype) for v in (x, dy)]
    outs += [jax.ShapeDtypeStruct((count * v.shape[0], v.shape[1]), v.dtype) for v in (wq, wd, w1, w2)]
    moved = sum(v.size * 2 for v in outs)
    return pl.pallas_call(
        functools.partial(gather_kernel, count),
        out_shape=outs,
        in_specs=[pl.BlockSpec(memory_space=pl.ANY)] * 6,
        out_specs=[pl.BlockSpec(memory_space=pl.ANY)] * 6,
        scratch_shapes=[
            pltpu.SemaphoreType.DMA((2, 5)),
            pltpu.SemaphoreType.DMA((2, 5)),
            pltpu.SemaphoreType.DMA((2,)),
            pltpu.SemaphoreType.DMA((16 * far,)),
            pltpu.SemaphoreType.DMA((16 * far,)),
            pltpu.SemaphoreType.DMA((4,)),
        ],
        compiler_params=pltpu.CompilerParams(
            collective_id=0, has_side_effects=True, vmem_limit_bytes=VMEM_LIMIT
        ),
        cost_estimate=pl.CostEstimate(flops=0, bytes_accessed=moved, transcendentals=0),
        name="gather_all",
    )(x, dy, wq, wd, w1, w2)


def dot_nn(a, b):
    return lax.dot_general(a, b, (((1,), (0,)), ((), ())), preferred_element_type=f32)


def dot_nt(a, b):
    return lax.dot_general(a, b, (((1,), (1,)), ((), ())), preferred_element_type=f32)


def dot_tn(a, b):
    return lax.dot_general(a, b, (((0,), (0,)), ((), ())), preferred_element_type=f32)


def normed(x):
    average = jnp.mean(x, axis=-1, keepdims=True)
    centered = x - average
    variance = jnp.mean(centered * centered, axis=-1, keepdims=True)
    scale = lax.rsqrt(variance + 1e-05)
    return centered * scale, scale


def swap_halves(v):
    half = ROT // 2
    lane = lax.broadcasted_iota(jnp.int32, v.shape, 1) % HEAD
    return jnp.where(lane < half, pltpu.roll(v, v.shape[1] - half, 1), pltpu.roll(v, half, 1))


def attention_kernel(
    heads, lim_ref, x_ref, dy_ref, wq_ref, wd_ref, gain_ref, bias_ref, qb_ref, rot_ref,
    h1_ref, h2_ref, dyb_ref, ctx_ref, dproj_ref, sum_ref,
    qs, ks, vs, dcs, dqs, dks, dvs, ctxs,
):
    seq = pl.program_id(0)
    limit = lim_ref[seq]

    @pl.when(seq == 0)
    def _():
        sum_ref[...] = jnp.zeros_like(sum_ref)

    @pl.loop(0, LEN // TILE)
    def _(i):
        rows = pl.ds(pl.multiple_of(i * TILE, TILE), TILE)
        xhat, _ = normed(x_ref[rows, :].astype(f32))
        h1 = (xhat * gain_ref[0:1, :] + bias_ref[0:1, :]).astype(bf16)
        h1_ref[rows, :] = h1
        h2_ref[rows, :] = (xhat * gain_ref[1:2, :] + bias_ref[1:2, :]).astype(bf16)
        proj = dot_nn(h1, wq_ref[...]) + qb_ref[...]
        place = i * TILE + lax.broadcasted_iota(jnp.int32, (TILE, 1), 0)
        dy = jnp.where(place < limit, dy_ref[rows, :].astype(f32), 0.0)
        sum_ref[4:5, :] += jnp.sum(dy, axis=0, keepdims=True)
        dyb = dy.astype(bf16)
        dyb_ref[rows, :] = dyb
        dctx = dot_nn(dyb, wd_ref[...]).astype(bf16)
        cosine, sine = rot_ref[rows, 0:128], rot_ref[rows, 128:256]
        for h in range(heads):
            pair = proj[:, 3 * HEAD * h : 3 * HEAD * h + 2 * HEAD]
            pair = pair * cosine + swap_halves(pair) * sine
            qs[h, rows, :] = (pair[:, :HEAD].astype(bf16) * 0.125).astype(bf16)
            ks[h, rows, :] = pair[:, HEAD:].astype(bf16)
            vs[h, rows, :] = proj[:, 3 * HEAD * h + 2 * HEAD : 3 * HEAD * (h + 1)].astype(bf16)
            dcs[h, rows, :] = dctx[:, HEAD * h : HEAD * (h + 1)]

    @pl.loop(0, heads)
    def _(h):
        for i in reversed(range(LEN // TILE)):
            seen = (i + 1) * TILE
            rows = slice(i * TILE, seen)
            q, do = qs[h, rows, :], dcs[h, rows, :]
            k, v = ks[h, :seen, :], vs[h, :seen, :]
            s = dot_nt(q, k)
            col = lax.broadcasted_iota(jnp.int32, (TILE, seen), 1)
            row = lax.broadcasted_iota(jnp.int32, (TILE, seen), 0) + i * TILE
            s = jnp.where((col <= row) & (col < limit), s, masked_score)
            p = jnp.exp(s - jnp.max(s, axis=1, keepdims=True))
            p = p * (1.0 / jnp.sum(p, axis=1, keepdims=True))
            pb = p.astype(bf16)
            ctxs[h, rows, :] = dot_nn(pb, v).astype(bf16)
            dp = dot_nt(do, v)
            ds = (p * (dp - jnp.sum(p * dp, axis=1, keepdims=True))).astype(bf16)
            dqs[h, rows, :] = dot_nn(ds, k) * 0.125
            dv_part = dot_tn(pb, do)
            dk_part = dot_tn(ds, q)
            if i == LEN // TILE - 1:
                dvs[h, :, :] = dv_part
                dks[h, :, :] = dk_part
            else:
                dvs[h, :seen, :] += dv_part
                dks[h, :seen, :] += dk_part

    @pl.loop(0, LEN // TILE)
    def _(i):
        rows = pl.ds(pl.multiple_of(i * TILE, TILE), TILE)
        cosine, sine = rot_ref[rows, 0:128], rot_ref[rows, 128:256]
        for h in range(heads):
            pair = jnp.concatenate([dqs[h, rows, :], dks[h, rows, :]], axis=1)
            pair = (pair * cosine - swap_halves(pair) * sine).astype(bf16)
            low = dvs[h, rows, :].astype(bf16)
            lo = 3 * HEAD * h
            dproj_ref[rows, lo : lo + 2 * HEAD] = pair
            dproj_ref[rows, lo + 2 * HEAD : lo + 3 * HEAD] = low
            sum_ref[5:6, lo : lo + 2 * HEAD] += jnp.sum(pair.astype(f32), axis=0, keepdims=True)
            sum_ref[5:6, lo + 2 * HEAD : lo + 3 * HEAD] += jnp.sum(low.astype(f32), axis=0, keepdims=True)
            ctx_ref[rows, HEAD * h : HEAD * (h + 1)] = ctxs[h, rows, :]


def attention_all(limits, xf, dyf, wqf, wdf, gains, biases, qkv_bias, rot):
    seqs = limits.shape[0]
    width = xf.shape[1]
    heads = wqf.shape[1] // (3 * HEAD)

    def per_seq(cols):
        return pl.BlockSpec((LEN, cols), lambda s: (s, 0))

    def whole(shape):
        return pl.BlockSpec(shape, lambda s: (0, 0))

    out = lambda cols: jax.ShapeDtypeStruct((seqs * LEN, cols), bf16)
    per_head = lambda dtype: pltpu.VMEM((heads, LEN, HEAD), dtype)
    return pl.pallas_call(
        functools.partial(attention_kernel, heads),
        grid=(seqs,),
        out_shape=[
            out(width), out(width), out(width), out(heads * HEAD), out(heads * 3 * HEAD),
            jax.ShapeDtypeStruct((8, width), f32),
        ],
        in_specs=[
            pl.BlockSpec(memory_space=pltpu.SMEM),
            per_seq(width), per_seq(width), whole(wqf.shape), whole(wdf.shape), whole(gains.shape),
            whole(biases.shape), whole(qkv_bias.shape), whole(rot.shape),
        ],
        out_specs=[
            per_seq(width), per_seq(width), per_seq(width), per_seq(heads * HEAD),
            per_seq(heads * 3 * HEAD), whole((8, width)),
        ],
        scratch_shapes=[per_head(bf16)] * 4 + [per_head(f32)] * 3 + [per_head(bf16)],
        compiler_params=pltpu.CompilerParams(vmem_limit_bytes=VMEM_LIMIT),
        cost_estimate=pl.CostEstimate(flops=int(1e10), bytes_accessed=int(3e7), transcendentals=int(1e7)),
        name="attention_all",
    )(limits, xf, dyf, wqf, wdf, gains, biases, qkv_bias, rot)


def gelu_both(x):
    bell = jnp.exp(-0.5 * x * x)
    u = jnp.abs(x) * (1.0 / math.sqrt(2.0))
    t = 1.0 / (1.0 + 0.3275911 * u)
    poly = t * (0.254829592 + t * (-0.284496736 + t * (1.421413741 + t * (-1.453152027 + t * 1.061405429))))
    tail = 0.5 * poly * bell
    phi = jnp.where(x < 0.0, tail, 1.0 - tail)
    return x * phi, phi + x * bell * (1.0 / math.sqrt(2.0 * math.pi))


def rows_kernel(
    x_ref, h2_ref, dyb_ref, ctx_ref, dproj_ref, wq_ref, wd_ref, w1_ref, w2_ref, gain_ref, fb_ref,
    act_ref, dab_ref, br_ref, e_ref, sum_ref,
):
    @pl.when(pl.program_id(0) == 0)
    def _():
        sum_ref[...] = jnp.zeros_like(sum_ref)

    pre = dot_nn(h2_ref[...], w1_ref[...]) + fb_ref[...]
    act, slope = gelu_both(pre)
    act = act.astype(bf16)
    act_ref[...] = act
    dab = (dot_nn(dyb_ref[...], w2_ref[...]) * slope).astype(bf16)
    dab_ref[...] = dab
    br_ref[...] = (dot_nt(ctx_ref[...], wd_ref[...]) + dot_nt(act, w2_ref[...])).astype(bf16)
    dh2 = dot_nt(dab, w1_ref[...])
    dh1 = dot_nt(dproj_ref[...], wq_ref[...])
    xhat, _ = normed(x_ref[...].astype(f32))
    e_ref[...] = (dh1 * gain_ref[0:1, :] + dh2 * gain_ref[1:2, :]).astype(bf16)
    total = lambda v: jnp.sum(v, axis=0, keepdims=True)
    sum_ref[0:1, :] += total(dh1 * xhat)
    sum_ref[1:2, :] += total(dh2 * xhat)
    sum_ref[2:3, :] += total(dh1)
    sum_ref[3:4, :] += total(dh2)
    sum_ref[6:7, :] += total(dab.astype(f32))


def rows_all(xf, h2, dyb, ctx, dproj, wqf, wdf, w1f, w2f, gains, fc1_bias):
    rows, width = xf.shape

    def tile(cols):
        return pl.BlockSpec((TILE, cols), lambda s: (s, 0))

    def whole(v):
        return pl.BlockSpec(v.shape, lambda s: (0, 0))

    out = lambda cols: jax.ShapeDtypeStruct((rows, cols), bf16)
    hidden = w1f.shape[1]
    return pl.pallas_call(
        rows_kernel,
        grid=(rows // TILE,),
        out_shape=[out(hidden), out(hidden), out(width), out(width), jax.ShapeDtypeStruct((8, width), f32)],
        in_specs=[tile(v.shape[1]) for v in (xf, h2, dyb, ctx, dproj)]
        + [whole(v) for v in (wqf, wdf, w1f, w2f, gains, fc1_bias)],
        out_specs=[tile(hidden), tile(hidden), tile(width), tile(width), pl.BlockSpec((8, width), lambda s: (0, 0))],
        compiler_params=pltpu.CompilerParams(vmem_limit_bytes=VMEM_LIMIT),
        cost_estimate=pl.CostEstimate(flops=int(2e10), bytes_accessed=int(3e7), transcendentals=int(4e6)),
        name="rows_all",
    )(xf, h2, dyb, ctx, dproj, wqf, wdf, w1f, w2f, gains, fc1_bias)


def weights_kernel(plan, h1_ref, ctx_ref, h2_ref, act_ref, dproj_ref, dyb_ref, dab_ref, g_ref):
    job = pl.program_id(0)
    lefts = (h1_ref, ctx_ref, h2_ref, act_ref)
    rights = (dproj_ref, dyb_ref, dab_ref, dyb_ref)
    for kind, (first, jobs, base, per_row) in enumerate(plan):

        @pl.when((job >= first) & (job < first + jobs))
        def _():
            grad = dot_tn(lefts[kind][...], rights[kind][...]).astype(bf16)
            start = base + (job - first) * (TILE // BLOCK) * per_row
            for r in range(TILE // BLOCK):
                for c in range(per_row):
                    g_ref[start + r * per_row + c] = grad[
                        r * BLOCK : (r + 1) * BLOCK, c * BLOCK : (c + 1) * BLOCK
                    ]


def weights_all(h1, ctx, h2, act, dproj, dyb, dab):
    rows = h1.shape[0]
    lefts, rights = (h1, ctx, h2, act), (dproj, dyb, dab, dyb)
    plan, first, base = [], 0, 0
    for left, right in zip(lefts, rights):
        jobs, per_row = left.shape[1] // TILE, right.shape[1] // BLOCK
        plan.append((first, jobs, base, per_row))
        first, base = first + jobs, base + jobs * (TILE // BLOCK) * per_row

    def tile(kind):
        begin, jobs = plan[kind][:2]
        return pl.BlockSpec((rows, TILE), lambda j: (0, jnp.clip(j - begin, 0, jobs - 1)))

    def whole(v):
        return pl.BlockSpec(v.shape, lambda j: (0, 0))

    return pl.pallas_call(
        functools.partial(weights_kernel, tuple(plan)),
        grid=(first,),
        out_shape=jax.ShapeDtypeStruct((base, BLOCK, BLOCK), bf16),
        in_specs=[tile(k) for k in range(4)] + [whole(dproj), whole(dyb), whole(dab)],
        out_specs=pl.BlockSpec((base, BLOCK, BLOCK), lambda j: (0, 0, 0)),
        compiler_params=pltpu.CompilerParams(vmem_limit_bytes=VMEM_LIMIT),
        cost_estimate=pl.CostEstimate(flops=int(1.3e10), bytes_accessed=int(3e7), transcendentals=0),
        name="weights_all",
    )(h1, ctx, h2, act, dproj, dyb, dab)


class Scatter:
    def __init__(self, ring, order, blocks, out, sbuf, rbuf, send, recv):
        self.ring, self.order, self.blocks, self.out = ring, order, blocks, out
        self.sbuf, self.rbuf, self.send, self.recv = sbuf, rbuf, send, recv
        self.per = out.shape[0]
        self.far = ring.count // 2

    def index(self, half, way, hop):
        return (half * 2 + way) * self.far + hop - 1

    def copy(self, half, way, hop):
        i = self.index(half, way, hop)
        return pltpu.make_async_remote_copy(
            src_ref=self.sbuf.at[i],
            dst_ref=self.rbuf.at[i],
            send_sem=self.send.at[i],
            recv_sem=self.recv.at[i],
            device_id=self.ring.peer[way],
            device_id_type=MESH,
        )

    def own(self, dest, half, k):
        return self.blocks[self.order[dest * self.per + k], half * 64 : half * 64 + 64, :].astype(f32)

    def step(self, half, way, hop, hops, first):
        dest = self.ring.at((hops + 1 - hop) if way == 0 else (hop - hops - 1))
        i = self.index(half, way, hop)
        if not first:
            self.copy(half, way, hop - 1).wait_recv()

        def one(k, carry):
            value = self.own(dest, half, k)
            if not first:
                value = value + self.rbuf[i - 1, k].astype(f32)
            self.sbuf[i, k] = value.astype(bf16)
            return carry

        lax.fori_loop(0, self.per, one, 0)
        self.copy(half, way, hop).start()

    def last(self, half, scale):
        came = []
        for way in range(2):
            hops = hop_count(half, way, self.ring.count)
            if hops >= 1:
                self.copy(half, way, hops).wait_recv()
                came.append(self.index(half, way, hops))
        me = self.ring.me

        def one(k, carry):
            value = self.own(me, half, k)
            for i in came:
                value = value + self.rbuf[i, k].astype(f32)
            self.out[k, half * 64 : half * 64 + 64, :] = value * scale
            return carry

        lax.fori_loop(0, self.per, one, 0)

    def finish(self):
        for half in range(2):
            for way in range(2):
                hops = hop_count(half, way, self.ring.count)
                for_hops(1, hops + 1, lambda hop: self.copy(half, way, hop).wait_send(), self.ring.count)


class RowSum:
    def __init__(self, part, out, r1, s2, r2, send, recv):
        self.tensor = lax.axis_index("tensor")
        self.dp = lax.axis_index("dp")
        self.near = self.tensor + 1 - 2 * (self.tensor % 2)
        self.across = (self.tensor + 2) % 4
        self.part, self.out, self.r1, self.s2, self.r2 = part, out, r1, s2, r2
        self.send, self.recv = send, recv
        self.rows = out.shape[0]

    def slot(self, owner):
        return self.part.at[pl.ds(pl.multiple_of(owner * self.rows, 16), self.rows)]

    def remote(self, src, dst, sem, device):
        return pltpu.make_async_remote_copy(
            src_ref=src, dst_ref=dst, send_sem=self.send.at[sem], recv_sem=self.recv.at[sem],
            device_id=(self.dp, device), device_id_type=MESH,
        )

    def pair(self, k):
        owner = (self.near + 2) % 4 if k == 0 else self.near
        return self.remote(self.slot(owner), self.r1.at[k], k, self.near)

    def cross(self):
        return self.remote(self.s2, self.r2, 2, self.across)

    def begin(self):
        self.pair(0).start()
        self.pair(1).start()

    def middle(self):
        self.pair(0).wait_recv()
        self.s2[...] = (self.slot(self.across)[...].astype(f32) + self.r1[0].astype(f32)).astype(bf16)
        self.cross().start()

    def end(self):
        self.pair(1).wait_recv()
        self.cross().wait_recv()
        self.out[...] = (
            self.slot(self.tensor)[...].astype(f32) + self.r1[1].astype(f32) + self.r2[...].astype(f32)
        )
        self.pair(0).wait_send()
        self.pair(1).wait_send()
        self.cross().wait_send()


def sums_kernel(
    count, scale, order, blocks, br, e, small, grad, br_sum, e_sum, small_sum,
    sbuf, rbuf, r1, s2, r2, t_in, d_in, d_out, ss, sr, rs, rr, ts, tr, ds, dr,
):
    ring = Ring(count)
    me, tensor = ring.me, ring.tensor
    scatter = Scatter(ring, order, blocks, grad, sbuf, rbuf, ss, sr)
    sums = [
        RowSum(part, out, r1.at[n], s2.at[n], r2.at[n], rs.at[n], rr.at[n])
        for n, (part, out) in enumerate(((br, br_sum), (e, e_sum)))
    ]

    def t_copy(step):
        return pltpu.make_async_remote_copy(
            src_ref=small, dst_ref=t_in.at[tensor], send_sem=ts.at[step], recv_sem=tr.at[step],
            device_id=(me, (tensor + step) % 4), device_id_type=MESH,
        )

    def d_copy(step):
        return pltpu.make_async_remote_copy(
            src_ref=d_out, dst_ref=d_in.at[me], send_sem=ds.at[step], recv_sem=dr.at[step],
            device_id=((me + step) % count, tensor), device_id_type=MESH,
        )

    barrier = pltpu.get_barrier_semaphore()
    for step in range(1, 4):
        pl.semaphore_signal(barrier, inc=1, device_id=(me, (tensor + step) % 4), device_id_type=MESH)

    @pl.loop(1, count)
    def _(step):
        pl.semaphore_signal(barrier, inc=1, device_id=((me + step) % count, tensor), device_id_type=MESH)

    pl.semaphore_wait(barrier, 3 + count - 1)

    far = count // 2
    for half in range(2):
        for way in (half, 1 - half):
            hops = hop_count(half, way, count)
            if hops >= 1:
                scatter.step(half, way, 1, hops, True)
    for step in range(1, 4):
        t_copy(step).start()
    for s in sums:
        s.begin()
    sums[0].middle()
    for step in range(1, 4):
        t_copy(step).wait_recv()
    t_in[tensor] = small[...]
    row = lax.broadcasted_iota(jnp.int32, small.shape, 0)
    total = t_in[0] + t_in[1] + t_in[2] + t_in[3]
    d_out[...] = jnp.where(row < 4, total, small[...])

    @pl.loop(1, count)
    def _(step):
        d_copy(step).start()

    def ring_step(hop):
        for half in range(2):
            for way in (half, 1 - half):
                hops = hop_count(half, way, count)
                if half == way:
                    scatter.step(half, way, hop, hops, False)
                else:

                    @pl.when(hop <= hops)
                    def _():
                        scatter.step(half, way, hop, hops, False)

    for_hops(2, far, ring_step, count)
    sums[1].middle()
    if far >= 2:
        ring_step(far)
    sums[0].end()

    @pl.loop(1, count)
    def _(step):
        d_copy(step).wait_recv()

    d_in[me] = d_out[...]
    small_sum[...] = lax.fori_loop(1, count, lambda k, acc: acc + d_in[k], d_in[0])
    sums[1].end()
    for half in range(2):
        scatter.last(half, scale)
    scatter.finish()
    for step in range(1, 4):
        t_copy(step).wait_send()

    @pl.loop(1, count)
    def _(step):
        d_copy(step).wait_send()


def sums_all(count, scale, order, blocks, br, e, small):
    per = blocks.shape[0] // count
    rows, width = br.shape[0] // 4, br.shape[1]
    far = count // 2
    vmem = pl.BlockSpec(memory_space=pltpu.VMEM)
    dma = lambda *n: pltpu.SemaphoreType.DMA(n)
    return pl.pallas_call(
        functools.partial(sums_kernel, count, scale),
        out_shape=[
            jax.ShapeDtypeStruct((per, BLOCK, BLOCK), f32),
            jax.ShapeDtypeStruct((rows, width), f32),
            jax.ShapeDtypeStruct((rows, width), f32),
            jax.ShapeDtypeStruct(small.shape, f32),
        ],
        in_specs=[pl.BlockSpec(memory_space=pltpu.SMEM)] + [vmem] * 4,
        out_specs=[vmem] * 4,
        scratch_shapes=[
            pltpu.VMEM((4 * far, per, 64, BLOCK), bf16),
            pltpu.VMEM((4 * far, per, 64, BLOCK), bf16),
            pltpu.VMEM((2, 2, rows, width), bf16),
            pltpu.VMEM((2, rows, width), bf16),
            pltpu.VMEM((2, rows, width), bf16),
            pltpu.VMEM((4,) + small.shape, f32),
            pltpu.VMEM((count,) + small.shape, f32),
            pltpu.VMEM(small.shape, f32),
            dma(4 * far), dma(4 * far), dma(2, 3), dma(2, 3), dma(4), dma(4), dma(count), dma(count),
        ],
        compiler_params=pltpu.CompilerParams(
            collective_id=1, has_side_effects=True, vmem_limit_bytes=VMEM_LIMIT
        ),
        cost_estimate=pl.CostEstimate(flops=0, bytes_accessed=int(3e7), transcendentals=0),
        name="sums_all",
    )(order, blocks, br, e, small)


def shards(
    tokens, out_grad, seq_lengths, norm_gains, row_biases, qkv_weight, qkv_bias, dense_weight, fc1_weight,
    fc1_bias, fc2_weight, block_slot, left_stat, right_stat, left_root, right_root, row_accum,
    qkv_bias_accum, fc1_bias_accum,
):
    tensor_count = lax.axis_size("tensor")
    dp_count = lax.axis_size("dp")
    tensor_rank = lax.axis_index("tensor")
    own_rows, width = tokens.shape
    group_rows = own_rows * tensor_count
    group_seqs = seq_lengths.shape[0]
    grad_scale = 1.0 / math.sqrt(group_rows * dp_count)
    blocks_tensor = block_slot.shape[0] // tensor_count
    per_dev = blocks_tensor // dp_count

    my_slots = lax.dynamic_slice_in_dim(block_slot, tensor_rank * blocks_tensor, blocks_tensor)
    position = my_slots // per_dev // tensor_count * per_dev + my_slots % per_dev
    places = jnp.arange(blocks_tensor, dtype=jnp.int32)
    order = jnp.sum(jnp.where(position[:, None] == places[None, :], places[:, None], 0), axis=0)

    xf, dyf, wqf, wdf, w1f, w2f = gather_all(
        dp_count, tokens, out_grad, qkv_weight, dense_weight.T, fc1_weight, fc2_weight.T
    )
    h1, h2, dyb, ctx, dproj, sum_a = attention_all(
        seq_lengths, xf, dyf, wqf, wdf, norm_gains, row_biases, qkv_bias[None], jnp.asarray(rotary_wide())
    )
    act, dab, br, e, sum_b = rows_all(
        xf, h2, dyb, ctx, dproj, wqf, wdf, w1f, w2f, norm_gains, fc1_bias[None]
    )
    blocks = weights_all(h1, ctx, h2, act, dproj, dyb, dab)
    own_grad, branch, e_sum, small = sums_all(dp_count, grad_scale, order, blocks, br, e, sum_a + sum_b)

    inputs = tokens.astype(f32)
    layer_out = (inputs + branch + row_biases[2] + row_biases[3]).astype(bf16)
    row_ids = tensor_rank * own_rows + jnp.arange(own_rows)
    seq_match = (row_ids // LEN)[:, None] == jnp.arange(group_seqs)[None, :]
    row_limit = jnp.sum(jnp.where(seq_match, seq_lengths[None, :], 0), axis=1)
    row_valid = (row_ids % LEN < row_limit).astype(f32)
    grad_out = out_grad.astype(f32) * row_valid[:, None]
    xhat, scale = normed(inputs)
    input_grad = grad_out + scale * (
        e_sum
        - jnp.mean(e_sum, axis=-1, keepdims=True)
        - xhat * jnp.mean(e_sum * xhat, axis=-1, keepdims=True)
    )

    left_next = stat_decay * left_stat + (1.0 - stat_decay) * jnp.einsum(
        "sij,skj->sik", own_grad, own_grad, precision=highest
    )
    right_next = stat_decay * right_stat + (1.0 - stat_decay) * jnp.einsum(
        "sji,sjk->sik", own_grad, own_grad, precision=highest
    )
    pushed = jnp.einsum("sij,sjk->sik", left_root, own_grad, precision=highest)
    change = -shampoo_rate * jnp.einsum("sij,sjk->sik", pushed, right_root, precision=highest)

    small = small * grad_scale
    row_grads = jnp.concatenate([small[:5], small[4:5]], axis=0)
    row_next, row_change = adagrad_step(row_grads, row_accum)
    qkv_next, qkv_change = adagrad_step(small[5, : qkv_bias.shape[0]], qkv_bias_accum)
    fc1_next, fc1_change = adagrad_step(small[6, : fc1_bias.shape[0]], fc1_bias_accum)
    return (
        layer_out, input_grad, own_grad, left_next, right_next, change,
        row_next, row_change, qkv_next, qkv_change, fc1_next, fc1_change,
    )


def solution(mesh):
    both = ("dp", "tensor")
    return jax.shard_map(
        shards,
        mesh=mesh,
        in_specs=(
            P(both, None), P(both, None), P("dp"), P(), P(), P("dp", "tensor"), P("tensor"),
            P("tensor", "dp"), P("dp", "tensor"), P("tensor"), P("tensor", "dp"), P(),
            P(both, None, None), P(both, None, None), P(both, None, None), P(both, None, None),
            P(), P("tensor"), P("tensor"),
        ),
        out_specs=(
            P(both, None), P(both, None), P(both, None, None), P(both, None, None),
            P(both, None, None), P(both, None, None), P(), P(), P("tensor"), P("tensor"),
            P("tensor"), P("tensor"),
        ),
        check_vma=False,
    )
```

```python
import functools
import math

import jax
import jax.numpy as jnp
import numpy as np
from jax import lax
from jax.experimental import pallas as pl
from jax.experimental.pallas import tpu as pltpu
from jax.sharding import PartitionSpec as P

HEAD = 64
ROT = 16
LEN = 1024
BLOCK = 128
TILE = 256
MESH = pl.DeviceIdType.MESH
VMEM_LIMIT = 60 * 1024 * 1024

highest = lax.Precision.HIGHEST
masked_score = -1e30
shampoo_rate = 0.03
adagrad_rate = 0.1
stat_decay = 0.5
f32 = jnp.float32
bf16 = jnp.bfloat16


def adagrad_step(grad_vec, accum):
    accum_next = accum + grad_vec * grad_vec
    return (accum_next, -adagrad_rate * grad_vec * lax.rsqrt(accum_next))


def rotary_rows():
    half = ROT // 2
    inverse = np.power(np.float32(10000.0), -(np.arange(half, dtype=np.float32) * np.float32(2.0 / ROT)))
    angles = inverse.astype(np.float32)[:, None] * np.arange(LEN, dtype=np.float32)[None, :]
    return np.concatenate([np.cos(angles), np.sin(angles)], axis=0).astype(np.float32)


def ring_place(me, count):
    low, high = me % 2, me // 2
    return low * (count - 1 - high) + (1 - low) * high


def ring_device(place, count):
    upper = place // (count // 2)
    return (1 - upper) * (2 * place) + upper * (2 * (count - 1 - place) + 1)


def hop_count(half, way, count):
    far = count // 2
    return far if half == way else far - 1


def for_hops(first, last, body, count):
    if count <= 8:
        for hop in range(first, last):
            body(hop)
    elif last > first:

        @pl.loop(first, last)
        def _(hop):
            body(hop)


class Ring:
    def __init__(self, count):
        self.count = count
        self.me = lax.axis_index("dp")
        self.tensor = lax.axis_index("tensor")
        self.place = ring_place(self.me, count)
        self.peer = [
            (ring_device((self.place + step) % count, count), self.tensor) for step in (1, count - 1)
        ]

    def at(self, offset):
        return ring_device((self.place + offset + 2 * self.count) % self.count, self.count)


class Gather:
    def __init__(self, ring, locals_, fulls, send, recv):
        self.ring, self.locals, self.fulls, self.send, self.recv = ring, locals_, fulls, send, recv
        self.far = ring.count // 2

    def part(self, ref, w, half, owner=None):
        rows, cols = self.locals[w].shape
        base = 0 if owner is None else owner * rows
        if rows % 32 == 0:
            return ref.at[pl.ds(pl.multiple_of(base + half * (rows // 2), 16), rows // 2)]
        return ref.at[pl.ds(base, rows), pl.ds(half * (cols // 2), cols // 2)]

    def sem(self, w, half, way, hop):
        return ((w * 2 + half) * 2 + way) * self.far + hop - 1

    def copy(self, w, half, way, hop, source):
        owner = self.ring.at((1 - hop) if way == 0 else (hop - 1))
        src = self.part(self.locals[w], w, half) if source else self.part(self.fulls[w], w, half, owner)
        return pltpu.make_async_remote_copy(
            src_ref=src,
            dst_ref=self.part(self.fulls[w], w, half, owner),
            send_sem=self.send.at[self.sem(w, half, way, hop)],
            recv_sem=self.recv.at[self.sem(w, half, way, hop)],
            device_id=self.ring.peer[way],
            device_id_type=MESH,
        )

    def arrival(self, w, half, way, hop):
        owner = self.ring.at(-hop if way == 0 else hop)
        dst = self.part(self.fulls[w], w, half, owner)
        return pltpu.make_async_remote_copy(
            src_ref=dst,
            dst_ref=dst,
            send_sem=self.send.at[self.sem(w, half, way, hop)],
            recv_sem=self.recv.at[self.sem(w, half, way, hop)],
            device_id=self.ring.peer[way],
            device_id_type=MESH,
        )

    def begin(self, w):
        for half in range(2):
            for way in range(2):
                if hop_count(half, way, self.ring.count) >= 1:
                    self.copy(w, half, way, 1, True).start()

    def forward(self, w, hop, last):
        for half in range(2):
            for way in range(2):
                hops = self.far if half == way else self.far - 1
                if last and hops != self.far:
                    continue
                self.arrival(w, half, way, hop).wait_recv()
                if not last:
                    more = self.far if half == way else self.far - 1
                    if more == self.far:
                        self.copy(w, half, way, hop + 1, False).start()
                    else:

                        @pl.when(hop + 1 <= more)
                        def _():
                            self.copy(w, half, way, hop + 1, False).start()

    def finish(self, w):
        for half in range(2):
            for way in range(2):
                hops = hop_count(half, way, self.ring.count)
                if hops >= 1:
                    self.copy(w, half, way, 1, True).wait_send()
                for_hops(
                    2, hops + 1, lambda hop: self.copy(w, half, way, hop, False).wait_send(), self.ring.count
                )


class Rows:
    def __init__(self, local, full, send, recv, own):
        self.tensor = lax.axis_index("tensor")
        self.dp = lax.axis_index("dp")
        self.near = self.tensor + 1 - 2 * (self.tensor % 2)
        self.across = (self.tensor + 2) % 4
        self.local, self.full, self.send, self.recv, self.own = local, full, send, recv, own
        self.rows = local.shape[0]

    def slot(self, owner, piece=None):
        if piece is None:
            return self.full.at[pl.ds(pl.multiple_of(owner * self.rows, 16), self.rows)]
        half = self.rows // 2
        return self.full.at[pl.ds(pl.multiple_of(owner * self.rows + piece * half, 16), half)]

    def remote(self, src, dst, sem, device):
        return pltpu.make_async_remote_copy(
            src_ref=src,
            dst_ref=dst,
            send_sem=self.send.at[sem],
            recv_sem=self.recv.at[sem],
            device_id=(self.dp, device),
            device_id_type=MESH,
        )

    def keep(self):
        return pltpu.make_async_copy(self.local, self.slot(self.tensor), self.own)

    def pair(self):
        return self.remote(self.local, self.slot(self.tensor), 0, self.near)

    def cross(self, piece):
        half = self.rows // 2
        return self.remote(
            self.local.at[pl.ds(piece * half, half)], self.slot(self.tensor, piece), 1 + piece, self.across
        )

    def onward(self, piece):
        here = self.slot(self.across, piece)
        return self.remote(here, here, 3 + piece, self.near)

    def begin_near(self):
        self.keep().start()
        self.pair().start()

    def begin_cross(self):
        for piece in range(2):
            self.cross(piece).start()

    def pass_on(self):
        for piece in range(2):
            self.cross(piece).wait_recv()
            self.onward(piece).start()

    def finish(self):
        self.keep().wait()
        self.pair().wait()
        for piece in range(2):
            self.cross(piece).wait_send()
            self.onward(piece).wait()


def greet(devices):
    barrier = pltpu.get_barrier_semaphore()
    for device in devices:
        pl.semaphore_signal(barrier, inc=1, device_id=device, device_id_type=MESH)
    pl.semaphore_wait(barrier, len(devices))


def dot_nn(a, b):
    return lax.dot_general(a, b, (((1,), (0,)), ((), ())), preferred_element_type=f32)


def dot_nt(a, b):
    return lax.dot_general(a, b, (((1,), (1,)), ((), ())), preferred_element_type=f32)


def dot_tn(a, b):
    return lax.dot_general(a, b, (((0,), (0,)), ((), ())), preferred_element_type=f32)


def normed(x):
    average = jnp.mean(x, axis=-1, keepdims=True)
    centered = x - average
    variance = jnp.mean(centered * centered, axis=-1, keepdims=True)
    scale = lax.rsqrt(variance + 1e-05)
    return centered * scale, scale


def mixed_kernel(
    count, lim_ref, gain_ref, bias_ref, qb_ref, rot_ref, x, dy, wqd, w1, w2,
    x_out, h1_out, dyb_out, ctx_out, dproj_out, wqd_out, w1f, w2f, sum_ref,
    xf, dyf, wf, h1s, ctxs, dps, qt, kt, vt, dct, ctt, dqt, kr, vr, dks, dvs,
    rs, rr, ro, gs, gr, go, os,
):
    ring = Ring(count)
    half_cols = wqd.shape[1] // 2
    pair_cols = 6 * HEAD
    views = [(wqd.at[:, pl.ds(p * half_cols, half_cols)], wf.at[:, pl.ds(p * half_cols, half_cols)]) for p in (0, 1)]
    views += [(w1, w1f), (w2, w2f)]
    gather = Gather(ring, [v[0] for v in views], [v[1] for v in views], gs, gr)
    rx = Rows(x, xf, rs.at[0], rr.at[0], ro.at[0])
    ry = Rows(dy, dyf, rs.at[1], rr.at[1], ro.at[1])
    greet([ring.peer[0], ring.peer[1], (ring.me, rx.near), (ring.me, rx.across)])
    far = count // 2
    own = []
    for k, (local, full) in enumerate(((wqd, wf), (w1, w1f), (w2, w2f))):
        rows = local.shape[0]
        own.append(
            pltpu.make_async_copy(local, full.at[pl.ds(pl.multiple_of(ring.me * rows, 16), rows)], go.at[k])
        )
    rx.begin_near()
    gather.begin(0)
    rx.begin_cross()
    ry.begin_near()
    for copy in own:
        copy.start()
    sum_ref[...] = jnp.zeros_like(sum_ref)
    tensor = ring.tensor
    tiles = LEN // TILE

    def whole_ring(w):
        for_hops(1, far, lambda hop: gather.forward(w, hop, False), count)
        gather.forward(w, far, True)

    def hop_at(w, hop):
        if count == 8:
            gather.forward(w, hop, hop == far)
        elif hop == 4:
            whole_ring(w)

    def rows_of(seq, i):
        return pl.ds(pl.multiple_of(seq * LEN + i * TILE, TILE), TILE)

    def norm_tile(seq, i):
        rows = rows_of(seq, i)
        xhat, _ = normed(xf[rows, :].astype(f32))
        h1s[rows, :] = (xhat * gain_ref[0:1, :] + bias_ref[0:1, :]).astype(bf16)

    def mask_tile(seq, i):
        rows = rows_of(seq, i)
        place = i * TILE + lax.broadcasted_iota(jnp.int32, (TILE, 1), 0)
        kept = jnp.where(place < lim_ref[seq], dyf[rows, :].astype(f32), 0.0)
        sum_ref[4:5, :] += jnp.sum(kept, axis=0, keepdims=True)
        dyf[rows, :] = kept.astype(bf16)

    def turned(first, second, cosine, sine):
        return first * cosine - second * sine, second * cosine + first * sine

    def prepare_tile(seq, pair, i):
        rows = rows_of(seq, i)
        cols = pl.ds(pl.multiple_of(i * TILE, TILE), TILE)
        begin = pl.multiple_of(pair * half_cols, BLOCK)
        proj = dot_nn(h1s[rows, :], wf[:, pl.ds(begin, pair_cols)])
        proj = proj + qb_ref[:, pl.ds(pl.multiple_of(pair * pair_cols, BLOCK), pair_cols)]
        proj = proj.T
        dctx = dot_nn(dyf[rows, :], wf[:, pl.ds(begin + pair_cols, 2 * HEAD)]).T
        cosine, sine = rot_ref[0:8, cols], rot_ref[8:16, cols]
        key = i * TILE + lax.broadcasted_iota(jnp.int32, (16, TILE), 1)
        row = lax.broadcasted_iota(jnp.int32, (16, TILE), 0)
        ones = jnp.where(row == 0, 1.0, 0.0)
        hidden = jnp.where((row == 0) & (key >= lim_ref[seq]), masked_score, 0.0)
        for hh in range(2):
            base = 3 * HEAD * hh
            q0, q1 = turned(proj[base : base + 8], proj[base + 8 : base + 16], cosine, sine)
            q = jnp.concatenate([q0, q1, proj[base + 16 : base + HEAD]], axis=0)
            q = q.astype(bf16).astype(f32) * 0.125
            qt[hh, :, cols] = jnp.concatenate([q, ones], axis=0).astype(bf16)
            base += HEAD
            k0, k1 = turned(proj[base : base + 8], proj[base + 8 : base + 16], cosine, sine)
            k = jnp.concatenate([k0, k1, proj[base + 16 : base + HEAD]], axis=0)
            kt[hh, :, cols] = k.astype(bf16)
            kr[hh, cols, :] = jnp.concatenate([k, hidden], axis=0).T.astype(bf16)
            base += HEAD
            v = proj[base : base + HEAD]
            vt[hh, :, cols] = jnp.concatenate([v, ones], axis=0).astype(bf16)
            vr[hh, cols, :] = v.T.astype(bf16)
            dct[hh, :, cols] = dctx[HEAD * hh : HEAD * (hh + 1)].astype(bf16)

    def attend(hh, i):
        here = slice(i * TILE, (i + 1) * TILE)
        chunks = [slice(c * TILE, (c + 1) * TILE) for c in range(i + 1)]
        q = qt[hh, :, here]
        scores = [dot_nn(kr[hh, c, :], q) for c in chunks]
        key = lax.broadcasted_iota(jnp.int32, (TILE, TILE), 0)
        query = lax.broadcasted_iota(jnp.int32, (TILE, TILE), 1)
        scores[i] = jnp.where(key <= query, scores[i], masked_score)
        top = jnp.max(scores[0], axis=0, keepdims=True)
        for s in scores[1:]:
            top = jnp.maximum(top, jnp.max(s, axis=0, keepdims=True))
        probs = [jnp.exp(s - top).astype(bf16) for s in scores]
        total = dot_nn(vt[hh, :, chunks[0]], probs[0])
        for c, p in zip(chunks[1:], probs[1:]):
            total = total + dot_nn(vt[hh, :, c], p)
        inverse = 1.0 / total[HEAD : HEAD + 1]
        context = total[:HEAD] * inverse
        ctt[hh, :, here] = context
        grad = dct[hh, :, here].astype(f32)
        delta = jnp.sum(grad * context, axis=0, keepdims=True) * inverse
        grad = (grad * inverse).astype(bf16)
        dq = None
        for n, (c, p) in enumerate(zip(chunks, probs)):
            dp = dot_nn(vr[hh, c, :], grad)
            ds = (p.astype(f32) * (dp - delta)).astype(bf16)
            part = dot_nn(kt[hh, :, c], ds)
            dq = part if dq is None else dq + part
            dk = dot_nt(ds, q[:HEAD])
            dv = dot_nt(p, grad)
            if i == tiles - 1:
                dks[hh, c, :] = dk
                dvs[hh, c, :] = dv
            else:
                dks[hh, c, :] += dk
                dvs[hh, c, :] += dv
        dqt[hh, :, here] = dq * 0.125

    def collect_tile(seq, pair, i):
        rows = rows_of(seq, i)
        cols = pl.ds(pl.multiple_of(i * TILE, TILE), TILE)
        cosine, sine = rot_ref[0:8, cols], rot_ref[8:16, cols]
        pieces = []
        for hh in range(2):
            for grad in (dqt[hh, :, cols], dks[hh, cols, :].T):
                pieces += [*turned(grad[0:8], grad[8:16], cosine, -sine), grad[16:HEAD]]
            pieces.append(dvs[hh, cols, :].T)
        low = jnp.concatenate(pieces, axis=0).T.astype(bf16)
        wide = pl.ds(pl.multiple_of(pair * pair_cols, BLOCK), pair_cols)
        dps[rows, wide] = low
        sum_ref[5:6, wide] += jnp.sum(low.astype(f32), axis=0, keepdims=True)
        ctx = jnp.concatenate([ctt[0, :, cols], ctt[1, :, cols]], axis=0).T
        ctxs[rows, pl.ds(pl.multiple_of(pair * 2 * HEAD, BLOCK), 2 * HEAD)] = ctx.astype(bf16)

    def save(k, src, dst, seq):
        rows = pl.ds(pl.multiple_of(seq * LEN, LEN), LEN)
        return pltpu.make_async_copy(src.at[rows], dst.at[rows], os.at[k])

    first = tensor // 2

    @pl.loop(0, 4)
    def _(g):
        turn, pair = g // 2, g % 2
        seq = turn + (1 - 2 * turn) * first

        def at(place):
            return pl.when(g == place)

        @at(0)
        def _():
            rx.keep().wait()
            rx.pair().wait_recv()

        @at(2)
        def _():
            for piece in range(2):
                rx.onward(piece).wait_recv()

        @pl.when(pair == 0)
        def _():
            @pl.loop(0, tiles)
            def _(i):
                norm_tile(seq, i)

                @pl.when((g == 0) & (i == 0))
                def _():
                    hop_at(0, 1)
                    gather.begin(1)

                @pl.when((g == 0) & (i == 1))
                def _():
                    hop_at(0, 2)
                    hop_at(1, 1)

                @pl.when((g == 0) & (i == 2))
                def _():
                    hop_at(0, 3)
                    hop_at(1, 2)
                    gather.begin(2)

            save(0, xf, x_out, seq).start()
            save(1, h1s, h1_out, seq).start()

        @at(0)
        def _():
            hop_at(0, 4)
            own[0].wait()
            ry.keep().wait()
            ry.pair().wait_recv()

        @at(1)
        def _():
            hop_at(2, 1)

        @at(2)
        def _():
            ry.pass_on()
            for piece in range(2):
                ry.onward(piece).wait()

        @at(3)
        def _():
            hop_at(3, 3)

        @pl.when(pair == 0)
        def _():
            @pl.loop(0, tiles)
            def _(i):
                mask_tile(seq, i)

            save(2, dyf, dyb_out, seq).start()

        @pl.loop(0, tiles)
        def _(i):
            prepare_tile(seq, pair, i)

        @at(0)
        def _():
            hop_at(1, 3)
            gather.begin(3)

        @at(1)
        def _():
            hop_at(3, 1)

        @pl.loop(0, 2)
        def _(hh):
            for i in reversed(range(tiles)):
                attend(hh, i)

            @pl.when((g == 0) & (hh == 0))
            def _():
                hop_at(1, 4)
                rx.pass_on()
                ry.begin_cross()

            @pl.when((g == 1) & (hh == 0))
            def _():
                hop_at(2, 2)

            @pl.when((g == 1) & (hh == 1))
            def _():
                hop_at(3, 2)

            @pl.when((g == 2) & (hh == 0))
            def _():
                hop_at(2, 3)

            @pl.when((g == 3) & (hh == 0))
            def _():
                hop_at(2, 4)

        @pl.loop(0, tiles)
        def _(i):
            collect_tile(seq, pair, i)

        @pl.when(pair == 1)
        def _():
            save(3, ctxs, ctx_out, seq).start()
            save(4, dps, dproj_out, seq).start()

        @pl.when(pair == 1)
        def _():
            for k, (src, dst) in enumerate(
                ((xf, x_out), (h1s, h1_out), (dyf, dyb_out), (ctxs, ctx_out), (dps, dproj_out))
            ):
                save(k, src, dst, seq).wait()

    keep = pltpu.make_async_copy(wf, wqd_out, os.at[5])
    keep.start()
    hop_at(3, 4)
    for w in range(4):
        gather.finish(w)
    own[1].wait()
    own[2].wait()
    rx.pair().wait_send()
    ry.pair().wait_send()
    for piece in range(2):
        rx.cross(piece).wait_send()
        rx.onward(piece).wait_send()
        ry.cross(piece).wait_send()
    keep.wait()


def mixed_all(count, limits, gains, biases, qkv_bias, rot, x, dy, wqd, w1, w2):
    far = count // 2
    rows, width = 4 * x.shape[0], x.shape[1]
    ctx_cols, proj_cols = 4 * HEAD, qkv_bias.shape[1]
    out = lambda r, c: jax.ShapeDtypeStruct((r, c), bf16)
    full = lambda v: out(count * v.shape[0], v.shape[1])
    any_, vmem = pl.BlockSpec(memory_space=pl.ANY), pl.BlockSpec(memory_space=pltpu.VMEM)
    dma = lambda *n: pltpu.SemaphoreType.DMA(n)
    buf = lambda dtype, *shape: pltpu.VMEM(shape, dtype)
    return pl.pallas_call(
        functools.partial(mixed_kernel, count),
        out_shape=[
            out(rows, width), out(rows, width), out(rows, width), out(rows, ctx_cols), out(rows, proj_cols),
            full(wqd), full(w1), full(w2), jax.ShapeDtypeStruct((8, width), f32),
        ],
        in_specs=[pl.BlockSpec(memory_space=pltpu.SMEM)] + [vmem] * 4 + [any_] * 5,
        out_specs=[any_] * 8 + [vmem],
        scratch_shapes=[
            buf(bf16, rows, width), buf(bf16, rows, width), buf(bf16, width, wqd.shape[1]),
            buf(bf16, rows, width), buf(bf16, rows, ctx_cols), buf(bf16, rows, proj_cols),
            buf(bf16, 2, HEAD + 16, LEN), buf(bf16, 2, HEAD, LEN), buf(bf16, 2, HEAD + 16, LEN),
            buf(bf16, 2, HEAD, LEN), buf(f32, 2, HEAD, LEN), buf(f32, 2, HEAD, LEN),
            buf(bf16, 2, LEN, HEAD + 16), buf(bf16, 2, LEN, HEAD), buf(f32, 2, LEN, HEAD), buf(f32, 2, LEN, HEAD),
            dma(2, 5), dma(2, 5), dma(2), dma(16 * far), dma(16 * far), dma(3), dma(6),
        ],
        compiler_params=pltpu.CompilerParams(
            collective_id=0, has_side_effects=True, vmem_limit_bytes=VMEM_LIMIT
        ),
        cost_estimate=pl.CostEstimate(flops=int(2e10), bytes_accessed=int(4e7), transcendentals=int(1e7)),
        name="mixed_all",
    )(limits, gains, biases, qkv_bias, rot, x, dy, wqd, w1, w2)


def gelu_both(x):
    bell = jnp.exp(-0.5 * x * x)
    u = jnp.abs(x) * (1.0 / math.sqrt(2.0))
    t = 1.0 / (1.0 + 0.3275911 * u)
    poly = t * (0.254829592 + t * (-0.284496736 + t * (1.421413741 + t * (-1.453152027 + t * 1.061405429))))
    tail = 0.5 * poly * bell
    phi = jnp.where(x < 0.0, tail, 1.0 - tail)
    return x * phi, phi + x * bell * (1.0 / math.sqrt(2.0 * math.pi))


def rows_kernel(
    x_ref, dyb_ref, ctx_ref, dproj_ref, wqd_ref, w1_ref, w2_ref, gain_ref, bias_ref, fb_ref,
    h2_ref, act_ref, dab_ref, br_ref, e_ref, sum_ref,
):
    @pl.when(pl.program_id(0) == 0)
    def _():
        sum_ref[...] = jnp.zeros_like(sum_ref)

    xhat, _ = normed(x_ref[...].astype(f32))
    h2 = (xhat * gain_ref[1:2, :] + bias_ref[1:2, :]).astype(bf16)
    h2_ref[...] = h2
    pre = dot_nn(h2, w1_ref[...]) + fb_ref[...]
    act, slope = gelu_both(pre)
    act = act.astype(bf16)
    act_ref[...] = act
    dab = (dot_nn(dyb_ref[...], w2_ref[...]) * slope).astype(bf16)
    dab_ref[...] = dab
    br = dot_nt(act, w2_ref[...])
    dh2 = dot_nt(dab, w1_ref[...])
    dh1 = None
    wide, thin = 6 * HEAD, 2 * HEAD
    for p in range(2):
        lo = p * (wide + thin)
        br = br + dot_nt(ctx_ref[:, p * thin : (p + 1) * thin], wqd_ref[:, lo + wide : lo + wide + thin])
        part = dot_nt(dproj_ref[:, p * wide : (p + 1) * wide], wqd_ref[:, lo : lo + wide])
        dh1 = part if dh1 is None else dh1 + part
    br_ref[...] = br.astype(bf16)
    e_ref[...] = (dh1 * gain_ref[0:1, :] + dh2 * gain_ref[1:2, :]).astype(bf16)
    total = lambda v: jnp.sum(v, axis=0, keepdims=True)
    sum_ref[0:1, :] += total(dh1 * xhat)
    sum_ref[1:2, :] += total(dh2 * xhat)
    sum_ref[2:3, :] += total(dh1)
    sum_ref[3:4, :] += total(dh2)
    sum_ref[6:7, :] += total(dab.astype(f32))


def rows_all(xf, dyb, ctx, dproj, wqdf, w1f, w2f, gains, biases, fc1_bias):
    rows, width = xf.shape

    def tile(cols):
        return pl.BlockSpec((TILE, cols), lambda s: (s, 0))

    def whole(v):
        return pl.BlockSpec(v.shape, lambda s: (0, 0))

    out = lambda cols: jax.ShapeDtypeStruct((rows, cols), bf16)
    hidden = w1f.shape[1]
    return pl.pallas_call(
        rows_kernel,
        grid=(rows // TILE,),
        out_shape=[out(width), out(hidden), out(hidden), out(width), out(width)]
        + [jax.ShapeDtypeStruct((8, width), f32)],
        in_specs=[tile(v.shape[1]) for v in (xf, dyb, ctx, dproj)]
        + [whole(v) for v in (wqdf, w1f, w2f, gains, biases, fc1_bias)],
        out_specs=[tile(width), tile(hidden), tile(hidden), tile(width), tile(width)]
        + [pl.BlockSpec((8, width), lambda s: (0, 0))],
        compiler_params=pltpu.CompilerParams(vmem_limit_bytes=VMEM_LIMIT),
        cost_estimate=pl.CostEstimate(flops=int(2e10), bytes_accessed=int(3e7), transcendentals=int(4e6)),
        name="rows_all",
    )(xf, dyb, ctx, dproj, wqdf, w1f, w2f, gains, biases, fc1_bias)


def weights_kernel(plan, h1_ref, ctx_ref, h2_ref, act_ref, dproj_ref, dyb_ref, dab_ref, g_ref):
    job = pl.program_id(0)
    lefts = (h1_ref, ctx_ref, h2_ref, act_ref)
    rights = (dproj_ref, dyb_ref, dab_ref, dyb_ref)
    for kind, (first, jobs, base, per_row) in enumerate(plan):

        @pl.when((job >= first) & (job < first + jobs))
        def _():
            grad = dot_tn(lefts[kind][...], rights[kind][...]).astype(bf16)
            start = base + (job - first) * (TILE // BLOCK) * per_row
            for r in range(TILE // BLOCK):
                for c in range(per_row):
                    g_ref[start + r * per_row + c] = grad[
                        r * BLOCK : (r + 1) * BLOCK, c * BLOCK : (c + 1) * BLOCK
                    ]


def weights_all(h1, ctx, h2, act, dproj, dyb, dab):
    rows = h1.shape[0]
    lefts, rights = (h1, ctx, h2, act), (dproj, dyb, dab, dyb)
    plan, first, base = [], 0, 0
    for left, right in zip(lefts, rights):
        jobs, per_row = left.shape[1] // TILE, right.shape[1] // BLOCK
        plan.append((first, jobs, base, per_row))
        first, base = first + jobs, base + jobs * (TILE // BLOCK) * per_row

    def tile(kind):
        begin, jobs = plan[kind][:2]
        return pl.BlockSpec((rows, TILE), lambda j: (0, jnp.clip(j - begin, 0, jobs - 1)))

    def whole(v):
        return pl.BlockSpec(v.shape, lambda j: (0, 0))

    return pl.pallas_call(
        functools.partial(weights_kernel, tuple(plan)),
        grid=(first,),
        out_shape=jax.ShapeDtypeStruct((base, BLOCK, BLOCK), bf16),
        in_specs=[tile(k) for k in range(4)] + [whole(dproj), whole(dyb), whole(dab)],
        out_specs=pl.BlockSpec((base, BLOCK, BLOCK), lambda j: (0, 0, 0)),
        compiler_params=pltpu.CompilerParams(vmem_limit_bytes=VMEM_LIMIT),
        cost_estimate=pl.CostEstimate(flops=int(1.3e10), bytes_accessed=int(3e7), transcendentals=0),
        name="weights_all",
    )(h1, ctx, h2, act, dproj, dyb, dab)


class Scatter:
    def __init__(self, ring, order, blocks, out, sbuf, rbuf, send, recv):
        self.ring, self.order, self.blocks, self.out = ring, order, blocks, out
        self.sbuf, self.rbuf, self.send, self.recv = sbuf, rbuf, send, recv
        self.per = out.shape[0]
        self.far = ring.count // 2

    def index(self, half, way, hop):
        return (half * 2 + way) * self.far + hop - 1

    def copy(self, half, way, hop):
        i = self.index(half, way, hop)
        return pltpu.make_async_remote_copy(
            src_ref=self.sbuf.at[i],
            dst_ref=self.rbuf.at[i],
            send_sem=self.send.at[i],
            recv_sem=self.recv.at[i],
            device_id=self.ring.peer[way],
            device_id_type=MESH,
        )

    def own(self, dest, half, k):
        return self.blocks[self.order[dest * self.per + k], half * 64 : half * 64 + 64, :].astype(f32)

    def step(self, half, way, hop, hops, first):
        dest = self.ring.at((hops + 1 - hop) if way == 0 else (hop - hops - 1))
        i = self.index(half, way, hop)
        if not first:
            self.copy(half, way, hop - 1).wait_recv()

        def one(k, carry):
            value = self.own(dest, half, k)
            if not first:
                value = value + self.rbuf[i - 1, k].astype(f32)
            self.sbuf[i, k] = value.astype(bf16)
            return carry

        lax.fori_loop(0, self.per, one, 0)
        self.copy(half, way, hop).start()

    def last(self, half, scale):
        came = []
        for way in range(2):
            hops = hop_count(half, way, self.ring.count)
            if hops >= 1:
                self.copy(half, way, hops).wait_recv()
                came.append(self.index(half, way, hops))
        me = self.ring.me

        def one(k, carry):
            value = self.own(me, half, k)
            for i in came:
                value = value + self.rbuf[i, k].astype(f32)
            self.out[k, half * 64 : half * 64 + 64, :] = value * scale
            return carry

        lax.fori_loop(0, self.per, one, 0)

    def finish(self):
        for half in range(2):
            for way in range(2):
                hops = hop_count(half, way, self.ring.count)
                for_hops(1, hops + 1, lambda hop: self.copy(half, way, hop).wait_send(), self.ring.count)


class RowSum:
    def __init__(self, part, out, r1, s2, r2, send, recv):
        self.tensor = lax.axis_index("tensor")
        self.dp = lax.axis_index("dp")
        self.near = self.tensor + 1 - 2 * (self.tensor % 2)
        self.across = (self.tensor + 2) % 4
        self.part, self.out, self.r1, self.s2, self.r2 = part, out, r1, s2, r2
        self.send, self.recv = send, recv
        self.rows = out.shape[0]

    def slot(self, owner):
        return self.part.at[pl.ds(pl.multiple_of(owner * self.rows, 16), self.rows)]

    def remote(self, src, dst, sem, device):
        return pltpu.make_async_remote_copy(
            src_ref=src, dst_ref=dst, send_sem=self.send.at[sem], recv_sem=self.recv.at[sem],
            device_id=(self.dp, device), device_id_type=MESH,
        )

    def pair(self, k):
        owner = (self.near + 2) % 4 if k == 0 else self.near
        return self.remote(self.slot(owner), self.r1.at[k], k, self.near)

    def cross(self):
        return self.remote(self.s2, self.r2, 2, self.across)

    def begin(self):
        self.pair(0).start()
        self.pair(1).start()

    def middle(self):
        self.pair(0).wait_recv()
        self.s2[...] = (self.slot(self.across)[...].astype(f32) + self.r1[0].astype(f32)).astype(bf16)
        self.cross().start()

    def end(self):
        self.pair(1).wait_recv()
        self.cross().wait_recv()
        self.out[...] = (
            self.slot(self.tensor)[...].astype(f32) + self.r1[1].astype(f32) + self.r2[...].astype(f32)
        )
        self.pair(0).wait_send()
        self.pair(1).wait_send()
        self.cross().wait_send()


def sums_kernel(
    count, scale, order, blocks, br, e, small, grad, br_sum, e_sum, small_sum,
    sbuf, rbuf, r1, s2, r2, t_in, d_in, d_out, ss, sr, rs, rr, ts, tr, ds, dr,
):
    ring = Ring(count)
    me, tensor = ring.me, ring.tensor
    scatter = Scatter(ring, order, blocks, grad, sbuf, rbuf, ss, sr)
    sums = [
        RowSum(part, out, r1.at[n], s2.at[n], r2.at[n], rs.at[n], rr.at[n])
        for n, (part, out) in enumerate(((br, br_sum), (e, e_sum)))
    ]

    def t_copy(step):
        return pltpu.make_async_remote_copy(
            src_ref=small, dst_ref=t_in.at[tensor], send_sem=ts.at[step], recv_sem=tr.at[step],
            device_id=(me, (tensor + step) % 4), device_id_type=MESH,
        )

    def d_copy(step):
        return pltpu.make_async_remote_copy(
            src_ref=d_out, dst_ref=d_in.at[me], send_sem=ds.at[step], recv_sem=dr.at[step],
            device_id=((me + step) % count, tensor), device_id_type=MESH,
        )

    barrier = pltpu.get_barrier_semaphore()
    for step in range(1, 4):
        pl.semaphore_signal(barrier, inc=1, device_id=(me, (tensor + step) % 4), device_id_type=MESH)

    @pl.loop(1, count)
    def _(step):
        pl.semaphore_signal(barrier, inc=1, device_id=((me + step) % count, tensor), device_id_type=MESH)

    pl.semaphore_wait(barrier, 3 + count - 1)

    far = count // 2
    for half in range(2):
        for way in (half, 1 - half):
            hops = hop_count(half, way, count)
            if hops >= 1:
                scatter.step(half, way, 1, hops, True)
    for step in range(1, 4):
        t_copy(step).start()
    for s in sums:
        s.begin()
    sums[0].middle()
    for step in range(1, 4):
        t_copy(step).wait_recv()
    t_in[tensor] = small[...]
    row = lax.broadcasted_iota(jnp.int32, small.shape, 0)
    total = t_in[0] + t_in[1] + t_in[2] + t_in[3]
    d_out[...] = jnp.where(row < 4, total, small[...])

    @pl.loop(1, count)
    def _(step):
        d_copy(step).start()

    def ring_step(hop):
        for half in range(2):
            for way in (half, 1 - half):
                hops = hop_count(half, way, count)
                if half == way:
                    scatter.step(half, way, hop, hops, False)
                else:

                    @pl.when(hop <= hops)
                    def _():
                        scatter.step(half, way, hop, hops, False)

    for_hops(2, far, ring_step, count)
    sums[1].middle()
    if far >= 2:
        ring_step(far)
    sums[0].end()

    @pl.loop(1, count)
    def _(step):
        d_copy(step).wait_recv()

    d_in[me] = d_out[...]
    small_sum[...] = lax.fori_loop(1, count, lambda k, acc: acc + d_in[k], d_in[0])
    sums[1].end()
    for half in range(2):
        scatter.last(half, scale)
    scatter.finish()
    for step in range(1, 4):
        t_copy(step).wait_send()

    @pl.loop(1, count)
    def _(step):
        d_copy(step).wait_send()


def sums_all(count, scale, order, blocks, br, e, small):
    per = blocks.shape[0] // count
    rows, width = br.shape[0] // 4, br.shape[1]
    far = count // 2
    vmem = pl.BlockSpec(memory_space=pltpu.VMEM)
    dma = lambda *n: pltpu.SemaphoreType.DMA(n)
    return pl.pallas_call(
        functools.partial(sums_kernel, count, scale),
        out_shape=[
            jax.ShapeDtypeStruct((per, BLOCK, BLOCK), f32),
            jax.ShapeDtypeStruct((rows, width), f32),
            jax.ShapeDtypeStruct((rows, width), f32),
            jax.ShapeDtypeStruct(small.shape, f32),
        ],
        in_specs=[pl.BlockSpec(memory_space=pltpu.SMEM)] + [vmem] * 4,
        out_specs=[vmem] * 4,
        scratch_shapes=[
            pltpu.VMEM((4 * far, per, 64, BLOCK), bf16),
            pltpu.VMEM((4 * far, per, 64, BLOCK), bf16),
            pltpu.VMEM((2, 2, rows, width), bf16),
            pltpu.VMEM((2, rows, width), bf16),
            pltpu.VMEM((2, rows, width), bf16),
            pltpu.VMEM((4,) + small.shape, f32),
            pltpu.VMEM((count,) + small.shape, f32),
            pltpu.VMEM(small.shape, f32),
            dma(4 * far), dma(4 * far), dma(2, 3), dma(2, 3), dma(4), dma(4), dma(count), dma(count),
        ],
        compiler_params=pltpu.CompilerParams(
            collective_id=1, has_side_effects=True, vmem_limit_bytes=VMEM_LIMIT
        ),
        cost_estimate=pl.CostEstimate(flops=0, bytes_accessed=int(3e7), transcendentals=0),
        name="sums_all",
    )(order, blocks, br, e, small)


def shards(
    tokens, out_grad, seq_lengths, norm_gains, row_biases, qkv_weight, qkv_bias, dense_weight, fc1_weight,
    fc1_bias, fc2_weight, block_slot, left_stat, right_stat, left_root, right_root, row_accum,
    qkv_bias_accum, fc1_bias_accum,
):
    tensor_count = lax.axis_size("tensor")
    dp_count = lax.axis_size("dp")
    tensor_rank = lax.axis_index("tensor")
    own_rows, width = tokens.shape
    group_rows = own_rows * tensor_count
    group_seqs = seq_lengths.shape[0]
    grad_scale = 1.0 / math.sqrt(group_rows * dp_count)
    blocks_tensor = block_slot.shape[0] // tensor_count
    per_dev = blocks_tensor // dp_count

    my_slots = lax.dynamic_slice_in_dim(block_slot, tensor_rank * blocks_tensor, blocks_tensor)
    position = my_slots // per_dev // tensor_count * per_dev + my_slots % per_dev
    places = jnp.arange(blocks_tensor, dtype=jnp.int32)
    order = jnp.sum(jnp.where(position[:, None] == places[None, :], places[:, None], 0), axis=0)

    wide, thin = 6 * HEAD, 2 * HEAD
    dense_turned = dense_weight.T
    wqd = jnp.concatenate(
        [qkv_weight[:, :wide], dense_turned[:, :thin], qkv_weight[:, wide:], dense_turned[:, thin:]], axis=1
    )
    xf, h1, dyb, ctx, dproj, wqdf, w1f, w2f, sum_a = mixed_all(
        dp_count, seq_lengths, norm_gains, row_biases, qkv_bias[None], jnp.asarray(rotary_rows()),
        tokens, out_grad, wqd, fc1_weight, fc2_weight.T,
    )
    h2, act, dab, br, e, sum_b = rows_all(
        xf, dyb, ctx, dproj, wqdf, w1f, w2f, norm_gains, row_biases, fc1_bias[None]
    )
    blocks = weights_all(h1, ctx, h2, act, dproj, dyb, dab)
    own_grad, branch, e_sum, small = sums_all(dp_count, grad_scale, order, blocks, br, e, sum_a + sum_b)

    inputs = tokens.astype(f32)
    layer_out = (inputs + branch + row_biases[2] + row_biases[3]).astype(bf16)
    row_ids = tensor_rank * own_rows + jnp.arange(own_rows)
    seq_match = (row_ids // LEN)[:, None] == jnp.arange(group_seqs)[None, :]
    row_limit = jnp.sum(jnp.where(seq_match, seq_lengths[None, :], 0), axis=1)
    row_valid = (row_ids % LEN < row_limit).astype(f32)
    grad_out = out_grad.astype(f32) * row_valid[:, None]
    xhat, scale = normed(inputs)
    input_grad = grad_out + scale * (
        e_sum
        - jnp.mean(e_sum, axis=-1, keepdims=True)
        - xhat * jnp.mean(e_sum * xhat, axis=-1, keepdims=True)
    )

    left_next = stat_decay * left_stat + (1.0 - stat_decay) * jnp.einsum(
        "sij,skj->sik", own_grad, own_grad, precision=highest
    )
    right_next = stat_decay * right_stat + (1.0 - stat_decay) * jnp.einsum(
        "sji,sjk->sik", own_grad, own_grad, precision=highest
    )
    pushed = jnp.einsum("sij,sjk->sik", left_root, own_grad, precision=highest)
    change = -shampoo_rate * jnp.einsum("sij,sjk->sik", pushed, right_root, precision=highest)

    small = small * grad_scale
    row_grads = jnp.concatenate([small[:5], small[4:5]], axis=0)
    row_next, row_change = adagrad_step(row_grads, row_accum)
    qkv_next, qkv_change = adagrad_step(small[5, : qkv_bias.shape[0]], qkv_bias_accum)
    fc1_next, fc1_change = adagrad_step(small[6, : fc1_bias.shape[0]], fc1_bias_accum)
    return (
        layer_out, input_grad, own_grad, left_next, right_next, change,
        row_next, row_change, qkv_next, qkv_change, fc1_next, fc1_change,
    )


def solution(mesh):
    both = ("dp", "tensor")
    return jax.shard_map(
        shards,
        mesh=mesh,
        in_specs=(
            P(both, None), P(both, None), P("dp"), P(), P(), P("dp", "tensor"), P("tensor"),
            P("tensor", "dp"), P("dp", "tensor"), P("tensor"), P("tensor", "dp"), P(),
            P(both, None, None), P(both, None, None), P(both, None, None), P(both, None, None),
            P(), P("tensor"), P("tensor"),
        ),
        out_specs=(
            P(both, None), P(both, None), P(both, None, None), P(both, None, None),
            P(both, None, None), P(both, None, None), P(), P(), P("tensor"), P("tensor"),
            P("tensor"), P("tensor"),
        ),
        check_vma=False,
    )
```

```python
import functools
import math

import jax
import jax.numpy as jnp
import numpy as np
from jax import lax
from jax.experimental import pallas as pl
from jax.experimental.pallas import tpu as pltpu
from jax.sharding import PartitionSpec as P

HEAD = 64
ROT = 16
LEN = 1024
BLOCK = 128
TILE = 256
WIDE = 512
MESH = pl.DeviceIdType.MESH
VMEM_LIMIT = 60 * 1024 * 1024

masked_score = -1e30
shampoo_rate = 0.03
adagrad_rate = 0.1
stat_decay = 0.5
f32 = jnp.float32
bf16 = jnp.bfloat16


def rotary_rows():
    half = ROT // 2
    inverse = np.power(np.float32(10000.0), -(np.arange(half, dtype=np.float32) * np.float32(2.0 / ROT)))
    angles = inverse.astype(np.float32)[:, None] * np.arange(LEN, dtype=np.float32)[None, :]
    return np.concatenate([np.cos(angles), np.sin(angles)], axis=0).astype(np.float32)


def ring_place(me, count):
    low, high = me % 2, me // 2
    return low * (count - 1 - high) + (1 - low) * high


def ring_device(place, count):
    upper = place // (count // 2)
    return (1 - upper) * (2 * place) + upper * (2 * (count - 1 - place) + 1)


def hop_count(half, way, count):
    far = count // 2
    return far if half == way else far - 1


def for_hops(first, last, body, count):
    if count <= 8:
        for hop in range(first, last):
            body(hop)
    elif last > first:

        @pl.loop(first, last)
        def _(hop):
            body(hop)


def as_rows(vec):
    return vec.reshape(-1, BLOCK)


def as_line(rows):
    return jnp.concatenate([rows[k : k + 1, :] for k in range(rows.shape[0])], axis=1)


class Ring:
    def __init__(self, count):
        self.count = count
        self.me = lax.axis_index("dp")
        self.tensor = lax.axis_index("tensor")
        self.place = ring_place(self.me, count)
        self.peer = [
            (ring_device((self.place + step) % count, count), self.tensor) for step in (1, count - 1)
        ]

    def at(self, offset):
        return ring_device((self.place + offset + 2 * self.count) % self.count, self.count)


class Gather:
    def __init__(self, ring, locals_, fulls, send, recv):
        self.ring, self.locals, self.fulls, self.send, self.recv = ring, locals_, fulls, send, recv
        self.far = ring.count // 2

    def part(self, ref, w, half, owner=None):
        rows, cols = self.locals[w].shape
        base = 0 if owner is None else owner * rows
        if rows % 32 == 0:
            return ref.at[pl.ds(pl.multiple_of(base + half * (rows // 2), 16), rows // 2)]
        return ref.at[pl.ds(base, rows), pl.ds(half * (cols // 2), cols // 2)]

    def sem(self, w, half, way, hop):
        return ((w * 2 + half) * 2 + way) * self.far + hop - 1

    def copy(self, w, half, way, hop, source):
        owner = self.ring.at((1 - hop) if way == 0 else (hop - 1))
        src = self.part(self.locals[w], w, half) if source else self.part(self.fulls[w], w, half, owner)
        return pltpu.make_async_remote_copy(
            src_ref=src,
            dst_ref=self.part(self.fulls[w], w, half, owner),
            send_sem=self.send.at[self.sem(w, half, way, hop)],
            recv_sem=self.recv.at[self.sem(w, half, way, hop)],
            device_id=self.ring.peer[way],
            device_id_type=MESH,
        )

    def arrival(self, w, half, way, hop):
        owner = self.ring.at(-hop if way == 0 else hop)
        dst = self.part(self.fulls[w], w, half, owner)
        return pltpu.make_async_remote_copy(
            src_ref=dst,
            dst_ref=dst,
            send_sem=self.send.at[self.sem(w, half, way, hop)],
            recv_sem=self.recv.at[self.sem(w, half, way, hop)],
            device_id=self.ring.peer[way],
            device_id_type=MESH,
        )

    def begin(self, w):
        for half in range(2):
            for way in range(2):
                if hop_count(half, way, self.ring.count) >= 1:
                    self.copy(w, half, way, 1, True).start()

    def forward(self, w, hop, last):
        for half in range(2):
            for way in range(2):
                hops = self.far if half == way else self.far - 1
                if last and hops != self.far:
                    continue
                self.arrival(w, half, way, hop).wait_recv()
                if not last:
                    more = self.far if half == way else self.far - 1
                    if more == self.far:
                        self.copy(w, half, way, hop + 1, False).start()
                    else:

                        @pl.when(hop + 1 <= more)
                        def _():
                            self.copy(w, half, way, hop + 1, False).start()

    def finish(self, w):
        for half in range(2):
            for way in range(2):
                hops = hop_count(half, way, self.ring.count)
                if hops >= 1:
                    self.copy(w, half, way, 1, True).wait_send()
                for_hops(
                    2, hops + 1, lambda hop: self.copy(w, half, way, hop, False).wait_send(), self.ring.count
                )


class Rows:
    def __init__(self, local, full, send, recv, own):
        self.tensor = lax.axis_index("tensor")
        self.dp = lax.axis_index("dp")
        self.near = self.tensor + 1 - 2 * (self.tensor % 2)
        self.across = (self.tensor + 2) % 4
        self.local, self.full, self.send, self.recv, self.own = local, full, send, recv, own
        self.rows = local.shape[0]

    def slot(self, owner, piece=None):
        if piece is None:
            return self.full.at[pl.ds(pl.multiple_of(owner * self.rows, 16), self.rows)]
        half = self.rows // 2
        return self.full.at[pl.ds(pl.multiple_of(owner * self.rows + piece * half, 16), half)]

    def remote(self, src, dst, sem, device):
        return pltpu.make_async_remote_copy(
            src_ref=src,
            dst_ref=dst,
            send_sem=self.send.at[sem],
            recv_sem=self.recv.at[sem],
            device_id=(self.dp, device),
            device_id_type=MESH,
        )

    def keep(self):
        return pltpu.make_async_copy(self.local, self.slot(self.tensor), self.own)

    def pair(self):
        return self.remote(self.local, self.slot(self.tensor), 0, self.near)

    def cross(self, piece):
        half = self.rows // 2
        return self.remote(
            self.local.at[pl.ds(piece * half, half)], self.slot(self.tensor, piece), 1 + piece, self.across
        )

    def onward(self, piece):
        here = self.slot(self.across, piece)
        return self.remote(here, here, 3 + piece, self.near)

    def begin_near(self):
        self.keep().start()
        self.pair().start()

    def begin_cross(self):
        for piece in range(2):
            self.cross(piece).start()

    def pass_on(self):
        for piece in range(2):
            self.cross(piece).wait_recv()
            self.onward(piece).start()

    def finish(self):
        self.keep().wait()
        self.pair().wait()
        for piece in range(2):
            self.cross(piece).wait_send()
            self.onward(piece).wait()


def greet(devices):
    barrier = pltpu.get_barrier_semaphore()
    for device in devices:
        pl.semaphore_signal(barrier, inc=1, device_id=device, device_id_type=MESH)
    pl.semaphore_wait(barrier, len(devices))


def dot_nn(a, b):
    return lax.dot_general(a, b, (((1,), (0,)), ((), ())), preferred_element_type=f32)


def dot_nt(a, b):
    return lax.dot_general(a, b, (((1,), (1,)), ((), ())), preferred_element_type=f32)


def dot_tn(a, b):
    return lax.dot_general(a, b, (((0,), (0,)), ((), ())), preferred_element_type=f32)


def normed(x):
    average = jnp.mean(x, axis=-1, keepdims=True)
    centered = x - average
    variance = jnp.mean(centered * centered, axis=-1, keepdims=True)
    scale = lax.rsqrt(variance + 1e-05)
    return centered * scale, scale


def mixed_kernel(
    count, lim_ref, gain_ref, bias_ref, qb_ref, rot_ref, x, dy, wqd, w1, w2,
    x_out, h1_out, dyb_out, ctx_out, dproj_out, wqd_out, w1f, w2f, sum_ref,
    xf, dyf, wf, h1s, ctxs, dps, qt, kt, vt, dct, ctt, dqt, kr, vr, dks, dvs,
    rs, rr, ro, gs, gr, go, os,
):
    ring = Ring(count)
    half_cols = wqd.shape[1] // 2
    pair_cols = 6 * HEAD
    views = [(wqd.at[:, pl.ds(p * half_cols, half_cols)], wf.at[:, pl.ds(p * half_cols, half_cols)]) for p in (0, 1)]
    views += [(w1, w1f), (w2, w2f)]
    gather = Gather(ring, [v[0] for v in views], [v[1] for v in views], gs, gr)
    rx = Rows(x, xf, rs.at[0], rr.at[0], ro.at[0])
    ry = Rows(dy, dyf, rs.at[1], rr.at[1], ro.at[1])
    greet([ring.peer[0], ring.peer[1], (ring.me, rx.near), (ring.me, rx.across)])
    far = count // 2
    own = []
    for k, (local, full) in enumerate(((wqd, wf), (w1, w1f), (w2, w2f))):
        rows = local.shape[0]
        own.append(
            pltpu.make_async_copy(local, full.at[pl.ds(pl.multiple_of(ring.me * rows, 16), rows)], go.at[k])
        )
    rx.begin_near()
    gather.begin(0)
    rx.begin_cross()
    ry.begin_near()
    for copy in own:
        copy.start()
    sum_ref[...] = jnp.zeros_like(sum_ref)
    tensor = ring.tensor
    tiles = LEN // TILE

    def whole_ring(w):
        for_hops(1, far, lambda hop: gather.forward(w, hop, False), count)
        gather.forward(w, far, True)

    def hop_at(w, hop):
        if count == 8:
            gather.forward(w, hop, hop == far)
        elif hop == 4:
            whole_ring(w)

    def rows_of(seq, i):
        return pl.ds(pl.multiple_of(seq * LEN + i * TILE, TILE), TILE)

    def norm_tile(seq, i):
        rows = rows_of(seq, i)
        xhat, _ = normed(xf[rows, :].astype(f32))
        h1s[rows, :] = (xhat * gain_ref[0:1, :] + bias_ref[0:1, :]).astype(bf16)

    def mask_tile(seq, i):
        rows = rows_of(seq, i)
        place = i * TILE + lax.broadcasted_iota(jnp.int32, (TILE, 1), 0)
        kept = jnp.where(place < lim_ref[seq], dyf[rows, :].astype(f32), 0.0)
        sum_ref[4:5, :] += jnp.sum(kept, axis=0, keepdims=True)
        dyf[rows, :] = kept.astype(bf16)

    def turned(first, second, cosine, sine):
        return first * cosine - second * sine, second * cosine + first * sine

    def prepare_tile(seq, pair, i):
        rows = rows_of(seq, i)
        cols = pl.ds(pl.multiple_of(i * TILE, TILE), TILE)
        begin = pl.multiple_of(pair * half_cols, BLOCK)
        proj = dot_nn(h1s[rows, :], wf[:, pl.ds(begin, pair_cols)])
        proj = proj + as_line(qb_ref[pl.ds(pair * (pair_cols // BLOCK), pair_cols // BLOCK), :])
        proj = proj.T
        dctx = dot_nn(dyf[rows, :], wf[:, pl.ds(begin + pair_cols, 2 * HEAD)]).T
        cosine, sine = rot_ref[0:8, cols], rot_ref[8:16, cols]
        key = i * TILE + lax.broadcasted_iota(jnp.int32, (16, TILE), 1)
        row = lax.broadcasted_iota(jnp.int32, (16, TILE), 0)
        ones = jnp.where(row == 0, 1.0, 0.0)
        hidden = jnp.where((row == 0) & (key >= lim_ref[seq]), masked_score, 0.0)
        for hh in range(2):
            base = 3 * HEAD * hh
            q0, q1 = turned(proj[base : base + 8], proj[base + 8 : base + 16], cosine, sine)
            q = jnp.concatenate([q0, q1, proj[base + 16 : base + HEAD]], axis=0)
            q = q.astype(bf16).astype(f32) * 0.125
            qt[hh, :, cols] = jnp.concatenate([q, ones], axis=0).astype(bf16)
            base += HEAD
            k0, k1 = turned(proj[base : base + 8], proj[base + 8 : base + 16], cosine, sine)
            k = jnp.concatenate([k0, k1, proj[base + 16 : base + HEAD]], axis=0)
            kt[hh, :, cols] = k.astype(bf16)
            kr[hh, cols, :] = jnp.concatenate([k, hidden], axis=0).T.astype(bf16)
            base += HEAD
            v = proj[base : base + HEAD]
            vt[hh, :, cols] = jnp.concatenate([v, ones], axis=0).astype(bf16)
            vr[hh, cols, :] = v.T.astype(bf16)
            dct[hh, :, cols] = dctx[HEAD * hh : HEAD * (hh + 1)].astype(bf16)

    def attend(hh, i):
        here = slice(i * TILE, (i + 1) * TILE)
        chunks = [slice(c * TILE, (c + 1) * TILE) for c in range(i + 1)]
        q = qt[hh, :, here]
        scores = [dot_nn(kr[hh, c, :], q) for c in chunks]
        key = lax.broadcasted_iota(jnp.int32, (TILE, TILE), 0)
        query = lax.broadcasted_iota(jnp.int32, (TILE, TILE), 1)
        scores[i] = jnp.where(key <= query, scores[i], masked_score)
        top = jnp.max(scores[0], axis=0, keepdims=True)
        for s in scores[1:]:
            top = jnp.maximum(top, jnp.max(s, axis=0, keepdims=True))
        probs = [jnp.exp(s - top).astype(bf16) for s in scores]
        total = dot_nn(vt[hh, :, chunks[0]], probs[0])
        for c, p in zip(chunks[1:], probs[1:]):
            total = total + dot_nn(vt[hh, :, c], p)
        inverse = 1.0 / total[HEAD : HEAD + 1]
        context = total[:HEAD] * inverse
        ctt[hh, :, here] = context
        grad = dct[hh, :, here].astype(f32)
        grad = (grad * inverse).astype(bf16)
        delta = jnp.sum(grad.astype(f32) * context, axis=0, keepdims=True)
        dq = None
        for n, (c, p) in enumerate(zip(chunks, probs)):
            dp = dot_nn(vr[hh, c, :], grad)
            ds = (p.astype(f32) * (dp - delta)).astype(bf16)
            part = dot_nn(kt[hh, :, c], ds)
            dq = part if dq is None else dq + part
            dk = dot_nt(ds, q[:HEAD])
            dv = dot_nt(p, grad)
            if i == tiles - 1:
                dks[hh, c, :] = dk
                dvs[hh, c, :] = dv
            else:
                dks[hh, c, :] += dk
                dvs[hh, c, :] += dv
        dqt[hh, :, here] = dq * 0.125

    def collect_tile(seq, pair, i):
        rows = rows_of(seq, i)
        cols = pl.ds(pl.multiple_of(i * TILE, TILE), TILE)
        cosine, sine = rot_ref[0:8, cols], rot_ref[8:16, cols]
        pieces = []
        for hh in range(2):
            for grad in (dqt[hh, :, cols], dks[hh, cols, :].T):
                pieces += [*turned(grad[0:8], grad[8:16], cosine, -sine), grad[16:HEAD]]
            pieces.append(dvs[hh, cols, :].T)
        low = jnp.concatenate(pieces, axis=0).T.astype(bf16)
        wide = pl.ds(pl.multiple_of(pair * pair_cols, BLOCK), pair_cols)
        dps[rows, wide] = low
        sum_ref[5:6, wide] += jnp.sum(low.astype(f32), axis=0, keepdims=True)
        ctx = jnp.concatenate([ctt[0, :, cols], ctt[1, :, cols]], axis=0).T
        ctxs[rows, pl.ds(pl.multiple_of(pair * 2 * HEAD, BLOCK), 2 * HEAD)] = ctx.astype(bf16)

    def save(k, src, dst, seq):
        rows = pl.ds(pl.multiple_of(seq * LEN, LEN), LEN)
        return pltpu.make_async_copy(src.at[rows], dst.at[rows], os.at[k])

    first = tensor // 2

    @pl.loop(0, 4)
    def _(g):
        turn, pair = g // 2, g % 2
        seq = turn + (1 - 2 * turn) * first

        def at(place):
            return pl.when(g == place)

        @at(0)
        def _():
            rx.keep().wait()
            rx.pair().wait_recv()

        @at(2)
        def _():
            for piece in range(2):
                rx.onward(piece).wait_recv()

        @pl.when(pair == 0)
        def _():
            @pl.loop(0, tiles)
            def _(i):
                norm_tile(seq, i)

                @pl.when((g == 0) & (i == 0))
                def _():
                    hop_at(0, 1)
                    gather.begin(1)

                @pl.when((g == 0) & (i == 1))
                def _():
                    hop_at(0, 2)
                    hop_at(1, 1)

                @pl.when((g == 0) & (i == 2))
                def _():
                    hop_at(0, 3)
                    hop_at(1, 2)
                    gather.begin(2)

            save(0, xf, x_out, seq).start()
            save(1, h1s, h1_out, seq).start()

        @at(0)
        def _():
            hop_at(0, 4)
            own[0].wait()
            ry.keep().wait()
            ry.pair().wait_recv()

        @at(1)
        def _():
            hop_at(2, 1)

        @at(2)
        def _():
            ry.pass_on()
            for piece in range(2):
                ry.onward(piece).wait()

        @at(3)
        def _():
            hop_at(3, 3)

        @pl.when(pair == 0)
        def _():
            @pl.loop(0, tiles)
            def _(i):
                mask_tile(seq, i)

            save(2, dyf, dyb_out, seq).start()

        @pl.loop(0, tiles)
        def _(i):
            prepare_tile(seq, pair, i)

        @at(0)
        def _():
            hop_at(1, 3)
            gather.begin(3)

        @at(1)
        def _():
            hop_at(3, 1)

        @pl.loop(0, 2)
        def _(hh):
            for i in reversed(range(tiles)):
                attend(hh, i)

            @pl.when((g == 0) & (hh == 0))
            def _():
                hop_at(1, 4)
                rx.pass_on()
                ry.begin_cross()

            @pl.when((g == 1) & (hh == 0))
            def _():
                hop_at(2, 2)

            @pl.when((g == 1) & (hh == 1))
            def _():
                hop_at(3, 2)

            @pl.when((g == 2) & (hh == 0))
            def _():
                hop_at(2, 3)

            @pl.when((g == 3) & (hh == 0))
            def _():
                hop_at(2, 4)

        @pl.loop(0, tiles)
        def _(i):
            collect_tile(seq, pair, i)

        @pl.when(pair == 1)
        def _():
            save(3, ctxs, ctx_out, seq).start()
            save(4, dps, dproj_out, seq).start()

        @pl.when(pair == 1)
        def _():
            for k, (src, dst) in enumerate(
                ((xf, x_out), (h1s, h1_out), (dyf, dyb_out), (ctxs, ctx_out), (dps, dproj_out))
            ):
                save(k, src, dst, seq).wait()

    keep = pltpu.make_async_copy(wf, wqd_out, os.at[5])
    keep.start()
    hop_at(3, 4)
    for w in range(4):
        gather.finish(w)
    own[1].wait()
    own[2].wait()
    rx.pair().wait_send()
    ry.pair().wait_send()
    for piece in range(2):
        rx.cross(piece).wait_send()
        rx.onward(piece).wait_send()
        ry.cross(piece).wait_send()
    keep.wait()


def mixed_all(count, limits, gains, biases, qkv_bias, rot, x, dy, wqd, w1, w2):
    far = count // 2
    rows, width = 4 * x.shape[0], x.shape[1]
    ctx_cols, proj_cols = 4 * HEAD, qkv_bias.size
    out = lambda r, c: jax.ShapeDtypeStruct((r, c), bf16)
    full = lambda v: out(count * v.shape[0], v.shape[1])
    any_, vmem = pl.BlockSpec(memory_space=pl.ANY), pl.BlockSpec(memory_space=pltpu.VMEM)
    dma = lambda *n: pltpu.SemaphoreType.DMA(n)
    buf = lambda dtype, *shape: pltpu.VMEM(shape, dtype)
    return pl.pallas_call(
        functools.partial(mixed_kernel, count),
        out_shape=[
            out(rows, width), out(rows, width), out(rows, width), out(rows, ctx_cols), out(rows, proj_cols),
            full(wqd), full(w1), full(w2), jax.ShapeDtypeStruct((8, width), f32),
        ],
        in_specs=[pl.BlockSpec(memory_space=pltpu.SMEM)] + [vmem] * 4 + [any_] * 5,
        out_specs=[any_] * 8 + [vmem],
        scratch_shapes=[
            buf(bf16, rows, width), buf(bf16, rows, width), buf(bf16, width, wqd.shape[1]),
            buf(bf16, rows, width), buf(bf16, rows, ctx_cols), buf(bf16, rows, proj_cols),
            buf(bf16, 2, HEAD + 16, LEN), buf(bf16, 2, HEAD, LEN), buf(bf16, 2, HEAD + 16, LEN),
            buf(bf16, 2, HEAD, LEN), buf(f32, 2, HEAD, LEN), buf(f32, 2, HEAD, LEN),
            buf(bf16, 2, LEN, HEAD + 16), buf(bf16, 2, LEN, HEAD), buf(f32, 2, LEN, HEAD), buf(f32, 2, LEN, HEAD),
            dma(2, 5), dma(2, 5), dma(2), dma(16 * far), dma(16 * far), dma(3), dma(6),
        ],
        compiler_params=pltpu.CompilerParams(
            collective_id=0, has_side_effects=True, vmem_limit_bytes=VMEM_LIMIT
        ),
        cost_estimate=pl.CostEstimate(flops=int(2e10), bytes_accessed=int(4e7), transcendentals=int(1e7)),
        name="mixed_all",
    )(limits, gains, biases, qkv_bias, rot, x, dy, wqd, w1, w2)


def gelu_both(x):
    bell = jnp.exp(-0.5 * x * x)
    u = jnp.abs(x) * (1.0 / math.sqrt(2.0))
    t = 1.0 / (1.0 + 0.3275911 * u)
    poly = t * (0.254829592 + t * (-0.284496736 + t * (1.421413741 + t * (-1.453152027 + t * 1.061405429))))
    tail = 0.5 * poly * bell
    phi = jnp.where(x < 0.0, tail, 1.0 - tail)
    return x * phi, phi + x * bell * (1.0 / math.sqrt(2.0 * math.pi))


def hidden_kernel(
    gain_ref, bias_ref, fb_ref, x, h1, dyb, ctx, dproj, w1, w2,
    act_out, dab_out, g_out, sum_ref,
    xs, h1s, dys, cs, ps, w1s, w2s, h2s, acts, dabs, gs, sem, osem, gsem,
):
    rows = x.shape[0]
    tiles = rows // WIDE

    def tile_copy(k, src, dst, i):
        at = pl.ds(pl.multiple_of(i * WIDE, WIDE), WIDE)
        return pltpu.make_async_copy(src.at[at], dst.at[at], sem.at[k, i])

    def whole(k, src, dst):
        return pltpu.make_async_copy(src, dst, sem.at[k, 0])

    whole(0, w1, w1s).start()
    tile_copy(2, x, xs, 0).start()
    whole(1, w2, w2s).start()
    tile_copy(3, dyb, dys, 0).start()
    for i in range(1, tiles):
        tile_copy(2, x, xs, i).start()
        tile_copy(3, dyb, dys, i).start()
    late = [whole(4, h1, h1s), whole(5, ctx, cs), whole(6, dproj, ps)]
    for copy in late:
        copy.start()
    sum_ref[...] = jnp.zeros_like(sum_ref)
    whole(0, w1, w1s).wait()

    def save(k, src, dst, i):
        at = pl.ds(pl.multiple_of(i * WIDE, WIDE), WIDE)
        return pltpu.make_async_copy(src.at[at], dst.at[at], osem.at[k, i])

    @pl.loop(0, tiles)
    def _(i):
        at = pl.ds(pl.multiple_of(i * WIDE, WIDE), WIDE)
        tile_copy(2, x, xs, i).wait()
        xhat, _ = normed(xs[at, :].astype(f32))
        h2 = (xhat * gain_ref[1:2, :] + bias_ref[1:2, :]).astype(bf16)
        h2s[at, :] = h2
        pre = dot_nn(h2, w1s[...]) + as_line(fb_ref[...])
        act, slope = gelu_both(pre)
        acts[at, :] = act.astype(bf16)
        save(0, acts, act_out, i).start()

        @pl.when(i == 0)
        def _():
            whole(1, w2, w2s).wait()

        tile_copy(3, dyb, dys, i).wait()
        dab = (dot_nn(dys[at, :], w2s[...]) * slope).astype(bf16)
        dabs[at, :] = dab
        save(1, dabs, dab_out, i).start()
        sum_ref[6:7, :] += jnp.sum(dab.astype(f32), axis=0, keepdims=True)

    for copy in late:
        copy.wait()
    base, spans = 0, []
    for kind, (left, right) in enumerate(((h1s, ps), (cs, dys), (h2s, dabs), (acts, dys))):
        tall = min(WIDE, left.shape[1])
        jobs, per_row = left.shape[1] // tall, right.shape[1] // BLOCK
        count = tall // BLOCK * per_row

        @pl.loop(0, jobs)
        def _(j):
            grad = dot_tn(left[:, pl.ds(pl.multiple_of(j * tall, tall), tall)], right[...]).astype(bf16)
            start = base + j * count
            for r in range(tall // BLOCK):
                for c in range(per_row):
                    gs[start + r * per_row + c] = grad[
                        r * BLOCK : (r + 1) * BLOCK, c * BLOCK : (c + 1) * BLOCK
                    ]

        span = pl.ds(base, jobs * count)
        spans.append(pltpu.make_async_copy(gs.at[span], g_out.at[span], gsem.at[kind]))
        spans[-1].start()
        base += jobs * count
    for copy in spans:
        copy.wait()
    for i in range(tiles):
        save(0, acts, act_out, i).wait()
        save(1, dabs, dab_out, i).wait()


def hidden_all(x, h1, dyb, ctx, dproj, w1, w2, gains, biases, fc1_bias):
    rows, width = x.shape
    hidden = w1.shape[1]
    blocks = (width * (dproj.shape[1] + hidden) + (ctx.shape[1] + hidden) * width) // (BLOCK * BLOCK)
    any_, vmem = pl.BlockSpec(memory_space=pl.ANY), pl.BlockSpec(memory_space=pltpu.VMEM)
    like = lambda v: pltpu.VMEM(v.shape, v.dtype)
    tiles = rows // WIDE
    return pl.pallas_call(
        hidden_kernel,
        out_shape=[
            jax.ShapeDtypeStruct((rows, hidden), bf16), jax.ShapeDtypeStruct((rows, hidden), bf16),
            jax.ShapeDtypeStruct((blocks, BLOCK, BLOCK), bf16), jax.ShapeDtypeStruct((8, width), f32),
        ],
        in_specs=[vmem] * 3 + [any_] * 7,
        out_specs=[any_] * 3 + [vmem],
        scratch_shapes=[like(v) for v in (x, h1, dyb, ctx, dproj, w1, w2)]
        + [
            pltpu.VMEM((rows, width), bf16), pltpu.VMEM((rows, hidden), bf16), pltpu.VMEM((rows, hidden), bf16),
            pltpu.VMEM((blocks, BLOCK, BLOCK), bf16),
            pltpu.SemaphoreType.DMA((7, tiles)), pltpu.SemaphoreType.DMA((2, tiles)),
            pltpu.SemaphoreType.DMA((4,)),
        ],
        compiler_params=pltpu.CompilerParams(vmem_limit_bytes=VMEM_LIMIT),
        cost_estimate=pl.CostEstimate(flops=int(2.2e10), bytes_accessed=int(4e7), transcendentals=int(4e6)),
        name="hidden_all",
    )(gains, biases, fc1_bias, x, h1, dyb, ctx, dproj, w1, w2)


class Scatter:
    def __init__(self, ring, order, blocks, out, sbuf, rbuf, send, recv):
        self.ring, self.order, self.blocks, self.out = ring, order, blocks, out
        self.sbuf, self.rbuf, self.send, self.recv = sbuf, rbuf, send, recv
        self.per = out.shape[0]
        self.far = ring.count // 2

    def index(self, half, way, hop):
        return (half * 2 + way) * self.far + hop - 1

    def copy(self, half, way, hop, first):
        i = self.index(half, way, hop)
        return pltpu.make_async_remote_copy(
            src_ref=self.sbuf.at[half * 2 + way] if first else self.rbuf.at[i - 1],
            dst_ref=self.rbuf.at[i],
            send_sem=self.send.at[i],
            recv_sem=self.recv.at[i],
            device_id=self.ring.peer[way],
            device_id_type=MESH,
        )

    def own(self, dest, half, k):
        return self.blocks[self.order[dest * self.per + k], half * 64 : half * 64 + 64, :].astype(f32)

    def step(self, half, way, hop, first):
        hops = hop_count(half, way, self.ring.count)
        dest = self.ring.at((hops + 1 - hop) if way == 0 else (hop - hops - 1))
        i = self.index(half, way, hop)
        if not first:
            self.copy(half, way, hop - 1, True).wait_recv()

        def one(k, carry):
            value = self.own(dest, half, k)
            if first:
                self.sbuf[half * 2 + way, k] = value.astype(bf16)
            else:
                self.rbuf[i - 1, k] = (value + self.rbuf[i - 1, k].astype(f32)).astype(bf16)
            return carry

        lax.fori_loop(0, self.per, one, 0)
        self.copy(half, way, hop, first).start()

    def last(self, half, scale):
        came = []
        for way in range(2):
            hops = hop_count(half, way, self.ring.count)
            if hops >= 1:
                self.copy(half, way, hops, True).wait_recv()
                came.append(self.index(half, way, hops))
        me = self.ring.me

        def one(k, carry):
            value = self.own(me, half, k)
            for i in came:
                value = value + self.rbuf[i, k].astype(f32)
            self.out[k, half * 64 : half * 64 + 64, :] = value * scale
            return carry

        lax.fori_loop(0, self.per, one, 0)

    def finish(self):
        for half in range(2):
            for way in range(2):
                hops = hop_count(half, way, self.ring.count)
                for_hops(
                    1, hops + 1, lambda hop: self.copy(half, way, hop, True).wait_send(), self.ring.count
                )


class RowSum:
    def __init__(self, parts, out, r1, r2, send, recv):
        self.tensor = lax.axis_index("tensor")
        self.dp = lax.axis_index("dp")
        self.near = self.tensor + 1 - 2 * (self.tensor % 2)
        self.across = (self.tensor + 2) % 4
        self.parts, self.out, self.r1, self.r2 = parts, out, r1, r2
        self.send, self.recv = send, recv

    def remote(self, src, dst, sem, device):
        return pltpu.make_async_remote_copy(
            src_ref=src, dst_ref=dst, send_sem=self.send.at[sem], recv_sem=self.recv.at[sem],
            device_id=(self.dp, device), device_id_type=MESH,
        )

    def pair(self, k):
        return self.remote(self.parts.at[2 * k], self.r1.at[k], k, self.near)

    def cross(self):
        return self.remote(self.parts.at[1], self.r2, 2, self.across)

    def middle(self):
        self.pair(0).wait_recv()
        self.parts[1] = (self.parts[1].astype(f32) + self.r1[0].astype(f32)).astype(bf16)

    def end(self):
        self.pair(1).wait_recv()
        self.cross().wait_recv()
        self.out[...] = self.parts[3].astype(f32) + self.r1[1].astype(f32) + self.r2[...].astype(f32)

    def finish(self):
        self.pair(0).wait_send()
        self.pair(1).wait_send()
        self.cross().wait_send()


def sums_kernel(
    count, scale, order, gain_ref, small_a, small_b, g_hbm, x, act, dab, ctx, dproj, wqd, w1, w2,
    grad, small_sum, br_out, e_out,
    gbuf, sbuf, rbuf, xs, acts, dabs, cs, ps, wqds, w1s, w2s, parts, r1, r2, tot, small, t_in, d_in, d_out,
    ss, sr, rs, rr, ts, tr, ds, dr, ls, ws, os,
):
    ring = Ring(count)
    me, tensor = ring.me, ring.tensor
    rows = r2.shape[1]
    load_g = pltpu.make_async_copy(g_hbm, gbuf, ws.at[0])
    load_g.start()
    scatter = Scatter(ring, order, gbuf, grad, sbuf, rbuf, ss, sr)
    sums = [
        RowSum(parts.at[n], tot.at[n], r1.at[n], r2.at[n], rs.at[n], rr.at[n]) for n in range(2)
    ]
    near, across = sums[0].near, sums[0].across
    owners = ((near + 2) % 4, across, near, tensor)

    def t_copy(step):
        return pltpu.make_async_remote_copy(
            src_ref=small, dst_ref=t_in.at[tensor], send_sem=ts.at[step], recv_sem=tr.at[step],
            device_id=(me, (tensor + step) % 4), device_id_type=MESH,
        )

    def d_copy(step):
        return pltpu.make_async_remote_copy(
            src_ref=d_out, dst_ref=d_in.at[me], send_sem=ds.at[step], recv_sem=dr.at[step],
            device_id=((me + step) % count, tensor), device_id_type=MESH,
        )

    barrier = pltpu.get_barrier_semaphore()
    for step in range(1, 4):
        pl.semaphore_signal(barrier, inc=1, device_id=(me, (tensor + step) % 4), device_id_type=MESH)

    @pl.loop(1, count)
    def _(step):
        pl.semaphore_signal(barrier, inc=1, device_id=((me + step) % count, tensor), device_id_type=MESH)

    weights = [
        pltpu.make_async_copy(src, dst, ws.at[1 + k])
        for k, (src, dst) in enumerate(((w2, w2s), (w1, w1s), (wqd, wqds)))
    ]

    def load(n):
        at = pl.ds(pl.multiple_of(owners[n] * rows, 16), rows)
        return [
            pltpu.make_async_copy(src.at[at], dst.at[n % 2], ls.at[k, n % 2])
            for k, (src, dst) in enumerate(((x, xs), (act, acts), (dab, dabs), (ctx, cs), (dproj, ps)))
        ]

    far = count // 2
    first, second = ((0, 0), (1, 1)), ((1, 0), (0, 1))
    load_g.wait()
    pl.semaphore_wait(barrier, 3 + count - 1)
    for half, way in first + second:
        if hop_count(half, way, count) >= 1:
            scatter.step(half, way, 1, True)
    for copy in weights + load(0):
        copy.start()
    small[...] = small_a[...] + small_b[...]

    def ring_step(hop, which):
        for half, way in which:
            if which is first:
                scatter.step(half, way, hop, False)
            else:

                @pl.when(hop <= far - 1)
                def _():
                    scatter.step(half, way, hop, False)

    wide, thin = 6 * HEAD, 2 * HEAD
    total = lambda v: jnp.sum(v, axis=0, keepdims=True)

    def work(n, r):
        slot, at = n % 2, slice(r * TILE, (r + 1) * TILE)
        br = dot_nt(acts[slot, at, :], w2s[...])
        dh1 = None
        for p in range(2):
            lo = p * (wide + thin)
            br = br + dot_nt(cs[slot, at, p * thin : (p + 1) * thin], wqds[:, lo + wide : lo + wide + thin])
            part = dot_nt(ps[slot, at, p * wide : (p + 1) * wide], wqds[:, lo : lo + wide])
            dh1 = part if dh1 is None else dh1 + part
        parts[0, n, at, :] = br.astype(bf16)
        dh2 = dot_nt(dabs[slot, at, :], w1s[...])
        xhat, _ = normed(xs[slot, at, :].astype(f32))
        parts[1, n, at, :] = (dh1 * gain_ref[0:1, :] + dh2 * gain_ref[1:2, :]).astype(bf16)
        small[0:1, :] += total(dh1 * xhat)
        small[1:2, :] += total(dh2 * xhat)
        small[2:3, :] += total(dh1)
        small[3:4, :] += total(dh2)

    for n in range(4):
        if n < 3:
            for copy in load(n + 1):
                copy.start()
        if n == 0:
            for copy in weights:
                copy.wait()
        for copy in load(n):
            copy.wait()
        for r in range(rows // TILE):
            work(n, r)
        if n in (0, 2):
            for s in sums:
                s.pair(n // 2).start()
        if n == 1:
            for s in sums:
                s.middle()
            sums[0].cross().start()
            if far >= 2 and count <= 8:
                ring_step(2, first)
        if n == 3 and far >= 2 and count <= 8:
            ring_step(2, second)

    for step in range(1, 4):
        t_copy(step).start()
    sums[1].cross().start()

    def both(hop):
        ring_step(hop, first)
        ring_step(hop, second)

    if count <= 8:
        both(3)
    else:
        for_hops(2, far + 1, both, count)
    for step in range(1, 4):
        t_copy(step).wait_recv()
    t_in[tensor] = small[...]
    row = lax.broadcasted_iota(jnp.int32, small.shape, 0)
    summed = t_in[0] + t_in[1] + t_in[2] + t_in[3]
    d_out[...] = jnp.where(row < 4, summed, small[...])

    @pl.loop(1, count)
    def _(step):
        d_copy(step).start()

    if count <= 8:
        both(4)
    sums[0].end()
    saves = [pltpu.make_async_copy(tot.at[n], out, os.at[n]) for n, out in enumerate((br_out, e_out))]
    saves[0].start()

    @pl.loop(1, count)
    def _(step):
        d_copy(step).wait_recv()

    d_in[me] = d_out[...]
    small_sum[...] = scale * lax.fori_loop(1, count, lambda k, acc: acc + d_in[k], d_in[0])
    sums[1].end()
    saves[1].start()
    for half in range(2):
        scatter.last(half, scale)
    scatter.finish()
    for s in sums:
        s.finish()
    for step in range(1, 4):
        t_copy(step).wait_send()

    @pl.loop(1, count)
    def _(step):
        d_copy(step).wait_send()

    for copy in saves:
        copy.wait()


def sums_all(count, scale, order, gains, small, small_b, blocks, x, act, dab, ctx, dproj, wqd, w1, w2):
    per = blocks.shape[0] // count
    rows, width = x.shape[0] // 4, x.shape[1]
    far = count // 2
    any_, vmem = pl.BlockSpec(memory_space=pl.ANY), pl.BlockSpec(memory_space=pltpu.VMEM)
    dma = lambda *n: pltpu.SemaphoreType.DMA(n)
    two = lambda v: pltpu.VMEM((2, rows, v.shape[1]), v.dtype)
    like = lambda v: pltpu.VMEM(v.shape, v.dtype)
    sum_shape = jax.ShapeDtypeStruct((rows, width), f32)
    return pl.pallas_call(
        functools.partial(sums_kernel, count, scale),
        out_shape=[
            jax.ShapeDtypeStruct((per, BLOCK, BLOCK), f32), jax.ShapeDtypeStruct(small.shape, f32),
            sum_shape, sum_shape,
        ],
        in_specs=[pl.BlockSpec(memory_space=pltpu.SMEM)] + [vmem] * 3 + [any_] * 9,
        out_specs=[vmem, vmem, any_, any_],
        scratch_shapes=[
            like(blocks),
            pltpu.VMEM((4, per, 64, BLOCK), bf16), pltpu.VMEM((4 * far, per, 64, BLOCK), bf16),
            two(x), two(act), two(dab), two(ctx), two(dproj), like(wqd), like(w1), like(w2),
            pltpu.VMEM((2, 4, rows, width), bf16), pltpu.VMEM((2, 2, rows, width), bf16),
            pltpu.VMEM((2, rows, width), bf16), pltpu.VMEM((2, rows, width), f32),
            pltpu.VMEM(small.shape, f32), pltpu.VMEM((4,) + small.shape, f32),
            pltpu.VMEM((count,) + small.shape, f32), pltpu.VMEM(small.shape, f32),
            dma(4 * far), dma(4 * far), dma(2, 3), dma(2, 3), dma(4), dma(4), dma(count), dma(count),
            dma(5, 2), dma(4), dma(2),
        ],
        compiler_params=pltpu.CompilerParams(
            collective_id=1, has_side_effects=True, vmem_limit_bytes=VMEM_LIMIT
        ),
        cost_estimate=pl.CostEstimate(flops=int(1.3e10), bytes_accessed=int(4e7), transcendentals=0),
        name="sums_all",
    )(order, gains, small, small_b, blocks, x, act, dab, ctx, dproj, wqd, w1, w2)


def finish_kernel(
    steps, lim_ref, bias_ref, small_ref, racc_ref, qacc_ref, facc_ref, grad, tok, dy, br, e, ls, rs, lr, rr,
    gout, out, dx, lout, rout, cout, racc, rupd, qacc, qupd, facc, fupd,
    g_v, tok_v, dy_v, br_v, e_v, ls_v, rs_v, lr_v, rr_v, out_v, dx_v, lo_v, ro_v, co_v, isem, osem,
):
    tensor = lax.axis_index("tensor")
    own_rows, blocks = tok.shape[0], grad.shape[0]
    rows, some = own_rows // steps, blocks // steps
    ins = [(grad, g_v), (ls, ls_v), (rs, rs_v), (lr, lr_v), (rr, rr_v), (tok, tok_v), (dy, dy_v), (br, br_v), (e, e_v)]
    outs = [(g_v, gout), (lo_v, lout), (ro_v, rout), (co_v, cout), (out_v, out), (dx_v, dx)]

    def span(ref, s):
        size = ref.shape[0] // steps
        return ref.at[pl.ds(s * size if ref.shape[0] == blocks else pl.multiple_of(s * size, 16), size)]

    def fetch(k, s):
        return pltpu.make_async_copy(span(ins[k][0], s), span(ins[k][1], s), isem.at[k, s])

    def store(k, s):
        return pltpu.make_async_copy(span(outs[k][0], s), span(outs[k][1], s), osem.at[k, s])

    for s in range(steps):
        for k in range(len(ins)):
            fetch(k, s).start()
    small = small_ref[...]

    def adagrad(grad_vec, accum, new, update):
        accum_next = accum + grad_vec * grad_vec
        new[...] = accum_next
        update[...] = -adagrad_rate * grad_vec * lax.rsqrt(accum_next)

    def stacked(line, count):
        return jnp.concatenate([line[:, k * BLOCK : (k + 1) * BLOCK] for k in range(count)], axis=0)

    adagrad(jnp.concatenate([small[0:5], small[4:5]], axis=0), racc_ref[...], racc, rupd)
    adagrad(stacked(small[5:6], qacc.shape[0]), qacc_ref[...], qacc, qupd)
    adagrad(stacked(small[6:7], facc.shape[0]), facc_ref[...], facc, fupd)
    shift = bias_ref[2:3, :] + bias_ref[3:4, :]

    @pl.loop(0, steps)
    def _(s):
        for k in range(len(ins)):
            fetch(k, s).wait()

        for b in range(some):
            k = s * some + b
            low = g_v[k].astype(bf16)
            lo_v[k] = stat_decay * ls_v[k] + (1.0 - stat_decay) * dot_nt(low, low)
            ro_v[k] = stat_decay * rs_v[k] + (1.0 - stat_decay) * dot_tn(low, low)
            pushed = dot_nn(lr_v[k].astype(bf16), low).astype(bf16)
            co_v[k] = -shampoo_rate * dot_nn(pushed, rr_v[k].astype(bf16))

        at = pl.ds(pl.multiple_of(s * rows, 16), rows)
        x = tok_v[at, :].astype(f32)
        out_v[at, :] = (x + br_v[at, :] + shift).astype(bf16)
        start = tensor * own_rows + s * rows
        place = start % LEN + lax.broadcasted_iota(jnp.int32, (rows, 1), 0)
        kept = jnp.where(place < lim_ref[start // LEN], dy_v[at, :].astype(f32), 0.0)
        xhat, scale = normed(x)
        v = e_v[at, :]
        dx_v[at, :] = kept + scale * (
            v - jnp.mean(v, axis=-1, keepdims=True) - xhat * jnp.mean(v * xhat, axis=-1, keepdims=True)
        )
        for k in range(len(outs)):
            store(k, s).start()

    for s in range(steps):
        for k in range(len(outs)):
            store(k, s).wait()


def finish_all(limits, biases, small, racc, qacc, facc, grad, tok, dy, br, e, ls, rs, lr, rr):
    steps = 4 if grad.shape[0] % 4 == 0 else 1
    any_, vmem = pl.BlockSpec(memory_space=pl.ANY), pl.BlockSpec(memory_space=pltpu.VMEM)
    shape = lambda v: jax.ShapeDtypeStruct(v.shape, v.dtype)
    like = lambda v: pltpu.VMEM(v.shape, v.dtype)
    vectors = [racc, racc, qacc, qacc, facc, facc]
    return pl.pallas_call(
        functools.partial(finish_kernel, steps),
        out_shape=[shape(grad), shape(tok), shape(e)] + [shape(grad)] * 3 + [shape(v) for v in vectors],
        in_specs=[pl.BlockSpec(memory_space=pltpu.SMEM)] + [vmem] * 5 + [any_] * 9,
        out_specs=[any_] * 6 + [vmem] * 6,
        scratch_shapes=[like(v) for v in (grad, tok, dy, br, e, ls, rs, lr, rr, tok, e, ls, ls, ls)]
        + [pltpu.SemaphoreType.DMA((9, steps)), pltpu.SemaphoreType.DMA((6, steps))],
        compiler_params=pltpu.CompilerParams(vmem_limit_bytes=VMEM_LIMIT),
        cost_estimate=pl.CostEstimate(flops=int(4e8), bytes_accessed=int(2e7), transcendentals=0),
        name="finish_all",
    )(limits, biases, small, racc, qacc, facc, grad, tok, dy, br, e, ls, rs, lr, rr)


def shards(
    tokens, out_grad, seq_lengths, norm_gains, row_biases, qkv_weight, qkv_bias, dense_weight, fc1_weight,
    fc1_bias, fc2_weight, block_slot, left_stat, right_stat, left_root, right_root, row_accum,
    qkv_bias_accum, fc1_bias_accum,
):
    tensor_count = lax.axis_size("tensor")
    dp_count = lax.axis_size("dp")
    tensor_rank = lax.axis_index("tensor")
    own_rows, width = tokens.shape
    group_rows = own_rows * tensor_count
    grad_scale = 1.0 / math.sqrt(group_rows * dp_count)
    blocks_tensor = block_slot.shape[0] // tensor_count
    per_dev = blocks_tensor // dp_count

    my_slots = lax.dynamic_slice_in_dim(block_slot, tensor_rank * blocks_tensor, blocks_tensor)
    position = my_slots // per_dev // tensor_count * per_dev + my_slots % per_dev
    places = jnp.arange(blocks_tensor, dtype=jnp.int32)
    order = jnp.sum(jnp.where(position[:, None] == places[None, :], places[:, None], 0), axis=0)

    wide, thin = 6 * HEAD, 2 * HEAD
    dense_turned = dense_weight.T
    wqd = jnp.concatenate(
        [qkv_weight[:, :wide], dense_turned[:, :thin], qkv_weight[:, wide:], dense_turned[:, thin:]], axis=1
    )
    xf, h1, dyb, ctx, dproj, wqdf, w1f, w2f, sum_a = mixed_all(
        dp_count, seq_lengths, norm_gains, row_biases, as_rows(qkv_bias), jnp.asarray(rotary_rows()),
        tokens, out_grad, wqd, fc1_weight, fc2_weight.T,
    )
    act, dab, blocks, sum_b = hidden_all(
        xf, h1, dyb, ctx, dproj, w1f, w2f, norm_gains, row_biases, as_rows(fc1_bias)
    )
    own_grad, small, branch, e_sum = sums_all(
        dp_count, grad_scale, order, norm_gains, sum_a, sum_b, blocks, xf, act, dab, ctx, dproj, wqdf, w1f, w2f
    )
    outs = finish_all(
        seq_lengths, row_biases, small, row_accum, as_rows(qkv_bias_accum), as_rows(fc1_bias_accum),
        own_grad, tokens, out_grad, branch, e_sum, left_stat, right_stat, left_root, right_root,
    )
    block_grad, layer_out, input_grad, left_new, right_new, change = outs[:6]
    return (
        layer_out, input_grad, block_grad, left_new, right_new, change,
        *outs[6:8], *(v.reshape(-1) for v in outs[8:]),
    )


def solution(mesh):
    both = ("dp", "tensor")
    return jax.shard_map(
        shards,
        mesh=mesh,
        in_specs=(
            P(both, None), P(both, None), P("dp"), P(), P(), P("dp", "tensor"), P("tensor"),
            P("tensor", "dp"), P("dp", "tensor"), P("tensor"), P("tensor", "dp"), P(),
            P(both, None, None), P(both, None, None), P(both, None, None), P(both, None, None),
            P(), P("tensor"), P("tensor"),
        ),
        out_specs=(
            P(both, None), P(both, None), P(both, None, None), P(both, None, None),
            P(both, None, None), P(both, None, None), P(), P(), P("tensor"), P("tensor"),
            P("tensor"), P("tensor"),
        ),
        check_vma=False,
    )
```

```python
import functools
import math

import jax
import jax.numpy as jnp
import numpy as np
from jax import lax
from jax.experimental import pallas as pl
from jax.experimental.pallas import tpu as pltpu
from jax.sharding import PartitionSpec as P

HEAD = 64
ROT = 16
LEN = 1024
BLOCK = 128
TILE = 256
WIDE = 512
MESH = pl.DeviceIdType.MESH
VMEM_LIMIT = 60 * 1024 * 1024

masked_score = -1e30
shampoo_rate = 0.03
adagrad_rate = 0.1
stat_decay = 0.5
f32 = jnp.float32
bf16 = jnp.bfloat16


def rotary_rows():
    half = ROT // 2
    inverse = np.power(np.float32(10000.0), -(np.arange(half, dtype=np.float32) * np.float32(2.0 / ROT)))
    angles = inverse.astype(np.float32)[:, None] * np.arange(LEN, dtype=np.float32)[None, :]
    return np.concatenate([np.cos(angles), np.sin(angles)], axis=0).astype(np.float32)


def ring_place(me, count):
    low, high = me % 2, me // 2
    return low * (count - 1 - high) + (1 - low) * high


def ring_device(place, count):
    upper = place // (count // 2)
    return (1 - upper) * (2 * place) + upper * (2 * (count - 1 - place) + 1)


def hop_count(half, way, count):
    far = count // 2
    return far if half == way else far - 1


def for_hops(first, last, body, count):
    if count <= 8:
        for hop in range(first, last):
            body(hop)
    elif last > first:

        @pl.loop(first, last)
        def _(hop):
            body(hop)


def as_rows(vec):
    return vec.reshape(-1, BLOCK)


def as_line(rows):
    return jnp.concatenate([rows[k : k + 1, :] for k in range(rows.shape[0])], axis=1)


class Ring:
    def __init__(self, count):
        self.count = count
        self.me = lax.axis_index("dp")
        self.tensor = lax.axis_index("tensor")
        self.place = ring_place(self.me, count)
        self.peer = [
            (ring_device((self.place + step) % count, count), self.tensor) for step in (1, count - 1)
        ]

    def at(self, offset):
        return ring_device((self.place + offset + 2 * self.count) % self.count, self.count)


class Gather:
    def __init__(self, ring, locals_, fulls, send, recv):
        self.ring, self.locals, self.fulls, self.send, self.recv = ring, locals_, fulls, send, recv
        self.far = ring.count // 2

    def part(self, ref, w, half, owner=None):
        rows, cols = self.locals[w].shape
        base = 0 if owner is None else owner * rows
        if rows % 32 == 0:
            return ref.at[pl.ds(pl.multiple_of(base + half * (rows // 2), 16), rows // 2)]
        return ref.at[pl.ds(base, rows), pl.ds(half * (cols // 2), cols // 2)]

    def sem(self, w, half, way, hop):
        return ((w * 2 + half) * 2 + way) * self.far + hop - 1

    def copy(self, w, half, way, hop, source):
        owner = self.ring.at((1 - hop) if way == 0 else (hop - 1))
        src = self.part(self.locals[w], w, half) if source else self.part(self.fulls[w], w, half, owner)
        return pltpu.make_async_remote_copy(
            src_ref=src,
            dst_ref=self.part(self.fulls[w], w, half, owner),
            send_sem=self.send.at[self.sem(w, half, way, hop)],
            recv_sem=self.recv.at[self.sem(w, half, way, hop)],
            device_id=self.ring.peer[way],
            device_id_type=MESH,
        )

    def arrival(self, w, half, way, hop):
        owner = self.ring.at(-hop if way == 0 else hop)
        dst = self.part(self.fulls[w], w, half, owner)
        return pltpu.make_async_remote_copy(
            src_ref=dst,
            dst_ref=dst,
            send_sem=self.send.at[self.sem(w, half, way, hop)],
            recv_sem=self.recv.at[self.sem(w, half, way, hop)],
            device_id=self.ring.peer[way],
            device_id_type=MESH,
        )

    def begin(self, w):
        for half in range(2):
            for way in range(2):
                if hop_count(half, way, self.ring.count) >= 1:
                    self.copy(w, half, way, 1, True).start()

    def forward(self, w, hop, last):
        for half in range(2):
            for way in range(2):
                hops = self.far if half == way else self.far - 1
                if last and hops != self.far:
                    continue
                self.arrival(w, half, way, hop).wait_recv()
                if not last:
                    more = self.far if half == way else self.far - 1
                    if more == self.far:
                        self.copy(w, half, way, hop + 1, False).start()
                    else:

                        @pl.when(hop + 1 <= more)
                        def _():
                            self.copy(w, half, way, hop + 1, False).start()

    def finish(self, w):
        for half in range(2):
            for way in range(2):
                hops = hop_count(half, way, self.ring.count)
                if hops >= 1:
                    self.copy(w, half, way, 1, True).wait_send()
                for_hops(
                    2, hops + 1, lambda hop: self.copy(w, half, way, hop, False).wait_send(), self.ring.count
                )


class Rows:
    def __init__(self, local, full, send, recv, own):
        self.tensor = lax.axis_index("tensor")
        self.dp = lax.axis_index("dp")
        self.near = self.tensor + 1 - 2 * (self.tensor % 2)
        self.across = (self.tensor + 2) % 4
        self.local, self.full, self.send, self.recv, self.own = local, full, send, recv, own
        self.rows = local.shape[0]

    def slot(self, owner, piece=None):
        if piece is None:
            return self.full.at[pl.ds(pl.multiple_of(owner * self.rows, 16), self.rows)]
        half = self.rows // 2
        return self.full.at[pl.ds(pl.multiple_of(owner * self.rows + piece * half, 16), half)]

    def remote(self, src, dst, sem, device):
        return pltpu.make_async_remote_copy(
            src_ref=src,
            dst_ref=dst,
            send_sem=self.send.at[sem],
            recv_sem=self.recv.at[sem],
            device_id=(self.dp, device),
            device_id_type=MESH,
        )

    def keep(self):
        return pltpu.make_async_copy(self.local, self.slot(self.tensor), self.own)

    def pair(self):
        return self.remote(self.local, self.slot(self.tensor), 0, self.near)

    def cross(self, piece):
        half = self.rows // 2
        return self.remote(
            self.local.at[pl.ds(piece * half, half)], self.slot(self.tensor, piece), 1 + piece, self.across
        )

    def onward(self, piece):
        here = self.slot(self.across, piece)
        return self.remote(here, here, 3 + piece, self.near)

    def begin_near(self):
        self.keep().start()
        self.pair().start()

    def begin_cross(self):
        for piece in range(2):
            self.cross(piece).start()

    def pass_piece(self, piece):
        self.cross(piece).wait_recv()
        self.onward(piece).start()

    def pass_on(self):
        for piece in range(2):
            self.pass_piece(piece)

    def finish(self):
        self.keep().wait()
        self.pair().wait()
        for piece in range(2):
            self.cross(piece).wait_send()
            self.onward(piece).wait()


def greet(devices):
    barrier = pltpu.get_barrier_semaphore()
    for device in devices:
        pl.semaphore_signal(barrier, inc=1, device_id=device, device_id_type=MESH)
    pl.semaphore_wait(barrier, len(devices))


def dot_nn(a, b):
    return lax.dot_general(a, b, (((1,), (0,)), ((), ())), preferred_element_type=f32)


def dot_nt(a, b):
    return lax.dot_general(a, b, (((1,), (1,)), ((), ())), preferred_element_type=f32)


def dot_tn(a, b):
    return lax.dot_general(a, b, (((0,), (0,)), ((), ())), preferred_element_type=f32)


def normed(x):
    average = jnp.mean(x, axis=-1, keepdims=True)
    centered = x - average
    variance = jnp.mean(centered * centered, axis=-1, keepdims=True)
    scale = lax.rsqrt(variance + 1e-05)
    return centered * scale, scale


def mixed_kernel(
    count, lim_ref, gain_ref, bias_ref, qb_ref, rot_ref, slot_ref, wd, w2, x, dy, wq, w1,
    x_out, h1_out, dyb_out, ctx_out, dproj_out, wqd_out, w1f, w2f, sum_ref, order_ref,
    xf, dyf, wf, wl, w2l, h1s, ctxs, dps, qt, kt, vt, dct, ctt, dqt, kr, vr, dkvs,
    rs, rr, ro, gs, gr, go, os,
):
    ring = Ring(count)
    pair_cols = 6 * HEAD
    half_cols = pair_cols + 2 * HEAD
    parts = [
        pltpu.make_async_copy(
            wq.at[:, pl.ds(p * pair_cols, pair_cols)], wl.at[:, pl.ds(p * half_cols, pair_cols)], os.at[p]
        )
        for p in range(2)
    ]
    for copy in parts:
        copy.start()
    turned_dense = wd[...].T
    for p in range(2):
        wl[:, p * half_cols + pair_cols : (p + 1) * half_cols] = turned_dense[:, p * 2 * HEAD : (p + 1) * 2 * HEAD]
    views = [(wl.at[:, pl.ds(p * half_cols, half_cols)], wf.at[:, pl.ds(p * half_cols, half_cols)]) for p in (0, 1)]
    views += [(w1, w1f), (w2l, w2f)]
    gather = Gather(ring, [v[0] for v in views], [v[1] for v in views], gs, gr)
    rx = Rows(x, xf, rs.at[0], rr.at[0], ro.at[0])
    ry = Rows(dy, dyf, rs.at[1], rr.at[1], ro.at[1])
    greet([ring.peer[0], ring.peer[1], (ring.me, rx.near), (ring.me, rx.across)])
    far = count // 2
    own = []
    for k, (local, full) in enumerate(((w1, w1f), (w2l, w2f))):
        rows = local.shape[0]
        own.append(
            pltpu.make_async_copy(local, full.at[pl.ds(pl.multiple_of(ring.me * rows, 16), rows)], go.at[k])
        )
    rx.begin_near()
    for copy in parts:
        copy.wait()
    gather.begin(0)
    rx.begin_cross()
    ry.begin_near()
    ry.begin_cross()
    wf[pl.ds(pl.multiple_of(ring.me * wl.shape[0], 16), wl.shape[0]), :] = wl[...]
    own[0].start()
    sum_ref[...] = jnp.zeros_like(sum_ref)
    tensor = ring.tensor
    tiles = LEN // TILE

    def whole_ring(w):
        for_hops(1, far, lambda hop: gather.forward(w, hop, False), count)
        gather.forward(w, far, True)

    def hop_at(w, hop):
        if count == 8:
            gather.forward(w, hop, hop == far)
        elif hop == 4:
            whole_ring(w)

    def rows_of(seq, i):
        return pl.ds(pl.multiple_of(seq * LEN + i * TILE, TILE), TILE)

    def norm_tile(seq, i):
        rows = rows_of(seq, i)
        xhat, _ = normed(xf[rows, :].astype(f32))
        h1s[rows, :] = (xhat * gain_ref[0:1, :] + bias_ref[0:1, :]).astype(bf16)

    def mask_tile(seq, i):
        rows = rows_of(seq, i)
        place = i * TILE + lax.broadcasted_iota(jnp.int32, (TILE, 1), 0)
        kept = jnp.where(place < lim_ref[seq], dyf[rows, :].astype(f32), 0.0)
        sum_ref[4:5, :] += jnp.sum(kept, axis=0, keepdims=True)
        dyf[rows, :] = kept.astype(bf16)

    def turned(first, second, cosine, sine):
        return first * cosine - second * sine, second * cosine + first * sine

    def prepare_tile(seq, pair, i):
        rows = rows_of(seq, i)
        cols = pl.ds(pl.multiple_of(i * TILE, TILE), TILE)
        proj = dot_nn(h1s[rows, :], wf[:, pl.ds(pl.multiple_of(pair * half_cols, BLOCK), pair_cols)])
        proj = proj + as_line(qb_ref[pl.ds(pair * (pair_cols // BLOCK), pair_cols // BLOCK), :])
        proj = proj.T
        cosine, sine = rot_ref[0:8, cols], rot_ref[8:16, cols]
        key = i * TILE + lax.broadcasted_iota(jnp.int32, (16, TILE), 1)
        row = lax.broadcasted_iota(jnp.int32, (16, TILE), 0)
        ones = jnp.where(row == 0, 1.0, 0.0).astype(bf16)
        hidden = jnp.where((row == 0) & (key >= lim_ref[seq]), masked_score, 0.0).astype(bf16)
        blank = jnp.zeros((48, TILE), bf16)
        none = jnp.zeros((HEAD, TILE), bf16)
        for hh in range(2):
            h = 2 * pair + hh
            base = 3 * HEAD * hh
            q0, q1 = turned(proj[base : base + 8], proj[base + 8 : base + 16], cosine, sine)
            q = jnp.concatenate([q0, q1, proj[base + 16 : base + HEAD]], axis=0).astype(bf16)
            q = (q.astype(f32) * 0.125).astype(bf16)
            qt[h, :, cols] = jnp.concatenate([q, ones, blank], axis=0)
            base += HEAD
            k0, k1 = turned(proj[base : base + 8], proj[base + 8 : base + 16], cosine, sine)
            k = jnp.concatenate([k0, k1, proj[base + 16 : base + HEAD]], axis=0).astype(bf16)
            kt[h, :, cols] = k
            kr[h, cols, :] = jnp.concatenate([k, hidden, blank], axis=0).T
            base += HEAD
            v = proj[base : base + HEAD].astype(bf16)
            vt[h, :, cols] = jnp.concatenate([v, ones], axis=0)
            vr[h, cols, :] = jnp.concatenate([none, v], axis=0).T

    def context_tile(seq, pair, i):
        cols = pl.ds(pl.multiple_of(i * TILE, TILE), TILE)
        begin = pair * half_cols + pair_cols
        dctx = dot_nn(dyf[rows_of(seq, i), :], wf[:, begin : begin + 2 * HEAD]).T.astype(bf16)
        for hh in range(2):
            dct[2 * pair + hh, :, cols] = dctx[HEAD * hh : HEAD * (hh + 1)]

    def back_tile(seq, i):
        mask_tile(seq, i)
        context_tile(seq, 0, i)
        context_tile(seq, 1, i)

    def attend(pair, i, fresh):
        here = slice(i * TILE, (i + 1) * TILE)
        chunks = [slice(c * TILE, (c + 1) * TILE) for c in range(i + 1)]
        heads = range(2)
        of = [2 * pair, 2 * pair + 1]
        key = lax.broadcasted_iota(jnp.int32, (TILE, TILE), 0)
        query = lax.broadcasted_iota(jnp.int32, (TILE, TILE), 1)
        q = [qt[of[hh], :, here] for hh in heads]
        scores = [[dot_nn(kr[of[hh], c, :], q[hh]) for c in chunks] for hh in heads]
        probs, grads, deltas, both = [], [], [], []
        none = jnp.zeros((HEAD, TILE), bf16)
        for hh in heads:
            scores[hh][i] = jnp.where(key <= query, scores[hh][i], masked_score)
            top = jnp.max(scores[hh][0], axis=0, keepdims=True)
            for s in scores[hh][1:]:
                top = jnp.maximum(top, jnp.max(s, axis=0, keepdims=True))
            probs.append([jnp.exp(s - top).astype(bf16) for s in scores[hh]])
        for hh in heads:
            total = dot_nn(vt[of[hh], :, chunks[0]], probs[hh][0])
            for c, p in zip(chunks[1:], probs[hh][1:]):
                total = total + dot_nn(vt[of[hh], :, c], p)
            inverse = 1.0 / total[HEAD : HEAD + 1]
            context = total[:HEAD] * inverse
            ctt[of[hh], :, here] = context
            grad = (dct[of[hh], :, here].astype(f32) * inverse).astype(bf16)
            deltas.append(jnp.sum(grad.astype(f32) * context, axis=0, keepdims=True))
            grad = jnp.concatenate([none, grad], axis=0)
            grads.append(grad)
            both.append(jnp.concatenate([jnp.concatenate([q[hh][:HEAD], none], axis=0), grad], axis=1))
        dq = [None, None]
        for n, c in enumerate(chunks):
            for hh in heads:
                p = probs[hh][n]
                dp = dot_nn(vr[of[hh], c, :], grads[hh])
                ds = (p.astype(f32) * (dp - deltas[hh])).astype(bf16)
                part = dot_nn(kt[of[hh], :, c], ds)
                dq[hh] = part if dq[hh] is None else dq[hh] + part
                dkv = dot_nt(jnp.concatenate([ds, p], axis=1), both[hh])
                if n in fresh:
                    dkvs[of[hh], c, :] = dkv
                else:
                    dkvs[of[hh], c, :] += dkv
        for hh in heads:
            dqt[of[hh], :, here] = dq[hh] * 0.125

    def collect_tile(seq, i):
        rows = rows_of(seq, i)
        cols = pl.ds(pl.multiple_of(i * TILE, TILE), TILE)
        cosine, sine = rot_ref[0:8, cols], rot_ref[8:16, cols]
        for pair in range(2):
            pieces = []
            for h in (2 * pair, 2 * pair + 1):
                dkv = dkvs[h, cols, :].T
                for grad in (dqt[h, :, cols], dkv[:HEAD]):
                    pieces += [*turned(grad[0:8], grad[8:16], cosine, -sine), grad[16:HEAD]]
                pieces.append(dkv[HEAD:])
            low = jnp.concatenate(pieces, axis=0).T.astype(bf16)
            wide = slice(pair * pair_cols, (pair + 1) * pair_cols)
            dps[rows, wide] = low
            sum_ref[5:6, wide] += jnp.sum(low.astype(f32), axis=0, keepdims=True)
            ctx = jnp.concatenate([ctt[2 * pair, :, cols], ctt[2 * pair + 1, :, cols]], axis=0).T
            ctxs[rows, pair * 2 * HEAD : (pair + 1) * 2 * HEAD] = ctx.astype(bf16)

    def save(turn, k, seq):
        src, dst = ((xf, x_out), (h1s, h1_out), (dyf, dyb_out), (ctxs, ctx_out), (dps, dproj_out))[k]
        rows = pl.ds(pl.multiple_of(seq * LEN, LEN), LEN)
        return pltpu.make_async_copy(src.at[rows], dst.at[rows], os.at[turn * 5 + k])

    mine = order_ref.shape[1]
    per = mine // count
    place = lax.broadcasted_iota(jnp.int32, (mine, 1), 0).astype(f32)
    owner = jnp.floor((place + 0.5) / per)
    wanted = (owner * 4.0 + lax.convert_element_type(tensor, f32)) * per + (place - owner * per)
    found = jnp.zeros(order_ref.shape, f32)
    for r in range(slot_ref.shape[0]):
        hit = jnp.where(slot_ref[r : r + 1, :].astype(f32) == wanted, 1.0, 0.0).astype(bf16)
        block = r * BLOCK + lax.broadcasted_iota(jnp.int32, (8, BLOCK), 1) - tensor * mine
        found = found + dot_nt(jnp.clip(block, 0, mine - 1).astype(f32).astype(bf16), hit)
    order_ref[...] = (found + 0.5).astype(jnp.int32)

    seq = tensor // 2
    rx.keep().wait()
    rx.pair().wait_recv()

    @pl.loop(0, tiles)
    def _(i):
        norm_tile(seq, i)

        @pl.when(i == 0)
        def _():
            hop_at(0, 1)
            gather.begin(1)

        @pl.when(i == 1)
        def _():
            hop_at(0, 2)
            hop_at(1, 1)

        @pl.when(i == 2)
        def _():
            hop_at(0, 3)
            hop_at(1, 2)
            gather.begin(2)

    save(0, 0, seq).start()
    save(0, 1, seq).start()
    w2l[...] = w2[...].T
    hop_at(0, 4)
    ry.keep().wait()
    ry.pair().wait_recv()

    @pl.loop(0, tiles // 2)
    def _(i):
        for sub in range(2):
            prepare_tile(seq, 0, 2 * i + sub)


    @pl.loop(0, tiles)
    def _(i):
        mask_tile(seq, i)
        context_tile(seq, 0, i)

    save(0, 2, seq).start()

    @pl.loop(0, 2)
    def _(pair):
        @pl.when(pair == 1)
        def _():
            hop_at(1, 4)
            hop_at(2, 1)

            @pl.loop(0, tiles // 2)
            def _(i):
                for sub in range(2):
                    prepare_tile(seq, 1, 2 * i + sub)
                    context_tile(seq, 1, 2 * i + sub)

        attend(pair, 3, (0, 1, 2, 3))

        @pl.when(pair == 0)
        def _():
            hop_at(1, 3)
            gather.begin(3)
            own[1].start()

        attend(pair, 2, ())

        @pl.when(pair == 0)
        def _():
            rx.pass_on()

        @pl.when(pair == 1)
        def _():
            hop_at(3, 1)

        attend(pair, 1, ())
        attend(pair, 0, ())

    @pl.loop(0, tiles)
    def _(i):
        collect_tile(seq, i)

    save(0, 3, seq).start()
    save(0, 4, seq).start()
    keep = pltpu.make_async_copy(wf, wqd_out, os.at[10])
    keep.start()

    seq = 1 - seq
    for piece in range(2):
        rx.onward(piece).wait_recv()

    @pl.loop(0, tiles)
    def _(i):
        norm_tile(seq, i)

    save(1, 0, seq).start()
    save(1, 1, seq).start()
    ry.pass_piece(0)

    for pair in range(2):

        @pl.loop(0, tiles // 2)
        def _(i):
            for sub in range(2):
                prepare_tile(seq, pair, 2 * i + sub)

        if pair == 0:
            hop_at(2, 2)

    ry.onward(0).wait()
    back_tile(seq, 0)
    back_tile(seq, 2)

    @pl.loop(0, 2)
    def _(pair):
        attend(pair, 2, (0, 1, 2))

        @pl.when(pair == 0)
        def _():
            hop_at(3, 2)

        attend(pair, 0, ())

    ry.pass_piece(1)
    ry.onward(1).wait()
    back_tile(seq, 1)
    back_tile(seq, 3)
    save(1, 2, seq).start()
    hop_at(2, 3)

    @pl.loop(0, 2)
    def _(pair):
        attend(pair, 3, (3,))

        @pl.when(pair == 1)
        def _():
            hop_at(3, 3)

        attend(pair, 1, ())

    @pl.loop(0, tiles)
    def _(i):
        collect_tile(seq, i)

    save(1, 3, seq).start()
    save(1, 4, seq).start()
    hop_at(2, 4)
    hop_at(3, 4)
    for w in range(4):
        gather.finish(w)
    own[0].wait()
    own[1].wait()
    rx.pair().wait_send()
    ry.pair().wait_send()
    for piece in range(2):
        rx.cross(piece).wait_send()
        rx.onward(piece).wait_send()
        ry.cross(piece).wait_send()
    for turn in range(2):
        for k in range(5):
            save(turn, k, turn + (1 - 2 * turn) * (tensor // 2)).wait()
    keep.wait()


def mixed_all(count, limits, gains, biases, qkv_bias, rot, slots, x, dy, wq, wd, w1, w2):
    far = count // 2
    rows, width = 4 * x.shape[0], x.shape[1]
    ctx_cols, proj_cols = wd.shape[0], wq.shape[1]
    shard = wq.shape[0]
    out = lambda r, c: jax.ShapeDtypeStruct((r, c), bf16)
    any_, vmem = pl.BlockSpec(memory_space=pl.ANY), pl.BlockSpec(memory_space=pltpu.VMEM)
    dma = lambda *n: pltpu.SemaphoreType.DMA(n)
    buf = lambda dtype, *shape: pltpu.VMEM(shape, dtype)
    heads, both = 4, ctx_cols + proj_cols
    return pl.pallas_call(
        functools.partial(mixed_kernel, count),
        out_shape=[
            out(rows, width), out(rows, width), out(rows, width), out(rows, ctx_cols), out(rows, proj_cols),
            out(width, both), out(width, w1.shape[1]), out(width, w2.shape[0]),
            jax.ShapeDtypeStruct((8, width), f32), jax.ShapeDtypeStruct((8, slots.size // 4), jnp.int32),
        ],
        in_specs=[pl.BlockSpec(memory_space=pltpu.SMEM)] + [vmem] * 7 + [any_] * 4,
        out_specs=[any_] * 8 + [vmem] * 2,
        scratch_shapes=[
            buf(bf16, rows, width), buf(bf16, rows, width), buf(bf16, width, both),
            buf(bf16, shard, both), buf(bf16, shard, w2.shape[0]),
            buf(bf16, rows, width), buf(bf16, rows, ctx_cols), buf(bf16, rows, proj_cols),
            buf(bf16, heads, 2 * HEAD, LEN), buf(bf16, heads, HEAD, LEN), buf(bf16, heads, HEAD + 16, LEN),
            buf(bf16, heads, HEAD, LEN), buf(f32, heads, HEAD, LEN), buf(f32, heads, HEAD, LEN),
            buf(bf16, heads, LEN, 2 * HEAD), buf(bf16, heads, LEN, 2 * HEAD), buf(f32, heads, LEN, 2 * HEAD),
            dma(2, 5), dma(2, 5), dma(2), dma(16 * far), dma(16 * far), dma(2), dma(11),
        ],
        compiler_params=pltpu.CompilerParams(
            collective_id=0, has_side_effects=True, vmem_limit_bytes=VMEM_LIMIT
        ),
        cost_estimate=pl.CostEstimate(flops=int(2e10), bytes_accessed=int(4e7), transcendentals=int(1e7)),
        name="mixed_all",
    )(limits, gains, biases, qkv_bias, rot, slots, wd, w2, x, dy, wq, w1)


def gelu_both(x):
    bell = jnp.exp(-0.5 * x * x)
    u = jnp.abs(x) * (1.0 / math.sqrt(2.0))
    t = 1.0 / (1.0 + 0.3275911 * u)
    poly = t * (0.254829592 + t * (-0.284496736 + t * (1.421413741 + t * (-1.453152027 + t * 1.061405429))))
    tail = 0.5 * poly * bell
    phi = jnp.where(x < 0.0, tail, 1.0 - tail)
    return x * phi, phi + x * bell * (1.0 / math.sqrt(2.0 * math.pi))


def hidden_kernel(
    gain_ref, bias_ref, fb_ref, x, h1, dyb, ctx, dproj, w1, w2,
    act_out, dab_out, g_out, sum_ref,
    xs, h1s, dys, cs, ps, w1s, w2s, h2s, acts, dabs, gs, sem, osem, gsem,
):
    rows = x.shape[0]
    tiles = rows // WIDE

    def tile_copy(k, src, dst, i):
        at = pl.ds(pl.multiple_of(i * WIDE, WIDE), WIDE)
        return pltpu.make_async_copy(src.at[at], dst.at[at], sem.at[k, i])

    def whole(k, src, dst):
        return pltpu.make_async_copy(src, dst, sem.at[k, 0])

    whole(0, w1, w1s).start()
    tile_copy(2, x, xs, 0).start()
    whole(1, w2, w2s).start()
    tile_copy(3, dyb, dys, 0).start()
    for i in range(1, tiles):
        tile_copy(2, x, xs, i).start()
        tile_copy(3, dyb, dys, i).start()
    late = [whole(4, h1, h1s), whole(5, ctx, cs), whole(6, dproj, ps)]
    for copy in late:
        copy.start()
    sum_ref[...] = jnp.zeros_like(sum_ref)
    whole(0, w1, w1s).wait()

    def save(k, src, dst, i):
        at = pl.ds(pl.multiple_of(i * WIDE, WIDE), WIDE)
        return pltpu.make_async_copy(src.at[at], dst.at[at], osem.at[k, i])

    whole(1, w2, w2s).wait()

    @pl.loop(0, tiles)
    def _(i):
        at = pl.ds(pl.multiple_of(i * WIDE, WIDE), WIDE)
        tile_copy(2, x, xs, i).wait()
        tile_copy(3, dyb, dys, i).wait()
        xhat, _ = normed(xs[at, :].astype(f32))
        h2 = (xhat * gain_ref[1:2, :] + bias_ref[1:2, :]).astype(bf16)
        h2s[at, :] = h2
        pre = dot_nn(h2, w1s[...]) + as_line(fb_ref[...])
        da = dot_nn(dys[at, :], w2s[...])
        act, slope = gelu_both(pre)
        acts[at, :] = act.astype(bf16)
        dab = (da * slope).astype(bf16)
        dabs[at, :] = dab
        save(0, acts, act_out, i).start()
        save(1, dabs, dab_out, i).start()
        sum_ref[6:7, :] += jnp.sum(dab.astype(f32), axis=0, keepdims=True)

    for copy in late:
        copy.wait()
    base, spans = 0, []
    for kind, (left, right) in enumerate(((h1s, ps), (cs, dys), (h2s, dabs), (acts, dys))):
        tall = min(WIDE, left.shape[1])
        jobs, per_row = left.shape[1] // tall, right.shape[1] // BLOCK
        count = tall // BLOCK * per_row

        @pl.loop(0, jobs)
        def _(j):
            grad = dot_tn(left[:, pl.ds(pl.multiple_of(j * tall, tall), tall)], right[...]).astype(bf16)
            start = base + j * count
            for r in range(tall // BLOCK):
                for c in range(per_row):
                    gs[start + r * per_row + c] = grad[
                        r * BLOCK : (r + 1) * BLOCK, c * BLOCK : (c + 1) * BLOCK
                    ]

        span = pl.ds(base, jobs * count)
        spans.append(pltpu.make_async_copy(gs.at[span], g_out.at[span], gsem.at[kind]))
        spans[-1].start()
        base += jobs * count
    for copy in spans:
        copy.wait()
    for i in range(tiles):
        save(0, acts, act_out, i).wait()
        save(1, dabs, dab_out, i).wait()


def hidden_all(x, h1, dyb, ctx, dproj, w1, w2, gains, biases, fc1_bias):
    rows, width = x.shape
    hidden = w1.shape[1]
    blocks = (width * (dproj.shape[1] + hidden) + (ctx.shape[1] + hidden) * width) // (BLOCK * BLOCK)
    any_, vmem = pl.BlockSpec(memory_space=pl.ANY), pl.BlockSpec(memory_space=pltpu.VMEM)
    like = lambda v: pltpu.VMEM(v.shape, v.dtype)
    tiles = rows // WIDE
    return pl.pallas_call(
        hidden_kernel,
        out_shape=[
            jax.ShapeDtypeStruct((rows, hidden), bf16), jax.ShapeDtypeStruct((rows, hidden), bf16),
            jax.ShapeDtypeStruct((blocks, BLOCK, BLOCK), bf16), jax.ShapeDtypeStruct((8, width), f32),
        ],
        in_specs=[vmem] * 3 + [any_] * 7,
        out_specs=[any_] * 3 + [vmem],
        scratch_shapes=[like(v) for v in (x, h1, dyb, ctx, dproj, w1, w2)]
        + [
            pltpu.VMEM((rows, width), bf16), pltpu.VMEM((rows, hidden), bf16), pltpu.VMEM((rows, hidden), bf16),
            pltpu.VMEM((blocks, BLOCK, BLOCK), bf16),
            pltpu.SemaphoreType.DMA((7, tiles)), pltpu.SemaphoreType.DMA((2, tiles)),
            pltpu.SemaphoreType.DMA((4,)),
        ],
        compiler_params=pltpu.CompilerParams(vmem_limit_bytes=VMEM_LIMIT),
        cost_estimate=pl.CostEstimate(flops=int(2.2e10), bytes_accessed=int(4e7), transcendentals=int(4e6)),
        name="hidden_all",
    )(gains, biases, fc1_bias, x, h1, dyb, ctx, dproj, w1, w2)


class Scatter:
    def __init__(self, ring, order, blocks, out, sbuf, rbuf, send, recv):
        self.ring, self.order, self.blocks, self.out = ring, order, blocks, out
        self.sbuf, self.rbuf, self.send, self.recv = sbuf, rbuf, send, recv
        self.per = out.shape[0]
        self.far = ring.count // 2

    def index(self, half, way, hop):
        return (half * 2 + way) * self.far + hop - 1

    def copy(self, half, way, hop, first):
        i = self.index(half, way, hop)
        return pltpu.make_async_remote_copy(
            src_ref=self.sbuf.at[half * 2 + way] if first else self.rbuf.at[i - 1],
            dst_ref=self.rbuf.at[i],
            send_sem=self.send.at[i],
            recv_sem=self.recv.at[i],
            device_id=self.ring.peer[way],
            device_id_type=MESH,
        )

    def own(self, dest, half, k):
        return self.blocks[self.order[0, dest * self.per + k], half * 64 : half * 64 + 64, :].astype(f32)

    def step(self, half, way, hop, first):
        hops = hop_count(half, way, self.ring.count)
        dest = self.ring.at((hops + 1 - hop) if way == 0 else (hop - hops - 1))
        i = self.index(half, way, hop)
        if not first:
            self.copy(half, way, hop - 1, True).wait_recv()

        def one(k, carry):
            value = self.own(dest, half, k)
            if first:
                self.sbuf[half * 2 + way, k] = value.astype(bf16)
            else:
                self.rbuf[i - 1, k] = (value + self.rbuf[i - 1, k].astype(f32)).astype(bf16)
            return carry

        lax.fori_loop(0, self.per, one, 0)
        self.copy(half, way, hop, first).start()

    def last(self, half, scale):
        came = []
        for way in range(2):
            hops = hop_count(half, way, self.ring.count)
            if hops >= 1:
                self.copy(half, way, hops, True).wait_recv()
                came.append(self.index(half, way, hops))
        me = self.ring.me

        def one(k, carry):
            value = self.own(me, half, k)
            for i in came:
                value = value + self.rbuf[i, k].astype(f32)
            self.out[k, half * 64 : half * 64 + 64, :] = value * scale
            return carry

        lax.fori_loop(0, self.per, one, 0)

    def finish(self):
        for half in range(2):
            for way in range(2):
                hops = hop_count(half, way, self.ring.count)
                for_hops(
                    1, hops + 1, lambda hop: self.copy(half, way, hop, True).wait_send(), self.ring.count
                )


class RowSum:
    def __init__(self, parts, out, r1, r2, send, recv):
        self.tensor = lax.axis_index("tensor")
        self.dp = lax.axis_index("dp")
        self.near = self.tensor + 1 - 2 * (self.tensor % 2)
        self.across = (self.tensor + 2) % 4
        self.parts, self.out, self.r1, self.r2 = parts, out, r1, r2
        self.send, self.recv = send, recv

    def remote(self, src, dst, sem, device):
        return pltpu.make_async_remote_copy(
            src_ref=src, dst_ref=dst, send_sem=self.send.at[sem], recv_sem=self.recv.at[sem],
            device_id=(self.dp, device), device_id_type=MESH,
        )

    def pair(self, k):
        return self.remote(self.parts.at[2 * k], self.r1.at[k], k, self.near)

    def cross(self):
        return self.remote(self.parts.at[1], self.r2, 2, self.across)

    def middle(self):
        self.pair(0).wait_recv()
        self.parts[1] = (self.parts[1].astype(f32) + self.r1[0].astype(f32)).astype(bf16)

    def end(self):
        self.pair(1).wait_recv()
        self.cross().wait_recv()
        self.out[...] = self.parts[3].astype(f32) + self.r1[1].astype(f32) + self.r2[...].astype(f32)

    def finish(self):
        self.pair(0).wait_send()
        self.pair(1).wait_send()
        self.cross().wait_send()


def sums_kernel(
    count, scale, order, gain_ref, small_a, small_b, g_hbm, x, act, dab, ctx, dproj, wqd, w1, w2,
    grad, small_sum, br_out, e_out,
    gbuf, sbuf, rbuf, xs, acts, dabs, cs, ps, wqds, w1s, w2s, parts, r1, r2, tot, small, t_in, d_in, d_out,
    ss, sr, rs, rr, ts, tr, ds, dr, ls, ws, os,
):
    ring = Ring(count)
    me, tensor = ring.me, ring.tensor
    rows = r2.shape[1]
    load_g = pltpu.make_async_copy(g_hbm, gbuf, ws.at[0])
    load_g.start()
    scatter = Scatter(ring, order, gbuf, grad, sbuf, rbuf, ss, sr)
    sums = [
        RowSum(parts.at[n], tot.at[n], r1.at[n], r2.at[n], rs.at[n], rr.at[n]) for n in range(2)
    ]
    near, across = sums[0].near, sums[0].across
    owners = ((near + 2) % 4, across, near, tensor)

    def t_copy(step):
        return pltpu.make_async_remote_copy(
            src_ref=small, dst_ref=t_in.at[tensor], send_sem=ts.at[step], recv_sem=tr.at[step],
            device_id=(me, (tensor + step) % 4), device_id_type=MESH,
        )

    def d_copy(step):
        return pltpu.make_async_remote_copy(
            src_ref=d_out, dst_ref=d_in.at[me], send_sem=ds.at[step], recv_sem=dr.at[step],
            device_id=((me + step) % count, tensor), device_id_type=MESH,
        )

    barrier = pltpu.get_barrier_semaphore()
    for step in range(1, 4):
        pl.semaphore_signal(barrier, inc=1, device_id=(me, (tensor + step) % 4), device_id_type=MESH)

    @pl.loop(1, count)
    def _(step):
        pl.semaphore_signal(barrier, inc=1, device_id=((me + step) % count, tensor), device_id_type=MESH)

    weights = [
        pltpu.make_async_copy(src, dst, ws.at[1 + k])
        for k, (src, dst) in enumerate(((w2, w2s), (w1, w1s), (wqd, wqds)))
    ]

    def load(n):
        at = pl.ds(pl.multiple_of(owners[n] * rows, 16), rows)
        return [
            pltpu.make_async_copy(src.at[at], dst.at[n % 2], ls.at[k, n % 2])
            for k, (src, dst) in enumerate(((x, xs), (act, acts), (dab, dabs), (ctx, cs), (dproj, ps)))
        ]

    far = count // 2
    first, second = ((0, 0), (1, 1)), ((1, 0), (0, 1))
    load_g.wait()
    pl.semaphore_wait(barrier, 3 + count - 1)
    for half, way in first + second:
        if hop_count(half, way, count) >= 1:
            scatter.step(half, way, 1, True)
    for copy in weights + load(0):
        copy.start()
    small[...] = small_a[...] + small_b[...]

    def ring_step(hop, which):
        for half, way in which:
            if which is first:
                scatter.step(half, way, hop, False)
            else:

                @pl.when(hop <= far - 1)
                def _():
                    scatter.step(half, way, hop, False)

    wide, thin = 6 * HEAD, 2 * HEAD
    total = lambda v: jnp.sum(v, axis=0, keepdims=True)

    def work(n, r):
        slot, at = n % 2, slice(r * TILE, (r + 1) * TILE)
        br = dot_nt(acts[slot, at, :], w2s[...])
        dh1 = None
        for p in range(2):
            lo = p * (wide + thin)
            br = br + dot_nt(cs[slot, at, p * thin : (p + 1) * thin], wqds[:, lo + wide : lo + wide + thin])
            part = dot_nt(ps[slot, at, p * wide : (p + 1) * wide], wqds[:, lo : lo + wide])
            dh1 = part if dh1 is None else dh1 + part
        parts[0, n, at, :] = br.astype(bf16)
        dh2 = dot_nt(dabs[slot, at, :], w1s[...])
        xhat, _ = normed(xs[slot, at, :].astype(f32))
        parts[1, n, at, :] = (dh1 * gain_ref[0:1, :] + dh2 * gain_ref[1:2, :]).astype(bf16)
        small[0:1, :] += total(dh1 * xhat)
        small[1:2, :] += total(dh2 * xhat)
        small[2:3, :] += total(dh1)
        small[3:4, :] += total(dh2)

    for n in range(4):
        if n < 3:
            for copy in load(n + 1):
                copy.start()
        if n == 0:
            for copy in weights:
                copy.wait()
        for copy in load(n):
            copy.wait()
        for r in range(rows // TILE):
            work(n, r)
        if n in (0, 2):
            for s in sums:
                s.pair(n // 2).start()
        if n == 1:
            for s in sums:
                s.middle()
            sums[0].cross().start()
            if far >= 2 and count <= 8:
                ring_step(2, first)
        if n == 3 and far >= 2 and count <= 8:
            ring_step(2, second)

    for step in range(1, 4):
        t_copy(step).start()
    sums[1].cross().start()

    def both(hop):
        ring_step(hop, first)
        ring_step(hop, second)

    if count <= 8:
        both(3)
    else:
        for_hops(2, far + 1, both, count)
    for step in range(1, 4):
        t_copy(step).wait_recv()
    t_in[tensor] = small[...]
    row = lax.broadcasted_iota(jnp.int32, small.shape, 0)
    summed = t_in[0] + t_in[1] + t_in[2] + t_in[3]
    d_out[...] = jnp.where(row < 4, summed, small[...])

    @pl.loop(1, count)
    def _(step):
        d_copy(step).start()

    if count <= 8:
        both(4)
    sums[0].end()
    saves = [pltpu.make_async_copy(tot.at[n], out, os.at[n]) for n, out in enumerate((br_out, e_out))]
    saves[0].start()

    @pl.loop(1, count)
    def _(step):
        d_copy(step).wait_recv()

    d_in[me] = d_out[...]
    small_sum[...] = scale * lax.fori_loop(1, count, lambda k, acc: acc + d_in[k], d_in[0])
    sums[1].end()
    saves[1].start()
    for half in range(2):
        scatter.last(half, scale)
    scatter.finish()
    for s in sums:
        s.finish()
    for step in range(1, 4):
        t_copy(step).wait_send()

    @pl.loop(1, count)
    def _(step):
        d_copy(step).wait_send()

    for copy in saves:
        copy.wait()


def sums_all(count, scale, order, gains, small, small_b, blocks, x, act, dab, ctx, dproj, wqd, w1, w2):
    per = blocks.shape[0] // count
    rows, width = x.shape[0] // 4, x.shape[1]
    far = count // 2
    any_, vmem = pl.BlockSpec(memory_space=pl.ANY), pl.BlockSpec(memory_space=pltpu.VMEM)
    dma = lambda *n: pltpu.SemaphoreType.DMA(n)
    two = lambda v: pltpu.VMEM((2, rows, v.shape[1]), v.dtype)
    like = lambda v: pltpu.VMEM(v.shape, v.dtype)
    sum_shape = jax.ShapeDtypeStruct((rows, width), f32)
    return pl.pallas_call(
        functools.partial(sums_kernel, count, scale),
        out_shape=[
            jax.ShapeDtypeStruct((per, BLOCK, BLOCK), f32), jax.ShapeDtypeStruct(small.shape, f32),
            sum_shape, sum_shape,
        ],
        in_specs=[pl.BlockSpec(memory_space=pltpu.SMEM)] + [vmem] * 3 + [any_] * 9,
        out_specs=[vmem, vmem, any_, any_],
        scratch_shapes=[
            like(blocks),
            pltpu.VMEM((4, per, 64, BLOCK), bf16), pltpu.VMEM((4 * far, per, 64, BLOCK), bf16),
            two(x), two(act), two(dab), two(ctx), two(dproj), like(wqd), like(w1), like(w2),
            pltpu.VMEM((2, 4, rows, width), bf16), pltpu.VMEM((2, 2, rows, width), bf16),
            pltpu.VMEM((2, rows, width), bf16), pltpu.VMEM((2, rows, width), f32),
            pltpu.VMEM(small.shape, f32), pltpu.VMEM((4,) + small.shape, f32),
            pltpu.VMEM((count,) + small.shape, f32), pltpu.VMEM(small.shape, f32),
            dma(4 * far), dma(4 * far), dma(2, 3), dma(2, 3), dma(4), dma(4), dma(count), dma(count),
            dma(5, 2), dma(4), dma(2),
        ],
        compiler_params=pltpu.CompilerParams(
            collective_id=1, has_side_effects=True, vmem_limit_bytes=VMEM_LIMIT
        ),
        cost_estimate=pl.CostEstimate(flops=int(1.3e10), bytes_accessed=int(4e7), transcendentals=0),
        name="sums_all",
    )(order, gains, small, small_b, blocks, x, act, dab, ctx, dproj, wqd, w1, w2)


def finish_kernel(
    steps, lim_ref, bias_ref, small_ref, racc_ref, qacc_ref, facc_ref, grad, tok, dy, br, e, ls, rs, lr, rr,
    gout, out, dx, lout, rout, cout, racc, rupd, qacc, qupd, facc, fupd,
    g_v, tok_v, dy_v, br_v, e_v, ls_v, rs_v, lr_v, rr_v, out_v, dx_v, lo_v, ro_v, co_v, isem, osem,
):
    tensor = lax.axis_index("tensor")
    own_rows, blocks = tok.shape[0], grad.shape[0]
    rows, some = own_rows // steps, blocks // steps
    ins = [(grad, g_v), (ls, ls_v), (rs, rs_v), (lr, lr_v), (rr, rr_v), (tok, tok_v), (dy, dy_v), (br, br_v), (e, e_v)]
    outs = [(g_v, gout), (lo_v, lout), (ro_v, rout), (co_v, cout), (out_v, out), (dx_v, dx)]

    def span(ref, s):
        size = ref.shape[0] // steps
        return ref.at[pl.ds(s * size if ref.shape[0] == blocks else pl.multiple_of(s * size, 16), size)]

    def fetch(k, s):
        return pltpu.make_async_copy(span(ins[k][0], s), span(ins[k][1], s), isem.at[k, s])

    def store(k, s):
        return pltpu.make_async_copy(span(outs[k][0], s), span(outs[k][1], s), osem.at[k, s])

    for s in range(steps):
        for k in range(len(ins)):
            fetch(k, s).start()
    small = small_ref[...]

    def adagrad(grad_vec, accum, new, update):
        accum_next = accum + grad_vec * grad_vec
        new[...] = accum_next
        update[...] = -adagrad_rate * grad_vec * lax.rsqrt(accum_next)

    def stacked(line, count):
        return jnp.concatenate([line[:, k * BLOCK : (k + 1) * BLOCK] for k in range(count)], axis=0)

    adagrad(jnp.concatenate([small[0:5], small[4:5]], axis=0), racc_ref[...], racc, rupd)
    adagrad(stacked(small[5:6], qacc.shape[0]), qacc_ref[...], qacc, qupd)
    adagrad(stacked(small[6:7], facc.shape[0]), facc_ref[...], facc, fupd)
    shift = bias_ref[2:3, :] + bias_ref[3:4, :]

    @pl.loop(0, steps)
    def _(s):
        for k in range(len(ins)):
            fetch(k, s).wait()

        for b in range(some):
            k = s * some + b
            low = g_v[k].astype(bf16)
            lo_v[k] = stat_decay * ls_v[k] + (1.0 - stat_decay) * dot_nt(low, low)
            ro_v[k] = stat_decay * rs_v[k] + (1.0 - stat_decay) * dot_tn(low, low)
            pushed = dot_nn(lr_v[k].astype(bf16), low).astype(bf16)
            co_v[k] = -shampoo_rate * dot_nn(pushed, rr_v[k].astype(bf16))

        at = pl.ds(pl.multiple_of(s * rows, 16), rows)
        x = tok_v[at, :].astype(f32)
        out_v[at, :] = (x + br_v[at, :] + shift).astype(bf16)
        start = tensor * own_rows + s * rows
        place = start % LEN + lax.broadcasted_iota(jnp.int32, (rows, 1), 0)
        kept = jnp.where(place < lim_ref[start // LEN], dy_v[at, :].astype(f32), 0.0)
        xhat, scale = normed(x)
        v = e_v[at, :]
        dx_v[at, :] = kept + scale * (
            v - jnp.mean(v, axis=-1, keepdims=True) - xhat * jnp.mean(v * xhat, axis=-1, keepdims=True)
        )
        for k in range(len(outs)):
            store(k, s).start()

    for s in range(steps):
        for k in range(len(outs)):
            store(k, s).wait()


def finish_all(limits, biases, small, racc, qacc, facc, grad, tok, dy, br, e, ls, rs, lr, rr):
    steps = 4 if grad.shape[0] % 4 == 0 else 1
    any_, vmem = pl.BlockSpec(memory_space=pl.ANY), pl.BlockSpec(memory_space=pltpu.VMEM)
    shape = lambda v: jax.ShapeDtypeStruct(v.shape, v.dtype)
    like = lambda v: pltpu.VMEM(v.shape, v.dtype)
    vectors = [racc, racc, qacc, qacc, facc, facc]
    return pl.pallas_call(
        functools.partial(finish_kernel, steps),
        out_shape=[shape(grad), shape(tok), shape(e)] + [shape(grad)] * 3 + [shape(v) for v in vectors],
        in_specs=[pl.BlockSpec(memory_space=pltpu.SMEM)] + [vmem] * 5 + [any_] * 9,
        out_specs=[any_] * 6 + [vmem] * 6,
        scratch_shapes=[like(v) for v in (grad, tok, dy, br, e, ls, rs, lr, rr, tok, e, ls, ls, ls)]
        + [pltpu.SemaphoreType.DMA((9, steps)), pltpu.SemaphoreType.DMA((6, steps))],
        compiler_params=pltpu.CompilerParams(vmem_limit_bytes=VMEM_LIMIT),
        cost_estimate=pl.CostEstimate(flops=int(4e8), bytes_accessed=int(2e7), transcendentals=0),
        name="finish_all",
    )(limits, biases, small, racc, qacc, facc, grad, tok, dy, br, e, ls, rs, lr, rr)


def shards(
    tokens, out_grad, seq_lengths, norm_gains, row_biases, qkv_weight, qkv_bias, dense_weight, fc1_weight,
    fc1_bias, fc2_weight, block_slot, left_stat, right_stat, left_root, right_root, row_accum,
    qkv_bias_accum, fc1_bias_accum,
):
    tensor_count = lax.axis_size("tensor")
    dp_count = lax.axis_size("dp")
    grad_scale = 1.0 / math.sqrt(tokens.shape[0] * tensor_count * dp_count)
    xf, h1, dyb, ctx, dproj, wqdf, w1f, w2f, sum_a, order = mixed_all(
        dp_count, seq_lengths, norm_gains, row_biases, as_rows(qkv_bias), jnp.asarray(rotary_rows()),
        as_rows(block_slot), tokens, out_grad, qkv_weight, dense_weight, fc1_weight, fc2_weight,
    )
    act, dab, blocks, sum_b = hidden_all(
        xf, h1, dyb, ctx, dproj, w1f, w2f, norm_gains, row_biases, as_rows(fc1_bias)
    )
    own_grad, small, branch, e_sum = sums_all(
        dp_count, grad_scale, order, norm_gains, sum_a, sum_b, blocks, xf, act, dab, ctx, dproj, wqdf, w1f, w2f
    )
    outs = finish_all(
        seq_lengths, row_biases, small, row_accum, as_rows(qkv_bias_accum), as_rows(fc1_bias_accum),
        own_grad, tokens, out_grad, branch, e_sum, left_stat, right_stat, left_root, right_root,
    )
    block_grad, layer_out, input_grad, left_new, right_new, change = outs[:6]
    return (
        layer_out, input_grad, block_grad, left_new, right_new, change,
        *outs[6:8], *(v.reshape(-1) for v in outs[8:]),
    )


def solution(mesh):
    both = ("dp", "tensor")
    return jax.shard_map(
        shards,
        mesh=mesh,
        in_specs=(
            P(both, None), P(both, None), P("dp"), P(), P(), P("dp", "tensor"), P("tensor"),
            P("tensor", "dp"), P("dp", "tensor"), P("tensor"), P("tensor", "dp"), P(),
            P(both, None, None), P(both, None, None), P(both, None, None), P(both, None, None),
            P(), P("tensor"), P("tensor"),
        ),
        out_specs=(
            P(both, None), P(both, None), P(both, None, None), P(both, None, None),
            P(both, None, None), P(both, None, None), P(), P(), P("tensor"), P("tensor"),
            P("tensor"), P("tensor"),
        ),
        check_vma=False,
    )
```

```python
import functools
import math

import jax
import jax.numpy as jnp
import numpy as np
from jax import lax
from jax.experimental import pallas as pl
from jax.experimental.pallas import tpu as pltpu
from jax.sharding import PartitionSpec as P

HEAD = 64
ROT = 16
LEN = 1024
BLOCK = 128
TILE = 256
WIDE = 512
MESH = pl.DeviceIdType.MESH
VMEM_LIMIT = 60 * 1024 * 1024

masked_score = -1e30
shampoo_rate = 0.03
adagrad_rate = 0.1
stat_decay = 0.5
f32 = jnp.float32
bf16 = jnp.bfloat16


def rotary_rows():
    half = ROT // 2
    inverse = np.power(np.float32(10000.0), -(np.arange(half, dtype=np.float32) * np.float32(2.0 / ROT)))
    angles = inverse.astype(np.float32)[:, None] * np.arange(LEN, dtype=np.float32)[None, :]
    return np.concatenate([np.cos(angles), np.sin(angles)], axis=0).astype(np.float32)


def ring_place(me, count):
    low, high = me % 2, me // 2
    return low * (count - 1 - high) + (1 - low) * high


def ring_device(place, count):
    upper = place // (count // 2)
    return (1 - upper) * (2 * place) + upper * (2 * (count - 1 - place) + 1)


def hop_count(half, way, count):
    far = count // 2
    return far if half == way else far - 1


def for_hops(first, last, body, count):
    if count <= 8:
        for hop in range(first, last):
            body(hop)
    elif last > first:

        @pl.loop(first, last)
        def _(hop):
            body(hop)


def as_rows(vec):
    return vec.reshape(-1, BLOCK)


def as_line(rows):
    return jnp.concatenate([rows[k : k + 1, :] for k in range(rows.shape[0])], axis=1)


class Ring:
    def __init__(self, count):
        self.count = count
        self.me = lax.axis_index("dp")
        self.tensor = lax.axis_index("tensor")
        self.place = ring_place(self.me, count)
        self.peer = [
            (ring_device((self.place + step) % count, count), self.tensor) for step in (1, count - 1)
        ]

    def at(self, offset):
        return ring_device((self.place + offset + 2 * self.count) % self.count, self.count)


class Gather:
    def __init__(self, ring, locals_, fulls, send, recv):
        self.ring, self.locals, self.fulls, self.send, self.recv = ring, locals_, fulls, send, recv
        self.far = ring.count // 2

    def part(self, ref, w, half, owner=None):
        rows, cols = self.locals[w].shape
        base = 0 if owner is None else owner * rows
        if rows % 32 == 0:
            return ref.at[pl.ds(pl.multiple_of(base + half * (rows // 2), 16), rows // 2)]
        return ref.at[pl.ds(base, rows), pl.ds(half * (cols // 2), cols // 2)]

    def sem(self, w, half, way, hop):
        return ((w * 2 + half) * 2 + way) * self.far + hop - 1

    def copy(self, w, half, way, hop, source):
        owner = self.ring.at((1 - hop) if way == 0 else (hop - 1))
        src = self.part(self.locals[w], w, half) if source else self.part(self.fulls[w], w, half, owner)
        return pltpu.make_async_remote_copy(
            src_ref=src,
            dst_ref=self.part(self.fulls[w], w, half, owner),
            send_sem=self.send.at[self.sem(w, half, way, hop)],
            recv_sem=self.recv.at[self.sem(w, half, way, hop)],
            device_id=self.ring.peer[way],
            device_id_type=MESH,
        )

    def arrival(self, w, half, way, hop):
        owner = self.ring.at(-hop if way == 0 else hop)
        dst = self.part(self.fulls[w], w, half, owner)
        return pltpu.make_async_remote_copy(
            src_ref=dst,
            dst_ref=dst,
            send_sem=self.send.at[self.sem(w, half, way, hop)],
            recv_sem=self.recv.at[self.sem(w, half, way, hop)],
            device_id=self.ring.peer[way],
            device_id_type=MESH,
        )

    def begin(self, w):
        for half in range(2):
            for way in range(2):
                if hop_count(half, way, self.ring.count) >= 1:
                    self.copy(w, half, way, 1, True).start()

    def forward(self, w, hop, last):
        for half in range(2):
            for way in range(2):
                hops = self.far if half == way else self.far - 1
                if last and hops != self.far:
                    continue
                self.arrival(w, half, way, hop).wait_recv()
                if not last:
                    more = self.far if half == way else self.far - 1
                    if more == self.far:
                        self.copy(w, half, way, hop + 1, False).start()
                    else:

                        @pl.when(hop + 1 <= more)
                        def _():
                            self.copy(w, half, way, hop + 1, False).start()

    def finish(self, w):
        for half in range(2):
            for way in range(2):
                hops = hop_count(half, way, self.ring.count)
                if hops >= 1:
                    self.copy(w, half, way, 1, True).wait_send()
                for_hops(
                    2, hops + 1, lambda hop: self.copy(w, half, way, hop, False).wait_send(), self.ring.count
                )


class Rows:
    def __init__(self, local, full, send, recv, own):
        self.tensor = lax.axis_index("tensor")
        self.dp = lax.axis_index("dp")
        self.near = self.tensor + 1 - 2 * (self.tensor % 2)
        self.across = (self.tensor + 2) % 4
        self.local, self.full, self.send, self.recv, self.own = local, full, send, recv, own
        self.rows = local.shape[0]

    def slot(self, owner, piece=None):
        if piece is None:
            return self.full.at[pl.ds(pl.multiple_of(owner * self.rows, 16), self.rows)]
        half = self.rows // 2
        return self.full.at[pl.ds(pl.multiple_of(owner * self.rows + piece * half, 16), half)]

    def remote(self, src, dst, sem, device):
        return pltpu.make_async_remote_copy(
            src_ref=src,
            dst_ref=dst,
            send_sem=self.send.at[sem],
            recv_sem=self.recv.at[sem],
            device_id=(self.dp, device),
            device_id_type=MESH,
        )

    def keep(self):
        return pltpu.make_async_copy(self.local, self.slot(self.tensor), self.own)

    def pair(self):
        return self.remote(self.local, self.slot(self.tensor), 0, self.near)

    def cross(self, piece):
        half = self.rows // 2
        return self.remote(
            self.local.at[pl.ds(piece * half, half)], self.slot(self.tensor, piece), 1 + piece, self.across
        )

    def onward(self, piece):
        here = self.slot(self.across, piece)
        return self.remote(here, here, 3 + piece, self.near)

    def begin_near(self):
        self.keep().start()
        self.pair().start()

    def begin_cross(self):
        for piece in range(2):
            self.cross(piece).start()

    def pass_piece(self, piece):
        self.cross(piece).wait_recv()
        self.onward(piece).start()

    def pass_on(self):
        for piece in range(2):
            self.pass_piece(piece)

    def finish(self):
        self.keep().wait()
        self.pair().wait()
        for piece in range(2):
            self.cross(piece).wait_send()
            self.onward(piece).wait()


def greet(devices):
    barrier = pltpu.get_barrier_semaphore()
    for device in devices:
        pl.semaphore_signal(barrier, inc=1, device_id=device, device_id_type=MESH)
    pl.semaphore_wait(barrier, len(devices))


def dot_nn(a, b):
    return lax.dot_general(a, b, (((1,), (0,)), ((), ())), preferred_element_type=f32)


def dot_nt(a, b):
    return lax.dot_general(a, b, (((1,), (1,)), ((), ())), preferred_element_type=f32)


def dot_tn(a, b):
    return lax.dot_general(a, b, (((0,), (0,)), ((), ())), preferred_element_type=f32)


def normed(x):
    average = jnp.mean(x, axis=-1, keepdims=True)
    centered = x - average
    variance = jnp.mean(centered * centered, axis=-1, keepdims=True)
    scale = lax.rsqrt(variance + 1e-05)
    return centered * scale, scale


def mixed_kernel(
    count, lim_ref, gain_ref, bias_ref, qb_ref, rot_ref, slot_ref, wd, w2, x, dy, wq, w1,
    x_out, h1_out, dyb_out, ctx_out, dproj_out, wqd_out, w1f, w2f, sum_ref, order_ref,
    xf, dyf, wf, wl, w2l, h1s, ctxs, dps, qt, kt, vt, dct, ctt, dqt, kr, vr, dkvs,
    rs, rr, ro, gs, gr, go, os,
):
    ring = Ring(count)
    pair_cols = 6 * HEAD
    half_cols = pair_cols + 2 * HEAD
    parts = [
        pltpu.make_async_copy(
            wq.at[:, pl.ds(p * pair_cols, pair_cols)], wl.at[:, pl.ds(p * half_cols, pair_cols)], os.at[p]
        )
        for p in range(2)
    ]
    for copy in parts:
        copy.start()
    turned_dense = wd[...].T
    for p in range(2):
        wl[:, p * half_cols + pair_cols : (p + 1) * half_cols] = turned_dense[:, p * 2 * HEAD : (p + 1) * 2 * HEAD]
    views = [(wl.at[:, pl.ds(p * half_cols, half_cols)], wf.at[:, pl.ds(p * half_cols, half_cols)]) for p in (0, 1)]
    views += [(w1, w1f), (w2l, w2f)]
    gather = Gather(ring, [v[0] for v in views], [v[1] for v in views], gs, gr)
    rx = Rows(x, xf, rs.at[0], rr.at[0], ro.at[0])
    ry = Rows(dy, dyf, rs.at[1], rr.at[1], ro.at[1])
    greet([ring.peer[0], ring.peer[1], (ring.me, rx.near), (ring.me, rx.across)])
    far = count // 2
    own = []
    for k, (local, full) in enumerate(((w1, w1f), (w2l, w2f))):
        rows = local.shape[0]
        own.append(
            pltpu.make_async_copy(local, full.at[pl.ds(pl.multiple_of(ring.me * rows, 16), rows)], go.at[k])
        )
    rx.begin_near()
    for copy in parts:
        copy.wait()
    gather.begin(0)
    rx.begin_cross()
    ry.begin_near()
    ry.begin_cross()
    wf[pl.ds(pl.multiple_of(ring.me * wl.shape[0], 16), wl.shape[0]), :] = wl[...]
    own[0].start()
    sum_ref[...] = jnp.zeros_like(sum_ref)
    tensor = ring.tensor
    tiles = LEN // TILE

    def whole_ring(w):
        for_hops(1, far, lambda hop: gather.forward(w, hop, False), count)
        gather.forward(w, far, True)

    def hop_at(w, hop):
        if count == 8:
            gather.forward(w, hop, hop == far)
        elif hop == 4:
            whole_ring(w)

    def rows_of(seq, i):
        return pl.ds(pl.multiple_of(seq * LEN + i * TILE, TILE), TILE)

    def norm_tile(seq, i):
        rows = rows_of(seq, i)
        xhat, _ = normed(xf[rows, :].astype(f32))
        h1s[rows, :] = (xhat * gain_ref[0:1, :] + bias_ref[0:1, :]).astype(bf16)

    def mask_tile(seq, i):
        rows = rows_of(seq, i)
        place = i * TILE + lax.broadcasted_iota(jnp.int32, (TILE, 1), 0)
        kept = jnp.where(place < lim_ref[seq], dyf[rows, :].astype(f32), 0.0)
        sum_ref[4:5, :] += jnp.sum(kept, axis=0, keepdims=True)
        dyf[rows, :] = kept.astype(bf16)

    def turned(first, second, cosine, sine):
        return first * cosine - second * sine, second * cosine + first * sine

    def prepare_tile(seq, pair, i):
        rows = rows_of(seq, i)
        cols = pl.ds(pl.multiple_of(i * TILE, TILE), TILE)
        proj = dot_nn(h1s[rows, :], wf[:, pl.ds(pl.multiple_of(pair * half_cols, BLOCK), pair_cols)])
        proj = proj + as_line(qb_ref[pl.ds(pair * (pair_cols // BLOCK), pair_cols // BLOCK), :])
        proj = proj.T
        cosine, sine = rot_ref[0:8, cols], rot_ref[8:16, cols]
        key = i * TILE + lax.broadcasted_iota(jnp.int32, (16, TILE), 1)
        row = lax.broadcasted_iota(jnp.int32, (16, TILE), 0)
        ones = jnp.where(row == 0, 1.0, 0.0).astype(bf16)
        hidden = jnp.where((row == 0) & (key >= lim_ref[seq]), masked_score, 0.0).astype(bf16)
        blank = jnp.zeros((48, TILE), bf16)
        none = jnp.zeros((HEAD, TILE), bf16)
        for hh in range(2):
            h = 2 * pair + hh
            base = 3 * HEAD * hh
            q0, q1 = turned(proj[base : base + 8], proj[base + 8 : base + 16], cosine, sine)
            q = jnp.concatenate([q0, q1, proj[base + 16 : base + HEAD]], axis=0).astype(bf16)
            q = (q.astype(f32) * 0.125).astype(bf16)
            qt[h, :, cols] = jnp.concatenate([q, ones, blank], axis=0)
            base += HEAD
            k0, k1 = turned(proj[base : base + 8], proj[base + 8 : base + 16], cosine, sine)
            k = jnp.concatenate([k0, k1, proj[base + 16 : base + HEAD]], axis=0).astype(bf16)
            kt[h, :, cols] = k
            kr[h, cols, :] = jnp.concatenate([k, hidden, blank], axis=0).T
            base += HEAD
            v = proj[base : base + HEAD].astype(bf16)
            vt[h, :, cols] = jnp.concatenate([v, ones], axis=0)
            vr[h, cols, :] = jnp.concatenate([none, v], axis=0).T

    def context_tile(seq, pair, i):
        cols = pl.ds(pl.multiple_of(i * TILE, TILE), TILE)
        begin = pair * half_cols + pair_cols
        dctx = dot_nn(dyf[rows_of(seq, i), :], wf[:, begin : begin + 2 * HEAD]).T.astype(bf16)
        for hh in range(2):
            dct[2 * pair + hh, :, cols] = dctx[HEAD * hh : HEAD * (hh + 1)]

    def back_tile(seq, i):
        mask_tile(seq, i)
        context_tile(seq, 0, i)
        context_tile(seq, 1, i)

    def attend(pair, i, fresh):
        here = slice(i * TILE, (i + 1) * TILE)
        chunks = [slice(c * TILE, (c + 1) * TILE) for c in range(i + 1)]
        heads = range(2)
        of = [2 * pair, 2 * pair + 1]
        key = lax.broadcasted_iota(jnp.int32, (TILE, TILE), 0)
        query = lax.broadcasted_iota(jnp.int32, (TILE, TILE), 1)
        q = [qt[of[hh], :, here] for hh in heads]
        scores = [[dot_nn(kr[of[hh], c, :], q[hh]) for c in chunks] for hh in heads]
        probs, grads, deltas, both = [], [], [], []
        none = jnp.zeros((HEAD, TILE), bf16)
        for hh in heads:
            scores[hh][i] = jnp.where(key <= query, scores[hh][i], masked_score)
            top = jnp.max(scores[hh][0], axis=0, keepdims=True)
            for s in scores[hh][1:]:
                top = jnp.maximum(top, jnp.max(s, axis=0, keepdims=True))
            probs.append([jnp.exp(s - top).astype(bf16) for s in scores[hh]])
        for hh in heads:
            total = dot_nn(vt[of[hh], :, chunks[0]], probs[hh][0])
            for c, p in zip(chunks[1:], probs[hh][1:]):
                total = total + dot_nn(vt[of[hh], :, c], p)
            inverse = 1.0 / total[HEAD : HEAD + 1]
            context = total[:HEAD] * inverse
            ctt[of[hh], :, here] = context
            grad = (dct[of[hh], :, here].astype(f32) * inverse).astype(bf16)
            deltas.append(jnp.sum(grad.astype(f32) * context, axis=0, keepdims=True))
            grad = jnp.concatenate([none, grad], axis=0)
            grads.append(grad)
            both.append(jnp.concatenate([jnp.concatenate([q[hh][:HEAD], none], axis=0), grad], axis=1))
        dq = [None, None]
        for n, c in enumerate(chunks):
            for hh in heads:
                p = probs[hh][n]
                dp = dot_nn(vr[of[hh], c, :], grads[hh])
                ds = (p.astype(f32) * (dp - deltas[hh])).astype(bf16)
                part = dot_nn(kt[of[hh], :, c], ds)
                dq[hh] = part if dq[hh] is None else dq[hh] + part
                dkv = dot_nt(jnp.concatenate([ds, p], axis=1), both[hh])
                if n in fresh:
                    dkvs[of[hh], c, :] = dkv
                else:
                    dkvs[of[hh], c, :] += dkv
        for hh in heads:
            dqt[of[hh], :, here] = dq[hh] * 0.125

    def collect_tile(seq, i):
        rows = rows_of(seq, i)
        cols = pl.ds(pl.multiple_of(i * TILE, TILE), TILE)
        cosine, sine = rot_ref[0:8, cols], rot_ref[8:16, cols]
        for pair in range(2):
            pieces = []
            for h in (2 * pair, 2 * pair + 1):
                dkv = dkvs[h, cols, :].T
                for grad in (dqt[h, :, cols], dkv[:HEAD]):
                    pieces += [*turned(grad[0:8], grad[8:16], cosine, -sine), grad[16:HEAD]]
                pieces.append(dkv[HEAD:])
            low = jnp.concatenate(pieces, axis=0).T.astype(bf16)
            wide = slice(pair * pair_cols, (pair + 1) * pair_cols)
            dps[rows, wide] = low
            sum_ref[5:6, wide] += jnp.sum(low.astype(f32), axis=0, keepdims=True)
            ctx = jnp.concatenate([ctt[2 * pair, :, cols], ctt[2 * pair + 1, :, cols]], axis=0).T
            ctxs[rows, pair * 2 * HEAD : (pair + 1) * 2 * HEAD] = ctx.astype(bf16)

    def save(turn, k, seq):
        src, dst = ((xf, x_out), (h1s, h1_out), (dyf, dyb_out), (ctxs, ctx_out), (dps, dproj_out))[k]
        rows = pl.ds(pl.multiple_of(seq * LEN, LEN), LEN)
        return pltpu.make_async_copy(src.at[rows], dst.at[rows], os.at[turn * 5 + k])

    mine = order_ref.shape[1]
    per = mine // count
    place = lax.broadcasted_iota(jnp.int32, (mine, 1), 0).astype(f32)
    owner = jnp.floor((place + 0.5) / per)
    wanted = (owner * 4.0 + lax.convert_element_type(tensor, f32)) * per + (place - owner * per)
    found = jnp.zeros(order_ref.shape, f32)
    for r in range(slot_ref.shape[0]):
        hit = jnp.where(slot_ref[r : r + 1, :].astype(f32) == wanted, 1.0, 0.0).astype(bf16)
        block = r * BLOCK + lax.broadcasted_iota(jnp.int32, (8, BLOCK), 1) - tensor * mine
        found = found + dot_nt(jnp.clip(block, 0, mine - 1).astype(f32).astype(bf16), hit)
    order_ref[...] = (found + 0.5).astype(jnp.int32)

    seq = tensor // 2
    rx.keep().wait()
    rx.pair().wait_recv()

    @pl.loop(0, tiles)
    def _(i):
        norm_tile(seq, i)

        @pl.when(i == 0)
        def _():
            hop_at(0, 1)
            gather.begin(1)

        @pl.when(i == 1)
        def _():
            hop_at(0, 2)
            hop_at(1, 1)

        @pl.when(i == 2)
        def _():
            hop_at(0, 3)
            hop_at(1, 2)
            gather.begin(2)

    save(0, 0, seq).start()
    save(0, 1, seq).start()
    w2l[...] = w2[...].T
    hop_at(0, 4)
    ry.keep().wait()
    ry.pair().wait_recv()

    @pl.loop(0, tiles // 2)
    def _(i):
        for sub in range(2):
            prepare_tile(seq, 0, 2 * i + sub)


    @pl.loop(0, tiles)
    def _(i):
        mask_tile(seq, i)
        context_tile(seq, 0, i)

    save(0, 2, seq).start()

    @pl.loop(0, 2)
    def _(pair):
        @pl.when(pair == 1)
        def _():
            hop_at(1, 4)
            hop_at(2, 1)

            @pl.loop(0, tiles // 2)
            def _(i):
                for sub in range(2):
                    prepare_tile(seq, 1, 2 * i + sub)
                    context_tile(seq, 1, 2 * i + sub)

        attend(pair, 3, (0, 1, 2, 3))

        @pl.when(pair == 0)
        def _():
            hop_at(1, 3)
            gather.begin(3)
            own[1].start()

        attend(pair, 2, ())

        @pl.when(pair == 0)
        def _():
            rx.pass_on()

        @pl.when(pair == 1)
        def _():
            hop_at(3, 1)

        attend(pair, 1, ())
        attend(pair, 0, ())

    @pl.loop(0, tiles)
    def _(i):
        collect_tile(seq, i)

    save(0, 3, seq).start()
    save(0, 4, seq).start()
    keep = pltpu.make_async_copy(wf, wqd_out, os.at[10])
    keep.start()

    seq = 1 - seq
    for piece in range(2):
        rx.onward(piece).wait_recv()

    @pl.loop(0, tiles)
    def _(i):
        norm_tile(seq, i)

    save(1, 0, seq).start()
    save(1, 1, seq).start()
    ry.pass_piece(0)

    for pair in range(2):

        @pl.loop(0, tiles // 2)
        def _(i):
            for sub in range(2):
                prepare_tile(seq, pair, 2 * i + sub)

        if pair == 0:
            hop_at(2, 2)

    ry.onward(0).wait()
    back_tile(seq, 0)
    back_tile(seq, 2)

    @pl.loop(0, 2)
    def _(pair):
        attend(pair, 2, (0, 1, 2))

        @pl.when(pair == 0)
        def _():
            hop_at(3, 2)

        attend(pair, 0, ())

    ry.pass_piece(1)
    ry.onward(1).wait()
    back_tile(seq, 1)
    back_tile(seq, 3)
    save(1, 2, seq).start()
    hop_at(2, 3)

    @pl.loop(0, 2)
    def _(pair):
        attend(pair, 3, (3,))

        @pl.when(pair == 1)
        def _():
            hop_at(3, 3)

        attend(pair, 1, ())

    @pl.loop(0, tiles)
    def _(i):
        collect_tile(seq, i)

    save(1, 3, seq).start()
    save(1, 4, seq).start()
    hop_at(2, 4)
    hop_at(3, 4)
    for w in range(4):
        gather.finish(w)
    own[0].wait()
    own[1].wait()
    rx.pair().wait_send()
    ry.pair().wait_send()
    for piece in range(2):
        rx.cross(piece).wait_send()
        rx.onward(piece).wait_send()
        ry.cross(piece).wait_send()
    for turn in range(2):
        for k in range(5):
            save(turn, k, turn + (1 - 2 * turn) * (tensor // 2)).wait()
    keep.wait()


def mixed_all(count, limits, gains, biases, qkv_bias, rot, slots, x, dy, wq, wd, w1, w2):
    far = count // 2
    rows, width = 4 * x.shape[0], x.shape[1]
    ctx_cols, proj_cols = wd.shape[0], wq.shape[1]
    shard = wq.shape[0]
    out = lambda r, c: jax.ShapeDtypeStruct((r, c), bf16)
    any_, vmem = pl.BlockSpec(memory_space=pl.ANY), pl.BlockSpec(memory_space=pltpu.VMEM)
    dma = lambda *n: pltpu.SemaphoreType.DMA(n)
    buf = lambda dtype, *shape: pltpu.VMEM(shape, dtype)
    heads, both = 4, ctx_cols + proj_cols
    return pl.pallas_call(
        functools.partial(mixed_kernel, count),
        out_shape=[
            out(rows, width), out(rows, width), out(rows, width), out(rows, ctx_cols), out(rows, proj_cols),
            out(width, both), out(width, w1.shape[1]), out(width, w2.shape[0]),
            jax.ShapeDtypeStruct((8, width), f32), jax.ShapeDtypeStruct((8, slots.size // 4), jnp.int32),
        ],
        in_specs=[pl.BlockSpec(memory_space=pltpu.SMEM)] + [vmem] * 7 + [any_] * 4,
        out_specs=[any_] * 8 + [vmem] * 2,
        scratch_shapes=[
            buf(bf16, rows, width), buf(bf16, rows, width), buf(bf16, width, both),
            buf(bf16, shard, both), buf(bf16, shard, w2.shape[0]),
            buf(bf16, rows, width), buf(bf16, rows, ctx_cols), buf(bf16, rows, proj_cols),
            buf(bf16, heads, 2 * HEAD, LEN), buf(bf16, heads, HEAD, LEN), buf(bf16, heads, HEAD + 16, LEN),
            buf(bf16, heads, HEAD, LEN), buf(f32, heads, HEAD, LEN), buf(f32, heads, HEAD, LEN),
            buf(bf16, heads, LEN, 2 * HEAD), buf(bf16, heads, LEN, 2 * HEAD), buf(f32, heads, LEN, 2 * HEAD),
            dma(2, 5), dma(2, 5), dma(2), dma(16 * far), dma(16 * far), dma(2), dma(11),
        ],
        compiler_params=pltpu.CompilerParams(
            collective_id=0, has_side_effects=True, vmem_limit_bytes=VMEM_LIMIT
        ),
        cost_estimate=pl.CostEstimate(flops=int(2e10), bytes_accessed=int(4e7), transcendentals=int(1e7)),
        name="mixed_all",
    )(limits, gains, biases, qkv_bias, rot, slots, wd, w2, x, dy, wq, w1)


def gelu_both(x):
    bell = jnp.exp(-0.5 * x * x)
    u = jnp.abs(x) * (1.0 / math.sqrt(2.0))
    t = 1.0 / (1.0 + 0.3275911 * u)
    poly = t * (0.254829592 + t * (-0.284496736 + t * (1.421413741 + t * (-1.453152027 + t * 1.061405429))))
    tail = 0.5 * poly * bell
    phi = jnp.where(x < 0.0, tail, 1.0 - tail)
    return x * phi, phi + x * bell * (1.0 / math.sqrt(2.0 * math.pi))


class Scatter:
    def __init__(self, ring, order, blocks, out, sbuf, rbuf, send, recv):
        self.ring, self.order, self.blocks, self.out = ring, order, blocks, out
        self.sbuf, self.rbuf, self.send, self.recv = sbuf, rbuf, send, recv
        self.per = out.shape[0]
        self.far = ring.count // 2

    def index(self, half, way, hop):
        return (half * 2 + way) * self.far + hop - 1

    def copy(self, half, way, hop, first):
        i = self.index(half, way, hop)
        return pltpu.make_async_remote_copy(
            src_ref=self.sbuf.at[half * 2 + way] if first else self.rbuf.at[i - 1],
            dst_ref=self.rbuf.at[i],
            send_sem=self.send.at[i],
            recv_sem=self.recv.at[i],
            device_id=self.ring.peer[way],
            device_id_type=MESH,
        )

    def own(self, dest, half, k):
        return self.blocks[self.order[0, dest * self.per + k], half * 64 : half * 64 + 64, :].astype(f32)

    def step(self, half, way, hop, first):
        hops = hop_count(half, way, self.ring.count)
        dest = self.ring.at((hops + 1 - hop) if way == 0 else (hop - hops - 1))
        i = self.index(half, way, hop)
        if not first:
            self.copy(half, way, hop - 1, True).wait_recv()

        def one(k, carry):
            value = self.own(dest, half, k)
            if first:
                self.sbuf[half * 2 + way, k] = value.astype(bf16)
            else:
                self.rbuf[i - 1, k] = (value + self.rbuf[i - 1, k].astype(f32)).astype(bf16)
            return carry

        lax.fori_loop(0, self.per, one, 0)
        self.copy(half, way, hop, first).start()

    def last(self, half, scale):
        came = []
        for way in range(2):
            hops = hop_count(half, way, self.ring.count)
            if hops >= 1:
                self.copy(half, way, hops, True).wait_recv()
                came.append(self.index(half, way, hops))
        me = self.ring.me

        def one(k, carry):
            value = self.own(me, half, k)
            for i in came:
                value = value + self.rbuf[i, k].astype(f32)
            self.out[k, half * 64 : half * 64 + 64, :] = value * scale
            return carry

        lax.fori_loop(0, self.per, one, 0)

    def finish(self):
        for half in range(2):
            for way in range(2):
                hops = hop_count(half, way, self.ring.count)
                for_hops(
                    1, hops + 1, lambda hop: self.copy(half, way, hop, True).wait_send(), self.ring.count
                )


class RowSum:
    def __init__(self, parts, r1, base, r2, send, recv):
        self.tensor = lax.axis_index("tensor")
        self.dp = lax.axis_index("dp")
        self.near = self.tensor + 1 - 2 * (self.tensor % 2)
        self.across = (self.tensor + 2) % 4
        self.r2, self.send, self.recv = r2, send, recv
        self.rows = r2.shape[0]
        self.parts = [parts.at[pl.ds(k * self.rows, self.rows)] for k in range(4)]
        self.r1 = [r1.at[pl.ds((base + k) * self.rows, self.rows)] for k in range(2)]

    def remote(self, src, dst, sem, device):
        return pltpu.make_async_remote_copy(
            src_ref=src, dst_ref=dst, send_sem=self.send.at[sem], recv_sem=self.recv.at[sem],
            device_id=(self.dp, device), device_id_type=MESH,
        )

    def pair(self, k):
        return self.remote(self.parts[2 * k], self.r1[k], k, self.near)

    def cross(self):
        return self.remote(self.parts[1], self.r2, 2, self.across)

    def middle(self):
        self.pair(0).wait_recv()
        self.parts[1][...] = (self.parts[1][...].astype(f32) + self.r1[0][...].astype(f32)).astype(bf16)

    def end(self, stage, out, sem):
        self.pair(1).wait_recv()
        self.cross().wait_recv()
        step = stage.shape[1]
        copies = []
        for k in range(self.rows // step):
            at = pl.ds(k * step, step)
            if k >= 2:
                copies[k - 2].wait()
            stage[k % 2] = (
                self.parts[3][at, :].astype(f32) + self.r1[1][at, :].astype(f32) + self.r2[at, :].astype(f32)
            )
            copies.append(pltpu.make_async_copy(stage.at[k % 2], out.at[at], sem.at[k % 2]))
            copies[-1].start()
        for copy in copies[-2:]:
            copy.wait()

    def finish(self):
        self.pair(0).wait_send()
        self.pair(1).wait_send()
        self.cross().wait_send()


def tail_kernel(
    count, scale, order, gain_ref, bias_ref, fb_ref, small_a, x, h1, dyb, ctx, dproj, wqd, w1, w2,
    grad, small_sum, br_out, e_out,
    xs, h1s, dys, cs, ps, wqds, w1s, w2s, h2s, acts, dabs, gs, sbuf, rbuf, r2, stage, small, t_in, d_in, d_out,
    sem, late_sem, ss, sr, rs, rr, ts, tr, ds, dr, os, free,
):
    ring = Ring(count)
    me, tensor = ring.me, ring.tensor
    rows = r2.shape[1]
    tiles = x.shape[0] // WIDE
    near = tensor + 1 - 2 * (tensor % 2)

    barrier = pltpu.get_barrier_semaphore()
    for step in range(1, 4):
        pl.semaphore_signal(barrier, inc=1, device_id=(me, (tensor + step) % 4), device_id_type=MESH)

    @pl.loop(1, count)
    def _(step):
        pl.semaphore_signal(barrier, inc=1, device_id=((me + step) % count, tensor), device_id_type=MESH)

    def tile_copy(k, src, dst, i):
        at = pl.ds(pl.multiple_of(i * WIDE, WIDE), WIDE)
        return pltpu.make_async_copy(src.at[at], dst.at[at], sem.at[k, i])

    late = [
        pltpu.make_async_copy(src, dst, late_sem.at[k])
        for k, (src, dst) in enumerate(((w1, w1s), (w2, w2s), (h1, h1s), (ctx, cs), (dproj, ps), (wqd, wqds)))
    ]
    late[0].start()
    tile_copy(0, x, xs, 0).start()
    late[1].start()
    tile_copy(1, dyb, dys, 0).start()
    for i in range(1, tiles):
        tile_copy(0, x, xs, i).start()
        tile_copy(1, dyb, dys, i).start()
    for copy in late[2:]:
        copy.start()
    small[...] = small_a[...]
    late[0].wait()
    late[1].wait()

    hidden = w1.shape[1]

    @pl.loop(0, tiles)
    def _(i):
        at = pl.ds(pl.multiple_of(i * WIDE, WIDE), WIDE)
        tile_copy(0, x, xs, i).wait()
        tile_copy(1, dyb, dys, i).wait()
        xhat, _ = normed(xs[at, :].astype(f32))
        h2s[at, :] = (xhat * gain_ref[1:2, :] + bias_ref[1:2, :]).astype(bf16)
        for c in range(2):
            wide = slice(c * (hidden // 2), (c + 1) * (hidden // 2))
            pre = dot_nn(h2s[at, :], w1s[:, wide]) + as_line(fb_ref[...])[:, wide]
            da = dot_nn(dys[at, :], w2s[:, wide])
            act, slope = gelu_both(pre)
            acts[at, wide] = act.astype(bf16)
            dab = (da * slope).astype(bf16)
            dabs[at, wide] = dab
            small[6:7, wide] += jnp.sum(dab.astype(f32), axis=0, keepdims=True)

    for copy in late[2:5]:
        copy.wait()
    base = 0
    for left, right in ((h1s, ps), (cs, dys), (h2s, dabs), (acts, dys)):
        tall = min(WIDE, left.shape[1])
        jobs, per_row = left.shape[1] // tall, right.shape[1] // BLOCK
        blocks = tall // BLOCK * per_row

        @pl.loop(0, jobs)
        def _(j):
            found = dot_tn(left[:, pl.ds(pl.multiple_of(j * tall, tall), tall)], right[...]).astype(bf16)
            start = base + j * blocks
            for r in range(tall // BLOCK):
                for c in range(per_row):
                    gs[start + r * per_row + c] = found[
                        r * BLOCK : (r + 1) * BLOCK, c * BLOCK : (c + 1) * BLOCK
                    ]

        base += jobs * blocks

    pl.semaphore_wait(barrier, 3 + count - 1)
    pl.semaphore_signal(free, inc=1, device_id=(me, near), device_id_type=MESH)
    scatter = Scatter(ring, order, gs, grad, sbuf, rbuf, ss, sr)
    kept = (h2s, dys)
    sums = [RowSum(kept[n], h1s, 2 * n, r2.at[n], rs.at[n], rr.at[n]) for n in range(2)]
    owners = ((near + 2) % 4, sums[0].across, near, tensor)

    def t_copy(step):
        return pltpu.make_async_remote_copy(
            src_ref=small, dst_ref=t_in.at[tensor], send_sem=ts.at[step], recv_sem=tr.at[step],
            device_id=(me, (tensor + step) % 4), device_id_type=MESH,
        )

    def d_copy(step):
        return pltpu.make_async_remote_copy(
            src_ref=d_out, dst_ref=d_in.at[me], send_sem=ds.at[step], recv_sem=dr.at[step],
            device_id=((me + step) % count, tensor), device_id_type=MESH,
        )

    far = count // 2
    first, second = ((0, 0), (1, 1)), ((1, 0), (0, 1))
    for half, way in first + second:
        if hop_count(half, way, count) >= 1:
            scatter.step(half, way, 1, True)

    def ring_step(hop, which):
        for half, way in which:
            if which is first:
                scatter.step(half, way, hop, False)
            else:

                @pl.when(hop <= far - 1)
                def _():
                    scatter.step(half, way, hop, False)

    wide, thin = 6 * HEAD, 2 * HEAD
    total = lambda v: jnp.sum(v, axis=0, keepdims=True)

    def work(n, r):
        at = pl.ds(pl.multiple_of(owners[n] * rows + r * TILE, TILE), TILE)
        to = slice(n * rows + r * TILE, n * rows + (r + 1) * TILE)
        br = dot_nt(acts[at, :], w2s[...])
        dh1 = None
        for p in range(2):
            lo = p * (wide + thin)
            br = br + dot_nt(cs[at, p * thin : (p + 1) * thin], wqds[:, lo + wide : lo + wide + thin])
            part = dot_nt(ps[at, p * wide : (p + 1) * wide], wqds[:, lo : lo + wide])
            dh1 = part if dh1 is None else dh1 + part
        kept[0][to, :] = br.astype(bf16)
        dh2 = dot_nt(dabs[at, :], w1s[...])
        xhat, _ = normed(xs[at, :].astype(f32))
        kept[1][to, :] = (dh1 * gain_ref[0:1, :] + dh2 * gain_ref[1:2, :]).astype(bf16)
        small[0:1, :] += total(dh1 * xhat)
        small[1:2, :] += total(dh2 * xhat)
        small[2:3, :] += total(dh1)
        small[3:4, :] += total(dh2)

    late[5].wait()
    for n in range(4):
        for r in range(rows // TILE):
            work(n, r)
        if n == 0:
            pl.semaphore_wait(free, 1)
        if n in (0, 2):
            for s in sums:
                s.pair(n // 2).start()
        if n == 1:
            for s in sums:
                s.middle()
            sums[0].cross().start()
            if far >= 2 and count <= 8:
                ring_step(2, first)
        if n == 3 and far >= 2 and count <= 8:
            ring_step(2, second)

    for step in range(1, 4):
        t_copy(step).start()
    sums[1].cross().start()

    def both(hop):
        ring_step(hop, first)
        ring_step(hop, second)

    if count <= 8:
        both(3)
    else:
        for_hops(2, far + 1, both, count)
    for step in range(1, 4):
        t_copy(step).wait_recv()
    t_in[tensor] = small[...]
    row = lax.broadcasted_iota(jnp.int32, small.shape, 0)
    summed = t_in[0] + t_in[1] + t_in[2] + t_in[3]
    d_out[...] = jnp.where(row < 4, summed, small[...])

    @pl.loop(1, count)
    def _(step):
        d_copy(step).start()

    if count <= 8:
        both(4)
    sums[0].end(stage, br_out, os)

    @pl.loop(1, count)
    def _(step):
        d_copy(step).wait_recv()

    d_in[me] = d_out[...]
    small_sum[...] = scale * lax.fori_loop(1, count, lambda k, acc: acc + d_in[k], d_in[0])
    sums[1].end(stage, e_out, os)
    for half in range(2):
        scatter.last(half, scale)
    scatter.finish()
    for s in sums:
        s.finish()
    for step in range(1, 4):
        t_copy(step).wait_send()

    @pl.loop(1, count)
    def _(step):
        d_copy(step).wait_send()


def tail_all(count, scale, order, gains, biases, fc1_bias, small, x, h1, dyb, ctx, dproj, wqd, w1, w2):
    rows, width = x.shape[0] // 4, x.shape[1]
    hidden = w1.shape[1]
    blocks = (width * (dproj.shape[1] + hidden) + (ctx.shape[1] + hidden) * width) // (BLOCK * BLOCK)
    per = blocks // count
    far = count // 2
    any_, vmem = pl.BlockSpec(memory_space=pl.ANY), pl.BlockSpec(memory_space=pltpu.VMEM)
    dma = lambda *n: pltpu.SemaphoreType.DMA(n)
    like = lambda v: pltpu.VMEM(v.shape, v.dtype)
    sum_shape = jax.ShapeDtypeStruct((rows, width), f32)
    tall = lambda cols: pltpu.VMEM((x.shape[0], cols), bf16)
    return pl.pallas_call(
        functools.partial(tail_kernel, count, scale),
        out_shape=[
            jax.ShapeDtypeStruct((per, BLOCK, BLOCK), f32), jax.ShapeDtypeStruct(small.shape, f32),
            sum_shape, sum_shape,
        ],
        in_specs=[pl.BlockSpec(memory_space=pltpu.SMEM)] + [vmem] * 4 + [any_] * 8,
        out_specs=[vmem, vmem, any_, any_],
        scratch_shapes=[like(v) for v in (x, h1, dyb, ctx, dproj, wqd, w1, w2)]
        + [
            tall(width), tall(hidden), tall(hidden), pltpu.VMEM((blocks, BLOCK, BLOCK), bf16),
            pltpu.VMEM((4, per, 64, BLOCK), bf16), pltpu.VMEM((4 * far, per, 64, BLOCK), bf16),
            pltpu.VMEM((2, rows, width), bf16), pltpu.VMEM((2, 64, width), f32),
            pltpu.VMEM(small.shape, f32), pltpu.VMEM((4,) + small.shape, f32),
            pltpu.VMEM((count,) + small.shape, f32), pltpu.VMEM(small.shape, f32),
            dma(2, x.shape[0] // WIDE), dma(6),
            dma(4 * far), dma(4 * far), dma(2, 3), dma(2, 3), dma(4), dma(4), dma(count), dma(count),
            dma(2), pltpu.SemaphoreType.REGULAR,
        ],
        compiler_params=pltpu.CompilerParams(
            collective_id=1, has_side_effects=True, vmem_limit_bytes=VMEM_LIMIT
        ),
        cost_estimate=pl.CostEstimate(flops=int(3.5e10), bytes_accessed=int(4e7), transcendentals=int(4e6)),
        name="tail_all",
    )(order, gains, biases, fc1_bias, small, x, h1, dyb, ctx, dproj, wqd, w1, w2)


def finish_kernel(
    steps, lim_ref, bias_ref, small_ref, racc_ref, qacc_ref, facc_ref, grad, tok, dy, br, e, ls, rs, lr, rr,
    gout, out, dx, lout, rout, cout, racc, rupd, qacc, qupd, facc, fupd,
    g_v, tok_v, dy_v, br_v, e_v, ls_v, rs_v, lr_v, rr_v, out_v, dx_v, lo_v, ro_v, co_v, isem, osem,
):
    tensor = lax.axis_index("tensor")
    own_rows, blocks = tok.shape[0], grad.shape[0]
    rows, some = own_rows // steps, blocks // steps
    ins = [(grad, g_v), (ls, ls_v), (rs, rs_v), (lr, lr_v), (rr, rr_v), (tok, tok_v), (dy, dy_v), (br, br_v), (e, e_v)]
    outs = [(g_v, gout), (lo_v, lout), (ro_v, rout), (co_v, cout), (out_v, out), (dx_v, dx)]

    def span(ref, s):
        size = ref.shape[0] // steps
        return ref.at[pl.ds(s * size if ref.shape[0] == blocks else pl.multiple_of(s * size, 16), size)]

    def fetch(k, s):
        return pltpu.make_async_copy(span(ins[k][0], s), span(ins[k][1], s), isem.at[k, s])

    def store(k, s):
        return pltpu.make_async_copy(span(outs[k][0], s), span(outs[k][1], s), osem.at[k, s])

    for s in range(steps):
        for k in range(len(ins)):
            fetch(k, s).start()
    small = small_ref[...]

    def adagrad(grad_vec, accum, new, update):
        accum_next = accum + grad_vec * grad_vec
        new[...] = accum_next
        update[...] = -adagrad_rate * grad_vec * lax.rsqrt(accum_next)

    def stacked(line, count):
        return jnp.concatenate([line[:, k * BLOCK : (k + 1) * BLOCK] for k in range(count)], axis=0)

    adagrad(jnp.concatenate([small[0:5], small[4:5]], axis=0), racc_ref[...], racc, rupd)
    adagrad(stacked(small[5:6], qacc.shape[0]), qacc_ref[...], qacc, qupd)
    adagrad(stacked(small[6:7], facc.shape[0]), facc_ref[...], facc, fupd)
    shift = bias_ref[2:3, :] + bias_ref[3:4, :]

    @pl.loop(0, steps)
    def _(s):
        for k in range(len(ins)):
            fetch(k, s).wait()

        for b in range(some):
            k = s * some + b
            low = g_v[k].astype(bf16)
            lo_v[k] = stat_decay * ls_v[k] + (1.0 - stat_decay) * dot_nt(low, low)
            ro_v[k] = stat_decay * rs_v[k] + (1.0 - stat_decay) * dot_tn(low, low)
            pushed = dot_nn(lr_v[k].astype(bf16), low).astype(bf16)
            co_v[k] = -shampoo_rate * dot_nn(pushed, rr_v[k].astype(bf16))

        at = pl.ds(pl.multiple_of(s * rows, 16), rows)
        x = tok_v[at, :].astype(f32)
        out_v[at, :] = (x + br_v[at, :] + shift).astype(bf16)
        start = tensor * own_rows + s * rows
        place = start % LEN + lax.broadcasted_iota(jnp.int32, (rows, 1), 0)
        kept = jnp.where(place < lim_ref[start // LEN], dy_v[at, :].astype(f32), 0.0)
        xhat, scale = normed(x)
        v = e_v[at, :]
        dx_v[at, :] = kept + scale * (
            v - jnp.mean(v, axis=-1, keepdims=True) - xhat * jnp.mean(v * xhat, axis=-1, keepdims=True)
        )
        for k in range(len(outs)):
            store(k, s).start()

    for s in range(steps):
        for k in range(len(outs)):
            store(k, s).wait()


def finish_all(limits, biases, small, racc, qacc, facc, grad, tok, dy, br, e, ls, rs, lr, rr):
    steps = 4 if grad.shape[0] % 4 == 0 else 1
    any_, vmem = pl.BlockSpec(memory_space=pl.ANY), pl.BlockSpec(memory_space=pltpu.VMEM)
    shape = lambda v: jax.ShapeDtypeStruct(v.shape, v.dtype)
    like = lambda v: pltpu.VMEM(v.shape, v.dtype)
    vectors = [racc, racc, qacc, qacc, facc, facc]
    return pl.pallas_call(
        functools.partial(finish_kernel, steps),
        out_shape=[shape(grad), shape(tok), shape(e)] + [shape(grad)] * 3 + [shape(v) for v in vectors],
        in_specs=[pl.BlockSpec(memory_space=pltpu.SMEM)] + [vmem] * 5 + [any_] * 9,
        out_specs=[any_] * 6 + [vmem] * 6,
        scratch_shapes=[like(v) for v in (grad, tok, dy, br, e, ls, rs, lr, rr, tok, e, ls, ls, ls)]
        + [pltpu.SemaphoreType.DMA((9, steps)), pltpu.SemaphoreType.DMA((6, steps))],
        compiler_params=pltpu.CompilerParams(vmem_limit_bytes=VMEM_LIMIT),
        cost_estimate=pl.CostEstimate(flops=int(4e8), bytes_accessed=int(2e7), transcendentals=0),
        name="finish_all",
    )(limits, biases, small, racc, qacc, facc, grad, tok, dy, br, e, ls, rs, lr, rr)


def shards(
    tokens, out_grad, seq_lengths, norm_gains, row_biases, qkv_weight, qkv_bias, dense_weight, fc1_weight,
    fc1_bias, fc2_weight, block_slot, left_stat, right_stat, left_root, right_root, row_accum,
    qkv_bias_accum, fc1_bias_accum,
):
    tensor_count = lax.axis_size("tensor")
    dp_count = lax.axis_size("dp")
    grad_scale = 1.0 / math.sqrt(tokens.shape[0] * tensor_count * dp_count)
    xf, h1, dyb, ctx, dproj, wqdf, w1f, w2f, sum_a, order = mixed_all(
        dp_count, seq_lengths, norm_gains, row_biases, as_rows(qkv_bias), jnp.asarray(rotary_rows()),
        as_rows(block_slot), tokens, out_grad, qkv_weight, dense_weight, fc1_weight, fc2_weight,
    )
    own_grad, small, branch, e_sum = tail_all(
        dp_count, grad_scale, order, norm_gains, row_biases, as_rows(fc1_bias), sum_a,
        xf, h1, dyb, ctx, dproj, wqdf, w1f, w2f,
    )
    outs = finish_all(
        seq_lengths, row_biases, small, row_accum, as_rows(qkv_bias_accum), as_rows(fc1_bias_accum),
        own_grad, tokens, out_grad, branch, e_sum, left_stat, right_stat, left_root, right_root,
    )
    block_grad, layer_out, input_grad, left_new, right_new, change = outs[:6]
    return (
        layer_out, input_grad, block_grad, left_new, right_new, change,
        *outs[6:8], *(v.reshape(-1) for v in outs[8:]),
    )


def solution(mesh):
    both = ("dp", "tensor")
    return jax.shard_map(
        shards,
        mesh=mesh,
        in_specs=(
            P(both, None), P(both, None), P("dp"), P(), P(), P("dp", "tensor"), P("tensor"),
            P("tensor", "dp"), P("dp", "tensor"), P("tensor"), P("tensor", "dp"), P(),
            P(both, None, None), P(both, None, None), P(both, None, None), P(both, None, None),
            P(), P("tensor"), P("tensor"),
        ),
        out_specs=(
            P(both, None), P(both, None), P(both, None, None), P(both, None, None),
            P(both, None, None), P(both, None, None), P(), P(), P("tensor"), P("tensor"),
            P("tensor"), P("tensor"),
        ),
        check_vma=False,
    )
```

```python
import functools
import math

import jax
import jax.numpy as jnp
import numpy as np
from jax import lax
from jax.experimental import pallas as pl
from jax.experimental.pallas import tpu as pltpu
from jax.sharding import PartitionSpec as P

HEAD = 64
ROT = 16
LEN = 1024
BLOCK = 128
TILE = 256
WIDE = 512
MESH = pl.DeviceIdType.MESH
VMEM_LIMIT = 60 * 1024 * 1024

masked_score = -1e30
shampoo_rate = 0.03
adagrad_rate = 0.1
stat_decay = 0.5
f32 = jnp.float32
bf16 = jnp.bfloat16


def rotary_rows():
    half = ROT // 2
    inverse = np.power(np.float32(10000.0), -(np.arange(half, dtype=np.float32) * np.float32(2.0 / ROT)))
    angles = inverse.astype(np.float32)[:, None] * np.arange(LEN, dtype=np.float32)[None, :]
    return np.concatenate([np.cos(angles), np.sin(angles)], axis=0).astype(np.float32)


def ring_place(me, count):
    low, high = me % 2, me // 2
    return low * (count - 1 - high) + (1 - low) * high


def ring_device(place, count):
    upper = place // (count // 2)
    return (1 - upper) * (2 * place) + upper * (2 * (count - 1 - place) + 1)


def hop_count(half, way, count):
    far = count // 2
    return far if half == way else far - 1


def for_hops(first, last, body, count):
    if count <= 8:
        for hop in range(first, last):
            body(hop)
    elif last > first:

        @pl.loop(first, last)
        def _(hop):
            body(hop)


def as_rows(vec):
    return vec.reshape(-1, BLOCK)


def as_line(rows):
    return jnp.concatenate([rows[k : k + 1, :] for k in range(rows.shape[0])], axis=1)


class Ring:
    def __init__(self, count):
        self.count = count
        self.me = lax.axis_index("dp")
        self.tensor = lax.axis_index("tensor")
        self.place = ring_place(self.me, count)
        self.peer = [
            (ring_device((self.place + step) % count, count), self.tensor) for step in (1, count - 1)
        ]

    def at(self, offset):
        return ring_device((self.place + offset + 2 * self.count) % self.count, self.count)


class Gather:
    def __init__(self, ring, locals_, fulls, send, recv):
        self.ring, self.locals, self.fulls, self.send, self.recv = ring, locals_, fulls, send, recv
        self.far = ring.count // 2

    def part(self, ref, w, half, owner=None):
        rows, cols = self.locals[w].shape
        base = 0 if owner is None else owner * rows
        if rows % 32 == 0:
            return ref.at[pl.ds(pl.multiple_of(base + half * (rows // 2), 16), rows // 2)]
        return ref.at[pl.ds(base, rows), pl.ds(half * (cols // 2), cols // 2)]

    def sem(self, w, half, way, hop):
        return ((w * 2 + half) * 2 + way) * self.far + hop - 1

    def copy(self, w, half, way, hop, source):
        owner = self.ring.at((1 - hop) if way == 0 else (hop - 1))
        src = self.part(self.locals[w], w, half) if source else self.part(self.fulls[w], w, half, owner)
        return pltpu.make_async_remote_copy(
            src_ref=src,
            dst_ref=self.part(self.fulls[w], w, half, owner),
            send_sem=self.send.at[self.sem(w, half, way, hop)],
            recv_sem=self.recv.at[self.sem(w, half, way, hop)],
            device_id=self.ring.peer[way],
            device_id_type=MESH,
        )

    def arrival(self, w, half, way, hop):
        owner = self.ring.at(-hop if way == 0 else hop)
        dst = self.part(self.fulls[w], w, half, owner)
        return pltpu.make_async_remote_copy(
            src_ref=dst,
            dst_ref=dst,
            send_sem=self.send.at[self.sem(w, half, way, hop)],
            recv_sem=self.recv.at[self.sem(w, half, way, hop)],
            device_id=self.ring.peer[way],
            device_id_type=MESH,
        )

    def begin(self, w):
        for half in range(2):
            for way in range(2):
                if hop_count(half, way, self.ring.count) >= 1:
                    self.copy(w, half, way, 1, True).start()

    def forward(self, w, hop, last):
        for half in range(2):
            for way in range(2):
                hops = self.far if half == way else self.far - 1
                if last and hops != self.far:
                    continue
                self.arrival(w, half, way, hop).wait_recv()
                if not last:
                    more = self.far if half == way else self.far - 1
                    if more == self.far:
                        self.copy(w, half, way, hop + 1, False).start()
                    else:

                        @pl.when(hop + 1 <= more)
                        def _():
                            self.copy(w, half, way, hop + 1, False).start()

    def finish(self, w):
        for half in range(2):
            for way in range(2):
                hops = hop_count(half, way, self.ring.count)
                if hops >= 1:
                    self.copy(w, half, way, 1, True).wait_send()
                for_hops(
                    2, hops + 1, lambda hop: self.copy(w, half, way, hop, False).wait_send(), self.ring.count
                )


class Rows:
    def __init__(self, local, full, send, recv, own):
        self.tensor = lax.axis_index("tensor")
        self.dp = lax.axis_index("dp")
        self.near = self.tensor + 1 - 2 * (self.tensor % 2)
        self.across = (self.tensor + 2) % 4
        self.local, self.full, self.send, self.recv, self.own = local, full, send, recv, own
        self.rows = local.shape[0]

    def slot(self, owner, piece=None):
        if piece is None:
            return self.full.at[pl.ds(pl.multiple_of(owner * self.rows, 16), self.rows)]
        half = self.rows // 2
        return self.full.at[pl.ds(pl.multiple_of(owner * self.rows + piece * half, 16), half)]

    def remote(self, src, dst, sem, device):
        return pltpu.make_async_remote_copy(
            src_ref=src,
            dst_ref=dst,
            send_sem=self.send.at[sem],
            recv_sem=self.recv.at[sem],
            device_id=(self.dp, device),
            device_id_type=MESH,
        )

    def keep(self):
        return pltpu.make_async_copy(self.local, self.slot(self.tensor), self.own)

    def pair(self):
        return self.remote(self.local, self.slot(self.tensor), 0, self.near)

    def cross(self, piece):
        half = self.rows // 2
        return self.remote(
            self.local.at[pl.ds(piece * half, half)], self.slot(self.tensor, piece), 1 + piece, self.across
        )

    def onward(self, piece):
        here = self.slot(self.across, piece)
        return self.remote(here, here, 3 + piece, self.near)

    def begin_near(self):
        self.keep().start()
        self.pair().start()

    def begin_cross(self):
        for piece in range(2):
            self.cross(piece).start()

    def pass_piece(self, piece):
        self.cross(piece).wait_recv()
        self.onward(piece).start()

    def pass_on(self):
        for piece in range(2):
            self.pass_piece(piece)

    def finish(self):
        self.keep().wait()
        self.pair().wait()
        for piece in range(2):
            self.cross(piece).wait_send()
            self.onward(piece).wait()


def greet(devices):
    barrier = pltpu.get_barrier_semaphore()
    for device in devices:
        pl.semaphore_signal(barrier, inc=1, device_id=device, device_id_type=MESH)
    pl.semaphore_wait(barrier, len(devices))


def dot_nn(a, b):
    return lax.dot_general(a, b, (((1,), (0,)), ((), ())), preferred_element_type=f32)


def dot_nt(a, b):
    return lax.dot_general(a, b, (((1,), (1,)), ((), ())), preferred_element_type=f32)


def dot_tn(a, b):
    return lax.dot_general(a, b, (((0,), (0,)), ((), ())), preferred_element_type=f32)


def normed(x):
    average = jnp.mean(x, axis=-1, keepdims=True)
    centered = x - average
    variance = jnp.mean(centered * centered, axis=-1, keepdims=True)
    scale = lax.rsqrt(variance + 1e-05)
    return centered * scale, scale


def mixed_kernel(
    count, lim_ref, gain_ref, bias_ref, qb_ref, rot_ref, slot_ref, wd, w2, x, dy, wq, w1,
    x_out, h1_out, dyb_out, ctx_out, dproj_out, wqd_out, w1f, w2f, sum_ref, order_ref,
    xf, dyf, wf, wl, w2l, h1s, ctxs, dps, qt, kt, vt, dct, ctt, dqt, kr, vr, dkvs,
    rs, rr, ro, gs, gr, go, os,
):
    ring = Ring(count)
    pair_cols = 6 * HEAD
    half_cols = pair_cols + 2 * HEAD
    parts = [
        pltpu.make_async_copy(
            wq.at[:, pl.ds(p * pair_cols, pair_cols)], wl.at[:, pl.ds(p * half_cols, pair_cols)], os.at[p]
        )
        for p in range(2)
    ]
    for copy in parts:
        copy.start()
    turned_dense = wd[...].T
    for p in range(2):
        wl[:, p * half_cols + pair_cols : (p + 1) * half_cols] = turned_dense[:, p * 2 * HEAD : (p + 1) * 2 * HEAD]
    views = [(wl.at[:, pl.ds(p * half_cols, half_cols)], wf.at[:, pl.ds(p * half_cols, half_cols)]) for p in (0, 1)]
    views += [(w1, w1f), (w2l, w2f)]
    gather = Gather(ring, [v[0] for v in views], [v[1] for v in views], gs, gr)
    rx = Rows(x, xf, rs.at[0], rr.at[0], ro.at[0])
    ry = Rows(dy, dyf, rs.at[1], rr.at[1], ro.at[1])
    greet([ring.peer[0], ring.peer[1], (ring.me, rx.near), (ring.me, rx.across)])
    far = count // 2
    own = []
    for k, (local, full) in enumerate(((w1, w1f), (w2l, w2f))):
        rows = local.shape[0]
        own.append(
            pltpu.make_async_copy(local, full.at[pl.ds(pl.multiple_of(ring.me * rows, 16), rows)], go.at[k])
        )
    rx.begin_near()
    for copy in parts:
        copy.wait()
    gather.begin(0)
    rx.begin_cross()
    ry.begin_near()
    ry.begin_cross()
    wf[pl.ds(pl.multiple_of(ring.me * wl.shape[0], 16), wl.shape[0]), :] = wl[...]
    own[0].start()
    sum_ref[...] = jnp.zeros_like(sum_ref)
    tensor = ring.tensor
    tiles = LEN // TILE

    def whole_ring(w):
        for_hops(1, far, lambda hop: gather.forward(w, hop, False), count)
        gather.forward(w, far, True)

    def hop_at(w, hop):
        if count == 8:
            gather.forward(w, hop, hop == far)
        elif hop == 4:
            whole_ring(w)

    def rows_of(seq, i):
        return pl.ds(pl.multiple_of(seq * LEN + i * TILE, TILE), TILE)

    def norm_tile(seq, i):
        rows = rows_of(seq, i)
        xhat, _ = normed(xf[rows, :].astype(f32))
        h1s[rows, :] = (xhat * gain_ref[0:1, :] + bias_ref[0:1, :]).astype(bf16)

    def mask_tile(seq, i):
        rows = rows_of(seq, i)
        place = i * TILE + lax.broadcasted_iota(jnp.int32, (TILE, 1), 0)
        kept = jnp.where(place < lim_ref[seq], dyf[rows, :].astype(f32), 0.0)
        sum_ref[4:5, :] += jnp.sum(kept, axis=0, keepdims=True)
        dyf[rows, :] = kept.astype(bf16)

    def turned(first, second, cosine, sine):
        return first * cosine - second * sine, second * cosine + first * sine

    def prepare_tile(seq, pair, i):
        rows = rows_of(seq, i)
        cols = pl.ds(pl.multiple_of(i * TILE, TILE), TILE)
        proj = dot_nn(h1s[rows, :], wf[:, pl.ds(pl.multiple_of(pair * half_cols, BLOCK), pair_cols)])
        proj = proj + as_line(qb_ref[pl.ds(pair * (pair_cols // BLOCK), pair_cols // BLOCK), :])
        proj = proj.T
        cosine, sine = rot_ref[0:8, cols], rot_ref[8:16, cols]
        key = i * TILE + lax.broadcasted_iota(jnp.int32, (16, TILE), 1)
        row = lax.broadcasted_iota(jnp.int32, (16, TILE), 0)
        ones = jnp.where(row == 0, 1.0, 0.0).astype(bf16)
        hidden = jnp.where((row == 0) & (key >= lim_ref[seq]), masked_score, 0.0).astype(bf16)
        blank = jnp.zeros((48, TILE), bf16)
        none = jnp.zeros((HEAD, TILE), bf16)
        for hh in range(2):
            h = 2 * pair + hh
            base = 3 * HEAD * hh
            q0, q1 = turned(proj[base : base + 8], proj[base + 8 : base + 16], cosine, sine)
            q = jnp.concatenate([q0, q1, proj[base + 16 : base + HEAD]], axis=0).astype(bf16)
            q = (q.astype(f32) * 0.125).astype(bf16)
            qt[h, :, cols] = jnp.concatenate([q, ones, blank], axis=0)
            base += HEAD
            k0, k1 = turned(proj[base : base + 8], proj[base + 8 : base + 16], cosine, sine)
            k = jnp.concatenate([k0, k1, proj[base + 16 : base + HEAD]], axis=0).astype(bf16)
            kt[h, :, cols] = k
            kr[h, cols, :] = jnp.concatenate([k, hidden, blank], axis=0).T
            base += HEAD
            v = proj[base : base + HEAD].astype(bf16)
            vt[h, :, cols] = jnp.concatenate([v, ones], axis=0)
            vr[h, cols, :] = jnp.concatenate([none, v], axis=0).T

    def context_tile(seq, pair, i):
        cols = pl.ds(pl.multiple_of(i * TILE, TILE), TILE)
        begin = pair * half_cols + pair_cols
        dctx = dot_nn(dyf[rows_of(seq, i), :], wf[:, begin : begin + 2 * HEAD]).T.astype(bf16)
        for hh in range(2):
            dct[2 * pair + hh, :, cols] = dctx[HEAD * hh : HEAD * (hh + 1)]

    def back_tile(seq, i):
        mask_tile(seq, i)
        context_tile(seq, 0, i)
        context_tile(seq, 1, i)

    def attend(pair, i, fresh):
        here = slice(i * TILE, (i + 1) * TILE)
        chunks = [slice(c * TILE, (c + 1) * TILE) for c in range(i + 1)]
        heads = range(2)
        of = [2 * pair, 2 * pair + 1]
        key = lax.broadcasted_iota(jnp.int32, (TILE, TILE), 0)
        query = lax.broadcasted_iota(jnp.int32, (TILE, TILE), 1)
        q = [qt[of[hh], :, here] for hh in heads]
        scores = [[dot_nn(kr[of[hh], c, :], q[hh]) for c in chunks] for hh in heads]
        probs, grads, deltas, both = [], [], [], []
        none = jnp.zeros((HEAD, TILE), bf16)
        for hh in heads:
            scores[hh][i] = jnp.where(key <= query, scores[hh][i], masked_score)
            top = jnp.max(scores[hh][0], axis=0, keepdims=True)
            for s in scores[hh][1:]:
                top = jnp.maximum(top, jnp.max(s, axis=0, keepdims=True))
            probs.append([jnp.exp(s - top).astype(bf16) for s in scores[hh]])
        for hh in heads:
            total = dot_nn(vt[of[hh], :, chunks[0]], probs[hh][0])
            for c, p in zip(chunks[1:], probs[hh][1:]):
                total = total + dot_nn(vt[of[hh], :, c], p)
            inverse = 1.0 / total[HEAD : HEAD + 1]
            context = total[:HEAD] * inverse
            ctt[of[hh], :, here] = context
            grad = (dct[of[hh], :, here].astype(f32) * inverse).astype(bf16)
            deltas.append(jnp.sum(grad.astype(f32) * context, axis=0, keepdims=True))
            grad = jnp.concatenate([none, grad], axis=0)
            grads.append(grad)
            both.append(jnp.concatenate([jnp.concatenate([q[hh][:HEAD], none], axis=0), grad], axis=1))
        dq = [None, None]
        for n, c in enumerate(chunks):
            for hh in heads:
                p = probs[hh][n]
                dp = dot_nn(vr[of[hh], c, :], grads[hh])
                ds = (p.astype(f32) * (dp - deltas[hh])).astype(bf16)
                part = dot_nn(kt[of[hh], :, c], ds)
                dq[hh] = part if dq[hh] is None else dq[hh] + part
                dkv = dot_nt(jnp.concatenate([ds, p], axis=1), both[hh])
                if n in fresh:
                    dkvs[of[hh], c, :] = dkv
                else:
                    dkvs[of[hh], c, :] += dkv
        for hh in heads:
            dqt[of[hh], :, here] = dq[hh] * 0.125

    def collect_tile(seq, i):
        rows = rows_of(seq, i)
        cols = pl.ds(pl.multiple_of(i * TILE, TILE), TILE)
        cosine, sine = rot_ref[0:8, cols], rot_ref[8:16, cols]
        for pair in range(2):
            pieces = []
            for h in (2 * pair, 2 * pair + 1):
                dkv = dkvs[h, cols, :].T
                for grad in (dqt[h, :, cols], dkv[:HEAD]):
                    pieces += [*turned(grad[0:8], grad[8:16], cosine, -sine), grad[16:HEAD]]
                pieces.append(dkv[HEAD:])
            low = jnp.concatenate(pieces, axis=0).T.astype(bf16)
            wide = slice(pair * pair_cols, (pair + 1) * pair_cols)
            dps[rows, wide] = low
            sum_ref[5:6, wide] += jnp.sum(low.astype(f32), axis=0, keepdims=True)
            ctx = jnp.concatenate([ctt[2 * pair, :, cols], ctt[2 * pair + 1, :, cols]], axis=0).T
            ctxs[rows, pair * 2 * HEAD : (pair + 1) * 2 * HEAD] = ctx.astype(bf16)

    def save(turn, k, seq):
        src, dst = ((xf, x_out), (h1s, h1_out), (dyf, dyb_out), (ctxs, ctx_out), (dps, dproj_out))[k]
        rows = pl.ds(pl.multiple_of(seq * LEN, LEN), LEN)
        return pltpu.make_async_copy(src.at[rows], dst.at[rows], os.at[turn * 5 + k])

    mine = order_ref.shape[1]
    per = mine // count
    place = lax.broadcasted_iota(jnp.int32, (mine, 1), 0).astype(f32)
    owner = jnp.floor((place + 0.5) / per)
    wanted = (owner * 4.0 + lax.convert_element_type(tensor, f32)) * per + (place - owner * per)
    found = jnp.zeros(order_ref.shape, f32)
    for r in range(slot_ref.shape[0]):
        hit = jnp.where(slot_ref[r : r + 1, :].astype(f32) == wanted, 1.0, 0.0).astype(bf16)
        block = r * BLOCK + lax.broadcasted_iota(jnp.int32, (8, BLOCK), 1) - tensor * mine
        found = found + dot_nt(jnp.clip(block, 0, mine - 1).astype(f32).astype(bf16), hit)
    order_ref[...] = (found + 0.5).astype(jnp.int32)

    seq = tensor // 2
    rx.keep().wait()
    rx.pair().wait_recv()

    @pl.loop(0, tiles)
    def _(i):
        norm_tile(seq, i)

        @pl.when(i == 0)
        def _():
            hop_at(0, 1)
            gather.begin(1)

        @pl.when(i == 1)
        def _():
            hop_at(0, 2)
            hop_at(1, 1)

        @pl.when(i == 2)
        def _():
            hop_at(0, 3)
            hop_at(1, 2)
            gather.begin(2)

    save(0, 0, seq).start()
    save(0, 1, seq).start()
    w2l[...] = w2[...].T
    hop_at(0, 4)
    ry.keep().wait()
    ry.pair().wait_recv()

    @pl.loop(0, tiles // 2)
    def _(i):
        for sub in range(2):
            prepare_tile(seq, 0, 2 * i + sub)


    @pl.loop(0, tiles)
    def _(i):
        mask_tile(seq, i)
        context_tile(seq, 0, i)

    save(0, 2, seq).start()

    @pl.loop(0, 2)
    def _(pair):
        @pl.when(pair == 1)
        def _():
            hop_at(1, 4)
            hop_at(2, 1)

            @pl.loop(0, tiles // 2)
            def _(i):
                for sub in range(2):
                    prepare_tile(seq, 1, 2 * i + sub)
                    context_tile(seq, 1, 2 * i + sub)

        attend(pair, 3, (0, 1, 2, 3))

        @pl.when(pair == 0)
        def _():
            hop_at(1, 3)
            gather.begin(3)
            own[1].start()

        attend(pair, 2, ())

        @pl.when(pair == 0)
        def _():
            rx.pass_on()

        @pl.when(pair == 1)
        def _():
            hop_at(3, 1)

        attend(pair, 1, ())
        attend(pair, 0, ())

    @pl.loop(0, tiles)
    def _(i):
        collect_tile(seq, i)

    save(0, 3, seq).start()
    save(0, 4, seq).start()
    keep = pltpu.make_async_copy(wf, wqd_out, os.at[10])
    keep.start()

    seq = 1 - seq
    for piece in range(2):
        rx.onward(piece).wait_recv()

    @pl.loop(0, tiles)
    def _(i):
        norm_tile(seq, i)

    save(1, 0, seq).start()
    save(1, 1, seq).start()
    ry.pass_piece(0)

    for pair in range(2):

        @pl.loop(0, tiles // 2)
        def _(i):
            for sub in range(2):
                prepare_tile(seq, pair, 2 * i + sub)

        if pair == 0:
            hop_at(2, 2)

    ry.onward(0).wait()
    back_tile(seq, 0)
    back_tile(seq, 2)

    @pl.loop(0, 2)
    def _(pair):
        attend(pair, 2, (0, 1, 2))

        @pl.when(pair == 0)
        def _():
            hop_at(3, 2)

        attend(pair, 0, ())

    ry.pass_piece(1)
    ry.onward(1).wait()
    back_tile(seq, 1)
    back_tile(seq, 3)
    save(1, 2, seq).start()
    hop_at(2, 3)

    @pl.loop(0, 2)
    def _(pair):
        attend(pair, 3, (3,))

        @pl.when(pair == 1)
        def _():
            hop_at(3, 3)

        attend(pair, 1, ())

    @pl.loop(0, tiles)
    def _(i):
        collect_tile(seq, i)

    save(1, 3, seq).start()
    save(1, 4, seq).start()
    hop_at(2, 4)
    hop_at(3, 4)
    for w in range(4):
        gather.finish(w)
    own[0].wait()
    own[1].wait()
    rx.pair().wait_send()
    ry.pair().wait_send()
    for piece in range(2):
        rx.cross(piece).wait_send()
        rx.onward(piece).wait_send()
        ry.cross(piece).wait_send()
    for turn in range(2):
        for k in range(5):
            save(turn, k, turn + (1 - 2 * turn) * (tensor // 2)).wait()
    keep.wait()


def mixed_all(count, limits, gains, biases, qkv_bias, rot, slots, x, dy, wq, wd, w1, w2):
    far = count // 2
    rows, width = 4 * x.shape[0], x.shape[1]
    ctx_cols, proj_cols = wd.shape[0], wq.shape[1]
    shard = wq.shape[0]
    out = lambda r, c: jax.ShapeDtypeStruct((r, c), bf16)
    any_, vmem = pl.BlockSpec(memory_space=pl.ANY), pl.BlockSpec(memory_space=pltpu.VMEM)
    dma = lambda *n: pltpu.SemaphoreType.DMA(n)
    buf = lambda dtype, *shape: pltpu.VMEM(shape, dtype)
    heads, both = 4, ctx_cols + proj_cols
    return pl.pallas_call(
        functools.partial(mixed_kernel, count),
        out_shape=[
            out(rows, width), out(rows, width), out(rows, width), out(rows, ctx_cols), out(rows, proj_cols),
            out(width, both), out(width, w1.shape[1]), out(width, w2.shape[0]),
            jax.ShapeDtypeStruct((8, width), f32), jax.ShapeDtypeStruct((8, slots.size // 4), jnp.int32),
        ],
        in_specs=[pl.BlockSpec(memory_space=pltpu.SMEM)] + [vmem] * 7 + [any_] * 4,
        out_specs=[any_] * 8 + [vmem] * 2,
        scratch_shapes=[
            buf(bf16, rows, width), buf(bf16, rows, width), buf(bf16, width, both),
            buf(bf16, shard, both), buf(bf16, shard, w2.shape[0]),
            buf(bf16, rows, width), buf(bf16, rows, ctx_cols), buf(bf16, rows, proj_cols),
            buf(bf16, heads, 2 * HEAD, LEN), buf(bf16, heads, HEAD, LEN), buf(bf16, heads, HEAD + 16, LEN),
            buf(bf16, heads, HEAD, LEN), buf(f32, heads, HEAD, LEN), buf(f32, heads, HEAD, LEN),
            buf(bf16, heads, LEN, 2 * HEAD), buf(bf16, heads, LEN, 2 * HEAD), buf(f32, heads, LEN, 2 * HEAD),
            dma(2, 5), dma(2, 5), dma(2), dma(16 * far), dma(16 * far), dma(2), dma(11),
        ],
        compiler_params=pltpu.CompilerParams(
            collective_id=0, has_side_effects=True, vmem_limit_bytes=VMEM_LIMIT
        ),
        cost_estimate=pl.CostEstimate(flops=int(2e10), bytes_accessed=int(4e7), transcendentals=int(1e7)),
        name="mixed_all",
    )(limits, gains, biases, qkv_bias, rot, slots, wd, w2, x, dy, wq, w1)


def gelu_both(x):
    bell = jnp.exp(-0.5 * x * x)
    u = jnp.abs(x) * (1.0 / math.sqrt(2.0))
    t = 1.0 / (1.0 + 0.3275911 * u)
    poly = t * (0.254829592 + t * (-0.284496736 + t * (1.421413741 + t * (-1.453152027 + t * 1.061405429))))
    tail = 0.5 * poly * bell
    phi = jnp.where(x < 0.0, tail, 1.0 - tail)
    return x * phi, phi + x * bell * (1.0 / math.sqrt(2.0 * math.pi))


class Scatter:
    def __init__(self, ring, order, blocks, out, sbuf, rbuf, send, recv):
        self.ring, self.order, self.blocks, self.out = ring, order, blocks, out
        self.sbuf, self.rbuf, self.send, self.recv = sbuf, rbuf, send, recv
        self.per = out.shape[0]
        self.far = ring.count // 2

    def index(self, half, way, hop):
        return (half * 2 + way) * self.far + hop - 1

    def copy(self, half, way, hop, first):
        i = self.index(half, way, hop)
        return pltpu.make_async_remote_copy(
            src_ref=self.sbuf.at[half * 2 + way] if first else self.rbuf.at[i - 1],
            dst_ref=self.rbuf.at[i],
            send_sem=self.send.at[i],
            recv_sem=self.recv.at[i],
            device_id=self.ring.peer[way],
            device_id_type=MESH,
        )

    def own(self, dest, half, k):
        return self.blocks[self.order[0, dest * self.per + k], half * 64 : half * 64 + 64, :].astype(f32)

    def step(self, half, way, hop, first):
        hops = hop_count(half, way, self.ring.count)
        dest = self.ring.at((hops + 1 - hop) if way == 0 else (hop - hops - 1))
        i = self.index(half, way, hop)
        if not first:
            self.copy(half, way, hop - 1, True).wait_recv()

        def one(k, carry):
            value = self.own(dest, half, k)
            if first:
                self.sbuf[half * 2 + way, k] = value.astype(bf16)
            else:
                self.rbuf[i - 1, k] = (value + self.rbuf[i - 1, k].astype(f32)).astype(bf16)
            return carry

        lax.fori_loop(0, self.per, one, 0)
        self.copy(half, way, hop, first).start()

    def last(self, half, scale):
        came = []
        for way in range(2):
            hops = hop_count(half, way, self.ring.count)
            if hops >= 1:
                self.copy(half, way, hops, True).wait_recv()
                came.append(self.index(half, way, hops))
        me = self.ring.me

        def one(k, carry):
            value = self.own(me, half, k)
            for i in came:
                value = value + self.rbuf[i, k].astype(f32)
            self.out[k, half * 64 : half * 64 + 64, :] = value * scale
            return carry

        lax.fori_loop(0, self.per, one, 0)

    def finish(self):
        for half in range(2):
            for way in range(2):
                hops = hop_count(half, way, self.ring.count)
                for_hops(
                    1, hops + 1, lambda hop: self.copy(half, way, hop, True).wait_send(), self.ring.count
                )


class RowSum:
    def __init__(self, parts, r1, base, r2, send, recv):
        self.tensor = lax.axis_index("tensor")
        self.dp = lax.axis_index("dp")
        self.near = self.tensor + 1 - 2 * (self.tensor % 2)
        self.across = (self.tensor + 2) % 4
        self.r2, self.send, self.recv = r2, send, recv
        self.rows = r2.shape[0]
        self.parts = [parts.at[pl.ds(k * self.rows, self.rows)] for k in range(4)]
        self.r1 = [r1.at[pl.ds((base + k) * self.rows, self.rows)] for k in range(2)]

    def remote(self, src, dst, sem, device):
        return pltpu.make_async_remote_copy(
            src_ref=src, dst_ref=dst, send_sem=self.send.at[sem], recv_sem=self.recv.at[sem],
            device_id=(self.dp, device), device_id_type=MESH,
        )

    def pair(self, k):
        return self.remote(self.parts[2 * k], self.r1[k], k, self.near)

    def cross(self):
        return self.remote(self.parts[1], self.r2, 2, self.across)

    def middle(self):
        self.pair(0).wait_recv()
        self.parts[1][...] = (self.parts[1][...].astype(f32) + self.r1[0][...].astype(f32)).astype(bf16)

    def end(self, stage, out, sem):
        self.pair(1).wait_recv()
        self.cross().wait_recv()
        step = stage.shape[1]
        copies = []
        for k in range(self.rows // step):
            at = pl.ds(k * step, step)
            if k >= 2:
                copies[k - 2].wait()
            stage[k % 2] = (
                self.parts[3][at, :].astype(f32) + self.r1[1][at, :].astype(f32) + self.r2[at, :].astype(f32)
            )
            copies.append(pltpu.make_async_copy(stage.at[k % 2], out.at[at], sem.at[k % 2]))
            copies[-1].start()
        for copy in copies[-2:]:
            copy.wait()

    def finish(self):
        self.pair(0).wait_send()
        self.pair(1).wait_send()
        self.cross().wait_send()


def tail_kernel(
    count, scale, order, gain_ref, bias_ref, fb_ref, small_a, x, h1, dyb, ctx, dproj, wqd, w1, w2,
    grad, small_sum, br_out, e_out,
    xs, h1s, dys, cs, ps, wqds, w1s, w2s, h2s, acts, dabs, gs, sbuf, rbuf, r2, stage, small, t_in, d_in, d_out,
    sem, late_sem, ss, sr, rs, rr, ts, tr, ds, dr, os, free,
):
    ring = Ring(count)
    me, tensor = ring.me, ring.tensor
    rows = r2.shape[1]
    tiles = x.shape[0] // WIDE
    near = tensor + 1 - 2 * (tensor % 2)

    barrier = pltpu.get_barrier_semaphore()
    for step in range(1, 4):
        pl.semaphore_signal(barrier, inc=1, device_id=(me, (tensor + step) % 4), device_id_type=MESH)

    @pl.loop(1, count)
    def _(step):
        pl.semaphore_signal(barrier, inc=1, device_id=((me + step) % count, tensor), device_id_type=MESH)

    def tile_copy(k, src, dst, i):
        at = pl.ds(pl.multiple_of(i * WIDE, WIDE), WIDE)
        return pltpu.make_async_copy(src.at[at], dst.at[at], sem.at[k, i])

    late = [
        pltpu.make_async_copy(src, dst, late_sem.at[k])
        for k, (src, dst) in enumerate(((w1, w1s), (w2, w2s), (h1, h1s), (ctx, cs), (dproj, ps), (wqd, wqds)))
    ]
    late[0].start()
    tile_copy(0, x, xs, 0).start()
    late[1].start()
    tile_copy(1, dyb, dys, 0).start()
    for i in range(1, tiles):
        tile_copy(0, x, xs, i).start()
        tile_copy(1, dyb, dys, i).start()
    for copy in late[2:]:
        copy.start()
    small[...] = small_a[...]
    late[0].wait()
    late[1].wait()

    hidden = w1.shape[1]

    @pl.loop(0, tiles)
    def _(i):
        at = pl.ds(pl.multiple_of(i * WIDE, WIDE), WIDE)
        tile_copy(0, x, xs, i).wait()
        tile_copy(1, dyb, dys, i).wait()
        xhat, _ = normed(xs[at, :].astype(f32))
        h2s[at, :] = (xhat * gain_ref[1:2, :] + bias_ref[1:2, :]).astype(bf16)
        for c in range(2):
            wide = slice(c * (hidden // 2), (c + 1) * (hidden // 2))
            pre = dot_nn(h2s[at, :], w1s[:, wide]) + as_line(fb_ref[...])[:, wide]
            da = dot_nn(dys[at, :], w2s[:, wide])
            act, slope = gelu_both(pre)
            acts[at, wide] = act.astype(bf16)
            dab = (da * slope).astype(bf16)
            dabs[at, wide] = dab
            small[6:7, wide] += jnp.sum(dab.astype(f32), axis=0, keepdims=True)

    for copy in late[2:5]:
        copy.wait()
    base = 0
    for left, right in ((h1s, ps), (cs, dys), (h2s, dabs), (acts, dys)):
        tall = min(WIDE, left.shape[1])
        jobs, per_row = left.shape[1] // tall, right.shape[1] // BLOCK
        blocks = tall // BLOCK * per_row

        @pl.loop(0, jobs)
        def _(j):
            found = dot_tn(left[:, pl.ds(pl.multiple_of(j * tall, tall), tall)], right[...]).astype(bf16)
            start = base + j * blocks
            for r in range(tall // BLOCK):
                for c in range(per_row):
                    gs[start + r * per_row + c] = found[
                        r * BLOCK : (r + 1) * BLOCK, c * BLOCK : (c + 1) * BLOCK
                    ]

        base += jobs * blocks

    pl.semaphore_wait(barrier, 3 + count - 1)
    pl.semaphore_signal(free, inc=1, device_id=(me, near), device_id_type=MESH)
    scatter = Scatter(ring, order, gs, grad, sbuf, rbuf, ss, sr)
    kept = (h2s, dys)
    sums = [RowSum(kept[n], h1s, 2 * n, r2.at[n], rs.at[n], rr.at[n]) for n in range(2)]

    def t_copy(step):
        return pltpu.make_async_remote_copy(
            src_ref=small, dst_ref=t_in.at[tensor], send_sem=ts.at[step], recv_sem=tr.at[step],
            device_id=(me, (tensor + step) % 4), device_id_type=MESH,
        )

    def d_copy(step):
        return pltpu.make_async_remote_copy(
            src_ref=d_out, dst_ref=d_in.at[me], send_sem=ds.at[step], recv_sem=dr.at[step],
            device_id=((me + step) % count, tensor), device_id_type=MESH,
        )

    far = count // 2
    first, second = ((0, 0), (1, 1)), ((1, 0), (0, 1))
    for half, way in first + second:
        if hop_count(half, way, count) >= 1:
            scatter.step(half, way, 1, True)

    def ring_step(hop, which):
        for half, way in which:
            if which is first:
                scatter.step(half, way, hop, False)
            else:

                @pl.when(hop <= far - 1)
                def _():
                    scatter.step(half, way, hop, False)

    wide, thin = 6 * HEAD, 2 * HEAD
    total = lambda v: jnp.sum(v, axis=0, keepdims=True)

    def work(n, r):
        owner = (near * (1 - n % 2) + tensor * (n % 2) + 2 * (1 - n // 2)) % 4
        at = pl.ds(pl.multiple_of(owner * rows + r * TILE, TILE), TILE)
        to = pl.ds(pl.multiple_of(n * rows + r * TILE, TILE), TILE)
        br = dot_nt(acts[at, :], w2s[...])
        dh1 = None
        for p in range(2):
            lo = p * (wide + thin)
            br = br + dot_nt(cs[at, p * thin : (p + 1) * thin], wqds[:, lo + wide : lo + wide + thin])
            part = dot_nt(ps[at, p * wide : (p + 1) * wide], wqds[:, lo : lo + wide])
            dh1 = part if dh1 is None else dh1 + part
        kept[0][to, :] = br.astype(bf16)
        dh2 = dot_nt(dabs[at, :], w1s[...])
        xhat, _ = normed(xs[at, :].astype(f32))
        kept[1][to, :] = (dh1 * gain_ref[0:1, :] + dh2 * gain_ref[1:2, :]).astype(bf16)
        small[0:1, :] += total(dh1 * xhat)
        small[1:2, :] += total(dh2 * xhat)
        small[2:3, :] += total(dh1)
        small[3:4, :] += total(dh2)

    late[5].wait()
    @pl.loop(0, 4)
    def _(n):
        @pl.loop(0, rows // TILE)
        def _(r):
            work(n, r)

        @pl.when(n == 0)
        def _():
            pl.semaphore_wait(free, 1)
            for s in sums:
                s.pair(0).start()

        @pl.when(n == 1)
        def _():
            for s in sums:
                s.middle()
            sums[0].cross().start()
            if far >= 2 and count <= 8:
                ring_step(2, first)

        @pl.when(n == 2)
        def _():
            for s in sums:
                s.pair(1).start()

        @pl.when(n == 3)
        def _():
            if far >= 2 and count <= 8:
                ring_step(2, second)

    for step in range(1, 4):
        t_copy(step).start()
    sums[1].cross().start()

    def both(hop):
        ring_step(hop, first)
        ring_step(hop, second)

    if count <= 8:
        both(3)
    else:
        for_hops(2, far + 1, both, count)
    for step in range(1, 4):
        t_copy(step).wait_recv()
    t_in[tensor] = small[...]
    row = lax.broadcasted_iota(jnp.int32, small.shape, 0)
    summed = t_in[0] + t_in[1] + t_in[2] + t_in[3]
    d_out[...] = jnp.where(row < 4, summed, small[...])

    @pl.loop(1, count)
    def _(step):
        d_copy(step).start()

    if count <= 8:
        both(4)
    sums[0].end(stage, br_out, os)

    @pl.loop(1, count)
    def _(step):
        d_copy(step).wait_recv()

    d_in[me] = d_out[...]
    small_sum[...] = scale * lax.fori_loop(1, count, lambda k, acc: acc + d_in[k], d_in[0])
    sums[1].end(stage, e_out, os)
    for half in range(2):
        scatter.last(half, scale)
    scatter.finish()
    for s in sums:
        s.finish()
    for step in range(1, 4):
        t_copy(step).wait_send()

    @pl.loop(1, count)
    def _(step):
        d_copy(step).wait_send()


def tail_all(count, scale, order, gains, biases, fc1_bias, small, x, h1, dyb, ctx, dproj, wqd, w1, w2):
    rows, width = x.shape[0] // 4, x.shape[1]
    hidden = w1.shape[1]
    blocks = (width * (dproj.shape[1] + hidden) + (ctx.shape[1] + hidden) * width) // (BLOCK * BLOCK)
    per = blocks // count
    far = count // 2
    any_, vmem = pl.BlockSpec(memory_space=pl.ANY), pl.BlockSpec(memory_space=pltpu.VMEM)
    dma = lambda *n: pltpu.SemaphoreType.DMA(n)
    like = lambda v: pltpu.VMEM(v.shape, v.dtype)
    sum_shape = jax.ShapeDtypeStruct((rows, width), f32)
    tall = lambda cols: pltpu.VMEM((x.shape[0], cols), bf16)
    return pl.pallas_call(
        functools.partial(tail_kernel, count, scale),
        out_shape=[
            jax.ShapeDtypeStruct((per, BLOCK, BLOCK), f32), jax.ShapeDtypeStruct(small.shape, f32),
            sum_shape, sum_shape,
        ],
        in_specs=[pl.BlockSpec(memory_space=pltpu.SMEM)] + [vmem] * 4 + [any_] * 8,
        out_specs=[vmem, vmem, any_, any_],
        scratch_shapes=[like(v) for v in (x, h1, dyb, ctx, dproj, wqd, w1, w2)]
        + [
            tall(width), tall(hidden), tall(hidden), pltpu.VMEM((blocks, BLOCK, BLOCK), bf16),
            pltpu.VMEM((4, per, 64, BLOCK), bf16), pltpu.VMEM((4 * far, per, 64, BLOCK), bf16),
            pltpu.VMEM((2, rows, width), bf16), pltpu.VMEM((2, 64, width), f32),
            pltpu.VMEM(small.shape, f32), pltpu.VMEM((4,) + small.shape, f32),
            pltpu.VMEM((count,) + small.shape, f32), pltpu.VMEM(small.shape, f32),
            dma(2, x.shape[0] // WIDE), dma(6),
            dma(4 * far), dma(4 * far), dma(2, 3), dma(2, 3), dma(4), dma(4), dma(count), dma(count),
            dma(2), pltpu.SemaphoreType.REGULAR,
        ],
        compiler_params=pltpu.CompilerParams(
            collective_id=1, has_side_effects=True, vmem_limit_bytes=VMEM_LIMIT
        ),
        cost_estimate=pl.CostEstimate(flops=int(3.5e10), bytes_accessed=int(4e7), transcendentals=int(4e6)),
        name="tail_all",
    )(order, gains, biases, fc1_bias, small, x, h1, dyb, ctx, dproj, wqd, w1, w2)


def finish_kernel(
    steps, lim_ref, bias_ref, small_ref, racc_ref, qacc_ref, facc_ref, grad, tok, dy, br, e, ls, rs, lr, rr,
    gout, out, dx, lout, rout, cout, racc, rupd, qacc, qupd, facc, fupd,
    g_v, tok_v, dy_v, br_v, e_v, ls_v, rs_v, lr_v, rr_v, out_v, dx_v, lo_v, ro_v, co_v, isem, osem,
):
    tensor = lax.axis_index("tensor")
    own_rows, blocks = tok.shape[0], grad.shape[0]
    rows, some = own_rows // steps, blocks // steps
    ins = [(grad, g_v), (ls, ls_v), (rs, rs_v), (lr, lr_v), (rr, rr_v), (tok, tok_v), (dy, dy_v), (br, br_v), (e, e_v)]
    outs = [(g_v, gout), (lo_v, lout), (ro_v, rout), (co_v, cout), (out_v, out), (dx_v, dx)]

    def span(ref, s):
        size = ref.shape[0] // steps
        return ref.at[pl.ds(s * size if ref.shape[0] == blocks else pl.multiple_of(s * size, 16), size)]

    def fetch(k, s):
        return pltpu.make_async_copy(span(ins[k][0], s), span(ins[k][1], s), isem.at[k, s])

    def store(k, s):
        return pltpu.make_async_copy(span(outs[k][0], s), span(outs[k][1], s), osem.at[k, s])

    for s in range(steps):
        for k in range(len(ins)):
            fetch(k, s).start()
    small = small_ref[...]

    def adagrad(grad_vec, accum, new, update):
        accum_next = accum + grad_vec * grad_vec
        new[...] = accum_next
        update[...] = -adagrad_rate * grad_vec * lax.rsqrt(accum_next)

    def stacked(line, count):
        return jnp.concatenate([line[:, k * BLOCK : (k + 1) * BLOCK] for k in range(count)], axis=0)

    adagrad(jnp.concatenate([small[0:5], small[4:5]], axis=0), racc_ref[...], racc, rupd)
    adagrad(stacked(small[5:6], qacc.shape[0]), qacc_ref[...], qacc, qupd)
    adagrad(stacked(small[6:7], facc.shape[0]), facc_ref[...], facc, fupd)
    shift = bias_ref[2:3, :] + bias_ref[3:4, :]

    @pl.loop(0, steps)
    def _(s):
        for k in range(len(ins)):
            fetch(k, s).wait()

        for b in range(some):
            k = s * some + b
            low = g_v[k].astype(bf16)
            lo_v[k] = stat_decay * ls_v[k] + (1.0 - stat_decay) * dot_nt(low, low)
            ro_v[k] = stat_decay * rs_v[k] + (1.0 - stat_decay) * dot_tn(low, low)
            pushed = dot_nn(lr_v[k].astype(bf16), low).astype(bf16)
            co_v[k] = -shampoo_rate * dot_nn(pushed, rr_v[k].astype(bf16))

        at = pl.ds(pl.multiple_of(s * rows, 16), rows)
        x = tok_v[at, :].astype(f32)
        out_v[at, :] = (x + br_v[at, :] + shift).astype(bf16)
        start = tensor * own_rows + s * rows
        place = start % LEN + lax.broadcasted_iota(jnp.int32, (rows, 1), 0)
        kept = jnp.where(place < lim_ref[start // LEN], dy_v[at, :].astype(f32), 0.0)
        xhat, scale = normed(x)
        v = e_v[at, :]
        dx_v[at, :] = kept + scale * (
            v - jnp.mean(v, axis=-1, keepdims=True) - xhat * jnp.mean(v * xhat, axis=-1, keepdims=True)
        )
        for k in range(len(outs)):
            store(k, s).start()

    for s in range(steps):
        for k in range(len(outs)):
            store(k, s).wait()


def finish_all(limits, biases, small, racc, qacc, facc, grad, tok, dy, br, e, ls, rs, lr, rr):
    steps = 4 if grad.shape[0] % 4 == 0 else 1
    any_, vmem = pl.BlockSpec(memory_space=pl.ANY), pl.BlockSpec(memory_space=pltpu.VMEM)
    shape = lambda v: jax.ShapeDtypeStruct(v.shape, v.dtype)
    like = lambda v: pltpu.VMEM(v.shape, v.dtype)
    vectors = [racc, racc, qacc, qacc, facc, facc]
    return pl.pallas_call(
        functools.partial(finish_kernel, steps),
        out_shape=[shape(grad), shape(tok), shape(e)] + [shape(grad)] * 3 + [shape(v) for v in vectors],
        in_specs=[pl.BlockSpec(memory_space=pltpu.SMEM)] + [vmem] * 5 + [any_] * 9,
        out_specs=[any_] * 6 + [vmem] * 6,
        scratch_shapes=[like(v) for v in (grad, tok, dy, br, e, ls, rs, lr, rr, tok, e, ls, ls, ls)]
        + [pltpu.SemaphoreType.DMA((9, steps)), pltpu.SemaphoreType.DMA((6, steps))],
        compiler_params=pltpu.CompilerParams(vmem_limit_bytes=VMEM_LIMIT),
        cost_estimate=pl.CostEstimate(flops=int(4e8), bytes_accessed=int(2e7), transcendentals=0),
        name="finish_all",
    )(limits, biases, small, racc, qacc, facc, grad, tok, dy, br, e, ls, rs, lr, rr)


def shards(
    tokens, out_grad, seq_lengths, norm_gains, row_biases, qkv_weight, qkv_bias, dense_weight, fc1_weight,
    fc1_bias, fc2_weight, block_slot, left_stat, right_stat, left_root, right_root, row_accum,
    qkv_bias_accum, fc1_bias_accum,
):
    tensor_count = lax.axis_size("tensor")
    dp_count = lax.axis_size("dp")
    grad_scale = 1.0 / math.sqrt(tokens.shape[0] * tensor_count * dp_count)
    xf, h1, dyb, ctx, dproj, wqdf, w1f, w2f, sum_a, order = mixed_all(
        dp_count, seq_lengths, norm_gains, row_biases, as_rows(qkv_bias), jnp.asarray(rotary_rows()),
        as_rows(block_slot), tokens, out_grad, qkv_weight, dense_weight, fc1_weight, fc2_weight,
    )
    own_grad, small, branch, e_sum = tail_all(
        dp_count, grad_scale, order, norm_gains, row_biases, as_rows(fc1_bias), sum_a,
        xf, h1, dyb, ctx, dproj, wqdf, w1f, w2f,
    )
    outs = finish_all(
        seq_lengths, row_biases, small, row_accum, as_rows(qkv_bias_accum), as_rows(fc1_bias_accum),
        own_grad, tokens, out_grad, branch, e_sum, left_stat, right_stat, left_root, right_root,
    )
    block_grad, layer_out, input_grad, left_new, right_new, change = outs[:6]
    return (
        layer_out, input_grad, block_grad, left_new, right_new, change,
        *outs[6:8], *(v.reshape(-1) for v in outs[8:]),
    )


def solution(mesh):
    both = ("dp", "tensor")
    return jax.shard_map(
        shards,
        mesh=mesh,
        in_specs=(
            P(both, None), P(both, None), P("dp"), P(), P(), P("dp", "tensor"), P("tensor"),
            P("tensor", "dp"), P("dp", "tensor"), P("tensor"), P("tensor", "dp"), P(),
            P(both, None, None), P(both, None, None), P(both, None, None), P(both, None, None),
            P(), P("tensor"), P("tensor"),
        ),
        out_specs=(
            P(both, None), P(both, None), P(both, None, None), P(both, None, None),
            P(both, None, None), P(both, None, None), P(), P(), P("tensor"), P("tensor"),
            P("tensor"), P("tensor"),
        ),
        check_vma=False,
    )
```

```python
import functools
import math

import jax
import jax.numpy as jnp
import numpy as np
from jax import lax
from jax.experimental import pallas as pl
from jax.experimental.pallas import tpu as pltpu
from jax.sharding import PartitionSpec as P

HEAD = 64
ROT = 16
LEN = 1024
BLOCK = 128
TILE = 256
WIDE = 512
MESH = pl.DeviceIdType.MESH
VMEM_LIMIT = 60 * 1024 * 1024

masked_score = -1e30
shampoo_rate = 0.03
adagrad_rate = 0.1
stat_decay = 0.5
f32 = jnp.float32
bf16 = jnp.bfloat16


def rotary_rows():
    half = ROT // 2
    inverse = np.power(np.float32(10000.0), -(np.arange(half, dtype=np.float32) * np.float32(2.0 / ROT)))
    angles = inverse.astype(np.float32)[:, None] * np.arange(LEN, dtype=np.float32)[None, :]
    return np.concatenate([np.cos(angles), np.sin(angles)], axis=0).astype(np.float32)


def ring_place(me, count):
    low, high = me % 2, me // 2
    return low * (count - 1 - high) + (1 - low) * high


def ring_device(place, count):
    upper = place // (count // 2)
    return (1 - upper) * (2 * place) + upper * (2 * (count - 1 - place) + 1)


def hop_count(half, way, count):
    far = count // 2
    return far if half == way else far - 1


def for_hops(first, last, body, count):
    if count <= 8:
        for hop in range(first, last):
            body(hop)
    elif last > first:

        @pl.loop(first, last)
        def _(hop):
            body(hop)


def as_rows(vec):
    return vec.reshape(-1, BLOCK)


def as_line(rows):
    return jnp.concatenate([rows[k : k + 1, :] for k in range(rows.shape[0])], axis=1)


class Ring:
    def __init__(self, count):
        self.count = count
        self.me = lax.axis_index("dp")
        self.tensor = lax.axis_index("tensor")
        self.place = ring_place(self.me, count)
        self.peer = [
            (ring_device((self.place + step) % count, count), self.tensor) for step in (1, count - 1)
        ]

    def at(self, offset):
        return ring_device((self.place + offset + 2 * self.count) % self.count, self.count)


class Gather:
    def __init__(self, ring, locals_, fulls, send, recv):
        self.ring, self.locals, self.fulls, self.send, self.recv = ring, locals_, fulls, send, recv
        self.far = ring.count // 2

    def part(self, ref, w, half, owner=None):
        rows, cols = self.locals[w].shape
        base = 0 if owner is None else owner * rows
        if rows % 32 == 0:
            return ref.at[pl.ds(pl.multiple_of(base + half * (rows // 2), 16), rows // 2)]
        return ref.at[pl.ds(base, rows), pl.ds(half * (cols // 2), cols // 2)]

    def sem(self, w, half, way, hop):
        return ((w * 2 + half) * 2 + way) * self.far + hop - 1

    def copy(self, w, half, way, hop, source):
        owner = self.ring.at((1 - hop) if way == 0 else (hop - 1))
        src = self.part(self.locals[w], w, half) if source else self.part(self.fulls[w], w, half, owner)
        return pltpu.make_async_remote_copy(
            src_ref=src,
            dst_ref=self.part(self.fulls[w], w, half, owner),
            send_sem=self.send.at[self.sem(w, half, way, hop)],
            recv_sem=self.recv.at[self.sem(w, half, way, hop)],
            device_id=self.ring.peer[way],
            device_id_type=MESH,
        )

    def arrival(self, w, half, way, hop):
        owner = self.ring.at(-hop if way == 0 else hop)
        dst = self.part(self.fulls[w], w, half, owner)
        return pltpu.make_async_remote_copy(
            src_ref=dst,
            dst_ref=dst,
            send_sem=self.send.at[self.sem(w, half, way, hop)],
            recv_sem=self.recv.at[self.sem(w, half, way, hop)],
            device_id=self.ring.peer[way],
            device_id_type=MESH,
        )

    def begin(self, w):
        for half in range(2):
            for way in range(2):
                if hop_count(half, way, self.ring.count) >= 1:
                    self.copy(w, half, way, 1, True).start()

    def forward(self, w, hop, last):
        for half in range(2):
            for way in range(2):
                hops = self.far if half == way else self.far - 1
                if last and hops != self.far:
                    continue
                self.arrival(w, half, way, hop).wait_recv()
                if not last:
                    more = self.far if half == way else self.far - 1
                    if more == self.far:
                        self.copy(w, half, way, hop + 1, False).start()
                    else:

                        @pl.when(hop + 1 <= more)
                        def _():
                            self.copy(w, half, way, hop + 1, False).start()

    def finish(self, w):
        for half in range(2):
            for way in range(2):
                hops = hop_count(half, way, self.ring.count)
                if hops >= 1:
                    self.copy(w, half, way, 1, True).wait_send()
                for_hops(
                    2, hops + 1, lambda hop: self.copy(w, half, way, hop, False).wait_send(), self.ring.count
                )


class Rows:
    def __init__(self, local, full, send, recv, own):
        self.tensor = lax.axis_index("tensor")
        self.dp = lax.axis_index("dp")
        self.near = self.tensor + 1 - 2 * (self.tensor % 2)
        self.across = (self.tensor + 2) % 4
        self.local, self.full, self.send, self.recv, self.own = local, full, send, recv, own
        self.rows = local.shape[0]

    def slot(self, owner, piece=None):
        if piece is None:
            return self.full.at[pl.ds(pl.multiple_of(owner * self.rows, 16), self.rows)]
        half = self.rows // 2
        return self.full.at[pl.ds(pl.multiple_of(owner * self.rows + piece * half, 16), half)]

    def remote(self, src, dst, sem, device):
        return pltpu.make_async_remote_copy(
            src_ref=src,
            dst_ref=dst,
            send_sem=self.send.at[sem],
            recv_sem=self.recv.at[sem],
            device_id=(self.dp, device),
            device_id_type=MESH,
        )

    def keep(self):
        return pltpu.make_async_copy(self.local, self.slot(self.tensor), self.own)

    def pair(self):
        return self.remote(self.local, self.slot(self.tensor), 0, self.near)

    def cross(self, piece):
        half = self.rows // 2
        return self.remote(
            self.local.at[pl.ds(piece * half, half)], self.slot(self.tensor, piece), 1 + piece, self.across
        )

    def onward(self, piece):
        here = self.slot(self.across, piece)
        return self.remote(here, here, 3 + piece, self.near)

    def begin_near(self):
        self.keep().start()
        self.pair().start()

    def begin_cross(self):
        for piece in range(2):
            self.cross(piece).start()

    def pass_piece(self, piece):
        self.cross(piece).wait_recv()
        self.onward(piece).start()

    def pass_on(self):
        for piece in range(2):
            self.pass_piece(piece)

    def finish(self):
        self.keep().wait()
        self.pair().wait()
        for piece in range(2):
            self.cross(piece).wait_send()
            self.onward(piece).wait()


def greet(devices):
    barrier = pltpu.get_barrier_semaphore()
    for device in devices:
        pl.semaphore_signal(barrier, inc=1, device_id=device, device_id_type=MESH)
    pl.semaphore_wait(barrier, len(devices))


def dot_nn(a, b):
    return lax.dot_general(a, b, (((1,), (0,)), ((), ())), preferred_element_type=f32)


def dot_nt(a, b):
    return lax.dot_general(a, b, (((1,), (1,)), ((), ())), preferred_element_type=f32)


def dot_tn(a, b):
    return lax.dot_general(a, b, (((0,), (0,)), ((), ())), preferred_element_type=f32)


def normed(x):
    average = jnp.mean(x, axis=-1, keepdims=True)
    centered = x - average
    variance = jnp.mean(centered * centered, axis=-1, keepdims=True)
    scale = lax.rsqrt(variance + 1e-05)
    return centered * scale, scale


def mixed_kernel(
    count, lim_ref, gain_ref, bias_ref, qb_ref, rot_ref, slot_ref, wd, w2, x, dy, wq, w1,
    x_out, h1_out, dyb_out, ctx_out, dproj_out, wqd_out, w1f, w2f, sum_ref, order_ref,
    xf, dyf, wf, wl, w2l, h1s, ctxs, dps, qt, kt, vt, dct, ctt, dqt, kr, vr, dkvs,
    rs, rr, ro, gs, gr, go, os,
):
    ring = Ring(count)
    pair_cols = 6 * HEAD
    half_cols = pair_cols + 2 * HEAD
    parts = [
        pltpu.make_async_copy(
            wq.at[:, pl.ds(p * pair_cols, pair_cols)], wl.at[:, pl.ds(p * half_cols, pair_cols)], os.at[p]
        )
        for p in range(2)
    ]
    for copy in parts:
        copy.start()
    turned_dense = wd[...].T
    for p in range(2):
        wl[:, p * half_cols + pair_cols : (p + 1) * half_cols] = turned_dense[:, p * 2 * HEAD : (p + 1) * 2 * HEAD]
    views = [(wl.at[:, pl.ds(p * half_cols, half_cols)], wf.at[:, pl.ds(p * half_cols, half_cols)]) for p in (0, 1)]
    views += [(w1, w1f), (w2l, w2f)]
    gather = Gather(ring, [v[0] for v in views], [v[1] for v in views], gs, gr)
    rx = Rows(x, xf, rs.at[0], rr.at[0], ro.at[0])
    ry = Rows(dy, dyf, rs.at[1], rr.at[1], ro.at[1])
    greet([ring.peer[0], ring.peer[1], (ring.me, rx.near), (ring.me, rx.across)])
    far = count // 2
    own = []
    for k, (local, full) in enumerate(((w1, w1f), (w2l, w2f))):
        rows = local.shape[0]
        own.append(
            pltpu.make_async_copy(local, full.at[pl.ds(pl.multiple_of(ring.me * rows, 16), rows)], go.at[k])
        )
    rx.begin_near()
    for copy in parts:
        copy.wait()
    gather.begin(0)
    rx.begin_cross()
    ry.begin_near()
    ry.begin_cross()
    wf[pl.ds(pl.multiple_of(ring.me * wl.shape[0], 16), wl.shape[0]), :] = wl[...]
    own[0].start()
    sum_ref[...] = jnp.zeros_like(sum_ref)
    tensor = ring.tensor
    tiles = LEN // TILE

    def whole_ring(w):
        for_hops(1, far, lambda hop: gather.forward(w, hop, False), count)
        gather.forward(w, far, True)

    def hop_at(w, hop):
        if count == 8:
            gather.forward(w, hop, hop == far)
        elif hop == 4:
            whole_ring(w)

    def rows_of(seq, i):
        return pl.ds(pl.multiple_of(seq * LEN + i * TILE, TILE), TILE)

    def norm_tile(seq, i):
        rows = rows_of(seq, i)
        xhat, _ = normed(xf[rows, :].astype(f32))
        h1s[rows, :] = (xhat * gain_ref[0:1, :] + bias_ref[0:1, :]).astype(bf16)

    def mask_tile(seq, i):
        rows = rows_of(seq, i)
        place = i * TILE + lax.broadcasted_iota(jnp.int32, (TILE, 1), 0)
        kept = jnp.where(place < lim_ref[seq], dyf[rows, :].astype(f32), 0.0)
        sum_ref[4:5, :] += jnp.sum(kept, axis=0, keepdims=True)
        dyf[rows, :] = kept.astype(bf16)

    def turned(first, second, cosine, sine):
        return first * cosine - second * sine, second * cosine + first * sine

    def prepare_tile(seq, pair, i):
        rows = rows_of(seq, i)
        cols = pl.ds(pl.multiple_of(i * TILE, TILE), TILE)
        proj = dot_nn(h1s[rows, :], wf[:, pl.ds(pl.multiple_of(pair * half_cols, BLOCK), pair_cols)])
        proj = proj + as_line(qb_ref[pl.ds(pair * (pair_cols // BLOCK), pair_cols // BLOCK), :])
        proj = proj.T
        cosine, sine = rot_ref[0:8, cols], rot_ref[8:16, cols]
        key = i * TILE + lax.broadcasted_iota(jnp.int32, (16, TILE), 1)
        row = lax.broadcasted_iota(jnp.int32, (16, TILE), 0)
        ones = jnp.where(row == 0, 1.0, 0.0).astype(bf16)
        hidden = jnp.where((row == 0) & (key >= lim_ref[seq]), masked_score, 0.0).astype(bf16)
        blank = jnp.zeros((48, TILE), bf16)
        none = jnp.zeros((HEAD, TILE), bf16)
        for hh in range(2):
            h = 2 * pair + hh
            base = 3 * HEAD * hh
            q0, q1 = turned(proj[base : base + 8], proj[base + 8 : base + 16], cosine, sine)
            q = jnp.concatenate([q0, q1, proj[base + 16 : base + HEAD]], axis=0).astype(bf16)
            q = (q.astype(f32) * 0.125).astype(bf16)
            qt[h, :, cols] = jnp.concatenate([q, ones, blank], axis=0)
            base += HEAD
            k0, k1 = turned(proj[base : base + 8], proj[base + 8 : base + 16], cosine, sine)
            k = jnp.concatenate([k0, k1, proj[base + 16 : base + HEAD]], axis=0).astype(bf16)
            kt[h, :, cols] = k
            kr[h, cols, :] = jnp.concatenate([k, hidden, blank], axis=0).T
            base += HEAD
            v = proj[base : base + HEAD].astype(bf16)
            vt[h, :, cols] = jnp.concatenate([v, ones], axis=0)
            vr[h, cols, :] = jnp.concatenate([none, v], axis=0).T

    def context_tile(seq, pair, i):
        cols = pl.ds(pl.multiple_of(i * TILE, TILE), TILE)
        begin = pair * half_cols + pair_cols
        dctx = dot_nn(dyf[rows_of(seq, i), :], wf[:, begin : begin + 2 * HEAD]).T.astype(bf16)
        for hh in range(2):
            dct[2 * pair + hh, :, cols] = dctx[HEAD * hh : HEAD * (hh + 1)]

    def back_tile(seq, i):
        mask_tile(seq, i)
        context_tile(seq, 0, i)
        context_tile(seq, 1, i)

    def attend(pair, i, fresh):
        here = slice(i * TILE, (i + 1) * TILE)
        chunks = [slice(c * TILE, (c + 1) * TILE) for c in range(i + 1)]
        heads = range(2)
        of = [2 * pair, 2 * pair + 1]
        key = lax.broadcasted_iota(jnp.int32, (TILE, TILE), 0)
        query = lax.broadcasted_iota(jnp.int32, (TILE, TILE), 1)
        q = [qt[of[hh], :, here] for hh in heads]
        scores = [[dot_nn(kr[of[hh], c, :], q[hh]) for c in chunks] for hh in heads]
        probs, grads, deltas, both = [], [], [], []
        none = jnp.zeros((HEAD, TILE), bf16)
        for hh in heads:
            scores[hh][i] = jnp.where(key <= query, scores[hh][i], masked_score)
            top = jnp.max(scores[hh][0], axis=0, keepdims=True)
            for s in scores[hh][1:]:
                top = jnp.maximum(top, jnp.max(s, axis=0, keepdims=True))
            probs.append([jnp.exp(s - top).astype(bf16) for s in scores[hh]])
        for hh in heads:
            total = dot_nn(vt[of[hh], :, chunks[0]], probs[hh][0])
            for c, p in zip(chunks[1:], probs[hh][1:]):
                total = total + dot_nn(vt[of[hh], :, c], p)
            inverse = 1.0 / total[HEAD : HEAD + 1]
            context = total[:HEAD] * inverse
            ctt[of[hh], :, here] = context
            grad = (dct[of[hh], :, here].astype(f32) * inverse).astype(bf16)
            deltas.append(jnp.sum(grad.astype(f32) * context, axis=0, keepdims=True))
            grad = jnp.concatenate([none, grad], axis=0)
            grads.append(grad)
            both.append(jnp.concatenate([jnp.concatenate([q[hh][:HEAD], none], axis=0), grad], axis=1))
        dq = [None, None]
        for n, c in enumerate(chunks):
            for hh in heads:
                p = probs[hh][n]
                dp = dot_nn(vr[of[hh], c, :], grads[hh])
                ds = (p.astype(f32) * (dp - deltas[hh])).astype(bf16)
                part = dot_nn(kt[of[hh], :, c], ds)
                dq[hh] = part if dq[hh] is None else dq[hh] + part
                dkv = dot_nt(jnp.concatenate([ds, p], axis=1), both[hh])
                if n in fresh:
                    dkvs[of[hh], c, :] = dkv
                else:
                    dkvs[of[hh], c, :] += dkv
        for hh in heads:
            dqt[of[hh], :, here] = dq[hh] * 0.125

    def collect_tile(seq, i):
        rows = rows_of(seq, i)
        cols = pl.ds(pl.multiple_of(i * TILE, TILE), TILE)
        cosine, sine = rot_ref[0:8, cols], rot_ref[8:16, cols]
        for pair in range(2):
            pieces = []
            for h in (2 * pair, 2 * pair + 1):
                dkv = dkvs[h, cols, :].T
                for grad in (dqt[h, :, cols], dkv[:HEAD]):
                    pieces += [*turned(grad[0:8], grad[8:16], cosine, -sine), grad[16:HEAD]]
                pieces.append(dkv[HEAD:])
            low = jnp.concatenate(pieces, axis=0).T.astype(bf16)
            wide = slice(pair * pair_cols, (pair + 1) * pair_cols)
            dps[rows, wide] = low
            sum_ref[5:6, wide] += jnp.sum(low.astype(f32), axis=0, keepdims=True)
            ctx = jnp.concatenate([ctt[2 * pair, :, cols], ctt[2 * pair + 1, :, cols]], axis=0).T
            ctxs[rows, pair * 2 * HEAD : (pair + 1) * 2 * HEAD] = ctx.astype(bf16)

    def save(turn, k, seq):
        src, dst = ((xf, x_out), (h1s, h1_out), (dyf, dyb_out), (ctxs, ctx_out), (dps, dproj_out))[k]
        rows = pl.ds(pl.multiple_of(seq * LEN, LEN), LEN)
        return pltpu.make_async_copy(src.at[rows], dst.at[rows], os.at[turn * 5 + k])

    mine = order_ref.shape[1]
    per = mine // count
    place = lax.broadcasted_iota(jnp.int32, (mine, 1), 0).astype(f32)
    owner = jnp.floor((place + 0.5) / per)
    wanted = (owner * 4.0 + lax.convert_element_type(tensor, f32)) * per + (place - owner * per)
    found = jnp.zeros(order_ref.shape, f32)
    for r in range(slot_ref.shape[0]):
        hit = jnp.where(slot_ref[r : r + 1, :].astype(f32) == wanted, 1.0, 0.0).astype(bf16)
        block = r * BLOCK + lax.broadcasted_iota(jnp.int32, (8, BLOCK), 1) - tensor * mine
        found = found + dot_nt(jnp.clip(block, 0, mine - 1).astype(f32).astype(bf16), hit)
    order_ref[...] = (found + 0.5).astype(jnp.int32)

    seq = tensor // 2
    rx.keep().wait()
    rx.pair().wait_recv()

    @pl.loop(0, tiles)
    def _(i):
        norm_tile(seq, i)

        @pl.when(i == 0)
        def _():
            hop_at(0, 1)
            gather.begin(1)

        @pl.when(i == 1)
        def _():
            hop_at(0, 2)
            hop_at(1, 1)

        @pl.when(i == 2)
        def _():
            hop_at(0, 3)
            hop_at(1, 2)
            gather.begin(2)

    save(0, 0, seq).start()
    save(0, 1, seq).start()
    w2l[...] = w2[...].T
    hop_at(0, 4)
    ry.keep().wait()
    ry.pair().wait_recv()

    @pl.loop(0, tiles // 2)
    def _(i):
        for sub in range(2):
            prepare_tile(seq, 0, 2 * i + sub)


    @pl.loop(0, tiles)
    def _(i):
        mask_tile(seq, i)
        context_tile(seq, 0, i)

    save(0, 2, seq).start()

    @pl.loop(0, 2)
    def _(pair):
        @pl.when(pair == 1)
        def _():
            hop_at(1, 4)
            hop_at(2, 1)

            @pl.loop(0, tiles // 2)
            def _(i):
                for sub in range(2):
                    prepare_tile(seq, 1, 2 * i + sub)
                    context_tile(seq, 1, 2 * i + sub)

        attend(pair, 3, (0, 1, 2, 3))

        @pl.when(pair == 0)
        def _():
            hop_at(1, 3)
            gather.begin(3)
            own[1].start()

        attend(pair, 2, ())

        @pl.when(pair == 0)
        def _():
            rx.pass_on()

        @pl.when(pair == 1)
        def _():
            hop_at(3, 1)

        attend(pair, 1, ())
        attend(pair, 0, ())

    @pl.loop(0, tiles)
    def _(i):
        collect_tile(seq, i)

    save(0, 3, seq).start()
    save(0, 4, seq).start()
    keep = pltpu.make_async_copy(wf, wqd_out, os.at[10])
    keep.start()

    seq = 1 - seq
    for piece in range(2):
        rx.onward(piece).wait_recv()

    @pl.loop(0, tiles)
    def _(i):
        norm_tile(seq, i)

    save(1, 0, seq).start()
    save(1, 1, seq).start()
    ry.pass_piece(0)

    for pair in range(2):

        @pl.loop(0, tiles // 2)
        def _(i):
            for sub in range(2):
                prepare_tile(seq, pair, 2 * i + sub)

        if pair == 0:
            hop_at(2, 2)

    ry.onward(0).wait()
    back_tile(seq, 0)
    back_tile(seq, 2)

    @pl.loop(0, 2)
    def _(pair):
        attend(pair, 2, (0, 1, 2))

        @pl.when(pair == 0)
        def _():
            hop_at(3, 2)

        attend(pair, 0, ())

    ry.pass_piece(1)
    ry.onward(1).wait()
    back_tile(seq, 1)
    back_tile(seq, 3)
    save(1, 2, seq).start()
    hop_at(2, 3)

    @pl.loop(0, 2)
    def _(pair):
        attend(pair, 3, (3,))

        @pl.when(pair == 1)
        def _():
            hop_at(3, 3)

        attend(pair, 1, ())

    @pl.loop(0, tiles)
    def _(i):
        collect_tile(seq, i)

    save(1, 3, seq).start()
    save(1, 4, seq).start()
    hop_at(2, 4)
    hop_at(3, 4)
    for w in range(4):
        gather.finish(w)
    own[0].wait()
    own[1].wait()
    rx.pair().wait_send()
    ry.pair().wait_send()
    for piece in range(2):
        rx.cross(piece).wait_send()
        rx.onward(piece).wait_send()
        ry.cross(piece).wait_send()
    for turn in range(2):
        for k in range(5):
            save(turn, k, turn + (1 - 2 * turn) * (tensor // 2)).wait()
    keep.wait()


def mixed_all(count, limits, gains, biases, qkv_bias, rot, slots, x, dy, wq, wd, w1, w2):
    far = count // 2
    rows, width = 4 * x.shape[0], x.shape[1]
    ctx_cols, proj_cols = wd.shape[0], wq.shape[1]
    shard = wq.shape[0]
    out = lambda r, c: jax.ShapeDtypeStruct((r, c), bf16)
    any_, vmem = pl.BlockSpec(memory_space=pl.ANY), pl.BlockSpec(memory_space=pltpu.VMEM)
    dma = lambda *n: pltpu.SemaphoreType.DMA(n)
    buf = lambda dtype, *shape: pltpu.VMEM(shape, dtype)
    heads, both = 4, ctx_cols + proj_cols
    return pl.pallas_call(
        functools.partial(mixed_kernel, count),
        out_shape=[
            out(rows, width), out(rows, width), out(rows, width), out(rows, ctx_cols), out(rows, proj_cols),
            out(width, both), out(width, w1.shape[1]), out(width, w2.shape[0]),
            jax.ShapeDtypeStruct((8, width), f32), jax.ShapeDtypeStruct((8, slots.size // 4), jnp.int32),
        ],
        in_specs=[pl.BlockSpec(memory_space=pltpu.SMEM)] + [vmem] * 7 + [any_] * 4,
        out_specs=[any_] * 8 + [vmem] * 2,
        scratch_shapes=[
            buf(bf16, rows, width), buf(bf16, rows, width), buf(bf16, width, both),
            buf(bf16, shard, both), buf(bf16, shard, w2.shape[0]),
            buf(bf16, rows, width), buf(bf16, rows, ctx_cols), buf(bf16, rows, proj_cols),
            buf(bf16, heads, 2 * HEAD, LEN), buf(bf16, heads, HEAD, LEN), buf(bf16, heads, HEAD + 16, LEN),
            buf(bf16, heads, HEAD, LEN), buf(f32, heads, HEAD, LEN), buf(f32, heads, HEAD, LEN),
            buf(bf16, heads, LEN, 2 * HEAD), buf(bf16, heads, LEN, 2 * HEAD), buf(f32, heads, LEN, 2 * HEAD),
            dma(2, 5), dma(2, 5), dma(2), dma(16 * far), dma(16 * far), dma(2), dma(11),
        ],
        compiler_params=pltpu.CompilerParams(
            collective_id=0, has_side_effects=True, vmem_limit_bytes=VMEM_LIMIT
        ),
        cost_estimate=pl.CostEstimate(flops=int(2e10), bytes_accessed=int(4e7), transcendentals=int(1e7)),
        name="mixed_all",
    )(limits, gains, biases, qkv_bias, rot, slots, wd, w2, x, dy, wq, w1)


def gelu_both(x):
    phi = 0.5 + 0.5 * lax.erf(x * (1.0 / math.sqrt(2.0)))
    bell = jnp.exp(-0.5 * x * x) * (1.0 / math.sqrt(2.0 * math.pi))
    return x * phi, phi + x * bell


class Scatter:
    def __init__(self, ring, order, blocks, out, sbuf, rbuf, send, recv):
        self.ring, self.order, self.blocks, self.out = ring, order, blocks, out
        self.sbuf, self.rbuf, self.send, self.recv = sbuf, rbuf, send, recv
        self.per = out.shape[0]
        self.together = 6 if self.per % 6 == 0 else 1
        self.far = ring.count // 2

    def index(self, half, way, hop):
        return (half * 2 + way) * self.far + hop - 1

    def copy(self, half, way, hop, first):
        i = self.index(half, way, hop)
        return pltpu.make_async_remote_copy(
            src_ref=self.sbuf.at[half * 2 + way] if first else self.rbuf.at[i - 1],
            dst_ref=self.rbuf.at[i],
            send_sem=self.send.at[i],
            recv_sem=self.recv.at[i],
            device_id=self.ring.peer[way],
            device_id_type=MESH,
        )

    def own(self, dest, half, k):
        return self.blocks[self.order[0, dest * self.per + k], half * 64 : half * 64 + 64, :]

    def step(self, half, way, hop, first):
        hops = hop_count(half, way, self.ring.count)
        dest = self.ring.at((hops + 1 - hop) if way == 0 else (hop - hops - 1))
        i = self.index(half, way, hop)
        if not first:
            self.copy(half, way, hop - 1, True).wait_recv()

        def one(k, carry):
            value = self.own(dest, half, k)
            if first:
                self.sbuf[half * 2 + way, k] = value
            else:
                self.rbuf[i - 1, k] = (value.astype(f32) + self.rbuf[i - 1, k].astype(f32)).astype(bf16)
            return carry

        lax.fori_loop(0, self.per, one, 0, unroll=self.together)
        self.copy(half, way, hop, first).start()

    def last(self, half, scale):
        came = []
        for way in range(2):
            hops = hop_count(half, way, self.ring.count)
            if hops >= 1:
                self.copy(half, way, hops, True).wait_recv()
                came.append(self.index(half, way, hops))
        me = self.ring.me

        def one(k, carry):
            value = self.own(me, half, k).astype(f32)
            for i in came:
                value = value + self.rbuf[i, k].astype(f32)
            self.out[k, half * 64 : half * 64 + 64, :] = value * scale
            return carry

        lax.fori_loop(0, self.per, one, 0, unroll=self.together)

    def finish(self):
        for half in range(2):
            for way in range(2):
                hops = hop_count(half, way, self.ring.count)
                for_hops(
                    1, hops + 1, lambda hop: self.copy(half, way, hop, True).wait_send(), self.ring.count
                )


class RowSum:
    def __init__(self, parts, r1, base, r2, send, recv):
        self.tensor = lax.axis_index("tensor")
        self.dp = lax.axis_index("dp")
        self.near = self.tensor + 1 - 2 * (self.tensor % 2)
        self.across = (self.tensor + 2) % 4
        self.r2, self.send, self.recv = r2, send, recv
        self.rows = r2.shape[0]
        self.parts = [parts.at[pl.ds(k * self.rows, self.rows)] for k in range(4)]
        self.r1 = [r1.at[pl.ds((base + k) * self.rows, self.rows)] for k in range(2)]

    def remote(self, src, dst, sem, device):
        return pltpu.make_async_remote_copy(
            src_ref=src, dst_ref=dst, send_sem=self.send.at[sem], recv_sem=self.recv.at[sem],
            device_id=(self.dp, device), device_id_type=MESH,
        )

    def pair(self, k):
        return self.remote(self.parts[2 * k], self.r1[k], k, self.near)

    def cross(self):
        return self.remote(self.parts[1], self.r2, 2, self.across)

    def middle(self):
        self.pair(0).wait_recv()
        self.parts[1][...] = (self.parts[1][...].astype(f32) + self.r1[0][...].astype(f32)).astype(bf16)

    def end(self, stage, out, sem):
        self.pair(1).wait_recv()
        self.cross().wait_recv()
        step = stage.shape[1]
        copies = []
        for k in range(self.rows // step):
            at = pl.ds(k * step, step)
            if k >= 2:
                copies[k - 2].wait()
            stage[k % 2] = (
                self.parts[3][at, :].astype(f32) + self.r1[1][at, :].astype(f32) + self.r2[at, :].astype(f32)
            )
            copies.append(pltpu.make_async_copy(stage.at[k % 2], out.at[at], sem.at[k % 2]))
            copies[-1].start()
        for copy in copies[-2:]:
            copy.wait()

    def finish(self):
        self.pair(0).wait_send()
        self.pair(1).wait_send()
        self.cross().wait_send()


def tail_kernel(
    count, scale, order, gain_ref, bias_ref, fb_ref, small_a, x, h1, dyb, ctx, dproj, wqd, w1, w2,
    grad, small_sum, br_out, e_out,
    xs, h1s, dys, cs, ps, wqds, w1s, w2s, h2s, acts, dabs, gs, sbuf, rbuf, r2, stage, small, t_in, d_in, d_out,
    sem, late_sem, ss, sr, rs, rr, ts, tr, ds, dr, os, free,
):
    ring = Ring(count)
    me, tensor = ring.me, ring.tensor
    rows = r2.shape[1]
    tiles = x.shape[0] // WIDE
    near = tensor + 1 - 2 * (tensor % 2)

    barrier = pltpu.get_barrier_semaphore()
    for step in range(1, 4):
        pl.semaphore_signal(barrier, inc=1, device_id=(me, (tensor + step) % 4), device_id_type=MESH)

    @pl.loop(1, count)
    def _(step):
        pl.semaphore_signal(barrier, inc=1, device_id=((me + step) % count, tensor), device_id_type=MESH)

    def tile_copy(k, src, dst, i):
        at = pl.ds(pl.multiple_of(i * WIDE, WIDE), WIDE)
        return pltpu.make_async_copy(src.at[at], dst.at[at], sem.at[k, i])

    late = [
        pltpu.make_async_copy(src, dst, late_sem.at[k])
        for k, (src, dst) in enumerate(((w1, w1s), (w2, w2s), (h1, h1s), (ctx, cs), (dproj, ps), (wqd, wqds)))
    ]
    late[0].start()
    tile_copy(0, x, xs, 0).start()
    late[1].start()
    tile_copy(1, dyb, dys, 0).start()
    for i in range(1, tiles):
        tile_copy(0, x, xs, i).start()
        tile_copy(1, dyb, dys, i).start()
    for copy in late[2:]:
        copy.start()
    small[...] = small_a[...]
    late[0].wait()
    late[1].wait()

    hidden = w1.shape[1]

    @pl.loop(0, tiles)
    def _(i):
        at = pl.ds(pl.multiple_of(i * WIDE, WIDE), WIDE)
        tile_copy(0, x, xs, i).wait()
        tile_copy(1, dyb, dys, i).wait()
        xhat, _ = normed(xs[at, :].astype(f32))
        h2s[at, :] = (xhat * gain_ref[1:2, :] + bias_ref[1:2, :]).astype(bf16)
        for c in range(2):
            wide = slice(c * (hidden // 2), (c + 1) * (hidden // 2))
            pre = dot_nn(h2s[at, :], w1s[:, wide]) + as_line(fb_ref[...])[:, wide]
            da = dot_nn(dys[at, :], w2s[:, wide])
            act, slope = gelu_both(pre)
            acts[at, wide] = act.astype(bf16)
            dab = (da * slope).astype(bf16)
            dabs[at, wide] = dab
            small[6:7, wide] += jnp.sum(dab.astype(f32), axis=0, keepdims=True)

    for copy in late[2:5]:
        copy.wait()
    base = 0
    for left, right in ((h1s, ps), (cs, dys), (h2s, dabs), (acts, dys)):
        tall = min(WIDE, left.shape[1])
        jobs, per_row = left.shape[1] // tall, right.shape[1] // BLOCK
        blocks = tall // BLOCK * per_row

        @pl.loop(0, jobs)
        def _(j):
            found = dot_tn(left[:, pl.ds(pl.multiple_of(j * tall, tall), tall)], right[...]).astype(bf16)
            start = base + j * blocks
            for r in range(tall // BLOCK):
                for c in range(per_row):
                    gs[start + r * per_row + c] = found[
                        r * BLOCK : (r + 1) * BLOCK, c * BLOCK : (c + 1) * BLOCK
                    ]

        base += jobs * blocks

    pl.semaphore_wait(barrier, 3 + count - 1)
    pl.semaphore_signal(free, inc=1, device_id=(me, near), device_id_type=MESH)
    scatter = Scatter(ring, order, gs, grad, sbuf, rbuf, ss, sr)
    kept = (h2s, dys)
    sums = [RowSum(kept[n], h1s, 2 * n, r2.at[n], rs.at[n], rr.at[n]) for n in range(2)]

    def t_copy(step):
        return pltpu.make_async_remote_copy(
            src_ref=small, dst_ref=t_in.at[tensor], send_sem=ts.at[step], recv_sem=tr.at[step],
            device_id=(me, (tensor + step) % 4), device_id_type=MESH,
        )

    def d_copy(step):
        return pltpu.make_async_remote_copy(
            src_ref=d_out, dst_ref=d_in.at[me], send_sem=ds.at[step], recv_sem=dr.at[step],
            device_id=((me + step) % count, tensor), device_id_type=MESH,
        )

    far = count // 2
    first, second = ((0, 0), (1, 1)), ((1, 0), (0, 1))
    for half, way in first + second:
        if hop_count(half, way, count) >= 1:
            scatter.step(half, way, 1, True)

    def ring_step(hop, which):
        for half, way in which:
            if which is first:
                scatter.step(half, way, hop, False)
            else:

                @pl.when(hop <= far - 1)
                def _():
                    scatter.step(half, way, hop, False)

    wide, thin = 6 * HEAD, 2 * HEAD
    total = lambda v: jnp.sum(v, axis=0, keepdims=True)

    def work(n, r):
        owner = (near * (1 - n % 2) + tensor * (n % 2) + 2 * (1 - n // 2)) % 4
        at = pl.ds(pl.multiple_of(owner * rows + r * TILE, TILE), TILE)
        to = pl.ds(pl.multiple_of(n * rows + r * TILE, TILE), TILE)
        br = dot_nt(acts[at, :], w2s[...])
        dh1 = None
        for p in range(2):
            lo = p * (wide + thin)
            br = br + dot_nt(cs[at, p * thin : (p + 1) * thin], wqds[:, lo + wide : lo + wide + thin])
            part = dot_nt(ps[at, p * wide : (p + 1) * wide], wqds[:, lo : lo + wide])
            dh1 = part if dh1 is None else dh1 + part
        kept[0][to, :] = br.astype(bf16)
        dh2 = dot_nt(dabs[at, :], w1s[...])
        xhat, _ = normed(xs[at, :].astype(f32))
        kept[1][to, :] = (dh1 * gain_ref[0:1, :] + dh2 * gain_ref[1:2, :]).astype(bf16)
        small[0:1, :] += total(dh1 * xhat)
        small[1:2, :] += total(dh2 * xhat)
        small[2:3, :] += total(dh1)
        small[3:4, :] += total(dh2)

    late[5].wait()
    @pl.loop(0, 4)
    def _(n):
        @pl.loop(0, rows // TILE)
        def _(r):
            work(n, r)

        @pl.when(n == 0)
        def _():
            pl.semaphore_wait(free, 1)
            for s in sums:
                s.pair(0).start()

        @pl.when(n == 1)
        def _():
            for s in sums:
                s.middle()
            sums[0].cross().start()
            if far >= 2 and count <= 8:
                ring_step(2, first)

        @pl.when(n == 2)
        def _():
            for s in sums:
                s.pair(1).start()

        @pl.when(n == 3)
        def _():
            if far >= 2 and count <= 8:
                ring_step(2, second)

    for step in range(1, 4):
        t_copy(step).start()
    sums[1].cross().start()

    def both(hop):
        ring_step(hop, first)
        ring_step(hop, second)

    if count <= 8:
        both(3)
    else:
        for_hops(2, far + 1, both, count)
    for step in range(1, 4):
        t_copy(step).wait_recv()
    t_in[tensor] = small[...]
    row = lax.broadcasted_iota(jnp.int32, small.shape, 0)
    summed = t_in[0] + t_in[1] + t_in[2] + t_in[3]
    d_out[...] = jnp.where(row < 4, summed, small[...])

    @pl.loop(1, count)
    def _(step):
        d_copy(step).start()

    if count <= 8:
        both(4)
    sums[0].end(stage, br_out, os)

    @pl.loop(1, count)
    def _(step):
        d_copy(step).wait_recv()

    d_in[me] = d_out[...]
    small_sum[...] = scale * lax.fori_loop(1, count, lambda k, acc: acc + d_in[k], d_in[0])
    sums[1].end(stage, e_out, os)
    for half in range(2):
        scatter.last(half, scale)
    scatter.finish()
    for s in sums:
        s.finish()
    for step in range(1, 4):
        t_copy(step).wait_send()

    @pl.loop(1, count)
    def _(step):
        d_copy(step).wait_send()


def tail_all(count, scale, order, gains, biases, fc1_bias, small, x, h1, dyb, ctx, dproj, wqd, w1, w2):
    rows, width = x.shape[0] // 4, x.shape[1]
    hidden = w1.shape[1]
    blocks = (width * (dproj.shape[1] + hidden) + (ctx.shape[1] + hidden) * width) // (BLOCK * BLOCK)
    per = blocks // count
    far = count // 2
    any_, vmem = pl.BlockSpec(memory_space=pl.ANY), pl.BlockSpec(memory_space=pltpu.VMEM)
    dma = lambda *n: pltpu.SemaphoreType.DMA(n)
    like = lambda v: pltpu.VMEM(v.shape, v.dtype)
    sum_shape = jax.ShapeDtypeStruct((rows, width), f32)
    tall = lambda cols: pltpu.VMEM((x.shape[0], cols), bf16)
    return pl.pallas_call(
        functools.partial(tail_kernel, count, scale),
        out_shape=[
            jax.ShapeDtypeStruct((per, BLOCK, BLOCK), f32), jax.ShapeDtypeStruct(small.shape, f32),
            sum_shape, sum_shape,
        ],
        in_specs=[pl.BlockSpec(memory_space=pltpu.SMEM)] + [vmem] * 4 + [any_] * 8,
        out_specs=[vmem, vmem, any_, any_],
        scratch_shapes=[like(v) for v in (x, h1, dyb, ctx, dproj, wqd, w1, w2)]
        + [
            tall(width), tall(hidden), tall(hidden), pltpu.VMEM((blocks, BLOCK, BLOCK), bf16),
            pltpu.VMEM((4, per, 64, BLOCK), bf16), pltpu.VMEM((4 * far, per, 64, BLOCK), bf16),
            pltpu.VMEM((2, rows, width), bf16), pltpu.VMEM((2, 64, width), f32),
            pltpu.VMEM(small.shape, f32), pltpu.VMEM((4,) + small.shape, f32),
            pltpu.VMEM((count,) + small.shape, f32), pltpu.VMEM(small.shape, f32),
            dma(2, x.shape[0] // WIDE), dma(6),
            dma(4 * far), dma(4 * far), dma(2, 3), dma(2, 3), dma(4), dma(4), dma(count), dma(count),
            dma(2), pltpu.SemaphoreType.REGULAR,
        ],
        compiler_params=pltpu.CompilerParams(
            collective_id=1, has_side_effects=True, vmem_limit_bytes=VMEM_LIMIT
        ),
        cost_estimate=pl.CostEstimate(flops=int(3.5e10), bytes_accessed=int(4e7), transcendentals=int(4e6)),
        name="tail_all",
    )(order, gains, biases, fc1_bias, small, x, h1, dyb, ctx, dproj, wqd, w1, w2)


def finish_kernel(
    steps, lim_ref, bias_ref, small_ref, racc_ref, qacc_ref, facc_ref, grad, tok, dy, br, e, ls, rs, lr, rr,
    gout, out, dx, lout, rout, cout, racc, rupd, qacc, qupd, facc, fupd,
    g_v, tok_v, dy_v, br_v, e_v, ls_v, rs_v, lr_v, rr_v, out_v, dx_v, lo_v, ro_v, co_v, isem, osem,
):
    tensor = lax.axis_index("tensor")
    own_rows, blocks = tok.shape[0], grad.shape[0]
    rows, some = own_rows // steps, blocks // steps
    ins = [(grad, g_v), (ls, ls_v), (rs, rs_v), (lr, lr_v), (rr, rr_v), (tok, tok_v), (dy, dy_v), (br, br_v), (e, e_v)]
    outs = [(g_v, gout), (lo_v, lout), (ro_v, rout), (co_v, cout), (out_v, out), (dx_v, dx)]

    def span(ref, s):
        size = ref.shape[0] // steps
        return ref.at[pl.ds(s * size if ref.shape[0] == blocks else pl.multiple_of(s * size, 16), size)]

    def fetch(k, s):
        return pltpu.make_async_copy(span(ins[k][0], s), span(ins[k][1], s), isem.at[k, s])

    def store(k, s):
        return pltpu.make_async_copy(span(outs[k][0], s), span(outs[k][1], s), osem.at[k, s])

    for s in range(steps):
        for k in range(len(ins)):
            fetch(k, s).start()
    small = small_ref[...]

    def adagrad(grad_vec, accum, new, update):
        accum_next = accum + grad_vec * grad_vec
        new[...] = accum_next
        update[...] = -adagrad_rate * grad_vec * lax.rsqrt(accum_next)

    def stacked(line, count):
        return jnp.concatenate([line[:, k * BLOCK : (k + 1) * BLOCK] for k in range(count)], axis=0)

    adagrad(jnp.concatenate([small[0:5], small[4:5]], axis=0), racc_ref[...], racc, rupd)
    adagrad(stacked(small[5:6], qacc.shape[0]), qacc_ref[...], qacc, qupd)
    adagrad(stacked(small[6:7], facc.shape[0]), facc_ref[...], facc, fupd)
    shift = bias_ref[2:3, :] + bias_ref[3:4, :]

    @pl.loop(0, steps)
    def _(s):
        for k in range(len(ins)):
            fetch(k, s).wait()

        for b in range(some):
            k = s * some + b
            low = g_v[k].astype(bf16)
            lo_v[k] = stat_decay * ls_v[k] + (1.0 - stat_decay) * dot_nt(low, low)
            ro_v[k] = stat_decay * rs_v[k] + (1.0 - stat_decay) * dot_tn(low, low)
            pushed = dot_nn(lr_v[k].astype(bf16), low).astype(bf16)
            co_v[k] = -shampoo_rate * dot_nn(pushed, rr_v[k].astype(bf16))

        at = pl.ds(pl.multiple_of(s * rows, 16), rows)
        x = tok_v[at, :].astype(f32)
        out_v[at, :] = (x + br_v[at, :] + shift).astype(bf16)
        start = tensor * own_rows + s * rows
        place = start % LEN + lax.broadcasted_iota(jnp.int32, (rows, 1), 0)
        kept = jnp.where(place < lim_ref[start // LEN], dy_v[at, :].astype(f32), 0.0)
        xhat, scale = normed(x)
        v = e_v[at, :]
        dx_v[at, :] = kept + scale * (
            v - jnp.mean(v, axis=-1, keepdims=True) - xhat * jnp.mean(v * xhat, axis=-1, keepdims=True)
        )
        for k in range(len(outs)):
            store(k, s).start()

    for s in range(steps):
        for k in range(len(outs)):
            store(k, s).wait()


def finish_all(limits, biases, small, racc, qacc, facc, grad, tok, dy, br, e, ls, rs, lr, rr):
    steps = 4 if grad.shape[0] % 4 == 0 else 1
    any_, vmem = pl.BlockSpec(memory_space=pl.ANY), pl.BlockSpec(memory_space=pltpu.VMEM)
    shape = lambda v: jax.ShapeDtypeStruct(v.shape, v.dtype)
    like = lambda v: pltpu.VMEM(v.shape, v.dtype)
    vectors = [racc, racc, qacc, qacc, facc, facc]
    return pl.pallas_call(
        functools.partial(finish_kernel, steps),
        out_shape=[shape(grad), shape(tok), shape(e)] + [shape(grad)] * 3 + [shape(v) for v in vectors],
        in_specs=[pl.BlockSpec(memory_space=pltpu.SMEM)] + [vmem] * 5 + [any_] * 9,
        out_specs=[any_] * 6 + [vmem] * 6,
        scratch_shapes=[like(v) for v in (grad, tok, dy, br, e, ls, rs, lr, rr, tok, e, ls, ls, ls)]
        + [pltpu.SemaphoreType.DMA((9, steps)), pltpu.SemaphoreType.DMA((6, steps))],
        compiler_params=pltpu.CompilerParams(vmem_limit_bytes=VMEM_LIMIT),
        cost_estimate=pl.CostEstimate(flops=int(4e8), bytes_accessed=int(2e7), transcendentals=0),
        name="finish_all",
    )(limits, biases, small, racc, qacc, facc, grad, tok, dy, br, e, ls, rs, lr, rr)


def shards(
    tokens, out_grad, seq_lengths, norm_gains, row_biases, qkv_weight, qkv_bias, dense_weight, fc1_weight,
    fc1_bias, fc2_weight, block_slot, left_stat, right_stat, left_root, right_root, row_accum,
    qkv_bias_accum, fc1_bias_accum,
):
    tensor_count = lax.axis_size("tensor")
    dp_count = lax.axis_size("dp")
    grad_scale = 1.0 / math.sqrt(tokens.shape[0] * tensor_count * dp_count)
    xf, h1, dyb, ctx, dproj, wqdf, w1f, w2f, sum_a, order = mixed_all(
        dp_count, seq_lengths, norm_gains, row_biases, as_rows(qkv_bias), jnp.asarray(rotary_rows()),
        as_rows(block_slot), tokens, out_grad, qkv_weight, dense_weight, fc1_weight, fc2_weight,
    )
    own_grad, small, branch, e_sum = tail_all(
        dp_count, grad_scale, order, norm_gains, row_biases, as_rows(fc1_bias), sum_a,
        xf, h1, dyb, ctx, dproj, wqdf, w1f, w2f,
    )
    outs = finish_all(
        seq_lengths, row_biases, small, row_accum, as_rows(qkv_bias_accum), as_rows(fc1_bias_accum),
        own_grad, tokens, out_grad, branch, e_sum, left_stat, right_stat, left_root, right_root,
    )
    block_grad, layer_out, input_grad, left_new, right_new, change = outs[:6]
    return (
        layer_out, input_grad, block_grad, left_new, right_new, change,
        *outs[6:8], *(v.reshape(-1) for v in outs[8:]),
    )


def solution(mesh):
    both = ("dp", "tensor")
    return jax.shard_map(
        shards,
        mesh=mesh,
        in_specs=(
            P(both, None), P(both, None), P("dp"), P(), P(), P("dp", "tensor"), P("tensor"),
            P("tensor", "dp"), P("dp", "tensor"), P("tensor"), P("tensor", "dp"), P(),
            P(both, None, None), P(both, None, None), P(both, None, None), P(both, None, None),
            P(), P("tensor"), P("tensor"),
        ),
        out_specs=(
            P(both, None), P(both, None), P(both, None, None), P(both, None, None),
            P(both, None, None), P(both, None, None), P(), P(), P("tensor"), P("tensor"),
            P("tensor"), P("tensor"),
        ),
        check_vma=False,
    )
```

```python
import functools
import math

import jax
import jax.numpy as jnp
import numpy as np
from jax import lax
from jax.experimental import pallas as pl
from jax.experimental.pallas import tpu as pltpu
from jax.sharding import PartitionSpec as P

HEAD = 64
ROT = 16
LEN = 1024
BLOCK = 128
TILE = 256
WIDE = 512
MESH = pl.DeviceIdType.MESH
VMEM_LIMIT = 60 * 1024 * 1024

masked_score = -1e30
shampoo_rate = 0.03
adagrad_rate = 0.1
stat_decay = 0.5
f32 = jnp.float32
bf16 = jnp.bfloat16


def rotary_rows():
    half = ROT // 2
    inverse = np.power(np.float32(10000.0), -(np.arange(half, dtype=np.float32) * np.float32(2.0 / ROT)))
    angles = inverse.astype(np.float32)[:, None] * np.arange(LEN, dtype=np.float32)[None, :]
    return np.concatenate([np.cos(angles), np.sin(angles)], axis=0).astype(np.float32)


def ring_place(me, count):
    low, high = me % 2, me // 2
    return low * (count - 1 - high) + (1 - low) * high


def ring_device(place, count):
    upper = place // (count // 2)
    return (1 - upper) * (2 * place) + upper * (2 * (count - 1 - place) + 1)


def hop_count(half, way, count):
    far = count // 2
    return far if half == way else far - 1


def for_hops(first, last, body, count):
    if count <= 8:
        for hop in range(first, last):
            body(hop)
    elif last > first:

        @pl.loop(first, last)
        def _(hop):
            body(hop)


def as_rows(vec):
    return vec.reshape(-1, BLOCK)


def as_line(rows):
    return jnp.concatenate([rows[k : k + 1, :] for k in range(rows.shape[0])], axis=1)


class Ring:
    def __init__(self, count):
        self.count = count
        self.me = lax.axis_index("dp")
        self.tensor = lax.axis_index("tensor")
        self.place = ring_place(self.me, count)
        self.peer = [
            (ring_device((self.place + step) % count, count), self.tensor) for step in (1, count - 1)
        ]

    def at(self, offset):
        return ring_device((self.place + offset + 2 * self.count) % self.count, self.count)


class Gather:
    def __init__(self, ring, locals_, fulls, send, recv):
        self.ring, self.locals, self.fulls, self.send, self.recv = ring, locals_, fulls, send, recv
        self.far = ring.count // 2

    def part(self, ref, w, half, owner=None):
        rows, cols = self.locals[w].shape
        base = 0 if owner is None else owner * rows
        if rows % 32 == 0:
            return ref.at[pl.ds(pl.multiple_of(base + half * (rows // 2), 16), rows // 2)]
        return ref.at[pl.ds(base, rows), pl.ds(half * (cols // 2), cols // 2)]

    def sem(self, w, half, way, hop):
        return ((w * 2 + half) * 2 + way) * self.far + hop - 1

    def copy(self, w, half, way, hop, source):
        owner = self.ring.at((1 - hop) if way == 0 else (hop - 1))
        src = self.part(self.locals[w], w, half) if source else self.part(self.fulls[w], w, half, owner)
        return pltpu.make_async_remote_copy(
            src_ref=src,
            dst_ref=self.part(self.fulls[w], w, half, owner),
            send_sem=self.send.at[self.sem(w, half, way, hop)],
            recv_sem=self.recv.at[self.sem(w, half, way, hop)],
            device_id=self.ring.peer[way],
            device_id_type=MESH,
        )

    def arrival(self, w, half, way, hop):
        owner = self.ring.at(-hop if way == 0 else hop)
        dst = self.part(self.fulls[w], w, half, owner)
        return pltpu.make_async_remote_copy(
            src_ref=dst,
            dst_ref=dst,
            send_sem=self.send.at[self.sem(w, half, way, hop)],
            recv_sem=self.recv.at[self.sem(w, half, way, hop)],
            device_id=self.ring.peer[way],
            device_id_type=MESH,
        )

    def begin(self, w):
        for half in range(2):
            for way in range(2):
                if hop_count(half, way, self.ring.count) >= 1:
                    self.copy(w, half, way, 1, True).start()

    def forward(self, w, hop, last):
        for half in range(2):
            for way in range(2):
                hops = self.far if half == way else self.far - 1
                if last and hops != self.far:
                    continue
                self.arrival(w, half, way, hop).wait_recv()
                if not last:
                    more = self.far if half == way else self.far - 1
                    if more == self.far:
                        self.copy(w, half, way, hop + 1, False).start()
                    else:

                        @pl.when(hop + 1 <= more)
                        def _():
                            self.copy(w, half, way, hop + 1, False).start()

    def finish(self, w):
        for half in range(2):
            for way in range(2):
                hops = hop_count(half, way, self.ring.count)
                if hops >= 1:
                    self.copy(w, half, way, 1, True).wait_send()
                for_hops(
                    2, hops + 1, lambda hop: self.copy(w, half, way, hop, False).wait_send(), self.ring.count
                )


class Rows:
    def __init__(self, local, full, send, recv, own):
        self.tensor = lax.axis_index("tensor")
        self.dp = lax.axis_index("dp")
        self.near = self.tensor + 1 - 2 * (self.tensor % 2)
        self.across = (self.tensor + 2) % 4
        self.local, self.full, self.send, self.recv, self.own = local, full, send, recv, own
        self.rows = local.shape[0]

    def slot(self, owner, piece=None):
        if piece is None:
            return self.full.at[pl.ds(pl.multiple_of(owner * self.rows, 16), self.rows)]
        half = self.rows // 2
        return self.full.at[pl.ds(pl.multiple_of(owner * self.rows + piece * half, 16), half)]

    def remote(self, src, dst, sem, device):
        return pltpu.make_async_remote_copy(
            src_ref=src,
            dst_ref=dst,
            send_sem=self.send.at[sem],
            recv_sem=self.recv.at[sem],
            device_id=(self.dp, device),
            device_id_type=MESH,
        )

    def keep(self):
        return pltpu.make_async_copy(self.local, self.slot(self.tensor), self.own)

    def pair(self):
        return self.remote(self.local, self.slot(self.tensor), 0, self.near)

    def cross(self, piece):
        half = self.rows // 2
        return self.remote(
            self.local.at[pl.ds(piece * half, half)], self.slot(self.tensor, piece), 1 + piece, self.across
        )

    def onward(self, piece):
        here = self.slot(self.across, piece)
        return self.remote(here, here, 3 + piece, self.near)

    def begin_near(self):
        self.keep().start()
        self.pair().start()

    def begin_cross(self):
        for piece in range(2):
            self.cross(piece).start()

    def pass_piece(self, piece):
        self.cross(piece).wait_recv()
        self.onward(piece).start()

    def pass_on(self):
        for piece in range(2):
            self.pass_piece(piece)

    def finish(self):
        self.keep().wait()
        self.pair().wait()
        for piece in range(2):
            self.cross(piece).wait_send()
            self.onward(piece).wait()


def greet(devices):
    barrier = pltpu.get_barrier_semaphore()
    for device in devices:
        pl.semaphore_signal(barrier, inc=1, device_id=device, device_id_type=MESH)
    pl.semaphore_wait(barrier, len(devices))


def dot_nn(a, b):
    return lax.dot_general(a, b, (((1,), (0,)), ((), ())), preferred_element_type=f32)


def dot_nt(a, b):
    return lax.dot_general(a, b, (((1,), (1,)), ((), ())), preferred_element_type=f32)


def dot_tn(a, b):
    return lax.dot_general(a, b, (((0,), (0,)), ((), ())), preferred_element_type=f32)


def normed(x):
    average = jnp.mean(x, axis=-1, keepdims=True)
    centered = x - average
    variance = jnp.mean(centered * centered, axis=-1, keepdims=True)
    scale = lax.rsqrt(variance + 1e-05)
    return centered * scale, scale


def mixed_kernel(
    count, lim_ref, gain_ref, bias_ref, qb_ref, rot_ref, slot_ref, wd, w2, x, dy, wq, w1,
    x_out, h1_out, dyb_out, ctx_out, dproj_out, wqd_out, w1f, w2f, sum_ref, order_ref,
    xf, dyf, wf, wl, w2l, h1s, ctxs, dps, qt, kt, vt, dct, ctt, dqt, kr, vr, dkvs,
    rs, rr, ro, gs, gr, go, os,
):
    ring = Ring(count)
    pair_cols = 6 * HEAD
    half_cols = pair_cols + 2 * HEAD
    parts = [
        pltpu.make_async_copy(
            wq.at[:, pl.ds(p * pair_cols, pair_cols)], wl.at[:, pl.ds(p * half_cols, pair_cols)], os.at[p]
        )
        for p in range(2)
    ]
    for copy in parts:
        copy.start()
    turned_dense = wd[...].T
    for p in range(2):
        wl[:, p * half_cols + pair_cols : (p + 1) * half_cols] = turned_dense[:, p * 2 * HEAD : (p + 1) * 2 * HEAD]
    views = [(wl.at[:, pl.ds(p * half_cols, half_cols)], wf.at[:, pl.ds(p * half_cols, half_cols)]) for p in (0, 1)]
    views += [(w1, w1f), (w2l, w2f)]
    gather = Gather(ring, [v[0] for v in views], [v[1] for v in views], gs, gr)
    rx = Rows(x, xf, rs.at[0], rr.at[0], ro.at[0])
    ry = Rows(dy, dyf, rs.at[1], rr.at[1], ro.at[1])
    greet([ring.peer[0], ring.peer[1], (ring.me, rx.near), (ring.me, rx.across)])
    far = count // 2
    own = []
    for k, (local, full) in enumerate(((w1, w1f), (w2l, w2f))):
        rows = local.shape[0]
        own.append(
            pltpu.make_async_copy(local, full.at[pl.ds(pl.multiple_of(ring.me * rows, 16), rows)], go.at[k])
        )
    rx.begin_near()
    for copy in parts:
        copy.wait()
    gather.begin(0)
    rx.begin_cross()
    ry.begin_near()
    ry.begin_cross()
    wf[pl.ds(pl.multiple_of(ring.me * wl.shape[0], 16), wl.shape[0]), :] = wl[...]
    own[0].start()
    sum_ref[...] = jnp.zeros_like(sum_ref)
    tensor = ring.tensor
    tiles = LEN // TILE

    def whole_ring(w):
        for_hops(1, far, lambda hop: gather.forward(w, hop, False), count)
        gather.forward(w, far, True)

    def hop_at(w, hop):
        if count == 8:
            gather.forward(w, hop, hop == far)
        elif hop == 4:
            whole_ring(w)

    def rows_of(seq, i):
        return pl.ds(pl.multiple_of(seq * LEN + i * TILE, TILE), TILE)

    def norm_tile(seq, i):
        rows = rows_of(seq, i)
        xhat, _ = normed(xf[rows, :].astype(f32))
        h1s[rows, :] = (xhat * gain_ref[0:1, :] + bias_ref[0:1, :]).astype(bf16)

    def mask_tile(seq, i):
        rows = rows_of(seq, i)
        place = i * TILE + lax.broadcasted_iota(jnp.int32, (TILE, 1), 0)
        kept = jnp.where(place < lim_ref[seq], dyf[rows, :].astype(f32), 0.0)
        sum_ref[4:5, :] += jnp.sum(kept, axis=0, keepdims=True)
        dyf[rows, :] = kept.astype(bf16)

    def turned(first, second, cosine, sine):
        return first * cosine - second * sine, second * cosine + first * sine

    def prepare_tile(seq, pair, i):
        rows = rows_of(seq, i)
        cols = pl.ds(pl.multiple_of(i * TILE, TILE), TILE)
        proj = dot_nn(h1s[rows, :], wf[:, pl.ds(pl.multiple_of(pair * half_cols, BLOCK), pair_cols)])
        proj = proj + as_line(qb_ref[pl.ds(pair * (pair_cols // BLOCK), pair_cols // BLOCK), :])
        proj = proj.T
        cosine, sine = rot_ref[0:8, cols], rot_ref[8:16, cols]
        key = i * TILE + lax.broadcasted_iota(jnp.int32, (16, TILE), 1)
        row = lax.broadcasted_iota(jnp.int32, (16, TILE), 0)
        ones = jnp.where(row == 0, 1.0, 0.0).astype(bf16)
        hidden = jnp.where((row == 0) & (key >= lim_ref[seq]), masked_score, 0.0).astype(bf16)
        blank = jnp.zeros((48, TILE), bf16)
        none = jnp.zeros((HEAD, TILE), bf16)
        for hh in range(2):
            h = 2 * pair + hh
            base = 3 * HEAD * hh
            q0, q1 = turned(proj[base : base + 8], proj[base + 8 : base + 16], cosine, sine)
            q = jnp.concatenate([q0, q1, proj[base + 16 : base + HEAD]], axis=0).astype(bf16)
            q = (q.astype(f32) * 0.125).astype(bf16)
            qt[h, :, cols] = jnp.concatenate([q, ones, blank], axis=0)
            base += HEAD
            k0, k1 = turned(proj[base : base + 8], proj[base + 8 : base + 16], cosine, sine)
            k = jnp.concatenate([k0, k1, proj[base + 16 : base + HEAD]], axis=0).astype(bf16)
            kt[h, :, cols] = k
            kr[h, cols, :] = jnp.concatenate([k, hidden, blank], axis=0).T
            base += HEAD
            v = proj[base : base + HEAD].astype(bf16)
            vt[h, :, cols] = jnp.concatenate([v, ones], axis=0)
            vr[h, cols, :] = jnp.concatenate([none, v], axis=0).T

    def context_tile(seq, pair, i):
        cols = pl.ds(pl.multiple_of(i * TILE, TILE), TILE)
        begin = pair * half_cols + pair_cols
        dctx = dot_nn(dyf[rows_of(seq, i), :], wf[:, begin : begin + 2 * HEAD]).T.astype(bf16)
        for hh in range(2):
            dct[2 * pair + hh, :, cols] = dctx[HEAD * hh : HEAD * (hh + 1)]

    def back_tile(seq, i):
        mask_tile(seq, i)
        context_tile(seq, 0, i)
        context_tile(seq, 1, i)

    def attend(pair, i, fresh):
        here = slice(i * TILE, (i + 1) * TILE)
        chunks = [slice(c * TILE, (c + 1) * TILE) for c in range(i + 1)]
        heads = range(2)
        of = [2 * pair, 2 * pair + 1]
        key = lax.broadcasted_iota(jnp.int32, (TILE, TILE), 0)
        query = lax.broadcasted_iota(jnp.int32, (TILE, TILE), 1)
        q = [qt[of[hh], :, here] for hh in heads]
        scores = [[dot_nn(kr[of[hh], c, :], q[hh]) for c in chunks] for hh in heads]
        probs, grads, deltas, both = [], [], [], []
        none = jnp.zeros((HEAD, TILE), bf16)
        for hh in heads:
            scores[hh][i] = jnp.where(key <= query, scores[hh][i], masked_score)
            top = jnp.max(scores[hh][0], axis=0, keepdims=True)
            for s in scores[hh][1:]:
                top = jnp.maximum(top, jnp.max(s, axis=0, keepdims=True))
            probs.append([jnp.exp(s - top).astype(bf16) for s in scores[hh]])
        for hh in heads:
            total = dot_nn(vt[of[hh], :, chunks[0]], probs[hh][0])
            for c, p in zip(chunks[1:], probs[hh][1:]):
                total = total + dot_nn(vt[of[hh], :, c], p)
            inverse = 1.0 / total[HEAD : HEAD + 1]
            context = total[:HEAD] * inverse
            ctt[of[hh], :, here] = context
            grad = (dct[of[hh], :, here].astype(f32) * inverse).astype(bf16)
            deltas.append(jnp.sum(grad.astype(f32) * context, axis=0, keepdims=True))
            grad = jnp.concatenate([none, grad], axis=0)
            grads.append(grad)
            both.append(jnp.concatenate([jnp.concatenate([q[hh][:HEAD], none], axis=0), grad], axis=1))
        dq = [None, None]
        for n, c in enumerate(chunks):
            for hh in heads:
                p = probs[hh][n]
                dp = dot_nn(vr[of[hh], c, :], grads[hh])
                ds = (p.astype(f32) * (dp - deltas[hh])).astype(bf16)
                part = dot_nn(kt[of[hh], :, c], ds)
                dq[hh] = part if dq[hh] is None else dq[hh] + part
                dkv = dot_nt(jnp.concatenate([ds, p], axis=1), both[hh])
                if n in fresh:
                    dkvs[of[hh], c, :] = dkv
                else:
                    dkvs[of[hh], c, :] += dkv
        for hh in heads:
            dqt[of[hh], :, here] = dq[hh] * 0.125

    def collect_tile(seq, i):
        rows = rows_of(seq, i)
        cols = pl.ds(pl.multiple_of(i * TILE, TILE), TILE)
        cosine, sine = rot_ref[0:8, cols], rot_ref[8:16, cols]
        for pair in range(2):
            pieces = []
            for h in (2 * pair, 2 * pair + 1):
                dkv = dkvs[h, cols, :].T
                for grad in (dqt[h, :, cols], dkv[:HEAD]):
                    pieces += [*turned(grad[0:8], grad[8:16], cosine, -sine), grad[16:HEAD]]
                pieces.append(dkv[HEAD:])
            low = jnp.concatenate(pieces, axis=0).T.astype(bf16)
            wide = slice(pair * pair_cols, (pair + 1) * pair_cols)
            dps[rows, wide] = low
            sum_ref[5:6, wide] += jnp.sum(low.astype(f32), axis=0, keepdims=True)
            ctx = jnp.concatenate([ctt[2 * pair, :, cols], ctt[2 * pair + 1, :, cols]], axis=0).T
            ctxs[rows, pair * 2 * HEAD : (pair + 1) * 2 * HEAD] = ctx.astype(bf16)

    def save(turn, k, seq):
        src, dst = ((xf, x_out), (h1s, h1_out), (dyf, dyb_out), (ctxs, ctx_out), (dps, dproj_out))[k]
        rows = pl.ds(pl.multiple_of(seq * LEN, LEN), LEN)
        return pltpu.make_async_copy(src.at[rows], dst.at[rows], os.at[turn * 5 + k])

    mine = order_ref.shape[1]
    per = mine // count
    place = lax.broadcasted_iota(jnp.int32, (mine, 1), 0).astype(f32)
    owner = jnp.floor((place + 0.5) / per)
    wanted = (owner * 4.0 + lax.convert_element_type(tensor, f32)) * per + (place - owner * per)
    found = jnp.zeros(order_ref.shape, f32)
    for r in range(slot_ref.shape[0]):
        hit = jnp.where(slot_ref[r : r + 1, :].astype(f32) == wanted, 1.0, 0.0).astype(bf16)
        block = r * BLOCK + lax.broadcasted_iota(jnp.int32, (8, BLOCK), 1) - tensor * mine
        found = found + dot_nt(jnp.clip(block, 0, mine - 1).astype(f32).astype(bf16), hit)
    order_ref[...] = (found + 0.5).astype(jnp.int32)

    seq = tensor // 2
    rx.keep().wait()
    rx.pair().wait_recv()

    @pl.loop(0, tiles)
    def _(i):
        norm_tile(seq, i)

        @pl.when(i == 0)
        def _():
            hop_at(0, 1)
            gather.begin(1)

        @pl.when(i == 1)
        def _():
            hop_at(0, 2)
            hop_at(1, 1)

        @pl.when(i == 2)
        def _():
            hop_at(0, 3)
            hop_at(1, 2)
            gather.begin(2)

    save(0, 0, seq).start()
    save(0, 1, seq).start()
    w2l[...] = w2[...].T
    hop_at(0, 4)
    ry.keep().wait()
    ry.pair().wait_recv()

    @pl.loop(0, tiles // 4)
    def _(i):
        for sub in range(4):
            prepare_tile(seq, 0, 4 * i + sub)


    @pl.loop(0, tiles)
    def _(i):
        mask_tile(seq, i)
        context_tile(seq, 0, i)

    save(0, 2, seq).start()

    @pl.loop(0, 2)
    def _(pair):
        @pl.when(pair == 1)
        def _():
            hop_at(1, 4)
            hop_at(2, 1)

            @pl.loop(0, tiles // 4)
            def _(i):
                for sub in range(4):
                    prepare_tile(seq, 1, 4 * i + sub)
                    context_tile(seq, 1, 4 * i + sub)

        attend(pair, 3, (0, 1, 2, 3))

        @pl.when(pair == 0)
        def _():
            hop_at(1, 3)
            gather.begin(3)
            own[1].start()

        attend(pair, 2, ())

        @pl.when(pair == 0)
        def _():
            rx.pass_on()

        @pl.when(pair == 1)
        def _():
            hop_at(3, 1)

        attend(pair, 1, ())
        attend(pair, 0, ())

    @pl.loop(0, tiles)
    def _(i):
        collect_tile(seq, i)

    save(0, 3, seq).start()
    save(0, 4, seq).start()
    keep = pltpu.make_async_copy(wf, wqd_out, os.at[10])
    keep.start()

    seq = 1 - seq
    for piece in range(2):
        rx.onward(piece).wait_recv()

    @pl.loop(0, tiles)
    def _(i):
        norm_tile(seq, i)

    save(1, 0, seq).start()
    save(1, 1, seq).start()
    ry.pass_piece(0)

    for pair in range(2):

        @pl.loop(0, tiles // 4)
        def _(i):
            for sub in range(4):
                prepare_tile(seq, pair, 4 * i + sub)

        if pair == 0:
            hop_at(2, 2)

    ry.onward(0).wait()
    back_tile(seq, 0)
    back_tile(seq, 2)

    @pl.loop(0, 2)
    def _(pair):
        attend(pair, 2, (0, 1, 2))

        @pl.when(pair == 0)
        def _():
            hop_at(3, 2)

        attend(pair, 0, ())

    ry.pass_piece(1)
    ry.onward(1).wait()
    back_tile(seq, 1)
    back_tile(seq, 3)
    save(1, 2, seq).start()
    hop_at(2, 3)

    @pl.loop(0, 2)
    def _(pair):
        attend(pair, 3, (3,))

        @pl.when(pair == 1)
        def _():
            hop_at(3, 3)

        attend(pair, 1, ())

    @pl.loop(0, tiles)
    def _(i):
        collect_tile(seq, i)

    save(1, 3, seq).start()
    save(1, 4, seq).start()
    hop_at(2, 4)
    hop_at(3, 4)
    for w in range(4):
        gather.finish(w)
    own[0].wait()
    own[1].wait()
    rx.pair().wait_send()
    ry.pair().wait_send()
    for piece in range(2):
        rx.cross(piece).wait_send()
        rx.onward(piece).wait_send()
        ry.cross(piece).wait_send()
    for turn in range(2):
        for k in range(5):
            save(turn, k, turn + (1 - 2 * turn) * (tensor // 2)).wait()
    keep.wait()


def mixed_all(count, limits, gains, biases, qkv_bias, rot, slots, x, dy, wq, wd, w1, w2):
    far = count // 2
    rows, width = 4 * x.shape[0], x.shape[1]
    ctx_cols, proj_cols = wd.shape[0], wq.shape[1]
    shard = wq.shape[0]
    out = lambda r, c: jax.ShapeDtypeStruct((r, c), bf16)
    any_, vmem = pl.BlockSpec(memory_space=pl.ANY), pl.BlockSpec(memory_space=pltpu.VMEM)
    dma = lambda *n: pltpu.SemaphoreType.DMA(n)
    buf = lambda dtype, *shape: pltpu.VMEM(shape, dtype)
    heads, both = 4, ctx_cols + proj_cols
    return pl.pallas_call(
        functools.partial(mixed_kernel, count),
        out_shape=[
            out(rows, width), out(rows, width), out(rows, width), out(rows, ctx_cols), out(rows, proj_cols),
            out(width, both), out(width, w1.shape[1]), out(width, w2.shape[0]),
            jax.ShapeDtypeStruct((8, width), f32), jax.ShapeDtypeStruct((8, slots.size // 4), jnp.int32),
        ],
        in_specs=[pl.BlockSpec(memory_space=pltpu.SMEM)] + [vmem] * 7 + [any_] * 4,
        out_specs=[any_] * 8 + [vmem] * 2,
        scratch_shapes=[
            buf(bf16, rows, width), buf(bf16, rows, width), buf(bf16, width, both),
            buf(bf16, shard, both), buf(bf16, shard, w2.shape[0]),
            buf(bf16, rows, width), buf(bf16, rows, ctx_cols), buf(bf16, rows, proj_cols),
            buf(bf16, heads, 2 * HEAD, LEN), buf(bf16, heads, HEAD, LEN), buf(bf16, heads, HEAD + 16, LEN),
            buf(bf16, heads, HEAD, LEN), buf(f32, heads, HEAD, LEN), buf(f32, heads, HEAD, LEN),
            buf(bf16, heads, LEN, 2 * HEAD), buf(bf16, heads, LEN, 2 * HEAD), buf(f32, heads, LEN, 2 * HEAD),
            dma(2, 5), dma(2, 5), dma(2), dma(16 * far), dma(16 * far), dma(2), dma(11),
        ],
        compiler_params=pltpu.CompilerParams(
            collective_id=0, has_side_effects=True, vmem_limit_bytes=VMEM_LIMIT
        ),
        cost_estimate=pl.CostEstimate(flops=int(2e10), bytes_accessed=int(4e7), transcendentals=int(1e7)),
        name="mixed_all",
    )(limits, gains, biases, qkv_bias, rot, slots, wd, w2, x, dy, wq, w1)


def gelu_both(x):
    phi = 0.5 + 0.5 * lax.erf(x * (1.0 / math.sqrt(2.0)))
    bell = jnp.exp(-0.5 * x * x) * (1.0 / math.sqrt(2.0 * math.pi))
    return x * phi, phi + x * bell


class Scatter:
    def __init__(self, ring, order, blocks, out, sbuf, rbuf, send, recv):
        self.ring, self.order, self.blocks, self.out = ring, order, blocks, out
        self.sbuf, self.rbuf, self.send, self.recv = sbuf, rbuf, send, recv
        self.per = out.shape[0]
        self.together = 6 if self.per % 6 == 0 else 1
        self.far = ring.count // 2

    def index(self, half, way, hop):
        return (half * 2 + way) * self.far + hop - 1

    def copy(self, half, way, hop, first):
        i = self.index(half, way, hop)
        return pltpu.make_async_remote_copy(
            src_ref=self.sbuf.at[half * 2 + way] if first else self.rbuf.at[i - 1],
            dst_ref=self.rbuf.at[i],
            send_sem=self.send.at[i],
            recv_sem=self.recv.at[i],
            device_id=self.ring.peer[way],
            device_id_type=MESH,
        )

    def own(self, dest, half, k):
        return self.blocks[self.order[0, dest * self.per + k], half * 64 : half * 64 + 64, :]

    def step(self, half, way, hop, first):
        hops = hop_count(half, way, self.ring.count)
        dest = self.ring.at((hops + 1 - hop) if way == 0 else (hop - hops - 1))
        i = self.index(half, way, hop)
        if not first:
            self.copy(half, way, hop - 1, True).wait_recv()

        def one(k, carry):
            value = self.own(dest, half, k)
            if first:
                self.sbuf[half * 2 + way, k] = value
            else:
                self.rbuf[i - 1, k] = (value.astype(f32) + self.rbuf[i - 1, k].astype(f32)).astype(bf16)
            return carry

        lax.fori_loop(0, self.per, one, 0, unroll=self.together)
        self.copy(half, way, hop, first).start()

    def last(self, half, scale):
        came = []
        for way in range(2):
            hops = hop_count(half, way, self.ring.count)
            if hops >= 1:
                self.copy(half, way, hops, True).wait_recv()
                came.append(self.index(half, way, hops))
        me = self.ring.me

        def one(k, carry):
            value = self.own(me, half, k).astype(f32)
            for i in came:
                value = value + self.rbuf[i, k].astype(f32)
            self.out[k, half * 64 : half * 64 + 64, :] = value * scale
            return carry

        lax.fori_loop(0, self.per, one, 0, unroll=self.together)

    def finish(self):
        for half in range(2):
            for way in range(2):
                hops = hop_count(half, way, self.ring.count)
                for_hops(
                    1, hops + 1, lambda hop: self.copy(half, way, hop, True).wait_send(), self.ring.count
                )


class RowSum:
    def __init__(self, parts, r1, base, r2, send, recv):
        self.tensor = lax.axis_index("tensor")
        self.dp = lax.axis_index("dp")
        self.near = self.tensor + 1 - 2 * (self.tensor % 2)
        self.across = (self.tensor + 2) % 4
        self.r2, self.send, self.recv = r2, send, recv
        self.rows = r2.shape[0]
        self.parts = [parts.at[pl.ds(k * self.rows, self.rows)] for k in range(4)]
        self.r1 = [r1.at[pl.ds((base + k) * self.rows, self.rows)] for k in range(2)]

    def remote(self, src, dst, sem, device):
        return pltpu.make_async_remote_copy(
            src_ref=src, dst_ref=dst, send_sem=self.send.at[sem], recv_sem=self.recv.at[sem],
            device_id=(self.dp, device), device_id_type=MESH,
        )

    def pair(self, k):
        return self.remote(self.parts[2 * k], self.r1[k], k, self.near)

    def cross(self):
        return self.remote(self.parts[1], self.r2, 2, self.across)

    def middle(self):
        self.pair(0).wait_recv()
        self.parts[1][...] = (self.parts[1][...].astype(f32) + self.r1[0][...].astype(f32)).astype(bf16)

    def end(self, stage, out, sem):
        self.pair(1).wait_recv()
        self.cross().wait_recv()
        step = stage.shape[1]
        copies = []
        for k in range(self.rows // step):
            at = pl.ds(k * step, step)
            if k >= 2:
                copies[k - 2].wait()
            stage[k % 2] = (
                self.parts[3][at, :].astype(f32) + self.r1[1][at, :].astype(f32) + self.r2[at, :].astype(f32)
            )
            copies.append(pltpu.make_async_copy(stage.at[k % 2], out.at[at], sem.at[k % 2]))
            copies[-1].start()
        for copy in copies[-2:]:
            copy.wait()

    def finish(self):
        self.pair(0).wait_send()
        self.pair(1).wait_send()
        self.cross().wait_send()


def tail_kernel(
    count, scale, order, gain_ref, bias_ref, fb_ref, small_a, x, h1, dyb, ctx, dproj, wqd, w1, w2,
    grad, small_sum, br_out, e_out,
    xs, h1s, dys, cs, ps, wqds, w1s, w2s, h2s, acts, dabs, gs, sbuf, rbuf, r2, stage, small, t_in, d_in, d_out,
    sem, late_sem, ss, sr, rs, rr, ts, tr, ds, dr, os, free,
):
    ring = Ring(count)
    me, tensor = ring.me, ring.tensor
    rows = r2.shape[1]
    tiles = x.shape[0] // WIDE
    near = tensor + 1 - 2 * (tensor % 2)

    barrier = pltpu.get_barrier_semaphore()
    for step in range(1, 4):
        pl.semaphore_signal(barrier, inc=1, device_id=(me, (tensor + step) % 4), device_id_type=MESH)

    @pl.loop(1, count)
    def _(step):
        pl.semaphore_signal(barrier, inc=1, device_id=((me + step) % count, tensor), device_id_type=MESH)

    def tile_copy(k, src, dst, i):
        at = pl.ds(pl.multiple_of(i * WIDE, WIDE), WIDE)
        return pltpu.make_async_copy(src.at[at], dst.at[at], sem.at[k, i])

    late = [
        pltpu.make_async_copy(src, dst, late_sem.at[k])
        for k, (src, dst) in enumerate(((w1, w1s), (w2, w2s), (h1, h1s), (ctx, cs), (dproj, ps), (wqd, wqds)))
    ]
    late[0].start()
    tile_copy(0, x, xs, 0).start()
    late[1].start()
    tile_copy(1, dyb, dys, 0).start()
    for i in range(1, tiles):
        tile_copy(0, x, xs, i).start()
        tile_copy(1, dyb, dys, i).start()
    for copy in late[2:]:
        copy.start()
    small[...] = small_a[...]
    late[0].wait()
    late[1].wait()

    hidden = w1.shape[1]

    @pl.loop(0, tiles)
    def _(i):
        at = pl.ds(pl.multiple_of(i * WIDE, WIDE), WIDE)
        tile_copy(0, x, xs, i).wait()
        tile_copy(1, dyb, dys, i).wait()
        xhat, _ = normed(xs[at, :].astype(f32))
        h2s[at, :] = (xhat * gain_ref[1:2, :] + bias_ref[1:2, :]).astype(bf16)
        for c in range(1):
            wide = slice(0, hidden)
            pre = dot_nn(h2s[at, :], w1s[:, wide]) + as_line(fb_ref[...])[:, wide]
            da = dot_nn(dys[at, :], w2s[:, wide])
            act, slope = gelu_both(pre)
            acts[at, wide] = act.astype(bf16)
            dab = (da * slope).astype(bf16)
            dabs[at, wide] = dab
            small[6:7, wide] += jnp.sum(dab.astype(f32), axis=0, keepdims=True)

    for copy in late[2:5]:
        copy.wait()
    base = 0
    for left, right in ((h1s, ps), (cs, dys), (h2s, dabs), (acts, dys)):
        tall = min(WIDE, left.shape[1])
        jobs, per_row = left.shape[1] // tall, right.shape[1] // BLOCK
        blocks = tall // BLOCK * per_row

        @pl.loop(0, jobs)
        def _(j):
            found = dot_tn(left[:, pl.ds(pl.multiple_of(j * tall, tall), tall)], right[...]).astype(bf16)
            start = base + j * blocks
            for r in range(tall // BLOCK):
                for c in range(per_row):
                    gs[start + r * per_row + c] = found[
                        r * BLOCK : (r + 1) * BLOCK, c * BLOCK : (c + 1) * BLOCK
                    ]

        base += jobs * blocks

    pl.semaphore_wait(barrier, 3 + count - 1)
    pl.semaphore_signal(free, inc=1, device_id=(me, near), device_id_type=MESH)
    scatter = Scatter(ring, order, gs, grad, sbuf, rbuf, ss, sr)
    kept = (h2s, dys)
    sums = [RowSum(kept[n], h1s, 2 * n, r2.at[n], rs.at[n], rr.at[n]) for n in range(2)]

    def t_copy(step):
        return pltpu.make_async_remote_copy(
            src_ref=small, dst_ref=t_in.at[tensor], send_sem=ts.at[step], recv_sem=tr.at[step],
            device_id=(me, (tensor + step) % 4), device_id_type=MESH,
        )

    def d_copy(step):
        return pltpu.make_async_remote_copy(
            src_ref=d_out, dst_ref=d_in.at[me], send_sem=ds.at[step], recv_sem=dr.at[step],
            device_id=((me + step) % count, tensor), device_id_type=MESH,
        )

    far = count // 2
    first, second = ((0, 0), (1, 1)), ((1, 0), (0, 1))
    for half, way in first + second:
        if hop_count(half, way, count) >= 1:
            scatter.step(half, way, 1, True)

    def ring_step(hop, which):
        for half, way in which:
            if which is first:
                scatter.step(half, way, hop, False)
            else:

                @pl.when(hop <= far - 1)
                def _():
                    scatter.step(half, way, hop, False)

    wide, thin = 6 * HEAD, 2 * HEAD
    total = lambda v: jnp.sum(v, axis=0, keepdims=True)

    def work(n, r):
        owner = (near * (1 - n % 2) + tensor * (n % 2) + 2 * (1 - n // 2)) % 4
        at = pl.ds(pl.multiple_of(owner * rows + r * TILE, TILE), TILE)
        to = pl.ds(pl.multiple_of(n * rows + r * TILE, TILE), TILE)
        br = dot_nt(acts[at, :], w2s[...])
        dh1 = None
        for p in range(2):
            lo = p * (wide + thin)
            br = br + dot_nt(cs[at, p * thin : (p + 1) * thin], wqds[:, lo + wide : lo + wide + thin])
            part = dot_nt(ps[at, p * wide : (p + 1) * wide], wqds[:, lo : lo + wide])
            dh1 = part if dh1 is None else dh1 + part
        kept[0][to, :] = br.astype(bf16)
        dh2 = dot_nt(dabs[at, :], w1s[...])
        xhat, _ = normed(xs[at, :].astype(f32))
        kept[1][to, :] = (dh1 * gain_ref[0:1, :] + dh2 * gain_ref[1:2, :]).astype(bf16)
        small[0:1, :] += total(dh1 * xhat)
        small[1:2, :] += total(dh2 * xhat)
        small[2:3, :] += total(dh1)
        small[3:4, :] += total(dh2)

    late[5].wait()
    @pl.loop(0, 4)
    def _(n):
        @pl.loop(0, rows // TILE)
        def _(r):
            work(n, r)

        @pl.when(n == 0)
        def _():
            pl.semaphore_wait(free, 1)
            for s in sums:
                s.pair(0).start()

        @pl.when(n == 1)
        def _():
            for s in sums:
                s.middle()
            sums[0].cross().start()
            if far >= 2 and count <= 8:
                ring_step(2, first)

        @pl.when(n == 2)
        def _():
            for s in sums:
                s.pair(1).start()

        @pl.when(n == 3)
        def _():
            if far >= 2 and count <= 8:
                ring_step(2, second)

    for step in range(1, 4):
        t_copy(step).start()
    sums[1].cross().start()

    def both(hop):
        ring_step(hop, first)
        ring_step(hop, second)

    if count <= 8:
        both(3)
    else:
        for_hops(2, far + 1, both, count)
    for step in range(1, 4):
        t_copy(step).wait_recv()
    t_in[tensor] = small[...]
    row = lax.broadcasted_iota(jnp.int32, small.shape, 0)
    summed = t_in[0] + t_in[1] + t_in[2] + t_in[3]
    d_out[...] = jnp.where(row < 4, summed, small[...])

    @pl.loop(1, count)
    def _(step):
        d_copy(step).start()

    if count <= 8:
        both(4)
    sums[0].end(stage, br_out, os)

    @pl.loop(1, count)
    def _(step):
        d_copy(step).wait_recv()

    d_in[me] = d_out[...]
    small_sum[...] = scale * lax.fori_loop(1, count, lambda k, acc: acc + d_in[k], d_in[0])
    sums[1].end(stage, e_out, os)
    for half in range(2):
        scatter.last(half, scale)
    scatter.finish()
    for s in sums:
        s.finish()
    for step in range(1, 4):
        t_copy(step).wait_send()

    @pl.loop(1, count)
    def _(step):
        d_copy(step).wait_send()


def tail_all(count, scale, order, gains, biases, fc1_bias, small, x, h1, dyb, ctx, dproj, wqd, w1, w2):
    rows, width = x.shape[0] // 4, x.shape[1]
    hidden = w1.shape[1]
    blocks = (width * (dproj.shape[1] + hidden) + (ctx.shape[1] + hidden) * width) // (BLOCK * BLOCK)
    per = blocks // count
    far = count // 2
    any_, vmem = pl.BlockSpec(memory_space=pl.ANY), pl.BlockSpec(memory_space=pltpu.VMEM)
    dma = lambda *n: pltpu.SemaphoreType.DMA(n)
    like = lambda v: pltpu.VMEM(v.shape, v.dtype)
    sum_shape = jax.ShapeDtypeStruct((rows, width), f32)
    tall = lambda cols: pltpu.VMEM((x.shape[0], cols), bf16)
    return pl.pallas_call(
        functools.partial(tail_kernel, count, scale),
        out_shape=[
            jax.ShapeDtypeStruct((per, BLOCK, BLOCK), f32), jax.ShapeDtypeStruct(small.shape, f32),
            sum_shape, sum_shape,
        ],
        in_specs=[pl.BlockSpec(memory_space=pltpu.SMEM)] + [vmem] * 4 + [any_] * 8,
        out_specs=[vmem, vmem, any_, any_],
        scratch_shapes=[like(v) for v in (x, h1, dyb, ctx, dproj, wqd, w1, w2)]
        + [
            tall(width), tall(hidden), tall(hidden), pltpu.VMEM((blocks, BLOCK, BLOCK), bf16),
            pltpu.VMEM((4, per, 64, BLOCK), bf16), pltpu.VMEM((4 * far, per, 64, BLOCK), bf16),
            pltpu.VMEM((2, rows, width), bf16), pltpu.VMEM((2, 64, width), f32),
            pltpu.VMEM(small.shape, f32), pltpu.VMEM((4,) + small.shape, f32),
            pltpu.VMEM((count,) + small.shape, f32), pltpu.VMEM(small.shape, f32),
            dma(2, x.shape[0] // WIDE), dma(6),
            dma(4 * far), dma(4 * far), dma(2, 3), dma(2, 3), dma(4), dma(4), dma(count), dma(count),
            dma(2), pltpu.SemaphoreType.REGULAR,
        ],
        compiler_params=pltpu.CompilerParams(
            collective_id=1, has_side_effects=True, vmem_limit_bytes=VMEM_LIMIT
        ),
        cost_estimate=pl.CostEstimate(flops=int(3.5e10), bytes_accessed=int(4e7), transcendentals=int(4e6)),
        name="tail_all",
    )(order, gains, biases, fc1_bias, small, x, h1, dyb, ctx, dproj, wqd, w1, w2)


def finish_kernel(
    steps, lim_ref, bias_ref, small_ref, racc_ref, qacc_ref, facc_ref, grad, tok, dy, br, e, ls, rs, lr, rr,
    gout, out, dx, lout, rout, cout, racc, rupd, qacc, qupd, facc, fupd,
    g_v, tok_v, dy_v, br_v, e_v, ls_v, rs_v, lr_v, rr_v, out_v, dx_v, lo_v, ro_v, co_v, isem, osem,
):
    tensor = lax.axis_index("tensor")
    own_rows, blocks = tok.shape[0], grad.shape[0]
    rows, some = own_rows // steps, blocks // steps
    ins = [(grad, g_v), (ls, ls_v), (rs, rs_v), (lr, lr_v), (rr, rr_v), (tok, tok_v), (dy, dy_v), (br, br_v), (e, e_v)]
    outs = [(g_v, gout), (lo_v, lout), (ro_v, rout), (co_v, cout), (out_v, out), (dx_v, dx)]

    def span(ref, s):
        size = ref.shape[0] // steps
        return ref.at[pl.ds(s * size if ref.shape[0] == blocks else pl.multiple_of(s * size, 16), size)]

    def fetch(k, s):
        return pltpu.make_async_copy(span(ins[k][0], s), span(ins[k][1], s), isem.at[k, s])

    def store(k, s):
        return pltpu.make_async_copy(span(outs[k][0], s), span(outs[k][1], s), osem.at[k, s])

    for s in range(steps):
        for k in range(len(ins)):
            fetch(k, s).start()
    small = small_ref[...]

    def adagrad(grad_vec, accum, new, update):
        accum_next = accum + grad_vec * grad_vec
        new[...] = accum_next
        update[...] = -adagrad_rate * grad_vec * lax.rsqrt(accum_next)

    def stacked(line, count):
        return jnp.concatenate([line[:, k * BLOCK : (k + 1) * BLOCK] for k in range(count)], axis=0)

    adagrad(jnp.concatenate([small[0:5], small[4:5]], axis=0), racc_ref[...], racc, rupd)
    adagrad(stacked(small[5:6], qacc.shape[0]), qacc_ref[...], qacc, qupd)
    adagrad(stacked(small[6:7], facc.shape[0]), facc_ref[...], facc, fupd)
    shift = bias_ref[2:3, :] + bias_ref[3:4, :]

    @pl.loop(0, steps)
    def _(s):
        for k in range(len(ins)):
            fetch(k, s).wait()

        for b in range(some):
            k = s * some + b
            low = g_v[k].astype(bf16)
            lo_v[k] = stat_decay * ls_v[k] + (1.0 - stat_decay) * dot_nt(low, low)
            ro_v[k] = stat_decay * rs_v[k] + (1.0 - stat_decay) * dot_tn(low, low)
            pushed = dot_nn(lr_v[k].astype(bf16), low).astype(bf16)
            co_v[k] = -shampoo_rate * dot_nn(pushed, rr_v[k].astype(bf16))

        at = pl.ds(pl.multiple_of(s * rows, 16), rows)
        x = tok_v[at, :].astype(f32)
        out_v[at, :] = (x + br_v[at, :] + shift).astype(bf16)
        start = tensor * own_rows + s * rows
        place = start % LEN + lax.broadcasted_iota(jnp.int32, (rows, 1), 0)
        kept = jnp.where(place < lim_ref[start // LEN], dy_v[at, :].astype(f32), 0.0)
        xhat, scale = normed(x)
        v = e_v[at, :]
        dx_v[at, :] = kept + scale * (
            v - jnp.mean(v, axis=-1, keepdims=True) - xhat * jnp.mean(v * xhat, axis=-1, keepdims=True)
        )
        for k in range(len(outs)):
            store(k, s).start()

    for s in range(steps):
        for k in range(len(outs)):
            store(k, s).wait()


def finish_all(limits, biases, small, racc, qacc, facc, grad, tok, dy, br, e, ls, rs, lr, rr):
    steps = 8 if grad.shape[0] % 8 == 0 else 1
    any_, vmem = pl.BlockSpec(memory_space=pl.ANY), pl.BlockSpec(memory_space=pltpu.VMEM)
    shape = lambda v: jax.ShapeDtypeStruct(v.shape, v.dtype)
    like = lambda v: pltpu.VMEM(v.shape, v.dtype)
    vectors = [racc, racc, qacc, qacc, facc, facc]
    return pl.pallas_call(
        functools.partial(finish_kernel, steps),
        out_shape=[shape(grad), shape(tok), shape(e)] + [shape(grad)] * 3 + [shape(v) for v in vectors],
        in_specs=[pl.BlockSpec(memory_space=pltpu.SMEM)] + [vmem] * 5 + [any_] * 9,
        out_specs=[any_] * 6 + [vmem] * 6,
        scratch_shapes=[like(v) for v in (grad, tok, dy, br, e, ls, rs, lr, rr, tok, e, ls, ls, ls)]
        + [pltpu.SemaphoreType.DMA((9, steps)), pltpu.SemaphoreType.DMA((6, steps))],
        compiler_params=pltpu.CompilerParams(vmem_limit_bytes=VMEM_LIMIT),
        cost_estimate=pl.CostEstimate(flops=int(4e8), bytes_accessed=int(2e7), transcendentals=0),
        name="finish_all",
    )(limits, biases, small, racc, qacc, facc, grad, tok, dy, br, e, ls, rs, lr, rr)


def shards(
    tokens, out_grad, seq_lengths, norm_gains, row_biases, qkv_weight, qkv_bias, dense_weight, fc1_weight,
    fc1_bias, fc2_weight, block_slot, left_stat, right_stat, left_root, right_root, row_accum,
    qkv_bias_accum, fc1_bias_accum,
):
    tensor_count = lax.axis_size("tensor")
    dp_count = lax.axis_size("dp")
    grad_scale = 1.0 / math.sqrt(tokens.shape[0] * tensor_count * dp_count)
    xf, h1, dyb, ctx, dproj, wqdf, w1f, w2f, sum_a, order = mixed_all(
        dp_count, seq_lengths, norm_gains, row_biases, as_rows(qkv_bias), jnp.asarray(rotary_rows()),
        as_rows(block_slot), tokens, out_grad, qkv_weight, dense_weight, fc1_weight, fc2_weight,
    )
    own_grad, small, branch, e_sum = tail_all(
        dp_count, grad_scale, order, norm_gains, row_biases, as_rows(fc1_bias), sum_a,
        xf, h1, dyb, ctx, dproj, wqdf, w1f, w2f,
    )
    outs = finish_all(
        seq_lengths, row_biases, small, row_accum, as_rows(qkv_bias_accum), as_rows(fc1_bias_accum),
        own_grad, tokens, out_grad, branch, e_sum, left_stat, right_stat, left_root, right_root,
    )
    block_grad, layer_out, input_grad, left_new, right_new, change = outs[:6]
    return (
        layer_out, input_grad, block_grad, left_new, right_new, change,
        *outs[6:8], *(v.reshape(-1) for v in outs[8:]),
    )


def solution(mesh):
    both = ("dp", "tensor")
    return jax.shard_map(
        shards,
        mesh=mesh,
        in_specs=(
            P(both, None), P(both, None), P("dp"), P(), P(), P("dp", "tensor"), P("tensor"),
            P("tensor", "dp"), P("dp", "tensor"), P("tensor"), P("tensor", "dp"), P(),
            P(both, None, None), P(both, None, None), P(both, None, None), P(both, None, None),
            P(), P("tensor"), P("tensor"),
        ),
        out_specs=(
            P(both, None), P(both, None), P(both, None, None), P(both, None, None),
            P(both, None, None), P(both, None, None), P(), P(), P("tensor"), P("tensor"),
            P("tensor"), P("tensor"),
        ),
        check_vma=False,
    )
```

```python
import functools
import math

import jax
import jax.numpy as jnp
import numpy as np
from jax import lax
from jax.experimental import pallas as pl
from jax.experimental.pallas import tpu as pltpu
from jax.sharding import PartitionSpec as P

HEAD = 64
ROT = 16
LEN = 1024
BLOCK = 128
TILE = 256
WIDE = 512
MESH = pl.DeviceIdType.MESH
VMEM_LIMIT = 60 * 1024 * 1024

masked_score = -1e30
shampoo_rate = 0.03
adagrad_rate = 0.1
stat_decay = 0.5
f32 = jnp.float32
bf16 = jnp.bfloat16


def rotary_rows():
    half = ROT // 2
    inverse = np.power(np.float32(10000.0), -(np.arange(half, dtype=np.float32) * np.float32(2.0 / ROT)))
    angles = inverse.astype(np.float32)[:, None] * np.arange(LEN, dtype=np.float32)[None, :]
    return np.concatenate([np.cos(angles), np.sin(angles)], axis=0).astype(np.float32)


def ring_place(me, count):
    low, high = me % 2, me // 2
    return low * (count - 1 - high) + (1 - low) * high


def ring_device(place, count):
    upper = place // (count // 2)
    return (1 - upper) * (2 * place) + upper * (2 * (count - 1 - place) + 1)


def hop_count(half, way, count):
    far = count // 2
    return far if half == way else far - 1


def for_hops(first, last, body, count):
    if count <= 8:
        for hop in range(first, last):
            body(hop)
    elif last > first:

        @pl.loop(first, last)
        def _(hop):
            body(hop)


def as_rows(vec):
    return vec.reshape(-1, BLOCK)


def as_line(rows):
    return jnp.concatenate([rows[k : k + 1, :] for k in range(rows.shape[0])], axis=1)


class Ring:
    def __init__(self, count):
        self.count = count
        self.me = lax.axis_index("dp")
        self.tensor = lax.axis_index("tensor")
        self.place = ring_place(self.me, count)
        self.peer = [
            (ring_device((self.place + step) % count, count), self.tensor) for step in (1, count - 1)
        ]

    def at(self, offset):
        return ring_device((self.place + offset + 2 * self.count) % self.count, self.count)


class Gather:
    def __init__(self, ring, locals_, fulls, send, recv):
        self.ring, self.locals, self.fulls, self.send, self.recv = ring, locals_, fulls, send, recv
        self.far = ring.count // 2

    def part(self, ref, w, half, owner=None):
        rows, cols = self.locals[w].shape
        base = 0 if owner is None else owner * rows
        if rows % 32 == 0:
            return ref.at[pl.ds(pl.multiple_of(base + half * (rows // 2), 16), rows // 2)]
        return ref.at[pl.ds(base, rows), pl.ds(half * (cols // 2), cols // 2)]

    def sem(self, w, half, way, hop):
        return ((w * 2 + half) * 2 + way) * self.far + hop - 1

    def copy(self, w, half, way, hop, source):
        owner = self.ring.at((1 - hop) if way == 0 else (hop - 1))
        src = self.part(self.locals[w], w, half) if source else self.part(self.fulls[w], w, half, owner)
        return pltpu.make_async_remote_copy(
            src_ref=src,
            dst_ref=self.part(self.fulls[w], w, half, owner),
            send_sem=self.send.at[self.sem(w, half, way, hop)],
            recv_sem=self.recv.at[self.sem(w, half, way, hop)],
            device_id=self.ring.peer[way],
            device_id_type=MESH,
        )

    def arrival(self, w, half, way, hop):
        owner = self.ring.at(-hop if way == 0 else hop)
        dst = self.part(self.fulls[w], w, half, owner)
        return pltpu.make_async_remote_copy(
            src_ref=dst,
            dst_ref=dst,
            send_sem=self.send.at[self.sem(w, half, way, hop)],
            recv_sem=self.recv.at[self.sem(w, half, way, hop)],
            device_id=self.ring.peer[way],
            device_id_type=MESH,
        )

    def begin(self, w):
        for half in range(2):
            for way in range(2):
                if hop_count(half, way, self.ring.count) >= 1:
                    self.copy(w, half, way, 1, True).start()

    def forward(self, w, hop, last):
        for half in range(2):
            for way in range(2):
                hops = self.far if half == way else self.far - 1
                if last and hops != self.far:
                    continue
                self.arrival(w, half, way, hop).wait_recv()
                if not last:
                    more = self.far if half == way else self.far - 1
                    if more == self.far:
                        self.copy(w, half, way, hop + 1, False).start()
                    else:

                        @pl.when(hop + 1 <= more)
                        def _():
                            self.copy(w, half, way, hop + 1, False).start()

    def finish(self, w):
        for half in range(2):
            for way in range(2):
                hops = hop_count(half, way, self.ring.count)
                if hops >= 1:
                    self.copy(w, half, way, 1, True).wait_send()
                for_hops(
                    2, hops + 1, lambda hop: self.copy(w, half, way, hop, False).wait_send(), self.ring.count
                )


class Rows:
    def __init__(self, local, full, send, recv, own):
        self.tensor = lax.axis_index("tensor")
        self.dp = lax.axis_index("dp")
        self.near = self.tensor + 1 - 2 * (self.tensor % 2)
        self.across = (self.tensor + 2) % 4
        self.local, self.full, self.send, self.recv, self.own = local, full, send, recv, own
        self.rows = local.shape[0]

    def slot(self, owner, piece=None):
        if piece is None:
            return self.full.at[pl.ds(pl.multiple_of(owner * self.rows, 16), self.rows)]
        half = self.rows // 2
        return self.full.at[pl.ds(pl.multiple_of(owner * self.rows + piece * half, 16), half)]

    def remote(self, src, dst, sem, device):
        return pltpu.make_async_remote_copy(
            src_ref=src,
            dst_ref=dst,
            send_sem=self.send.at[sem],
            recv_sem=self.recv.at[sem],
            device_id=(self.dp, device),
            device_id_type=MESH,
        )

    def keep(self):
        return pltpu.make_async_copy(self.local, self.slot(self.tensor), self.own)

    def pair(self):
        return self.remote(self.local, self.slot(self.tensor), 0, self.near)

    def cross(self, piece):
        half = self.rows // 2
        return self.remote(
            self.local.at[pl.ds(piece * half, half)], self.slot(self.tensor, piece), 1 + piece, self.across
        )

    def onward(self, piece):
        here = self.slot(self.across, piece)
        return self.remote(here, here, 3 + piece, self.near)

    def begin_near(self):
        self.keep().start()
        self.pair().start()

    def begin_cross(self):
        for piece in range(2):
            self.cross(piece).start()

    def pass_piece(self, piece):
        self.cross(piece).wait_recv()
        self.onward(piece).start()

    def pass_on(self):
        for piece in range(2):
            self.pass_piece(piece)

    def finish(self):
        self.keep().wait()
        self.pair().wait()
        for piece in range(2):
            self.cross(piece).wait_send()
            self.onward(piece).wait()


def greet(devices):
    barrier = pltpu.get_barrier_semaphore()
    for device in devices:
        pl.semaphore_signal(barrier, inc=1, device_id=device, device_id_type=MESH)
    pl.semaphore_wait(barrier, len(devices))


def dot_nn(a, b):
    return lax.dot_general(a, b, (((1,), (0,)), ((), ())), preferred_element_type=f32)


def dot_nt(a, b):
    return lax.dot_general(a, b, (((1,), (1,)), ((), ())), preferred_element_type=f32)


def dot_tn(a, b):
    return lax.dot_general(a, b, (((0,), (0,)), ((), ())), preferred_element_type=f32)


def normed(x):
    average = jnp.mean(x, axis=-1, keepdims=True)
    centered = x - average
    variance = jnp.mean(centered * centered, axis=-1, keepdims=True)
    scale = lax.rsqrt(variance + 1e-05)
    return centered * scale, scale


def mixed_kernel(
    count, lim_ref, gain_ref, bias_ref, qb_ref, rot_ref, slot_ref, wd, w2, x, dy, wq, w1,
    x_out, h1_out, dyb_out, ctx_out, dproj_out, wqd_out, w1f, w2f, sum_ref, order_ref,
    xf, dyf, wf, wl, w2l, h1s, ctxs, dps, qt, kt, vt, dct, ctt, dqt, kr, vr, dkvs,
    rs, rr, ro, gs, gr, go, os,
):
    ring = Ring(count)
    pair_cols = 6 * HEAD
    half_cols = pair_cols + 2 * HEAD
    parts = [
        pltpu.make_async_copy(
            wq.at[:, pl.ds(p * pair_cols, pair_cols)], wl.at[:, pl.ds(p * half_cols, pair_cols)], os.at[p]
        )
        for p in range(2)
    ]
    for copy in parts:
        copy.start()
    turned_dense = wd[...].T
    for p in range(2):
        wl[:, p * half_cols + pair_cols : (p + 1) * half_cols] = turned_dense[:, p * 2 * HEAD : (p + 1) * 2 * HEAD]
    views = [(wl.at[:, pl.ds(p * half_cols, half_cols)], wf.at[:, pl.ds(p * half_cols, half_cols)]) for p in (0, 1)]
    views += [(w1, w1f), (w2l, w2f)]
    gather = Gather(ring, [v[0] for v in views], [v[1] for v in views], gs, gr)
    rx = Rows(x, xf, rs.at[0], rr.at[0], ro.at[0])
    ry = Rows(dy, dyf, rs.at[1], rr.at[1], ro.at[1])
    greet([ring.peer[0], ring.peer[1], (ring.me, rx.near), (ring.me, rx.across)])
    far = count // 2
    own = []
    for k, (local, full) in enumerate(((w1, w1f), (w2l, w2f))):
        rows = local.shape[0]
        own.append(
            pltpu.make_async_copy(local, full.at[pl.ds(pl.multiple_of(ring.me * rows, 16), rows)], go.at[k])
        )
    rx.begin_near()
    for copy in parts:
        copy.wait()
    gather.begin(0)
    rx.begin_cross()
    ry.begin_near()
    ry.begin_cross()
    wf[pl.ds(pl.multiple_of(ring.me * wl.shape[0], 16), wl.shape[0]), :] = wl[...]
    own[0].start()
    sum_ref[...] = jnp.zeros_like(sum_ref)
    tensor = ring.tensor
    tiles = LEN // TILE

    def whole_ring(w):
        for_hops(1, far, lambda hop: gather.forward(w, hop, False), count)
        gather.forward(w, far, True)

    def hop_at(w, hop):
        if count == 8:
            gather.forward(w, hop, hop == far)
        elif hop == 4:
            whole_ring(w)

    def rows_of(seq, i):
        return pl.ds(pl.multiple_of(seq * LEN + i * TILE, TILE), TILE)

    def norm_tile(seq, i):
        rows = rows_of(seq, i)
        xhat, _ = normed(xf[rows, :].astype(f32))
        h1s[rows, :] = (xhat * gain_ref[0:1, :] + bias_ref[0:1, :]).astype(bf16)

    def mask_tile(seq, i):
        rows = rows_of(seq, i)
        place = i * TILE + lax.broadcasted_iota(jnp.int32, (TILE, 1), 0)
        kept = jnp.where(place < lim_ref[seq], dyf[rows, :].astype(f32), 0.0)
        sum_ref[4:5, :] += jnp.sum(kept, axis=0, keepdims=True)
        dyf[rows, :] = kept.astype(bf16)

    def turned(first, second, cosine, sine):
        return first * cosine - second * sine, second * cosine + first * sine

    def prepare_tile(seq, pair, i):
        rows = rows_of(seq, i)
        cols = pl.ds(pl.multiple_of(i * TILE, TILE), TILE)
        proj = dot_nn(h1s[rows, :], wf[:, pl.ds(pl.multiple_of(pair * half_cols, BLOCK), pair_cols)])
        proj = proj + as_line(qb_ref[pl.ds(pair * (pair_cols // BLOCK), pair_cols // BLOCK), :])
        proj = proj.T
        cosine, sine = rot_ref[0:8, cols], rot_ref[8:16, cols]
        key = i * TILE + lax.broadcasted_iota(jnp.int32, (16, TILE), 1)
        row = lax.broadcasted_iota(jnp.int32, (16, TILE), 0)
        ones = jnp.where(row == 0, 1.0, 0.0).astype(bf16)
        hidden = jnp.where((row == 0) & (key >= lim_ref[seq]), masked_score, 0.0).astype(bf16)
        blank = jnp.zeros((48, TILE), bf16)
        none = jnp.zeros((HEAD, TILE), bf16)
        for hh in range(2):
            h = 2 * pair + hh
            base = 3 * HEAD * hh
            q0, q1 = turned(proj[base : base + 8], proj[base + 8 : base + 16], cosine, sine)
            q = jnp.concatenate([q0, q1, proj[base + 16 : base + HEAD]], axis=0).astype(bf16)
            q = (q.astype(f32) * 0.125).astype(bf16)
            qt[h, :, cols] = jnp.concatenate([q, ones, blank], axis=0)
            base += HEAD
            k0, k1 = turned(proj[base : base + 8], proj[base + 8 : base + 16], cosine, sine)
            k = jnp.concatenate([k0, k1, proj[base + 16 : base + HEAD]], axis=0).astype(bf16)
            kt[h, :, cols] = k
            kr[h, cols, :] = jnp.concatenate([k, hidden, blank], axis=0).T
            base += HEAD
            v = proj[base : base + HEAD].astype(bf16)
            vt[h, :, cols] = jnp.concatenate([v, ones], axis=0)
            vr[h, cols, :] = jnp.concatenate([none, v], axis=0).T

    def context_tile(seq, pair, i):
        cols = pl.ds(pl.multiple_of(i * TILE, TILE), TILE)
        begin = pair * half_cols + pair_cols
        dctx = dot_nn(dyf[rows_of(seq, i), :], wf[:, begin : begin + 2 * HEAD]).T.astype(bf16)
        for hh in range(2):
            dct[2 * pair + hh, :, cols] = dctx[HEAD * hh : HEAD * (hh + 1)]

    def back_tile(seq, i):
        mask_tile(seq, i)
        context_tile(seq, 0, i)
        context_tile(seq, 1, i)

    def attend(pair, i, fresh):
        here = slice(i * TILE, (i + 1) * TILE)
        chunks = [slice(c * TILE, (c + 1) * TILE) for c in range(i + 1)]
        heads = range(2)
        of = [2 * pair, 2 * pair + 1]
        key = lax.broadcasted_iota(jnp.int32, (TILE, TILE), 0)
        query = lax.broadcasted_iota(jnp.int32, (TILE, TILE), 1)
        q = [qt[of[hh], :, here] for hh in heads]
        scores = [[dot_nn(kr[of[hh], c, :], q[hh]) for c in chunks] for hh in heads]
        probs, grads, deltas, both = [], [], [], []
        none = jnp.zeros((HEAD, TILE), bf16)
        for hh in heads:
            scores[hh][i] = jnp.where(key <= query, scores[hh][i], masked_score)
            top = jnp.max(scores[hh][0], axis=0, keepdims=True)
            for s in scores[hh][1:]:
                top = jnp.maximum(top, jnp.max(s, axis=0, keepdims=True))
            probs.append([jnp.exp(s - top).astype(bf16) for s in scores[hh]])
        for hh in heads:
            total = dot_nn(vt[of[hh], :, chunks[0]], probs[hh][0])
            for c, p in zip(chunks[1:], probs[hh][1:]):
                total = total + dot_nn(vt[of[hh], :, c], p)
            inverse = 1.0 / total[HEAD : HEAD + 1]
            context = total[:HEAD] * inverse
            ctt[of[hh], :, here] = context
            grad = (dct[of[hh], :, here].astype(f32) * inverse).astype(bf16)
            deltas.append(jnp.sum(grad.astype(f32) * context, axis=0, keepdims=True))
            grad = jnp.concatenate([none, grad], axis=0)
            grads.append(grad)
            both.append(jnp.concatenate([jnp.concatenate([q[hh][:HEAD], none], axis=0), grad], axis=1))
        dq = [None, None]
        for n, c in enumerate(chunks):
            for hh in heads:
                p = probs[hh][n]
                dp = dot_nn(vr[of[hh], c, :], grads[hh])
                ds = (p.astype(f32) * (dp - deltas[hh])).astype(bf16)
                part = dot_nn(kt[of[hh], :, c], ds)
                dq[hh] = part if dq[hh] is None else dq[hh] + part
                dkv = dot_nt(jnp.concatenate([ds, p], axis=1), both[hh])
                if n in fresh:
                    dkvs[of[hh], c, :] = dkv
                else:
                    dkvs[of[hh], c, :] += dkv
        for hh in heads:
            dqt[of[hh], :, here] = dq[hh] * 0.125

    def collect_tile(seq, i):
        rows = rows_of(seq, i)
        cols = pl.ds(pl.multiple_of(i * TILE, TILE), TILE)
        cosine, sine = rot_ref[0:8, cols], rot_ref[8:16, cols]
        for pair in range(2):
            pieces = []
            for h in (2 * pair, 2 * pair + 1):
                dkv = dkvs[h, cols, :].T
                for grad in (dqt[h, :, cols], dkv[:HEAD]):
                    pieces += [*turned(grad[0:8], grad[8:16], cosine, -sine), grad[16:HEAD]]
                pieces.append(dkv[HEAD:])
            low = jnp.concatenate(pieces, axis=0).T.astype(bf16)
            wide = slice(pair * pair_cols, (pair + 1) * pair_cols)
            dps[rows, wide] = low
            sum_ref[5:6, wide] += jnp.sum(low.astype(f32), axis=0, keepdims=True)
            ctx = jnp.concatenate([ctt[2 * pair, :, cols], ctt[2 * pair + 1, :, cols]], axis=0).T
            ctxs[rows, pair * 2 * HEAD : (pair + 1) * 2 * HEAD] = ctx.astype(bf16)

    def save(turn, k, seq):
        src, dst = ((xf, x_out), (h1s, h1_out), (dyf, dyb_out), (ctxs, ctx_out), (dps, dproj_out))[k]
        rows = pl.ds(pl.multiple_of(seq * LEN, LEN), LEN)
        return pltpu.make_async_copy(src.at[rows], dst.at[rows], os.at[turn * 5 + k])

    mine = order_ref.shape[1]
    per = mine // count
    place = lax.broadcasted_iota(jnp.int32, (mine, 1), 0).astype(f32)
    owner = jnp.floor((place + 0.5) / per)
    wanted = (owner * 4.0 + lax.convert_element_type(tensor, f32)) * per + (place - owner * per)
    found = jnp.zeros(order_ref.shape, f32)
    for r in range(slot_ref.shape[0]):
        hit = jnp.where(slot_ref[r : r + 1, :].astype(f32) == wanted, 1.0, 0.0).astype(bf16)
        block = r * BLOCK + lax.broadcasted_iota(jnp.int32, (8, BLOCK), 1) - tensor * mine
        found = found + dot_nt(jnp.clip(block, 0, mine - 1).astype(f32).astype(bf16), hit)
    order_ref[...] = (found + 0.5).astype(jnp.int32)

    seq = tensor // 2
    rx.keep().wait()
    rx.pair().wait_recv()

    @pl.loop(0, tiles)
    def _(i):
        norm_tile(seq, i)

        @pl.when(i == 0)
        def _():
            hop_at(0, 1)
            gather.begin(1)

        @pl.when(i == 1)
        def _():
            hop_at(0, 2)
            hop_at(1, 1)

        @pl.when(i == 2)
        def _():
            hop_at(0, 3)
            hop_at(1, 2)
            gather.begin(2)

    save(0, 0, seq).start()
    save(0, 1, seq).start()
    w2l[...] = w2[...].T
    hop_at(0, 4)
    ry.keep().wait()
    ry.pair().wait_recv()

    @pl.loop(0, tiles // 4)
    def _(i):
        for sub in range(4):
            prepare_tile(seq, 0, 4 * i + sub)


    @pl.loop(0, tiles)
    def _(i):
        mask_tile(seq, i)
        context_tile(seq, 0, i)

    save(0, 2, seq).start()

    @pl.loop(0, 2)
    def _(pair):
        @pl.when(pair == 1)
        def _():
            hop_at(1, 4)
            hop_at(2, 1)

            @pl.loop(0, tiles // 4)
            def _(i):
                for sub in range(4):
                    prepare_tile(seq, 1, 4 * i + sub)
                    context_tile(seq, 1, 4 * i + sub)

        attend(pair, 3, (0, 1, 2, 3))

        @pl.when(pair == 0)
        def _():
            hop_at(1, 3)
            gather.begin(3)
            own[1].start()

        attend(pair, 2, ())

        @pl.when(pair == 0)
        def _():
            rx.pass_on()

        @pl.when(pair == 1)
        def _():
            hop_at(3, 1)

        attend(pair, 1, ())
        attend(pair, 0, ())

    @pl.loop(0, tiles)
    def _(i):
        collect_tile(seq, i)

    save(0, 3, seq).start()
    save(0, 4, seq).start()
    keep = pltpu.make_async_copy(wf, wqd_out, os.at[10])
    keep.start()

    seq = 1 - seq
    for piece in range(2):
        rx.onward(piece).wait_recv()

    @pl.loop(0, tiles)
    def _(i):
        norm_tile(seq, i)

    save(1, 0, seq).start()
    save(1, 1, seq).start()
    ry.pass_piece(0)

    for pair in range(2):

        @pl.loop(0, tiles // 4)
        def _(i):
            for sub in range(4):
                prepare_tile(seq, pair, 4 * i + sub)

        if pair == 0:
            hop_at(2, 2)

    ry.onward(0).wait()
    back_tile(seq, 0)
    back_tile(seq, 2)

    @pl.loop(0, 2)
    def _(pair):
        attend(pair, 2, (0, 1, 2))

        @pl.when(pair == 0)
        def _():
            hop_at(3, 2)

        attend(pair, 0, ())

    ry.pass_piece(1)
    ry.onward(1).wait()
    back_tile(seq, 1)
    back_tile(seq, 3)
    save(1, 2, seq).start()
    hop_at(2, 3)

    @pl.loop(0, 2)
    def _(pair):
        attend(pair, 3, (3,))

        @pl.when(pair == 1)
        def _():
            hop_at(3, 3)

        attend(pair, 1, ())

    @pl.loop(0, tiles)
    def _(i):
        collect_tile(seq, i)

    save(1, 3, seq).start()
    save(1, 4, seq).start()
    hop_at(2, 4)
    hop_at(3, 4)
    for w in range(4):
        gather.finish(w)
    own[0].wait()
    own[1].wait()
    rx.pair().wait_send()
    ry.pair().wait_send()
    for piece in range(2):
        rx.cross(piece).wait_send()
        rx.onward(piece).wait_send()
        ry.cross(piece).wait_send()
    for turn in range(2):
        for k in range(5):
            save(turn, k, turn + (1 - 2 * turn) * (tensor // 2)).wait()
    keep.wait()


def mixed_all(count, limits, gains, biases, qkv_bias, rot, slots, x, dy, wq, wd, w1, w2):
    far = count // 2
    rows, width = 4 * x.shape[0], x.shape[1]
    ctx_cols, proj_cols = wd.shape[0], wq.shape[1]
    shard = wq.shape[0]
    out = lambda r, c: jax.ShapeDtypeStruct((r, c), bf16)
    any_, vmem = pl.BlockSpec(memory_space=pl.ANY), pl.BlockSpec(memory_space=pltpu.VMEM)
    dma = lambda *n: pltpu.SemaphoreType.DMA(n)
    buf = lambda dtype, *shape: pltpu.VMEM(shape, dtype)
    heads, both = 4, ctx_cols + proj_cols
    return pl.pallas_call(
        functools.partial(mixed_kernel, count),
        out_shape=[
            out(rows, width), out(rows, width), out(rows, width), out(rows, ctx_cols), out(rows, proj_cols),
            out(width, both), out(width, w1.shape[1]), out(width, w2.shape[0]),
            jax.ShapeDtypeStruct((8, width), f32), jax.ShapeDtypeStruct((8, slots.size // 4), jnp.int32),
        ],
        in_specs=[pl.BlockSpec(memory_space=pltpu.SMEM)] + [vmem] * 7 + [any_] * 4,
        out_specs=[any_] * 8 + [vmem] * 2,
        scratch_shapes=[
            buf(bf16, rows, width), buf(bf16, rows, width), buf(bf16, width, both),
            buf(bf16, shard, both), buf(bf16, shard, w2.shape[0]),
            buf(bf16, rows, width), buf(bf16, rows, ctx_cols), buf(bf16, rows, proj_cols),
            buf(bf16, heads, 2 * HEAD, LEN), buf(bf16, heads, HEAD, LEN), buf(bf16, heads, HEAD + 16, LEN),
            buf(bf16, heads, HEAD, LEN), buf(f32, heads, HEAD, LEN), buf(f32, heads, HEAD, LEN),
            buf(bf16, heads, LEN, 2 * HEAD), buf(bf16, heads, LEN, 2 * HEAD), buf(f32, heads, LEN, 2 * HEAD),
            dma(2, 5), dma(2, 5), dma(2), dma(16 * far), dma(16 * far), dma(2), dma(11),
        ],
        compiler_params=pltpu.CompilerParams(
            collective_id=0, has_side_effects=True, vmem_limit_bytes=VMEM_LIMIT
        ),
        cost_estimate=pl.CostEstimate(flops=int(2e10), bytes_accessed=int(4e7), transcendentals=int(1e7)),
        name="mixed_all",
    )(limits, gains, biases, qkv_bias, rot, slots, wd, w2, x, dy, wq, w1)


def gelu_both(x):
    phi = 0.5 + 0.5 * lax.erf(x * (1.0 / math.sqrt(2.0)))
    bell = jnp.exp(-0.5 * x * x) * (1.0 / math.sqrt(2.0 * math.pi))
    return x * phi, phi + x * bell


class Scatter:
    def __init__(self, ring, order, blocks, out, sbuf, rbuf, send, recv):
        self.ring, self.order, self.blocks, self.out = ring, order, blocks, out
        self.sbuf, self.rbuf, self.send, self.recv = sbuf, rbuf, send, recv
        self.per = out.shape[0]
        self.together = 6 if self.per % 6 == 0 else 1
        self.far = ring.count // 2

    def index(self, half, way, hop):
        return (half * 2 + way) * self.far + hop - 1

    def copy(self, half, way, hop, first):
        i = self.index(half, way, hop)
        return pltpu.make_async_remote_copy(
            src_ref=self.sbuf.at[half * 2 + way] if first else self.rbuf.at[i - 1],
            dst_ref=self.rbuf.at[i],
            send_sem=self.send.at[i],
            recv_sem=self.recv.at[i],
            device_id=self.ring.peer[way],
            device_id_type=MESH,
        )

    def own(self, dest, half, k):
        return self.blocks[self.order[0, dest * self.per + k], half * 64 : half * 64 + 64, :]

    def step(self, half, way, hop, first):
        hops = hop_count(half, way, self.ring.count)
        dest = self.ring.at((hops + 1 - hop) if way == 0 else (hop - hops - 1))
        i = self.index(half, way, hop)
        if not first:
            self.copy(half, way, hop - 1, True).wait_recv()

        def one(k, carry):
            value = self.own(dest, half, k)
            if first:
                self.sbuf[half * 2 + way, k] = value
            else:
                self.rbuf[i - 1, k] = (value.astype(f32) + self.rbuf[i - 1, k].astype(f32)).astype(bf16)
            return carry

        lax.fori_loop(0, self.per, one, 0, unroll=self.together)
        self.copy(half, way, hop, first).start()

    def last(self, half, scale):
        came = []
        for way in range(2):
            hops = hop_count(half, way, self.ring.count)
            if hops >= 1:
                self.copy(half, way, hops, True).wait_recv()
                came.append(self.index(half, way, hops))
        me = self.ring.me

        def one(k, carry):
            value = self.own(me, half, k).astype(f32)
            for i in came:
                value = value + self.rbuf[i, k].astype(f32)
            self.out[k, half * 64 : half * 64 + 64, :] = value * scale
            return carry

        lax.fori_loop(0, self.per, one, 0, unroll=self.together)

    def finish(self):
        for half in range(2):
            for way in range(2):
                hops = hop_count(half, way, self.ring.count)
                for_hops(
                    1, hops + 1, lambda hop: self.copy(half, way, hop, True).wait_send(), self.ring.count
                )


class RowSum:
    def __init__(self, parts, r1, base, r2, send, recv):
        self.tensor = lax.axis_index("tensor")
        self.dp = lax.axis_index("dp")
        self.near = self.tensor + 1 - 2 * (self.tensor % 2)
        self.across = (self.tensor + 2) % 4
        self.r2, self.send, self.recv = r2, send, recv
        self.rows = r2.shape[0]
        self.parts = [parts.at[pl.ds(k * self.rows, self.rows)] for k in range(4)]
        self.r1 = [r1.at[pl.ds((base + k) * self.rows, self.rows)] for k in range(2)]

    def remote(self, src, dst, sem, device):
        return pltpu.make_async_remote_copy(
            src_ref=src, dst_ref=dst, send_sem=self.send.at[sem], recv_sem=self.recv.at[sem],
            device_id=(self.dp, device), device_id_type=MESH,
        )

    def pair(self, k):
        return self.remote(self.parts[2 * k], self.r1[k], k, self.near)

    def cross(self):
        return self.remote(self.parts[1], self.r2, 2, self.across)

    def middle(self):
        self.pair(0).wait_recv()
        self.parts[1][...] = (self.parts[1][...].astype(f32) + self.r1[0][...].astype(f32)).astype(bf16)

    def end(self, stage, out, sem):
        self.pair(1).wait_recv()
        self.cross().wait_recv()
        step = stage.shape[1]
        copies = []
        for k in range(self.rows // step):
            at = pl.ds(k * step, step)
            if k >= 2:
                copies[k - 2].wait()
            stage[k % 2] = (
                self.parts[3][at, :].astype(f32) + self.r1[1][at, :].astype(f32) + self.r2[at, :].astype(f32)
            )
            copies.append(pltpu.make_async_copy(stage.at[k % 2], out.at[at], sem.at[k % 2]))
            copies[-1].start()
        for copy in copies[-2:]:
            copy.wait()

    def finish(self):
        self.pair(0).wait_send()
        self.pair(1).wait_send()
        self.cross().wait_send()


def tail_kernel(
    count, scale, order, gain_ref, bias_ref, fb_ref, small_a, x, h1, dyb, ctx, dproj, wqd, w1, w2,
    grad_out, small_sum, br_out, e_out,
    grad, xs, h1s, dys, cs, ps, wqds, w1s, w2s, h2s, acts, dabs, gs, sbuf, rbuf, r2, stage, small, t_in, d_in, d_out,
    sem, late_sem, ss, sr, rs, rr, ts, tr, ds, dr, os, gsem, free,
):
    ring = Ring(count)
    me, tensor = ring.me, ring.tensor
    rows = r2.shape[1]
    tiles = x.shape[0] // WIDE
    near = tensor + 1 - 2 * (tensor % 2)

    barrier = pltpu.get_barrier_semaphore()
    for step in range(1, 4):
        pl.semaphore_signal(barrier, inc=1, device_id=(me, (tensor + step) % 4), device_id_type=MESH)

    @pl.loop(1, count)
    def _(step):
        pl.semaphore_signal(barrier, inc=1, device_id=((me + step) % count, tensor), device_id_type=MESH)

    def tile_copy(k, src, dst, i):
        at = pl.ds(pl.multiple_of(i * WIDE, WIDE), WIDE)
        return pltpu.make_async_copy(src.at[at], dst.at[at], sem.at[k, i])

    late = [
        pltpu.make_async_copy(src, dst, late_sem.at[k])
        for k, (src, dst) in enumerate(((w1, w1s), (w2, w2s), (h1, h1s), (ctx, cs), (dproj, ps), (wqd, wqds)))
    ]
    late[0].start()
    tile_copy(0, x, xs, 0).start()
    late[1].start()
    tile_copy(1, dyb, dys, 0).start()
    for i in range(1, tiles):
        tile_copy(0, x, xs, i).start()
        tile_copy(1, dyb, dys, i).start()
    for copy in late[2:]:
        copy.start()
    small[...] = small_a[...]
    late[0].wait()
    late[1].wait()

    hidden = w1.shape[1]

    @pl.loop(0, tiles)
    def _(i):
        at = pl.ds(pl.multiple_of(i * WIDE, WIDE), WIDE)
        tile_copy(0, x, xs, i).wait()
        tile_copy(1, dyb, dys, i).wait()
        xhat, _ = normed(xs[at, :].astype(f32))
        h2s[at, :] = (xhat * gain_ref[1:2, :] + bias_ref[1:2, :]).astype(bf16)
        for c in range(1):
            wide = slice(0, hidden)
            pre = dot_nn(h2s[at, :], w1s[:, wide]) + as_line(fb_ref[...])[:, wide]
            da = dot_nn(dys[at, :], w2s[:, wide])
            act, slope = gelu_both(pre)
            acts[at, wide] = act.astype(bf16)
            dab = (da * slope).astype(bf16)
            dabs[at, wide] = dab
            small[6:7, wide] += jnp.sum(dab.astype(f32), axis=0, keepdims=True)

    for copy in late[2:5]:
        copy.wait()
    base = 0
    for left, right in ((h1s, ps), (cs, dys), (h2s, dabs), (acts, dys)):
        tall = min(WIDE, left.shape[1])
        jobs, per_row = left.shape[1] // tall, right.shape[1] // BLOCK
        blocks = tall // BLOCK * per_row

        @pl.loop(0, jobs)
        def _(j):
            found = dot_tn(left[:, pl.ds(pl.multiple_of(j * tall, tall), tall)], right[...]).astype(bf16)
            start = base + j * blocks
            for r in range(tall // BLOCK):
                for c in range(per_row):
                    gs[start + r * per_row + c] = found[
                        r * BLOCK : (r + 1) * BLOCK, c * BLOCK : (c + 1) * BLOCK
                    ]

        base += jobs * blocks

    pl.semaphore_wait(barrier, 3 + count - 1)
    pl.semaphore_signal(free, inc=1, device_id=(me, near), device_id_type=MESH)
    scatter = Scatter(ring, order, gs, grad, sbuf, rbuf, ss, sr)
    kept = (h2s, dys)
    sums = [RowSum(kept[n], h1s, 2 * n, r2.at[n], rs.at[n], rr.at[n]) for n in range(2)]

    def t_copy(step):
        return pltpu.make_async_remote_copy(
            src_ref=small, dst_ref=t_in.at[tensor], send_sem=ts.at[step], recv_sem=tr.at[step],
            device_id=(me, (tensor + step) % 4), device_id_type=MESH,
        )

    def d_copy(step):
        return pltpu.make_async_remote_copy(
            src_ref=d_out, dst_ref=d_in.at[me], send_sem=ds.at[step], recv_sem=dr.at[step],
            device_id=((me + step) % count, tensor), device_id_type=MESH,
        )

    far = count // 2
    first, second = ((0, 0), (1, 1)), ((1, 0), (0, 1))
    for half, way in first + second:
        if hop_count(half, way, count) >= 1:
            scatter.step(half, way, 1, True)

    def ring_step(hop, which):
        for half, way in which:
            if which is first:
                scatter.step(half, way, hop, False)
            else:

                @pl.when(hop <= far - 1)
                def _():
                    scatter.step(half, way, hop, False)

    wide, thin = 6 * HEAD, 2 * HEAD
    total = lambda v: jnp.sum(v, axis=0, keepdims=True)

    def work(n, r):
        owner = (near * (1 - n % 2) + tensor * (n % 2) + 2 * (1 - n // 2)) % 4
        at = pl.ds(pl.multiple_of(owner * rows + r * TILE, TILE), TILE)
        to = pl.ds(pl.multiple_of(n * rows + r * TILE, TILE), TILE)
        br = dot_nt(acts[at, :], w2s[...])
        dh1 = None
        for p in range(2):
            lo = p * (wide + thin)
            br = br + dot_nt(cs[at, p * thin : (p + 1) * thin], wqds[:, lo + wide : lo + wide + thin])
            part = dot_nt(ps[at, p * wide : (p + 1) * wide], wqds[:, lo : lo + wide])
            dh1 = part if dh1 is None else dh1 + part
        kept[0][to, :] = br.astype(bf16)
        dh2 = dot_nt(dabs[at, :], w1s[...])
        xhat, _ = normed(xs[at, :].astype(f32))
        kept[1][to, :] = (dh1 * gain_ref[0:1, :] + dh2 * gain_ref[1:2, :]).astype(bf16)
        small[0:1, :] += total(dh1 * xhat)
        small[1:2, :] += total(dh2 * xhat)
        small[2:3, :] += total(dh1)
        small[3:4, :] += total(dh2)

    late[5].wait()
    @pl.loop(0, 4)
    def _(n):
        @pl.loop(0, rows // TILE)
        def _(r):
            work(n, r)

        @pl.when(n == 0)
        def _():
            pl.semaphore_wait(free, 1)
            for s in sums:
                s.pair(0).start()

        @pl.when(n == 1)
        def _():
            for s in sums:
                s.middle()
            sums[0].cross().start()
            if far >= 2 and count <= 8:
                ring_step(2, first)

        @pl.when(n == 2)
        def _():
            for s in sums:
                s.pair(1).start()

        @pl.when(n == 3)
        def _():
            if far >= 2 and count <= 8:
                ring_step(2, second)

    for step in range(1, 4):
        t_copy(step).start()
    sums[1].cross().start()

    def both(hop):
        ring_step(hop, first)
        ring_step(hop, second)

    if count <= 8:
        both(3)
    else:
        for_hops(2, far + 1, both, count)
    for step in range(1, 4):
        t_copy(step).wait_recv()
    t_in[tensor] = small[...]
    row = lax.broadcasted_iota(jnp.int32, small.shape, 0)
    summed = t_in[0] + t_in[1] + t_in[2] + t_in[3]
    d_out[...] = jnp.where(row < 4, summed, small[...])

    @pl.loop(1, count)
    def _(step):
        d_copy(step).start()

    if count <= 8:
        both(4)
    sums[0].end(stage, br_out, os)

    @pl.loop(1, count)
    def _(step):
        d_copy(step).wait_recv()

    d_in[me] = d_out[...]
    small_sum[...] = scale * lax.fori_loop(1, count, lambda k, acc: acc + d_in[k], d_in[0])
    sums[1].end(stage, e_out, os)
    parts_out = []
    for half in range(2):
        scatter.last(half, scale)
        at = pl.ds(half * 64, 64)
        parts_out.append(pltpu.make_async_copy(grad.at[:, at], grad_out.at[:, at], gsem.at[half]))
        parts_out[-1].start()
    scatter.finish()
    for s in sums:
        s.finish()
    for step in range(1, 4):
        t_copy(step).wait_send()

    @pl.loop(1, count)
    def _(step):
        d_copy(step).wait_send()

    for copy in parts_out:
        copy.wait()


def tail_all(count, scale, order, gains, biases, fc1_bias, small, x, h1, dyb, ctx, dproj, wqd, w1, w2):
    rows, width = x.shape[0] // 4, x.shape[1]
    hidden = w1.shape[1]
    blocks = (width * (dproj.shape[1] + hidden) + (ctx.shape[1] + hidden) * width) // (BLOCK * BLOCK)
    per = blocks // count
    far = count // 2
    any_, vmem = pl.BlockSpec(memory_space=pl.ANY), pl.BlockSpec(memory_space=pltpu.VMEM)
    dma = lambda *n: pltpu.SemaphoreType.DMA(n)
    like = lambda v: pltpu.VMEM(v.shape, v.dtype)
    sum_shape = jax.ShapeDtypeStruct((rows, width), f32)
    tall = lambda cols: pltpu.VMEM((x.shape[0], cols), bf16)
    return pl.pallas_call(
        functools.partial(tail_kernel, count, scale),
        out_shape=[
            jax.ShapeDtypeStruct((per, BLOCK, BLOCK), f32), jax.ShapeDtypeStruct(small.shape, f32),
            sum_shape, sum_shape,
        ],
        in_specs=[pl.BlockSpec(memory_space=pltpu.SMEM)] + [vmem] * 4 + [any_] * 8,
        out_specs=[any_, vmem, any_, any_],
        scratch_shapes=[pltpu.VMEM((per, BLOCK, BLOCK), f32)]
        + [like(v) for v in (x, h1, dyb, ctx, dproj, wqd, w1, w2)]
        + [
            tall(width), tall(hidden), tall(hidden), pltpu.VMEM((blocks, BLOCK, BLOCK), bf16),
            pltpu.VMEM((4, per, 64, BLOCK), bf16), pltpu.VMEM((4 * far, per, 64, BLOCK), bf16),
            pltpu.VMEM((2, rows, width), bf16), pltpu.VMEM((2, 64, width), f32),
            pltpu.VMEM(small.shape, f32), pltpu.VMEM((4,) + small.shape, f32),
            pltpu.VMEM((count,) + small.shape, f32), pltpu.VMEM(small.shape, f32),
            dma(2, x.shape[0] // WIDE), dma(6),
            dma(4 * far), dma(4 * far), dma(2, 3), dma(2, 3), dma(4), dma(4), dma(count), dma(count),
            dma(2), dma(2), pltpu.SemaphoreType.REGULAR,
        ],
        compiler_params=pltpu.CompilerParams(
            collective_id=1, has_side_effects=True, vmem_limit_bytes=VMEM_LIMIT
        ),
        cost_estimate=pl.CostEstimate(flops=int(3.5e10), bytes_accessed=int(4e7), transcendentals=int(4e6)),
        name="tail_all",
    )(order, gains, biases, fc1_bias, small, x, h1, dyb, ctx, dproj, wqd, w1, w2)


def finish_kernel(
    steps, lim_ref, bias_ref, small_ref, racc_ref, qacc_ref, facc_ref, grad, tok, dy, br, e, ls, rs, lr, rr,
    gout, out, dx, lout, rout, cout, racc, rupd, qacc, qupd, facc, fupd,
    g_v, tok_v, dy_v, br_v, e_v, ls_v, rs_v, lr_v, rr_v, out_v, dx_v, lo_v, ro_v, co_v, isem, osem,
):
    tensor = lax.axis_index("tensor")
    own_rows, blocks = tok.shape[0], grad.shape[0]
    rows, some = own_rows // steps, blocks // steps
    ins = [(grad, g_v), (ls, ls_v), (rs, rs_v), (lr, lr_v), (rr, rr_v), (tok, tok_v), (dy, dy_v), (br, br_v), (e, e_v)]
    outs = [(g_v, gout), (lo_v, lout), (ro_v, rout), (co_v, cout), (out_v, out), (dx_v, dx)]

    def span(ref, s):
        size = ref.shape[0] // steps
        return ref.at[pl.ds(s * size if ref.shape[0] == blocks else pl.multiple_of(s * size, 16), size)]

    def fetch(k, s):
        return pltpu.make_async_copy(span(ins[k][0], s), span(ins[k][1], s), isem.at[k, s])

    def store(k, s):
        return pltpu.make_async_copy(span(outs[k][0], s), span(outs[k][1], s), osem.at[k, s])

    for s in range(steps):
        for k in range(len(ins)):
            fetch(k, s).start()
    small = small_ref[...]

    def adagrad(grad_vec, accum, new, update):
        accum_next = accum + grad_vec * grad_vec
        new[...] = accum_next
        update[...] = -adagrad_rate * grad_vec * lax.rsqrt(accum_next)

    def stacked(line, count):
        return jnp.concatenate([line[:, k * BLOCK : (k + 1) * BLOCK] for k in range(count)], axis=0)

    adagrad(jnp.concatenate([small[0:5], small[4:5]], axis=0), racc_ref[...], racc, rupd)
    adagrad(stacked(small[5:6], qacc.shape[0]), qacc_ref[...], qacc, qupd)
    adagrad(stacked(small[6:7], facc.shape[0]), facc_ref[...], facc, fupd)
    shift = bias_ref[2:3, :] + bias_ref[3:4, :]

    @pl.loop(0, steps)
    def _(s):
        for k in range(len(ins)):
            fetch(k, s).wait()

        for b in range(some):
            k = s * some + b
            low = g_v[k].astype(bf16)
            lo_v[k] = stat_decay * ls_v[k] + (1.0 - stat_decay) * dot_nt(low, low)
            ro_v[k] = stat_decay * rs_v[k] + (1.0 - stat_decay) * dot_tn(low, low)
            pushed = dot_nn(lr_v[k].astype(bf16), low).astype(bf16)
            co_v[k] = -shampoo_rate * dot_nn(pushed, rr_v[k].astype(bf16))

        at = pl.ds(pl.multiple_of(s * rows, 16), rows)
        x = tok_v[at, :].astype(f32)
        out_v[at, :] = (x + br_v[at, :] + shift).astype(bf16)
        start = tensor * own_rows + s * rows
        place = start % LEN + lax.broadcasted_iota(jnp.int32, (rows, 1), 0)
        kept = jnp.where(place < lim_ref[start // LEN], dy_v[at, :].astype(f32), 0.0)
        xhat, scale = normed(x)
        v = e_v[at, :]
        dx_v[at, :] = kept + scale * (
            v - jnp.mean(v, axis=-1, keepdims=True) - xhat * jnp.mean(v * xhat, axis=-1, keepdims=True)
        )
        for k in range(len(outs)):
            store(k, s).start()

    for s in range(steps):
        for k in range(len(outs)):
            store(k, s).wait()


def finish_all(limits, biases, small, racc, qacc, facc, grad, tok, dy, br, e, ls, rs, lr, rr):
    steps = 8 if grad.shape[0] % 8 == 0 else 1
    any_, vmem = pl.BlockSpec(memory_space=pl.ANY), pl.BlockSpec(memory_space=pltpu.VMEM)
    shape = lambda v: jax.ShapeDtypeStruct(v.shape, v.dtype)
    like = lambda v: pltpu.VMEM(v.shape, v.dtype)
    vectors = [racc, racc, qacc, qacc, facc, facc]
    return pl.pallas_call(
        functools.partial(finish_kernel, steps),
        out_shape=[shape(grad), shape(tok), shape(e)] + [shape(grad)] * 3 + [shape(v) for v in vectors],
        in_specs=[pl.BlockSpec(memory_space=pltpu.SMEM)] + [vmem] * 5 + [any_] * 9,
        out_specs=[any_] * 6 + [vmem] * 6,
        scratch_shapes=[like(v) for v in (grad, tok, dy, br, e, ls, rs, lr, rr, tok, e, ls, ls, ls)]
        + [pltpu.SemaphoreType.DMA((9, steps)), pltpu.SemaphoreType.DMA((6, steps))],
        compiler_params=pltpu.CompilerParams(vmem_limit_bytes=VMEM_LIMIT),
        cost_estimate=pl.CostEstimate(flops=int(4e8), bytes_accessed=int(2e7), transcendentals=0),
        name="finish_all",
    )(limits, biases, small, racc, qacc, facc, grad, tok, dy, br, e, ls, rs, lr, rr)


def shards(
    tokens, out_grad, seq_lengths, norm_gains, row_biases, qkv_weight, qkv_bias, dense_weight, fc1_weight,
    fc1_bias, fc2_weight, block_slot, left_stat, right_stat, left_root, right_root, row_accum,
    qkv_bias_accum, fc1_bias_accum,
):
    tensor_count = lax.axis_size("tensor")
    dp_count = lax.axis_size("dp")
    grad_scale = 1.0 / math.sqrt(tokens.shape[0] * tensor_count * dp_count)
    xf, h1, dyb, ctx, dproj, wqdf, w1f, w2f, sum_a, order = mixed_all(
        dp_count, seq_lengths, norm_gains, row_biases, as_rows(qkv_bias), jnp.asarray(rotary_rows()),
        as_rows(block_slot), tokens, out_grad, qkv_weight, dense_weight, fc1_weight, fc2_weight,
    )
    own_grad, small, branch, e_sum = tail_all(
        dp_count, grad_scale, order, norm_gains, row_biases, as_rows(fc1_bias), sum_a,
        xf, h1, dyb, ctx, dproj, wqdf, w1f, w2f,
    )
    outs = finish_all(
        seq_lengths, row_biases, small, row_accum, as_rows(qkv_bias_accum), as_rows(fc1_bias_accum),
        own_grad, tokens, out_grad, branch, e_sum, left_stat, right_stat, left_root, right_root,
    )
    block_grad, layer_out, input_grad, left_new, right_new, change = outs[:6]
    return (
        layer_out, input_grad, block_grad, left_new, right_new, change,
        *outs[6:8], *(v.reshape(-1) for v in outs[8:]),
    )


def solution(mesh):
    both = ("dp", "tensor")
    return jax.shard_map(
        shards,
        mesh=mesh,
        in_specs=(
            P(both, None), P(both, None), P("dp"), P(), P(), P("dp", "tensor"), P("tensor"),
            P("tensor", "dp"), P("dp", "tensor"), P("tensor"), P("tensor", "dp"), P(),
            P(both, None, None), P(both, None, None), P(both, None, None), P(both, None, None),
            P(), P("tensor"), P("tensor"),
        ),
        out_specs=(
            P(both, None), P(both, None), P(both, None, None), P(both, None, None),
            P(both, None, None), P(both, None, None), P(), P(), P("tensor"), P("tensor"),
            P("tensor"), P("tensor"),
        ),
        check_vma=False,
    )
```
